32 devices in a mesh: section: 4 (over y, x), dp: 8 (over z, core).
Axes of the slice: x: 2, y: 2, z: 4, core: 2. Of those that a mesh axis runs over, the one named last changes fastest.
Arguments:
- images: bfloat16 [4, 8, 8, 24, 512], P(None, 'dp')
- image_group: int32 [4, 8], P(None, 'dp'), may hold values from 0 to 2, as said below
- group_size: int32 [3, 2], replicated, may hold values from 4 to 24, as said below
- conv_weight: bfloat16 [4, 512, 3, 3, 512], P('section'), may hold values from -0.09375 to 0.09375
- bn_gain: float32 [4, 512], P('section'), may hold values from 0.1 to 1.9
- bn_bias: float32 [4, 512], P('section'), may hold values from -3 to 3
- cotangent: bfloat16 [4, 8, 8, 24, 512], P(None, 'dp'), may hold values from -6 to 6
Outputs:
- activations: bfloat16 [4, 8, 8, 24, 512], P('section', 'dp')
- input_grad: bfloat16 [4, 8, 8, 24, 512], P('section', 'dp')
- weight_grad: float32 [4, 512, 3, 3, 512], P('section', 'dp')
- gain_grad: float32 [4, 512], P('section', 'dp')
- bias_grad: float32 [4, 512], P('section', 'dp')
The draws below stay inside these ranges and needn't reach their ends.
Inputs may be any that keep to these rules, and one draw needn't show every extreme that they name: `image_group`: in every micro-batch some image is of group 0. `group_size`: row g holds the height and the width of group g; group 0 fills the canvas, 8 by 24; heights are at least 4 and widths at least 12.
All inputs are finite; a program needn't handle non-finite values.
Results may differ from the reference program's by a relative error of at most 0.04.
Values may be sent and summed in bfloat16 or wider, within the bound.
No kernel may reach another device: no remote copies, remote signals or barrier semaphores. Data moves between devices by JAX's collectives and lax.ppermute only.
A program may use at most 256 MiB of HBM per device.

```python
from functools import partial
import jax
import jax.numpy as jnp
from jax import lax

C = 512
CH = 8
CW = 24
MICRO = 4
CONVS = 2
GROUPS = 3
LAYERS = 4
IMAGES = 8


def draw_images(key, part):
    key = jax.random.fold_in(key, 11)
    noise_key, scale_key, shift_key = jax.random.split(key, 3)
    full_shape = (MICRO, IMAGES, CH, CW, C)
    noise = jax.random.normal(noise_key, full_shape, jnp.float32)
    spread = jnp.exp(jax.random.uniform(scale_key, (MICRO, IMAGES), jnp.float32, -0.4, 0.4))
    offset = 0.5 * jax.random.normal(shift_key, (MICRO, IMAGES, C), jnp.float32)
    ramp_scale = jnp.power(3.0, jnp.arange(IMAGES, dtype=jnp.float32) / max(IMAGES - 1, 1))
    values = (noise + offset[:, :, None, None, :]) * (spread * ramp_scale)[:, :, None, None, None]
    return values.astype(jnp.bfloat16)


def draw_image_group(key, part):
    key = jax.random.fold_in(key, 23)
    main_key, other_key, mixing_key, full_key = jax.random.split(key, 4)
    main_group = jax.random.randint(main_key, (MICRO, 1), 0, GROUPS)
    other_group = jax.random.randint(other_key, (MICRO, IMAGES), 0, GROUPS)
    mixing = jax.random.randint(mixing_key, (MICRO, IMAGES), 0, 4)
    chosen = jnp.where(mixing == 0, other_group, main_group)
    full_slot = jax.random.randint(full_key, (MICRO, 1), 0, IMAGES)
    positions = jnp.arange(IMAGES, dtype=jnp.int32)[None, :]
    return jnp.where(positions == full_slot, 0, chosen).astype(jnp.int32)


def draw_group_size(key, part):
    key = jax.random.fold_in(key, 37)
    tall_key, wide_key = jax.random.split(key)
    heights = jax.random.randint(tall_key, (GROUPS,), CH // 2, CH + 1)
    widths = jax.random.randint(wide_key, (GROUPS,), CW // 2, CW + 1)
    leading = jnp.arange(GROUPS) == 0
    heights = jnp.where(leading, CH, heights)
    widths = jnp.where(leading, CW, widths)
    return jnp.stack([heights, widths], axis=1).astype(jnp.int32)


def block_scale(stream_key, shape, shards, least, top_value):
    gain, own = 1.0, jax.random.fold_in(stream_key, 6)
    for axis_at, blocks in shards:
        steps = jnp.exp(jax.random.uniform(jax.random.fold_in(own, axis_at), (blocks,), jnp.float32, least / len(shards), top_value / len(shards)))
        gain = gain * jnp.repeat(steps, shape[axis_at] // blocks).reshape([-1 if axis == axis_at else 1 for axis in range(len(shape))])
    return gain


def bell_draw(own_key, extent, scale, bound, cuts=(), kind=jnp.bfloat16):
    array = scale * jax.random.normal(own_key, extent, jnp.float32)
    if cuts:
        array = array * block_scale(own_key, extent, cuts, -0.22, 0.18)
    return jnp.clip(array, -bound, bound).astype(kind)


def setup_inputs(seed: int = 0) -> dict:
    arg_keys = jax.random.split(jax.random.key(seed), 8)
    images = draw_images(jax.random.fold_in(arg_keys[7], 71), 0)
    image_group = draw_image_group(jax.random.fold_in(arg_keys[7], 71), 0)
    group_size = draw_group_size(jax.random.fold_in(arg_keys[7], 71), 0)
    conv_weight = bell_draw(arg_keys[3], (LAYERS, C, 3, 3, C), (9 * C) ** -0.5, 0.09375, ((0, 4),))
    bn_gain = jnp.clip(1.0 + 0.18 * jax.random.normal(arg_keys[4], (LAYERS, C), jnp.float32), 0.1, 1.9)
    bn_bias = bell_draw(arg_keys[5], (LAYERS, C), 0.5, 3.0, ((0, 4),), jnp.float32)
    cotangent = bell_draw(arg_keys[6], (MICRO, IMAGES, CH, CW, C), 1.0, 6.0, ((1, 8),))
    return dict(images=images, image_group=image_group, group_size=group_size, conv_weight=conv_weight, bn_gain=bn_gain, bn_bias=bn_bias, cotangent=cotangent)


eps = 1e-05

@jax.custom_vjp
def low(v):
    return lax.optimization_barrier(v.astype(jnp.bfloat16)).astype(jnp.float32)

@jax.custom_vjp
def low_back(v):
    return v

def low_keep(v):
    return (low(v), None)

def low_pass(kept, grad):
    return (grad,)

def back_keep(v):
    return (v, None)

def back_low(kept, grad):
    return (low(grad),)
low.defvjp(low_keep, low_pass)
low_back.defvjp(back_keep, back_low)

def canvas_mask(image_group, group_size, canvas_rows, canvas_cols):
    groups_n = group_size.shape[0]
    onehot = image_group[..., None] == jnp.arange(groups_n, dtype=jnp.int32)
    height = lax.optimization_barrier(jnp.sum(jnp.where(onehot, group_size[:, 0], 0), axis=-1))
    breadth = lax.optimization_barrier(jnp.sum(jnp.where(onehot, group_size[:, 1], 0), axis=-1))
    inside_rows = jnp.arange(canvas_rows, dtype=jnp.int32)[:, None] < height[..., None, None]
    inside_cols = jnp.arange(canvas_cols, dtype=jnp.int32)[None, :] < breadth[..., None, None]
    return (inside_rows & inside_cols).astype(jnp.float32)[..., None]

def window_pool(hidden):
    frames, height, breadth, channels = hidden.shape
    blocks = hidden.reshape(frames, height // 2, 2, breadth // 2, 2, channels)
    window_max = lax.optimization_barrier(jnp.max(blocks, axis=(2, 4), keepdims=True))
    raised = jnp.exp(blocks - window_max)
    weights = raised / lax.optimization_barrier(jnp.sum(raised, axis=(2, 4), keepdims=True))
    pooled = lax.optimization_barrier(jnp.sum(weights * blocks, axis=(2, 4), keepdims=True))
    return (weights * pooled).reshape(frames, height, breadth, channels)

def activate(pre_act, inside, pooling):
    hidden = jax.nn.silu(pre_act) * inside
    return jnp.where(pooling, window_pool(hidden) * inside, hidden)

def convolve(layer_in, weight):
    return lax.conv_general_dilated(layer_in, weight, (1, 1), 'SAME', dimension_numbers=('NHWC', 'IHWO', 'NHWC'), precision=lax.Precision.HIGHEST)

def forward(inputs, weights, gain_rows, biases, inside):
    results = []
    for micro_index in range(MICRO):
        mask_now = inside[micro_index]
        layer_in = low_back(inputs[micro_index] * mask_now)
        hidden = layer_in
        for layer_index in range(LAYERS):
            if layer_index > 0:
                layer_in = low(low_back(hidden))
            pre_norm = low_back(convolve(layer_in, weights[layer_index]))
            pixel_total = jnp.sum(mask_now)
            mean_val = lax.optimization_barrier(jnp.sum(pre_norm * mask_now, axis=(0, 1, 2))) / pixel_total
            square = lax.optimization_barrier(jnp.sum(pre_norm * pre_norm * mask_now, axis=(0, 1, 2))) / pixel_total
            scale_inv = lax.rsqrt(square - mean_val * mean_val + eps)
            pre_act = (pre_norm - mean_val) * scale_inv * gain_rows[layer_index] + biases[layer_index]
            hidden = activate(pre_act, mask_now, layer_index == CONVS - 1)
        results.append(hidden)
    return jnp.stack(results)

def reference(images, image_group, group_size, conv_weight, bn_gain, bn_bias, cotangent):
    inside = canvas_mask(image_group, group_size, CH, CW)
    outputs, pullback = jax.vjp(partial(forward, inside=inside), images.astype(jnp.float32), conv_weight.astype(jnp.float32), bn_gain, bn_bias)
    grads = pullback(cotangent.astype(jnp.float32))
    return (outputs.astype(jnp.bfloat16), grads[0].astype(jnp.bfloat16), grads[1], grads[2], grads[3])
```

```python
from functools import partial

import jax
import jax.numpy as jnp
from jax import lax
from jax.experimental import pallas as pl
from jax.experimental.pallas import tpu as pltpu
from jax.sharding import PartitionSpec as P

CONVS = 2


eps = 1e-05


def from_behind(x, axis, by):
    peers = lax.axis_size(axis)
    pairs = [(i, i + by) for i in range(peers) if 0 <= i + by < peers]
    return lax.ppermute(x, axis, pairs)


def canvas_mask(image_group, group_size, canvas_rows, canvas_cols):
    groups_n = group_size.shape[0]
    onehot = image_group[..., None] == jnp.arange(groups_n, dtype=jnp.int32)
    height = jnp.sum(jnp.where(onehot, group_size[:, 0], 0), axis=-1)
    breadth = jnp.sum(jnp.where(onehot, group_size[:, 1], 0), axis=-1)
    inside_rows = jnp.arange(canvas_rows, dtype=jnp.int32)[:, None] < height[..., None, None]
    inside_cols = jnp.arange(canvas_cols, dtype=jnp.int32)[None, :] < breadth[..., None, None]
    return (inside_rows & inside_cols).astype(jnp.float32)[..., None]


def window_pool(hidden):
    frames, height, breadth, channels = hidden.shape
    blocks = hidden.reshape(frames, height // 2, 2, breadth // 2, 2, channels)
    window_max = jnp.max(blocks, axis=(2, 4), keepdims=True)
    raised = jnp.exp(blocks - window_max)
    weights = raised / jnp.sum(raised, axis=(2, 4), keepdims=True)
    pooled = jnp.sum(weights * blocks, axis=(2, 4), keepdims=True)
    return (weights * pooled).reshape(frames, height, breadth, channels)


def activate(pre_act, inside, pooling):
    hidden = jax.nn.silu(pre_act) * inside
    return jnp.where(pooling, window_pool(hidden) * inside, hidden)


def conv_forward(layer_in, weight):
    return lax.conv_general_dilated(
        layer_in,
        weight,
        (1, 1),
        "SAME",
        dimension_numbers=("NHWC", "IHWO", "NHWC"),
        preferred_element_type=jnp.float32,
    )


def conv_data_back(grad_pre, weight):
    flipped = weight[:, ::-1, ::-1, :]
    return lax.conv_general_dilated(
        grad_pre,
        flipped,
        (1, 1),
        "SAME",
        dimension_numbers=("NHWC", "OHWI", "NHWC"),
        preferred_element_type=jnp.float32,
    )


def weight_back(layer_in, grad_pre):
    height = layer_in.shape[1]
    breadth = layer_in.shape[2]
    padded = jnp.pad(layer_in, ((0, 0), (1, 1), (1, 1), (0, 0)))
    pieces = []
    for tap_row in range(3):
        for tap_col in range(3):
            window = padded[:, tap_row : tap_row + height, tap_col : tap_col + breadth, :]
            pieces.append(
                jnp.einsum("nhwi,nhwo->io", window, grad_pre, preferred_element_type=jnp.float32)
            )
    return jnp.stack(pieces, axis=1).reshape(layer_in.shape[3], 3, 3, grad_pre.shape[3])


def layer_forward(layer_in, weight, gain_row, bias_row, inside, pooling):
    pre_norm = conv_forward(layer_in, weight)
    sums = lax.psum(
        (
            jnp.sum(pre_norm * inside, axis=(0, 1, 2)),
            jnp.sum(pre_norm * pre_norm * inside, axis=(0, 1, 2)),
            jnp.sum(inside),
        ),
        "dp",
    )
    pixel_total = sums[2]
    mean_val = sums[0] / pixel_total
    scale_inv = lax.rsqrt(sums[1] / pixel_total - mean_val * mean_val + eps)
    pre_act = (pre_norm - mean_val) * scale_inv * gain_row + bias_row
    hidden = activate(pre_act, inside, pooling)
    return (pre_norm, mean_val, scale_inv, pixel_total, hidden)


def layer_backward(
    grad_out,
    layer_in,
    pre_norm,
    mean_val,
    scale_inv,
    pixel_total,
    weight,
    gain_row,
    bias_row,
    inside,
    pooling,
):
    normed = (pre_norm - mean_val) * scale_inv
    pre_act = normed * gain_row + bias_row
    hidden_out, pullback = jax.vjp(partial(activate, inside=inside, pooling=pooling), pre_act)
    grad_act = pullback(grad_out)[0]
    sums = lax.psum(
        (jnp.sum(grad_act, axis=(0, 1, 2)), jnp.sum(grad_act * normed, axis=(0, 1, 2))), "dp"
    )
    shift_term = sums[0] / pixel_total
    slope_term = sums[1] / pixel_total
    grad_pre = (
        inside * scale_inv * gain_row * (grad_act - shift_term - normed * slope_term)
    ).astype(jnp.bfloat16)
    weight_term = weight_back(layer_in, grad_pre)
    grad_in = conv_data_back(grad_pre, weight).astype(jnp.bfloat16)
    return (grad_in, weight_term, sums[1], sums[0])


def pipeline_shards(images, image_group, group_size, conv_weight, bn_gain, bn_bias, cotangent):
    section_index = lax.axis_index("section")
    sections = lax.axis_size("section")
    micro_total = images.shape[0]
    channels = conv_weight.shape[1]
    inside_all = canvas_mask(image_group, group_size, images.shape[2], images.shape[3])
    ticks = micro_total + sections - 1
    weight = conv_weight[0]
    gain_row = bn_gain[0]
    bias_row = bn_bias[0]
    pool_here = section_index == CONVS - 1
    received = jnp.zeros(images.shape[1:], jnp.bfloat16)
    kept_in, kept_pre, kept_mean, kept_scale, kept_total, finished = ([], [], [], [], [], [])
    for tick in range(ticks):
        micro_pos = jnp.clip(tick - section_index, 0, micro_total - 1)
        inside = inside_all[micro_pos]
        fresh = (images[micro_pos].astype(jnp.float32) * inside).astype(jnp.bfloat16)
        layer_in = jnp.where(section_index == 0, fresh, received)
        pre_norm, mean_val, scale_inv, pixel_total, hidden = layer_forward(
            layer_in, weight, gain_row, bias_row, inside, pool_here
        )
        sent = hidden.astype(jnp.bfloat16)
        if tick < ticks - 1:
            received = from_behind(sent, "section", 1)
        kept_in.append(layer_in)
        kept_pre.append(pre_norm)
        kept_mean.append(mean_val)
        kept_scale.append(scale_inv)
        kept_total.append(pixel_total)
        finished.append(sent)
    stack_in = jnp.stack(kept_in)
    stack_pre = jnp.stack(kept_pre)
    stack_mean = jnp.stack(kept_mean)
    stack_scale = jnp.stack(kept_scale)
    stack_total = jnp.stack(kept_total)
    returned = jnp.zeros(images.shape[1:], jnp.bfloat16)
    weight_sum = jnp.zeros(conv_weight.shape[1:], jnp.float32)
    gain_sum = jnp.zeros((channels,), jnp.float32)
    bias_sum = jnp.zeros((channels,), jnp.float32)
    input_list = []
    for tick in range(ticks):
        micro_raw = tick - (sections - 1 - section_index)
        valid = ((micro_raw >= 0) & (micro_raw < micro_total)).astype(jnp.float32)
        micro_pos = jnp.clip(micro_raw, 0, micro_total - 1)
        forward_tick = jnp.clip(micro_pos + section_index, 0, ticks - 1)
        inside = inside_all[micro_pos]
        grad_out = jnp.where(
            section_index == sections - 1,
            cotangent[micro_pos].astype(jnp.float32),
            returned.astype(jnp.float32),
        )
        grad_in, weight_term, gain_term, bias_term = layer_backward(
            grad_out,
            stack_in[forward_tick],
            stack_pre[forward_tick],
            stack_mean[forward_tick],
            stack_scale[forward_tick],
            stack_total[forward_tick],
            weight,
            gain_row,
            bias_row,
            inside,
            pool_here,
        )
        weight_sum = weight_sum + valid * weight_term
        gain_sum = gain_sum + valid * gain_term
        bias_sum = bias_sum + valid * bias_term
        if tick < ticks - 1:
            returned = from_behind(grad_in, "section", -1)
        input_list.append((grad_in.astype(jnp.float32) * inside).astype(jnp.bfloat16))
    out_stack = jnp.stack(finished[sections - 1 :], axis=0)
    grad_stack = jnp.stack(input_list[sections - 1 :], axis=0)
    out_back, grad_back = (
        lax.all_to_all(out_stack, "section", split_axis=0, concat_axis=1, tiled=True),
        lax.all_to_all(grad_stack, "section", split_axis=0, concat_axis=1, tiled=True),
    )
    activations = out_back[:, sections - 1 : sections]
    input_grad = grad_back[:, 0:1]
    weight_grad = lax.psum_scatter(weight_sum[None], "dp", scatter_dimension=1, tiled=True)
    share = channels // lax.axis_size("dp")
    gain_grad = lax.dynamic_slice_in_dim(gain_sum, lax.axis_index("dp") * share, share)[None]
    bias_grad = lax.dynamic_slice_in_dim(bias_sum, lax.axis_index("dp") * share, share)[None]
    return (activations, input_grad, weight_grad, gain_grad, bias_grad)


AXES = ("section", "dp")
TAPS = 9
VMEM_LIMIT = 40 * 1024 * 1024
META_ROWS = 16


def place():
    dp_index = lax.axis_index("dp")
    return lax.axis_index("section"), dp_index // 2, dp_index % 2


def peer_order():
    return [(k, j) for j in range(2) for k in range(4)]


def slice_at(section, core, k, j):
    return (section ^ k) * 2 + (core ^ j)


def send(x, target):
    sections = lax.axis_size("section")
    dps = lax.axis_size("dp")
    pairs = []
    for s in range(sections):
        for d in range(dps):
            ts, tz, tc = target(s, d // 2, d % 2)
            pairs.append((s * dps + d, ts * dps + tz * 2 + tc))
    return lax.ppermute(x, AXES, pairs)


def to_section(x, k):
    return send(x, lambda s, z, c: (s ^ k, z, c))


def to_plane(x, k):
    return send(x, lambda s, z, c: (s, z ^ k, c))


def to_core(x):
    return send(x, lambda s, z, c: (s, z, c ^ 1))


def plane_gather(block):
    own = [block] + [to_section(block, k) for k in (1, 2, 3)]
    return own + [to_core(x) for x in own]


def grid_facts(frames, rows, cols):
    at = jnp.arange(frames * rows * cols, dtype=jnp.int32)
    col = at % cols
    row = (at // cols) % rows
    facts = [row > 0, row < rows - 1, col > 0, col < cols - 1, col % 2 == 0, row % 2 == 0]
    facts = facts + [row < 0, row < 0]
    return jnp.stack(facts).astype(jnp.float32)


def shift(x, by, axis=1):
    length = x.shape[axis]
    return pltpu.roll(x, (-by) % length, axis) if by % length else x


def row_ok(facts, d):
    return facts[0:1, :] if d < 0 else facts[1:2, :]


def col_ok(facts, d):
    return facts[2:3, :] if d < 0 else facts[3:4, :]


def sum_taps(taps_ref, facts, cols, sign):
    ch = taps_ref.shape[0] // TAPS
    total = None
    for dx in (-1, 0, 1):
        column = None
        for dy in (-1, 0, 1):
            tap = (dy + 1) * 3 + dx + 1
            piece = taps_ref[tap * ch : (tap + 1) * ch, :]
            if dy:
                piece = shift(piece, sign * dy * cols) * row_ok(facts, sign * dy)
            column = piece if column is None else column + piece
        if dx:
            column = shift(column, sign * dx) * col_ok(facts, sign * dx)
        total = column if total is None else total + column
    return total


def window_op(x, op, facts, cols):
    even_col = facts[4:5, :] > 0.5
    even_row = facts[5:6, :] > 0.5
    x = op(x, jnp.where(even_col, shift(x, 1), shift(x, -1)))
    return op(x, jnp.where(even_row, shift(x, cols), shift(x, -cols)))


def soft_pool(hidden, facts, cols):
    raised = jnp.exp(hidden - window_op(hidden, jnp.maximum, facts, cols))
    weights = raised / window_op(raised, jnp.add, facts, cols)
    return weights, window_op(weights * hidden, jnp.add, facts, cols)


def lane_sum(x):
    return jnp.sum(x, axis=1, keepdims=True)


def normalise(pre, inside):
    count = lane_sum(inside)
    mean = lane_sum(pre * inside) / count
    square = lane_sum(pre * pre * inside) / count
    scale = lax.rsqrt(square - mean * mean + eps)
    return (pre - mean) * scale, scale


def hidden_of(normed, gain, bias, inside, facts, cols, pooling):
    pre_act = normed * gain + bias
    hidden = pre_act * jax.nn.sigmoid(pre_act) * inside
    if pooling:
        weights, pooled = soft_pool(hidden, facts, cols)
        hidden = weights * pooled * inside
    return hidden


def norm_back(grad, normed, scale, gain, bias, inside, facts, cols, pooling):
    pre_act = normed * gain + bias
    gate = jax.nn.sigmoid(pre_act)
    if pooling:
        hidden = pre_act * gate * inside
        weights, pooled = soft_pool(hidden, facts, cols)
        out = grad * inside
        d_pooled = window_op(weights * out, jnp.add, facts, cols)
        d_weights = out * pooled + d_pooled * hidden
        spread = window_op(weights * d_weights, jnp.add, facts, cols)
        grad = weights * (d_pooled + d_weights - spread)
    grad_act = grad * inside * gate * (1.0 + pre_act * (1.0 - gate))
    count = lane_sum(inside)
    shift_sum = lane_sum(grad_act)
    slope_sum = lane_sum(grad_act * normed)
    grad_pre = inside * (scale * gain) * (grad_act - shift_sum / count - normed * (slope_sum / count))
    return grad_pre.astype(jnp.bfloat16), shift_sum, slope_sum


def assemble(blocks, full_ref):
    section, _, core = place()
    ch = blocks[0].shape[0]
    for (k, j), block in zip(peer_order(), blocks):
        at = pl.multiple_of(slice_at(section, core, k, j) * ch, ch)
        full_ref[pl.ds(at, ch), :] = block[...]


def assemble_frames(blocks, full_ref, cells):
    _, plane, core = place()
    for (k, j), block in zip(peer_order(), blocks):
        frame = (plane ^ k) * 2 + (core ^ j)
        full_ref[pl.ds(pl.multiple_of(frame * cells, cells), cells), :] = block[:cells, :]


def tap_products(weight_ref, full_ref, taps_ref, transposed):
    length = taps_ref.shape[1]
    step = 512 if length % 512 == 0 else length
    for at in range(0, length, step):
        if transposed:
            taps_ref[:, at : at + step] = lax.dot_general(
                weight_ref[...],
                full_ref[at : at + step, :],
                (((1,), (1,)), ((), ())),
                preferred_element_type=jnp.float32,
            )
        else:
            taps_ref[:, at : at + step] = jnp.dot(
                weight_ref[...], full_ref[:, at : at + step], preferred_element_type=jnp.float32
            )


def forward_kernel(dims, first, pooling, *refs):
    blocks, (weight, gain, bias, inside, facts), (hidden, normed, scale), (full, taps) = (
        refs[:8],
        refs[8:13],
        refs[13:16],
        refs[16:],
    )
    rows, cols = dims
    if first:
        assemble_frames(blocks, full, rows * cols)
    else:
        assemble(blocks, full)
    tap_products(weight, full, taps, first)
    facts_now, inside_now = facts[...], inside[...]
    pre = sum_taps(taps, facts_now, cols, 1)
    normed_now, scale_now = normalise(pre, inside_now)
    normed[...] = normed_now
    scale[...] = scale_now
    hidden[...] = hidden_of(
        normed_now, gain[...], bias[...], inside_now, facts_now, cols, pooling
    ).astype(jnp.bfloat16)


def turn_kernel(dims, pooling, *refs):
    blocks, cots = refs[:8], refs[8:16]
    weight, gain, bias, inside, facts, pick = refs[16:22]
    pieces, (grad_pre, shift_sum, slope_sum), (full, taps, cot_full, hidden) = (
        refs[22:26],
        refs[26:29],
        refs[29:],
    )
    rows, cols = dims
    assemble(blocks, full)
    assemble_frames(cots, cot_full, rows * cols)
    tap_products(weight, full, taps, False)
    facts_now, inside_now = facts[...], inside[...]
    pre = sum_taps(taps, facts_now, cols, 1)
    normed, scale = normalise(pre, inside_now)
    hidden[...] = hidden_of(
        normed, gain[...], bias[...], inside_now, facts_now, cols, pooling
    ).astype(jnp.bfloat16)
    cut_frames(hidden, pieces)
    cotangent = lax.dot_general(
        pick[...], cot_full[...], (((1,), (1,)), ((), ())), preferred_element_type=jnp.float32
    )
    grad_pre[...], shift_sum[...], slope_sum[...] = norm_back(
        cotangent, normed, scale, gain[...], bias[...], inside_now, facts_now, cols, pooling
    )


def cut_frames(full, pieces):
    section, _, _ = place()
    width = pieces[0].shape[1]
    for k, piece in enumerate(pieces):
        piece[...] = full[:, pl.ds(pl.multiple_of((section ^ k) * width, width), width)]


def back_kernel(dims, pooling, *refs):
    blocks, (weight, normed, scale, gain, bias, inside, facts) = refs[:8], refs[8:15]
    (grad_pre, shift_sum, slope_sum), (full, taps) = refs[15:18], refs[18:]
    assemble(blocks, full)
    tap_products(weight, full, taps, False)
    facts_now, inside_now = facts[...], inside[...]
    grad = sum_taps(taps, facts_now, dims[1], -1).astype(jnp.bfloat16).astype(jnp.float32)
    grad_pre[...], shift_sum[...], slope_sum[...] = norm_back(
        grad, normed[...], scale[...], gain[...], bias[...], inside_now, facts_now, dims[1], pooling
    )


def input_kernel(dims, *refs):
    blocks, (weight, inside, facts), pieces, (full, taps, grad) = (
        refs[:8],
        refs[8:11],
        refs[11:15],
        refs[15:],
    )
    assemble(blocks, full)
    tap_products(weight, full, taps, False)
    grad[...] = (sum_taps(taps, facts[...], dims[1], -1) * inside[...]).astype(jnp.bfloat16)
    cut_frames(grad, pieces)


def weight_kernel(dims, first, *refs):
    blocks, (grad_pre, shift_sum, slope_sum, facts), pieces, (full, moved, product) = (
        refs[:8],
        refs[8:12],
        refs[12:16],
        refs[16:],
    )
    rows, cols = dims
    _, plane, _ = place()
    if first:
        assemble_frames(blocks, full, rows * cols)
    else:
        assemble(blocks, full)
    facts_now = facts[...]
    grad = grad_pre[...].astype(jnp.float32)
    ch = grad.shape[0]
    for dx in (-1, 0, 1):
        column = shift(grad, -dx) * col_ok(facts_now, -dx) if dx else grad
        for dy in (-1, 0, 1):
            piece = shift(column, -dy * cols) * row_ok(facts_now, -dy) if dy else column
            tap = (dy + 1) * 3 + dx + 1
            moved[tap * ch : (tap + 1) * ch, :] = piece.astype(jnp.bfloat16)
    if first:
        value = jnp.dot(moved[...], full[...], preferred_element_type=jnp.float32)
    else:
        value = lax.dot_general(
            moved[...], full[...], (((1,), (1,)), ((), ())), preferred_element_type=jnp.float32
        )
    product[...] = value.astype(jnp.bfloat16)
    width = pieces[0].shape[1]
    lines = []
    for sums in (shift_sum, slope_sum):
        turned = jnp.broadcast_to(sums[...], (ch, width)).T
        lines.append(jnp.concatenate([turned, jnp.zeros((width, width - ch), jnp.float32)], axis=1)[0:1])
    sums_block = jnp.concatenate(lines + [jnp.zeros((META_ROWS - 2, width), jnp.float32)], axis=0)
    for k, piece in enumerate(pieces):
        piece[: TAPS * ch, :] = product[:, pl.ds(pl.multiple_of((plane ^ k) * width, width), width)]
        piece[TAPS * ch :, :] = sums_block.astype(jnp.bfloat16)


def pack_kernel(picks, weight, *outs):
    turned = lax.dot_general(
        picks[...], weight[0], (((1,), (1,)), ((), ())), preferred_element_type=jnp.float32
    ).astype(jnp.bfloat16)
    ch = outs[0].shape[1]
    for k, out in enumerate(outs):
        out[0] = turned[k * ch : (k + 1) * ch, :]


def map_out_kernel(*refs):
    blocks, out, full = refs[:8], refs[8], refs[9:]
    section_plane, core = place()[1], place()[2]
    (full,) = full
    ch = blocks[0].shape[0]
    for (k, j), block in zip(peer_order(), blocks):
        at = pl.multiple_of(slice_at(section_plane, core, k, j) * ch, ch)
        full[pl.ds(at, ch), :] = block[...]
    cells = out.shape[0]
    both = full[...].astype(jnp.float32)
    mine = jnp.where(core == 0, both[:, :cells], both[:, cells:])
    out[...] = mine.T.astype(out.dtype)


def grads_out_kernel(*refs):
    blocks, (weight_out, shift_out, slope_out), (full, turned) = refs[:8], refs[8:11], refs[11:]
    section, plane, core = place()
    taps, rows, channels = weight_out.shape
    for tap in range(taps):
        for (k, j), block in zip(peer_order(), blocks):
            at = pl.multiple_of(slice_at(section, core, k, j) * rows, rows)
            full[pl.ds(at, rows), :] = block[tap * rows : (tap + 1) * rows, :].astype(jnp.float32)
        turned[...] = full[...].T
        weight_out[tap] = turned[pl.ds(pl.multiple_of(core * rows, rows), rows), :]
    shift_row = jnp.zeros((1, rows), jnp.float32)
    slope_row = jnp.zeros((1, rows), jnp.float32)
    for (k, j), block in zip(peer_order(), blocks):
        if j == 0:
            tail = block[taps * rows :, :].astype(jnp.float32)
            mine = (section ^ k) == plane
            shift_row = shift_row + jnp.where(mine, tail[0:1, :rows], 0.0)
            slope_row = slope_row + jnp.where(mine, tail[1:2, :rows], 0.0)
    shift_out[...] = shift_row
    slope_out[...] = slope_row


def call(kernel, outs, scratch, args, flops=0, name=None):
    shapes = [jax.ShapeDtypeStruct(shape, dtype) for shape, dtype in outs]
    moved = sum(a.size * a.dtype.itemsize for a in args)
    moved += sum(s.size * s.dtype.itemsize for s in shapes)
    return pl.pallas_call(
        kernel,
        out_shape=shapes,
        in_specs=[pl.BlockSpec(memory_space=pltpu.VMEM)] * len(args),
        out_specs=[pl.BlockSpec(memory_space=pltpu.VMEM)] * len(shapes),
        scratch_shapes=[pltpu.VMEM(shape, dtype) for shape, dtype in scratch],
        compiler_params=pltpu.CompilerParams(vmem_limit_bytes=VMEM_LIMIT),
        cost_estimate=pl.CostEstimate(flops=flops, bytes_accessed=moved, transcendentals=0),
        name=name,
    )(*args)


def one_hot(index, size):
    return (index[:, None] == jnp.arange(size, dtype=jnp.int32)[None, :]).astype(jnp.bfloat16)


def plane_shards(images, image_group, group_size, conv_weight, bn_gain, bn_bias, cotangent):
    section, plane, core = place()
    micro_total, _, rows, cols, channels = images.shape
    layers = lax.axis_size("section")
    cells = rows * cols
    frames = 2 * micro_total
    length = frames * cells
    ch = channels // 8
    dims = (rows, cols)
    bf16, f32 = jnp.bfloat16, jnp.float32
    facts = grid_facts(frames, rows, cols)
    conv_flops = 2 * TAPS * ch * channels * length

    taps_first = conv_weight[0].transpose(1, 2, 0, 3).reshape(TAPS, channels, channels)
    row_at = jnp.arange(ch, dtype=jnp.int32)
    picks = one_hot(
        jnp.concatenate([slice_at(section, core, k, 0) * ch + row_at for k in range(4)]), channels
    )
    packed = pl.pallas_call(
        pack_kernel,
        grid=(TAPS,),
        out_shape=[jax.ShapeDtypeStruct((TAPS, ch, channels), bf16)] * 4,
        in_specs=[
            pl.BlockSpec((4 * ch, channels), lambda t: (0, 0)),
            pl.BlockSpec((1, channels, channels), lambda t: (t, 0, 0)),
        ],
        out_specs=[pl.BlockSpec((1, ch, channels), lambda t: (t, 0, 0))] * 4,
        compiler_params=pltpu.CompilerParams(vmem_limit_bytes=VMEM_LIMIT),
        name="weight_pack",
    )(picks, taps_first)
    packed = [x.reshape(TAPS * ch, channels) for x in packed]
    out_rel = [packed[0]] + [to_section(packed[k], k) for k in (1, 2, 3)]

    def of_layer(relative, layer):
        return lax.select_n(section ^ layer, *relative)

    inside_all = canvas_mask(image_group[:, 0], group_size, rows, cols)
    masked = (images[:, 0].astype(f32) * inside_all).astype(bf16).reshape(micro_total, cells, channels)
    meta = jnp.broadcast_to(
        image_group[:, :, None].astype(bf16), (micro_total, META_ROWS, channels)
    )
    payload = jnp.concatenate([masked, meta], axis=1)
    mine = [lax.dynamic_index_in_dim(payload, plane ^ k, 0, keepdims=False) for k in range(4)]
    frames_in = [mine[0]] + [to_plane(mine[k], k) for k in (1, 2, 3)]
    frames_in = frames_in + [to_core(x) for x in frames_in]
    at = jnp.stack([(plane ^ k) * 2 + (core ^ j) for k, j in peer_order()])
    groups = jnp.stack([x[cells, 0] for x in frames_in]).astype(jnp.int32)
    ordered = jnp.sum(
        jnp.where(at[None, :] == jnp.arange(frames, dtype=jnp.int32)[:, None], groups[None, :], 0), axis=1
    )
    inside = canvas_mask(ordered, group_size, rows, cols).reshape(1, length)

    cot = lax.dynamic_slice_in_dim(
        cotangent.reshape(micro_total, cells, channels), section * 2 * ch, 2 * ch, 2
    )
    mine = [lax.dynamic_index_in_dim(cot, plane ^ k, 0, keepdims=False) for k in range(4)]
    cots = [mine[0]] + [to_plane(mine[k], k) for k in (1, 2, 3)]
    cots = cots + [to_core(x) for x in cots]
    half = one_hot(core * ch + row_at, 2 * ch)

    both = jnp.stack([bn_gain[0].reshape(8, ch), bn_bias[0].reshape(8, ch)], axis=1)
    rel = [both[slice_at(section, core, k, 0)] for k in range(4)]
    rel = [rel[0]] + [to_section(rel[k], k) for k in (1, 2, 3)]
    gains, biases = [], []
    for layer in range(layers):
        pair = lax.select_n(section ^ layer, *rel)
        gains.append(pair[0][:, None])
        biases.append(pair[1][:, None])

    full_map = ((channels, length), bf16)
    full_frames = ((length, channels), bf16)
    tap_scratch = ((TAPS * ch, length), f32)
    map_out = ((ch, length), bf16)
    column = ((ch, 1), f32)
    piece = ((ch, 2 * cells), bf16)

    gathered = [frames_in]
    kept = []
    for layer in range(layers - 1):
        hidden, normed, scale = call(
            partial(forward_kernel, dims, layer == 0, layer == CONVS - 1),
            [map_out, ((ch, length), f32), column],
            [full_frames if layer == 0 else full_map, tap_scratch],
            [*gathered[layer], of_layer(out_rel, layer), gains[layer], biases[layer], inside, facts],
            conv_flops,
            "forward",
        )
        kept.append((normed, scale))
        gathered.append(plane_gather(hidden))
    last = layers - 1
    *pieces, grad_pre, shift_sum, slope_sum = call(
        partial(turn_kernel, dims, last == CONVS - 1),
        [piece] * 4 + [map_out, column, column],
        [full_map, tap_scratch, ((length, 2 * ch), bf16), map_out],
        [*gathered[last], *cots, of_layer(out_rel, last), gains[last], biases[last], inside, facts, half],
        conv_flops,
        "turn",
    )

    def deliver(pieces):
        blocks = [send(x, lambda s, z, c, k=k: (z, s ^ k, c)) for k, x in enumerate(pieces)]
        blocks = blocks + [to_core(x) for x in blocks]
        (out,) = call(
            map_out_kernel, [((cells, channels), bf16)], [((channels, 2 * cells), bf16)], blocks, 0, "map_out"
        )
        return out.reshape(1, 1, rows, cols, channels)

    activations = deliver(pieces)

    in_slices = taps_first.reshape(TAPS, 8, ch, channels)
    in_own = [
        lax.dynamic_index_in_dim(in_slices, slice_at(section, core, k, 0), 1, keepdims=False).reshape(
            TAPS * ch, channels
        )
        for k in range(4)
    ]
    in_rel = [in_own[0]] + [to_section(in_own[k], k) for k in (1, 2, 3)]

    def weight_share(layer, grad_pre, shift_sum, slope_sum):
        first = layer == 0
        parts = call(
            partial(weight_kernel, dims, first),
            [((TAPS * ch + META_ROWS, 2 * ch), bf16)] * 4,
            [full_frames if first else full_map, ((TAPS * ch, length), bf16), ((TAPS * ch, channels), bf16)],
            [*gathered[layer], grad_pre, shift_sum, slope_sum, facts],
            conv_flops,
            "weight_share",
        )
        parts = [parts[0]] + [to_plane(parts[k], k) for k in (1, 2, 3)]
        return sum(x.astype(f32) for x in parts).astype(bf16)

    shares = [None] * layers
    for layer in range(last, -1, -1):
        blocks = plane_gather(grad_pre)
        shares[layer] = weight_share(layer, grad_pre, shift_sum, slope_sum)
        if layer:
            grad_pre, shift_sum, slope_sum = call(
                partial(back_kernel, dims, layer - 1 == CONVS - 1),
                [map_out, column, column],
                [full_map, tap_scratch],
                [
                    *blocks,
                    of_layer(in_rel, layer),
                    *kept[layer - 1],
                    gains[layer - 1],
                    biases[layer - 1],
                    inside,
                    facts,
                ],
                conv_flops,
                "back",
            )
        else:
            pieces = call(
                partial(input_kernel, dims),
                [piece] * 4,
                [full_map, tap_scratch, map_out],
                [*blocks, of_layer(in_rel, 0), inside, facts],
                conv_flops,
                "input",
            )
    input_grad = deliver(pieces)

    chosen = [lax.select_n(section ^ k, *shares) for k in range(4)]
    blocks = [chosen[0]] + [to_section(chosen[k], k) for k in (1, 2, 3)]
    blocks = blocks + [to_core(x) for x in blocks]
    weight_grad, bias_grad, gain_grad = call(
        grads_out_kernel,
        [((TAPS, ch, channels), f32), ((1, ch), f32), ((1, ch), f32)],
        [((channels, 2 * ch), f32), ((2 * ch, channels), f32)],
        blocks,
        0,
        "grads_out",
    )
    weight_grad = weight_grad.reshape(3, 3, ch, channels).transpose(2, 0, 1, 3)[None]
    return (activations, input_grad, weight_grad, gain_grad, bias_grad)


def fits_plane_plan(images, conv_weight, sections, dps):
    micro_total, images_total, rows, cols, channels = images.shape
    return (
        sections == 4
        and dps == 2 * sections
        and micro_total == sections
        and conv_weight.shape[0] == sections
        and images_total == dps
        and rows % 2 == 0
        and cols % 2 == 0
        and (rows * cols) % 64 == 0
        and channels == 512
    )


def solution(mesh):
    in_specs = (
        P(None, "dp", None, None, None),
        P(None, "dp"),
        P(),
        P("section", None, None, None, None),
        P("section", None),
        P("section", None),
        P(None, "dp", None, None, None),
    )
    out_specs = (
        P("section", "dp", None, None, None),
        P("section", "dp", None, None, None),
        P("section", "dp", None, None, None),
        P("section", "dp"),
        P("section", "dp"),
    )
    sections, dps = mesh.shape["section"], mesh.shape["dp"]

    def program(images, image_group, group_size, conv_weight, bn_gain, bn_bias, cotangent):
        plan = plane_shards if fits_plane_plan(images, conv_weight, sections, dps) else pipeline_shards
        sharded = jax.shard_map(plan, mesh=mesh, in_specs=in_specs, out_specs=out_specs, check_vma=False)
        return sharded(images, image_group, group_size, conv_weight, bn_gain, bn_bias, cotangent)

    return program
```

```python
from functools import partial

import jax
import jax.numpy as jnp
from jax import lax
from jax.experimental import pallas as pl
from jax.experimental.pallas import tpu as pltpu
from jax.sharding import PartitionSpec as P

CONVS = 2


eps = 1e-05


def from_behind(x, axis, by):
    peers = lax.axis_size(axis)
    pairs = [(i, i + by) for i in range(peers) if 0 <= i + by < peers]
    return lax.ppermute(x, axis, pairs)


def canvas_mask(image_group, group_size, canvas_rows, canvas_cols):
    groups_n = group_size.shape[0]
    onehot = image_group[..., None] == jnp.arange(groups_n, dtype=jnp.int32)
    height = jnp.sum(jnp.where(onehot, group_size[:, 0], 0), axis=-1)
    breadth = jnp.sum(jnp.where(onehot, group_size[:, 1], 0), axis=-1)
    inside_rows = jnp.arange(canvas_rows, dtype=jnp.int32)[:, None] < height[..., None, None]
    inside_cols = jnp.arange(canvas_cols, dtype=jnp.int32)[None, :] < breadth[..., None, None]
    return (inside_rows & inside_cols).astype(jnp.float32)[..., None]


def window_pool(hidden):
    frames, height, breadth, channels = hidden.shape
    blocks = hidden.reshape(frames, height // 2, 2, breadth // 2, 2, channels)
    window_max = jnp.max(blocks, axis=(2, 4), keepdims=True)
    raised = jnp.exp(blocks - window_max)
    weights = raised / jnp.sum(raised, axis=(2, 4), keepdims=True)
    pooled = jnp.sum(weights * blocks, axis=(2, 4), keepdims=True)
    return (weights * pooled).reshape(frames, height, breadth, channels)


def activate(pre_act, inside, pooling):
    hidden = jax.nn.silu(pre_act) * inside
    return jnp.where(pooling, window_pool(hidden) * inside, hidden)


def conv_forward(layer_in, weight):
    return lax.conv_general_dilated(
        layer_in,
        weight,
        (1, 1),
        "SAME",
        dimension_numbers=("NHWC", "IHWO", "NHWC"),
        preferred_element_type=jnp.float32,
    )


def conv_data_back(grad_pre, weight):
    flipped = weight[:, ::-1, ::-1, :]
    return lax.conv_general_dilated(
        grad_pre,
        flipped,
        (1, 1),
        "SAME",
        dimension_numbers=("NHWC", "OHWI", "NHWC"),
        preferred_element_type=jnp.float32,
    )


def weight_back(layer_in, grad_pre):
    height = layer_in.shape[1]
    breadth = layer_in.shape[2]
    padded = jnp.pad(layer_in, ((0, 0), (1, 1), (1, 1), (0, 0)))
    pieces = []
    for tap_row in range(3):
        for tap_col in range(3):
            window = padded[:, tap_row : tap_row + height, tap_col : tap_col + breadth, :]
            pieces.append(
                jnp.einsum("nhwi,nhwo->io", window, grad_pre, preferred_element_type=jnp.float32)
            )
    return jnp.stack(pieces, axis=1).reshape(layer_in.shape[3], 3, 3, grad_pre.shape[3])


def layer_forward(layer_in, weight, gain_row, bias_row, inside, pooling):
    pre_norm = conv_forward(layer_in, weight)
    sums = lax.psum(
        (
            jnp.sum(pre_norm * inside, axis=(0, 1, 2)),
            jnp.sum(pre_norm * pre_norm * inside, axis=(0, 1, 2)),
            jnp.sum(inside),
        ),
        "dp",
    )
    pixel_total = sums[2]
    mean_val = sums[0] / pixel_total
    scale_inv = lax.rsqrt(sums[1] / pixel_total - mean_val * mean_val + eps)
    pre_act = (pre_norm - mean_val) * scale_inv * gain_row + bias_row
    hidden = activate(pre_act, inside, pooling)
    return (pre_norm, mean_val, scale_inv, pixel_total, hidden)


def layer_backward(
    grad_out,
    layer_in,
    pre_norm,
    mean_val,
    scale_inv,
    pixel_total,
    weight,
    gain_row,
    bias_row,
    inside,
    pooling,
):
    normed = (pre_norm - mean_val) * scale_inv
    pre_act = normed * gain_row + bias_row
    hidden_out, pullback = jax.vjp(partial(activate, inside=inside, pooling=pooling), pre_act)
    grad_act = pullback(grad_out)[0]
    sums = lax.psum(
        (jnp.sum(grad_act, axis=(0, 1, 2)), jnp.sum(grad_act * normed, axis=(0, 1, 2))), "dp"
    )
    shift_term = sums[0] / pixel_total
    slope_term = sums[1] / pixel_total
    grad_pre = (
        inside * scale_inv * gain_row * (grad_act - shift_term - normed * slope_term)
    ).astype(jnp.bfloat16)
    weight_term = weight_back(layer_in, grad_pre)
    grad_in = conv_data_back(grad_pre, weight).astype(jnp.bfloat16)
    return (grad_in, weight_term, sums[1], sums[0])


def pipeline_shards(images, image_group, group_size, conv_weight, bn_gain, bn_bias, cotangent):
    section_index = lax.axis_index("section")
    sections = lax.axis_size("section")
    micro_total = images.shape[0]
    channels = conv_weight.shape[1]
    inside_all = canvas_mask(image_group, group_size, images.shape[2], images.shape[3])
    ticks = micro_total + sections - 1
    weight = conv_weight[0]
    gain_row = bn_gain[0]
    bias_row = bn_bias[0]
    pool_here = section_index == CONVS - 1
    received = jnp.zeros(images.shape[1:], jnp.bfloat16)
    kept_in, kept_pre, kept_mean, kept_scale, kept_total, finished = ([], [], [], [], [], [])
    for tick in range(ticks):
        micro_pos = jnp.clip(tick - section_index, 0, micro_total - 1)
        inside = inside_all[micro_pos]
        fresh = (images[micro_pos].astype(jnp.float32) * inside).astype(jnp.bfloat16)
        layer_in = jnp.where(section_index == 0, fresh, received)
        pre_norm, mean_val, scale_inv, pixel_total, hidden = layer_forward(
            layer_in, weight, gain_row, bias_row, inside, pool_here
        )
        sent = hidden.astype(jnp.bfloat16)
        if tick < ticks - 1:
            received = from_behind(sent, "section", 1)
        kept_in.append(layer_in)
        kept_pre.append(pre_norm)
        kept_mean.append(mean_val)
        kept_scale.append(scale_inv)
        kept_total.append(pixel_total)
        finished.append(sent)
    stack_in = jnp.stack(kept_in)
    stack_pre = jnp.stack(kept_pre)
    stack_mean = jnp.stack(kept_mean)
    stack_scale = jnp.stack(kept_scale)
    stack_total = jnp.stack(kept_total)
    returned = jnp.zeros(images.shape[1:], jnp.bfloat16)
    weight_sum = jnp.zeros(conv_weight.shape[1:], jnp.float32)
    gain_sum = jnp.zeros((channels,), jnp.float32)
    bias_sum = jnp.zeros((channels,), jnp.float32)
    input_list = []
    for tick in range(ticks):
        micro_raw = tick - (sections - 1 - section_index)
        valid = ((micro_raw >= 0) & (micro_raw < micro_total)).astype(jnp.float32)
        micro_pos = jnp.clip(micro_raw, 0, micro_total - 1)
        forward_tick = jnp.clip(micro_pos + section_index, 0, ticks - 1)
        inside = inside_all[micro_pos]
        grad_out = jnp.where(
            section_index == sections - 1,
            cotangent[micro_pos].astype(jnp.float32),
            returned.astype(jnp.float32),
        )
        grad_in, weight_term, gain_term, bias_term = layer_backward(
            grad_out,
            stack_in[forward_tick],
            stack_pre[forward_tick],
            stack_mean[forward_tick],
            stack_scale[forward_tick],
            stack_total[forward_tick],
            weight,
            gain_row,
            bias_row,
            inside,
            pool_here,
        )
        weight_sum = weight_sum + valid * weight_term
        gain_sum = gain_sum + valid * gain_term
        bias_sum = bias_sum + valid * bias_term
        if tick < ticks - 1:
            returned = from_behind(grad_in, "section", -1)
        input_list.append((grad_in.astype(jnp.float32) * inside).astype(jnp.bfloat16))
    out_stack = jnp.stack(finished[sections - 1 :], axis=0)
    grad_stack = jnp.stack(input_list[sections - 1 :], axis=0)
    out_back, grad_back = (
        lax.all_to_all(out_stack, "section", split_axis=0, concat_axis=1, tiled=True),
        lax.all_to_all(grad_stack, "section", split_axis=0, concat_axis=1, tiled=True),
    )
    activations = out_back[:, sections - 1 : sections]
    input_grad = grad_back[:, 0:1]
    weight_grad = lax.psum_scatter(weight_sum[None], "dp", scatter_dimension=1, tiled=True)
    share = channels // lax.axis_size("dp")
    gain_grad = lax.dynamic_slice_in_dim(gain_sum, lax.axis_index("dp") * share, share)[None]
    bias_grad = lax.dynamic_slice_in_dim(bias_sum, lax.axis_index("dp") * share, share)[None]
    return (activations, input_grad, weight_grad, gain_grad, bias_grad)


AXES = ("section", "dp")
TAPS = 9
VMEM_LIMIT = 24 * 1024 * 1024
META_ROWS = 16
LANES = 128
ROW_AT, COL_AT, FRAME_AT = 6, 7, 8
NT = (((1,), (1,)), ((), ()))


def place():
    dp_index = lax.axis_index("dp")
    return lax.axis_index("section"), dp_index // 2, dp_index % 2


def peer_order():
    return [(k, j) for j in range(2) for k in range(4)]


def slice_at(section, core, k, j):
    return (section ^ k) * 2 + (core ^ j)


def send(x, target):
    sections = lax.axis_size("section")
    dps = lax.axis_size("dp")
    pairs = []
    for s in range(sections):
        for d in range(dps):
            ts, tz, tc = target(s, d // 2, d % 2)
            pairs.append((s * dps + d, ts * dps + tz * 2 + tc))
    return lax.ppermute(x, AXES, pairs)


def to_section(x, k):
    return send(x, lambda s, z, c: (s ^ k, z, c))


def to_plane(x, k):
    return send(x, lambda s, z, c: (s, z ^ k, c))


def to_core(x):
    return send(x, lambda s, z, c: (s, z, c ^ 1))


def spread(blocks, move):
    return [blocks[0]] + [move(blocks[k], k) for k in (1, 2, 3)]


def with_core(blocks):
    return blocks + [to_core(x) for x in blocks]


def after(x, *first):
    return lax.optimization_barrier((x, first))[0]


def grid_facts(frames, rows, cols):
    at = jnp.arange(frames * rows * cols, dtype=jnp.int32)
    col = at % cols
    row = (at // cols) % rows
    facts = [row > 0, row < rows - 1, col > 0, col < cols - 1, col % 2 == 0, row % 2 == 0, row, col]
    facts = facts + [at // (rows * cols) == frame for frame in range(frames)]
    return jnp.stack([x.astype(jnp.float32) for x in facts])


def shift(x, by):
    length = x.shape[1]
    return pltpu.roll(x, (-by) % length, 1) if by % length else x


def row_ok(facts, d):
    return facts[0:1, :] if d < 0 else facts[1:2, :]


def col_ok(facts, d):
    return facts[2:3, :] if d < 0 else facts[3:4, :]


def sum_taps(taps_ref, facts, cols):
    ch = taps_ref.shape[0] // TAPS
    total = None
    for dx in (-1, 0, 1):
        column = None
        for dy in (-1, 0, 1):
            tap = (dy + 1) * 3 + dx + 1
            piece = taps_ref[tap * ch : (tap + 1) * ch, :]
            if dy:
                piece = shift(piece, dy * cols) * row_ok(facts, dy)
            column = piece if column is None else column + piece
        if dx:
            column = shift(column, dx) * col_ok(facts, dx)
        total = column if total is None else total + column
    return total


def spread_taps(grad, moved_ref, base, facts, cols):
    ch = grad.shape[0]
    for dx in (-1, 0, 1):
        column = shift(grad, -dx) * col_ok(facts, -dx) if dx else grad
        for dy in (-1, 0, 1):
            piece = shift(column, -dy * cols) * row_ok(facts, -dy) if dy else column
            at = base + ((dy + 1) * 3 + dx + 1) * ch
            moved_ref[at : at + ch, :] = piece.astype(jnp.bfloat16)


def corner_sum(x, cols):
    x = x + shift(x, 1)
    return x + shift(x, cols)


def from_corner(x, facts, cols):
    x = jnp.where(facts[4:5, :] > 0.5, x, shift(x, -1))
    return jnp.where(facts[5:6, :] > 0.5, x, shift(x, -cols))


def lane_sum(x):
    return jnp.sum(x, axis=1, keepdims=True)


def normalise(pre, inside):
    count = lane_sum(inside)
    mean = lane_sum(pre * inside) / count
    square = lane_sum(pre * pre * inside) / count
    scale = lax.rsqrt(square - mean * mean + eps)
    return (pre - mean) * scale, scale


def hidden_of(normed, gain, bias, inside, facts, cols, pooling):
    pre_act = normed * gain + bias
    hidden = pre_act * jax.nn.sigmoid(pre_act) * inside
    if pooling:
        raised = jnp.exp(hidden)
        total = corner_sum(raised, cols)
        pooled = corner_sum(raised * hidden, cols) / total
        hidden = raised * from_corner(pooled / total, facts, cols) * inside
    return hidden


def norm_back(grad, normed, scale, gain, bias, inside, facts, cols, pooling):
    pre_act = normed * gain + bias
    gate = jax.nn.sigmoid(pre_act)
    if pooling:
        hidden = pre_act * gate * inside
        raised = jnp.exp(hidden)
        out = grad * inside
        total = 1.0 / corner_sum(raised, cols)
        pooled = corner_sum(raised * hidden, cols) * total
        d_pooled = corner_sum(raised * out, cols) * total
        by_out = from_corner(pooled * total, facts, cols)
        by_hidden = from_corner(d_pooled * total, facts, cols)
        rest = from_corner(d_pooled * total * (1.0 - 2.0 * pooled), facts, cols)
        grad = raised * (out * by_out + hidden * by_hidden + rest)
    grad_act = grad * inside * gate * (1.0 + pre_act * (1.0 - gate))
    count = lane_sum(inside)
    shift_sum = lane_sum(grad_act)
    slope_sum = lane_sum(grad_act * normed)
    grad_pre = inside * (scale * gain) * (grad_act - shift_sum / count - normed * (slope_sum / count))
    return grad_pre.astype(jnp.bfloat16), shift_sum, slope_sum


def assemble(blocks, full_ref):
    section, _, core = place()
    ch = blocks[0].shape[0]
    for (k, j), block in zip(peer_order(), blocks):
        at = pl.multiple_of(slice_at(section, core, k, j) * ch, ch)
        full_ref[pl.ds(at, ch), :] = block[...]


def assemble_frames(blocks, full_ref, first, last):
    _, plane, core = place()
    size = last - first
    for (k, j), block in zip(peer_order(), blocks):
        frame = (plane ^ k) * 2 + (core ^ j)
        full_ref[pl.ds(pl.multiple_of(frame * size, size), size), :] = block[first:last, :]


def tap_products(weight, full_ref, taps_ref, by_cells):
    length = taps_ref.shape[1]
    step = 512 if length % 512 == 0 else length
    for at in range(0, length, step):
        if by_cells:
            taps_ref[:, at : at + step] = lax.dot_general(
                weight, full_ref[at : at + step, :], NT, preferred_element_type=jnp.float32
            )
        else:
            taps_ref[:, at : at + step] = jnp.dot(
                weight, full_ref[:, at : at + step], preferred_element_type=jnp.float32
            )


def pick_layer(layer, sources, start, target, sem):
    section, _, _ = place()
    for k, source in enumerate(sources):

        @pl.when((section ^ layer) == k)
        def _():
            pltpu.make_async_copy(source.at[pl.ds(start, target.shape[0])], target, sem).start()

    return pltpu.make_async_copy(sources[0].at[pl.ds(start, target.shape[0])], target, sem)


def affine(meta, ch):
    parts = meta[:, :LANES].astype(jnp.float32).T[:ch]
    return (
        parts[:, 0:1] + parts[:, 1:2] + parts[:, 2:3],
        parts[:, 3:4] + parts[:, 4:5] + parts[:, 5:6],
    )


def plane_inside(metas, sizes, facts):
    frames = metas.shape[0] // META_ROWS
    groups = [metas[f * META_ROWS : f * META_ROWS + 1, 0:1].astype(jnp.float32) for f in range(frames)]
    group = groups[0] * facts[FRAME_AT : FRAME_AT + 1, :]
    for f in range(1, frames):
        group = group + groups[f] * facts[FRAME_AT + f : FRAME_AT + f + 1, :]
    height = jnp.zeros_like(group)
    breadth = jnp.zeros_like(group)
    for g in range(sizes.shape[0]):
        of_group = group == float(g)
        height = jnp.where(of_group, sizes[g, 0].astype(jnp.float32), height)
        breadth = jnp.where(of_group, sizes[g, 1].astype(jnp.float32), breadth)
    on = (facts[ROW_AT : ROW_AT + 1, :] < height) & (facts[COL_AT : COL_AT + 1, :] < breadth)
    return jnp.where(on, 1.0, 0.0)


def frames_kernel(dims, groups, sizes, images, cots, *outs):
    section, plane, _ = place()
    rows, cols = dims
    cells = rows * cols
    payloads, cot_outs = outs[:4], outs[4:]
    at = lax.broadcasted_iota(jnp.int32, (cells, LANES), 0).astype(jnp.float32)
    row = jnp.floor((at + 0.5) * (1.0 / cols))
    col = at - row * cols
    channels = images.shape[2]
    width = cot_outs[0].shape[1]
    for k in range(4):
        micro = plane ^ k
        group = groups[micro, 0]
        height = sizes[0, 0]
        breadth = sizes[0, 1]
        for g in range(1, sizes.shape[0]):
            height = jnp.where(group == g, sizes[g, 0], height)
            breadth = jnp.where(group == g, sizes[g, 1], breadth)
        on = (row < height.astype(jnp.float32)) & (col < breadth.astype(jnp.float32))
        on = jnp.where(on, 1.0, 0.0)
        image = images[micro]
        for c in range(0, channels, LANES):
            piece = image[:, c : c + LANES].astype(jnp.float32) * on
            payloads[k][:cells, c : c + LANES] = piece.astype(jnp.bfloat16)
        payloads[k][cells:, :] = jnp.full((META_ROWS, channels), group.astype(jnp.float32)).astype(
            jnp.bfloat16
        )
        cot_outs[k][...] = cots[micro, :, pl.ds(pl.multiple_of(section * width, width), width)]


def pack_kernel(picks, gain, bias, weight, *outs):
    section, _, core = place()
    turned = lax.dot_general(picks[...], weight[0], NT, preferred_element_type=jnp.float32)
    tap = pl.program_id(0)
    ch = outs[0].shape[0] // TAPS // 16 * 16
    for k, out in enumerate(outs):
        at = pl.multiple_of(tap * ch, ch)
        out[pl.ds(at, ch), :] = turned[k * ch : (k + 1) * ch, :].astype(jnp.bfloat16)

    @pl.when(tap == TAPS - 1)
    def _():
        for k, out in enumerate(outs):
            lines = []
            start = pl.multiple_of((section ^ k) * 2 * ch, 2 * ch)
            for table in (gain, bias):
                line = table[:, pl.ds(start, 2 * ch)]
                line = jnp.where(core == 0, line, pltpu.roll(line, ch, 1))
                for _ in range(3):
                    part = line.astype(jnp.bfloat16).astype(jnp.float32)
                    lines.append(part)
                    line = line - part
            lines.append(jnp.zeros((META_ROWS - len(lines), 2 * ch), jnp.float32))
            block = jnp.concatenate(lines, axis=0).astype(jnp.bfloat16)
            out[TAPS * ch :, :] = jnp.zeros((META_ROWS, out.shape[1]), jnp.bfloat16)
            out[TAPS * ch :, : 2 * ch] = block


def forward_kernel(dims, layer, first, pooling, *refs):
    blocks, weights, rest = refs[:8], refs[8:12], refs[12:]
    rows, cols = dims
    cells = rows * cols
    if first:
        sizes, facts, hidden, kept, inside_out, full, taps, metas, weight, sem = rest
    else:
        inside, facts, hidden, kept, full, taps, weight, sem = rest
    copy = pick_layer(layer, weights, 0, weight, sem)
    facts_now = facts[...]
    if first:
        assemble_frames(blocks, full, 0, cells)
        assemble_frames(blocks, metas, cells, cells + META_ROWS)
        inside_now = plane_inside(metas, sizes, facts_now)
        inside_out[...] = inside_now
    else:
        assemble(blocks, full)
        inside_now = inside[...]
    copy.wait()
    ch = hidden.shape[0]
    tap_products(weight[: TAPS * ch, :], full, taps, first)
    pre = sum_taps(taps, facts_now, cols)
    normed, scale = normalise(pre, inside_now)
    length = normed.shape[1]
    kept[:, :length] = normed
    kept[:, length:] = jnp.broadcast_to(scale, (ch, LANES))
    gain, bias = affine(weight[TAPS * ch :, :], ch)
    hidden[...] = hidden_of(normed, gain, bias, inside_now, facts_now, cols, pooling).astype(jnp.bfloat16)


def turn_kernel(dims, layer, pooling, *refs):
    blocks, cots, weights = refs[:8], refs[8:16], refs[16:20]
    inside, facts, pick, hidden, grad_pre, sums, full, taps, cot_full, weight, sem = refs[20:]
    rows, cols = dims
    copy = pick_layer(layer, weights, 0, weight, sem)
    assemble(blocks, full)
    assemble_frames(cots, cot_full, 0, rows * cols)
    copy.wait()
    ch = hidden.shape[0]
    tap_products(weight[: TAPS * ch, :], full, taps, False)
    facts_now, inside_now = facts[...], inside[...]
    pre = sum_taps(taps, facts_now, cols)
    normed, scale = normalise(pre, inside_now)
    gain, bias = affine(weight[TAPS * ch :, :], ch)
    hidden[...] = hidden_of(normed, gain, bias, inside_now, facts_now, cols, pooling).astype(jnp.bfloat16)
    cotangent = lax.dot_general(pick[...], cot_full[...], NT, preferred_element_type=jnp.float32)
    grad_pre[...], shift_sum, slope_sum = norm_back(
        cotangent, normed, scale, gain, bias, inside_now, facts_now, cols, pooling
    )
    keep_sums(sums, shift_sum, slope_sum)


def keep_sums(sums, shift_sum, slope_sum):
    ch = shift_sum.shape[0]
    sums[:, :LANES] = jnp.broadcast_to(shift_sum, (ch, LANES))
    sums[:, LANES:] = jnp.broadcast_to(slope_sum, (ch, LANES))


def add_blocks(blocks):
    total = blocks[0][...].astype(jnp.float32)
    for block in blocks[1:]:
        total = total + block[...].astype(jnp.float32)
    return total


def norm_back_kernel(dims, layer, pooling, *refs):
    blocks, weights = refs[:4], refs[4:8]
    kept, inside, facts, grad_pre, sums, meta, sem = refs[8:]
    ch, length = grad_pre.shape
    copy = pick_layer(layer, weights, TAPS * ch, meta, sem)
    grad = add_blocks(blocks).astype(jnp.bfloat16).astype(jnp.float32)
    copy.wait()
    gain, bias = affine(meta[...], ch)
    grad_pre[...], shift_sum, slope_sum = norm_back(
        grad,
        kept[:, :length],
        kept[:, length : length + 1],
        gain,
        bias,
        inside[...],
        facts[...],
        dims[1],
        pooling,
    )
    keep_sums(sums, shift_sum, slope_sum)


def conv_back_kernel(dims, own, other, weight, facts, *refs):
    outs, moved = refs[:4], refs[4]
    ch = own.shape[0]
    facts_now = facts[...]
    spread_taps(own[...].astype(jnp.float32), moved, 0, facts_now, dims[1])
    spread_taps(other[...].astype(jnp.float32), moved, TAPS * ch, facts_now, dims[1])
    for k, out in enumerate(outs):
        out[...] = jnp.dot(
            weight[k * ch : (k + 1) * ch, :], moved[...], preferred_element_type=jnp.float32
        ).astype(jnp.bfloat16)


def turn_weights_kernel(picks, *refs):
    sources, outs, (full, sems) = refs[:8], refs[8:12], refs[12:]
    rows = full.shape[2]
    for layer, out in enumerate(outs):
        copies = [
            pick_layer(layer, sources[4 * j : 4 * j + 4], 0, full.at[layer % 2, j], sems.at[layer % 2, j])
            for j in range(2)
        ]
        for j in range(2):
            copies[j].wait()
            out[:, j * rows : (j + 1) * rows] = lax.dot_general(
                picks[...], full[layer % 2, j], NT, preferred_element_type=jnp.float32
            ).astype(jnp.bfloat16)


def weight_kernel(dims, first, *refs):
    blocks, (grad_pre, sums, facts), pieces, (full, moved, product) = (
        refs[:8],
        refs[8:11],
        refs[11:15],
        refs[15:],
    )
    rows, cols = dims
    _, plane, _ = place()
    if first:
        assemble_frames(blocks, full, 0, rows * cols)
    else:
        assemble(blocks, full)
    ch = grad_pre.shape[0]
    spread_taps(grad_pre[...].astype(jnp.float32), moved, 0, facts[...], cols)
    if first:
        value = jnp.dot(moved[...], full[...], preferred_element_type=jnp.float32)
    else:
        value = lax.dot_general(moved[...], full[...], NT, preferred_element_type=jnp.float32)
    product[...] = value.astype(jnp.bfloat16)
    width = pieces[0].shape[1]
    lines = []
    for at in (0, LANES):
        turned = sums[:, at : at + LANES].T
        lines.append(jnp.concatenate([turned, jnp.zeros((LANES, width - ch), jnp.float32)], axis=1)[0:1])
    sums_block = jnp.concatenate(lines + [jnp.zeros((META_ROWS - 2, width), jnp.float32)], axis=0)
    for k, piece in enumerate(pieces):
        piece[: TAPS * ch, :] = product[:, pl.ds(pl.multiple_of((plane ^ k) * width, width), width)]
        piece[TAPS * ch :, :] = sums_block.astype(jnp.bfloat16)


def input_kernel(*refs):
    blocks, (hidden, inside), pieces, (full,) = refs[:4], refs[4:6], refs[6:10], refs[10:]
    section, _, _ = place()
    ch = hidden.shape[0]
    full[:ch, :] = hidden[...]
    full[ch:, :] = (add_blocks(blocks) * inside[...]).astype(jnp.bfloat16)
    width = pieces[0].shape[1]
    for k, piece in enumerate(pieces):
        piece[...] = full[:, pl.ds(pl.multiple_of((section ^ k) * width, width), width)]


def maps_out_kernel(*refs):
    blocks, outs, (full,) = refs[:8], refs[8:10], refs[10:]
    _, plane, core = place()
    ch = blocks[0].shape[0] // 2
    cells = outs[0].shape[0]
    for n, out in enumerate(outs):
        for (k, j), block in zip(peer_order(), blocks):
            at = pl.multiple_of(slice_at(plane, core, k, j) * ch, ch)
            full[pl.ds(at, ch), :] = block[n * ch : (n + 1) * ch, :]
        both = full[...].astype(jnp.float32)
        mine = jnp.where(core == 0, both[:, :cells], both[:, cells:])
        out[...] = mine.T.astype(out.dtype)


def grads_out_kernel(*refs):
    blocks, (weight_out, shift_out, slope_out), (full, turned) = refs[:8], refs[8:11], refs[11:]
    section, plane, core = place()
    taps, rows, channels = weight_out.shape
    for tap in range(taps):
        for (k, j), block in zip(peer_order(), blocks):
            at = pl.multiple_of(slice_at(section, core, k, j) * rows, rows)
            full[pl.ds(at, rows), :] = block[tap * rows : (tap + 1) * rows, :].astype(jnp.float32)
        turned[...] = full[...].T
        weight_out[tap] = turned[pl.ds(pl.multiple_of(core * rows, rows), rows), :]
    shift_row = jnp.zeros((1, rows), jnp.float32)
    slope_row = jnp.zeros((1, rows), jnp.float32)
    for (k, j), block in zip(peer_order(), blocks):
        if j == 0:
            tail = block[taps * rows :, :].astype(jnp.float32)
            mine = (section ^ k) == plane
            shift_row = shift_row + jnp.where(mine, tail[0:1, :rows], 0.0)
            slope_row = slope_row + jnp.where(mine, tail[1:2, :rows], 0.0)
    shift_out[...] = shift_row
    slope_out[...] = slope_row


def call(kernel, outs, scratch, args, name, held=(), scalars=(), flops=0, copies=None):
    shapes = [jax.ShapeDtypeStruct(shape, dtype) for shape, dtype in outs]
    moved = sum(a.size * a.dtype.itemsize for a in args)
    moved += sum(s.size * s.dtype.itemsize for s in shapes)
    spaces = [
        pltpu.SMEM if n in scalars else pl.ANY if n in held else pltpu.VMEM for n in range(len(args))
    ]
    scratch_shapes = [pltpu.VMEM(shape, dtype) for shape, dtype in scratch]
    if copies is not None:
        scratch_shapes.append(pltpu.SemaphoreType.DMA(copies))
    return pl.pallas_call(
        kernel,
        out_shape=shapes,
        in_specs=[pl.BlockSpec(memory_space=space) for space in spaces],
        out_specs=[pl.BlockSpec(memory_space=pltpu.VMEM)] * len(shapes),
        scratch_shapes=scratch_shapes,
        compiler_params=pltpu.CompilerParams(vmem_limit_bytes=VMEM_LIMIT),
        cost_estimate=pl.CostEstimate(flops=flops, bytes_accessed=moved, transcendentals=0),
        name=name,
    )(*args)


def one_hot(index, size):
    return (index[:, None] == jnp.arange(size, dtype=jnp.int32)[None, :]).astype(jnp.bfloat16)


def plane_shards(images, image_group, group_size, conv_weight, bn_gain, bn_bias, cotangent):
    section, plane, core = place()
    micro_total, _, rows, cols, channels = images.shape
    layers = lax.axis_size("section")
    last = layers - 1
    cells = rows * cols
    frames = 2 * micro_total
    length = frames * cells
    ch = channels // 8
    dims = (rows, cols)
    bf16, f32 = jnp.bfloat16, jnp.float32
    facts = grid_facts(frames, rows, cols)
    conv_flops = 2 * TAPS * ch * channels * length
    slice_rows = TAPS * ch + META_ROWS

    full_map = ((channels, length), bf16)
    full_frames = ((length, channels), bf16)
    tap_scratch = ((TAPS * ch, length), f32)
    weight_scratch = ((slice_rows, channels), bf16)
    map_out = ((ch, length), bf16)
    sums_out = ((ch, 2 * LANES), f32)

    sent = call(
        partial(frames_kernel, dims),
        [((cells + META_ROWS, channels), bf16)] * 4 + [((cells, 2 * ch), bf16)] * 4,
        [],
        [
            image_group,
            group_size,
            images.reshape(micro_total, cells, channels),
            cotangent.reshape(micro_total, cells, channels),
        ],
        "frames",
        scalars=(0, 1),
    )
    frames_in = with_core(spread(sent[:4], to_plane))

    taps_first = conv_weight[0].transpose(1, 2, 0, 3).reshape(TAPS, channels, channels)
    row_at = jnp.arange(ch, dtype=jnp.int32)
    picks = one_hot(
        jnp.concatenate([slice_at(section, core, k, 0) * ch + row_at for k in range(4)]), channels
    )
    packed = pl.pallas_call(
        pack_kernel,
        grid=(TAPS,),
        out_shape=[jax.ShapeDtypeStruct((slice_rows, channels), bf16)] * 4,
        in_specs=[
            pl.BlockSpec((4 * ch, channels), lambda t: (0, 0)),
            pl.BlockSpec((1, channels), lambda t: (0, 0)),
            pl.BlockSpec((1, channels), lambda t: (0, 0)),
            pl.BlockSpec((1, channels, channels), lambda t: (t, 0, 0)),
        ],
        out_specs=[pl.BlockSpec((slice_rows, channels), lambda t: (0, 0))] * 4,
        compiler_params=pltpu.CompilerParams(vmem_limit_bytes=VMEM_LIMIT),
        name="weight_pack",
    )(picks, bn_gain, bn_bias, taps_first)
    slices = spread(packed, to_section)

    gathered = [frames_in]
    kept = []
    inside = None
    for layer in range(last):
        first = layer == 0
        hidden, normed, *mask = call(
            partial(forward_kernel, dims, layer, first, layer == CONVS - 1),
            [map_out, ((ch, length + LANES), f32)] + ([((1, length), f32)] if first else []),
            [full_frames if first else full_map, tap_scratch]
            + ([((frames * META_ROWS, channels), bf16)] if first else [])
            + [weight_scratch],
            [*gathered[layer], *slices, group_size if first else inside, facts],
            "forward",
            held=range(8, 12),
            scalars=(12,) if first else (),
            flops=conv_flops,
            copies=(),
        )
        kept.append(normed)
        if first:
            inside = mask[0]
            cot_sent = after(sent[4:], hidden)
            cots = with_core(spread(cot_sent, to_plane))
            slice_pairs = slices + [to_core(x) for x in after(slices, hidden)]
        if layer == 1:
            turned = call(
                turn_weights_kernel,
                [((4 * ch, 2 * TAPS * ch), bf16)] * layers,
                [((2, 2, TAPS * ch, channels), bf16)],
                [after(picks, hidden), *slice_pairs],
                "turn_weights",
                held=range(1, 9),
                copies=(2, 2),
            )
        gathered.append(with_core(spread([hidden] * 4, to_section)))
        if first:
            gathered[1] = list(after(gathered[1], cots))
        if layer == 1:
            gathered[2] = list(after(gathered[2], turned))
    activation, grad_pre, sums = call(
        partial(turn_kernel, dims, last, last == CONVS - 1),
        [map_out, map_out, sums_out],
        [full_map, tap_scratch, ((length, 2 * ch), bf16), weight_scratch],
        [*gathered[last], *cots, *slices, inside, facts, one_hot(core * ch + row_at, 2 * ch)],
        "turn",
        held=range(16, 20),
        flops=conv_flops,
        copies=(),
    )

    shares = [None] * layers
    for layer in range(last, -1, -1):
        parts = call(
            partial(conv_back_kernel, dims),
            [map_out] * 4,
            [((2 * TAPS * ch, length), bf16)],
            [grad_pre, to_core(grad_pre), turned[layer], facts],
            "conv_back",
            flops=conv_flops,
        )
        first = layer == 0
        pieces = call(
            partial(weight_kernel, dims, first),
            [((slice_rows, 2 * ch), bf16)] * 4,
            [full_frames if first else full_map, ((TAPS * ch, length), bf16), ((TAPS * ch, channels), bf16)],
            [*gathered[layer], after(grad_pre, parts), sums, facts],
            "weight_share",
            flops=conv_flops,
        )
        blocks = spread(parts, to_section)
        blocks = after(blocks, pieces)
        shares[layer] = sum(x.astype(f32) for x in spread(pieces, to_plane)).astype(bf16)
        if layer:
            grad_pre, sums = call(
                partial(norm_back_kernel, dims, layer - 1, layer - 1 == CONVS - 1),
                [map_out, sums_out],
                [((META_ROWS, channels), bf16)],
                [*blocks, *slices, kept[layer - 1], inside, facts],
                "norm_back",
                held=range(4, 8),
                copies=(),
            )
    maps = call(
        input_kernel,
        [((2 * ch, 2 * cells), bf16)] * 4,
        [((2 * ch, length), bf16)],
        [*blocks, activation, inside],
        "input",
    )
    maps = [send(x, lambda s, z, c, k=k: (z, s ^ k, c)) for k, x in enumerate(maps)]
    activations, input_grad = call(
        maps_out_kernel,
        [((cells, channels), bf16)] * 2,
        [((channels, 2 * cells), bf16)],
        with_core(maps),
        "maps_out",
    )

    chosen = [lax.select_n(section ^ k, *shares) for k in range(4)]
    weight_grad, bias_grad, gain_grad = call(
        grads_out_kernel,
        [((TAPS, ch, channels), f32), ((1, ch), f32), ((1, ch), f32)],
        [((channels, 2 * ch), f32), ((2 * ch, channels), f32)],
        with_core(spread(chosen, to_section)),
        "grads_out",
    )
    weight_grad = weight_grad.reshape(3, 3, ch, channels).transpose(2, 0, 1, 3)[None]
    return (
        activations.reshape(1, 1, rows, cols, channels),
        input_grad.reshape(1, 1, rows, cols, channels),
        weight_grad,
        gain_grad,
        bias_grad,
    )


def fits_plane_plan(images, conv_weight, sections, dps):
    micro_total, images_total, rows, cols, channels = images.shape
    return (
        sections == 4
        and dps == 2 * sections
        and micro_total == sections
        and conv_weight.shape[0] == sections
        and images_total == dps
        and rows % 2 == 0
        and cols % 2 == 0
        and (rows * cols) % 64 == 0
        and channels == 512
    )


def solution(mesh):
    in_specs = (
        P(None, "dp", None, None, None),
        P(None, "dp"),
        P(),
        P("section", None, None, None, None),
        P("section", None),
        P("section", None),
        P(None, "dp", None, None, None),
    )
    out_specs = (
        P("section", "dp", None, None, None),
        P("section", "dp", None, None, None),
        P("section", "dp", None, None, None),
        P("section", "dp"),
        P("section", "dp"),
    )
    sections, dps = mesh.shape["section"], mesh.shape["dp"]

    def program(images, image_group, group_size, conv_weight, bn_gain, bn_bias, cotangent):
        plan = plane_shards if fits_plane_plan(images, conv_weight, sections, dps) else pipeline_shards
        sharded = jax.shard_map(plan, mesh=mesh, in_specs=in_specs, out_specs=out_specs, check_vma=False)
        return sharded(images, image_group, group_size, conv_weight, bn_gain, bn_bias, cotangent)

    return program
```

```python
import math
from functools import partial

import jax
import jax.numpy as jnp
import numpy as np
from jax import lax
from jax.experimental import pallas as pl
from jax.experimental.pallas import tpu as pltpu
from jax.sharding import PartitionSpec as P

CONVS = 2


eps = 1e-05


def from_behind(x, axis, by):
    peers = lax.axis_size(axis)
    pairs = [(i, i + by) for i in range(peers) if 0 <= i + by < peers]
    return lax.ppermute(x, axis, pairs)


def canvas_mask(image_group, group_size, canvas_rows, canvas_cols):
    groups_n = group_size.shape[0]
    onehot = image_group[..., None] == jnp.arange(groups_n, dtype=jnp.int32)
    height = jnp.sum(jnp.where(onehot, group_size[:, 0], 0), axis=-1)
    breadth = jnp.sum(jnp.where(onehot, group_size[:, 1], 0), axis=-1)
    inside_rows = jnp.arange(canvas_rows, dtype=jnp.int32)[:, None] < height[..., None, None]
    inside_cols = jnp.arange(canvas_cols, dtype=jnp.int32)[None, :] < breadth[..., None, None]
    return (inside_rows & inside_cols).astype(jnp.float32)[..., None]


def window_pool(hidden):
    frames, height, breadth, channels = hidden.shape
    blocks = hidden.reshape(frames, height // 2, 2, breadth // 2, 2, channels)
    window_max = jnp.max(blocks, axis=(2, 4), keepdims=True)
    raised = jnp.exp(blocks - window_max)
    weights = raised / jnp.sum(raised, axis=(2, 4), keepdims=True)
    pooled = jnp.sum(weights * blocks, axis=(2, 4), keepdims=True)
    return (weights * pooled).reshape(frames, height, breadth, channels)


def activate(pre_act, inside, pooling):
    hidden = jax.nn.silu(pre_act) * inside
    return jnp.where(pooling, window_pool(hidden) * inside, hidden)


def conv_forward(layer_in, weight):
    return lax.conv_general_dilated(
        layer_in,
        weight,
        (1, 1),
        "SAME",
        dimension_numbers=("NHWC", "IHWO", "NHWC"),
        preferred_element_type=jnp.float32,
    )


def conv_data_back(grad_pre, weight):
    flipped = weight[:, ::-1, ::-1, :]
    return lax.conv_general_dilated(
        grad_pre,
        flipped,
        (1, 1),
        "SAME",
        dimension_numbers=("NHWC", "OHWI", "NHWC"),
        preferred_element_type=jnp.float32,
    )


def weight_back(layer_in, grad_pre):
    height = layer_in.shape[1]
    breadth = layer_in.shape[2]
    padded = jnp.pad(layer_in, ((0, 0), (1, 1), (1, 1), (0, 0)))
    pieces = []
    for tap_row in range(3):
        for tap_col in range(3):
            window = padded[:, tap_row : tap_row + height, tap_col : tap_col + breadth, :]
            pieces.append(
                jnp.einsum("nhwi,nhwo->io", window, grad_pre, preferred_element_type=jnp.float32)
            )
    return jnp.stack(pieces, axis=1).reshape(layer_in.shape[3], 3, 3, grad_pre.shape[3])


def layer_forward(layer_in, weight, gain_row, bias_row, inside, pooling):
    pre_norm = conv_forward(layer_in, weight)
    sums = lax.psum(
        (
            jnp.sum(pre_norm * inside, axis=(0, 1, 2)),
            jnp.sum(pre_norm * pre_norm * inside, axis=(0, 1, 2)),
            jnp.sum(inside),
        ),
        "dp",
    )
    pixel_total = sums[2]
    mean_val = sums[0] / pixel_total
    scale_inv = lax.rsqrt(sums[1] / pixel_total - mean_val * mean_val + eps)
    pre_act = (pre_norm - mean_val) * scale_inv * gain_row + bias_row
    hidden = activate(pre_act, inside, pooling)
    return (pre_norm, mean_val, scale_inv, pixel_total, hidden)


def layer_backward(
    grad_out,
    layer_in,
    pre_norm,
    mean_val,
    scale_inv,
    pixel_total,
    weight,
    gain_row,
    bias_row,
    inside,
    pooling,
):
    normed = (pre_norm - mean_val) * scale_inv
    pre_act = normed * gain_row + bias_row
    hidden_out, pullback = jax.vjp(partial(activate, inside=inside, pooling=pooling), pre_act)
    grad_act = pullback(grad_out)[0]
    sums = lax.psum(
        (jnp.sum(grad_act, axis=(0, 1, 2)), jnp.sum(grad_act * normed, axis=(0, 1, 2))), "dp"
    )
    shift_term = sums[0] / pixel_total
    slope_term = sums[1] / pixel_total
    grad_pre = (
        inside * scale_inv * gain_row * (grad_act - shift_term - normed * slope_term)
    ).astype(jnp.bfloat16)
    weight_term = weight_back(layer_in, grad_pre)
    grad_in = conv_data_back(grad_pre, weight).astype(jnp.bfloat16)
    return (grad_in, weight_term, sums[1], sums[0])


def pipeline_shards(images, image_group, group_size, conv_weight, bn_gain, bn_bias, cotangent):
    section_index = lax.axis_index("section")
    sections = lax.axis_size("section")
    micro_total = images.shape[0]
    channels = conv_weight.shape[1]
    inside_all = canvas_mask(image_group, group_size, images.shape[2], images.shape[3])
    ticks = micro_total + sections - 1
    weight = conv_weight[0]
    gain_row = bn_gain[0]
    bias_row = bn_bias[0]
    pool_here = section_index == CONVS - 1
    received = jnp.zeros(images.shape[1:], jnp.bfloat16)
    kept_in, kept_pre, kept_mean, kept_scale, kept_total, finished = ([], [], [], [], [], [])
    for tick in range(ticks):
        micro_pos = jnp.clip(tick - section_index, 0, micro_total - 1)
        inside = inside_all[micro_pos]
        fresh = (images[micro_pos].astype(jnp.float32) * inside).astype(jnp.bfloat16)
        layer_in = jnp.where(section_index == 0, fresh, received)
        pre_norm, mean_val, scale_inv, pixel_total, hidden = layer_forward(
            layer_in, weight, gain_row, bias_row, inside, pool_here
        )
        sent = hidden.astype(jnp.bfloat16)
        if tick < ticks - 1:
            received = from_behind(sent, "section", 1)
        kept_in.append(layer_in)
        kept_pre.append(pre_norm)
        kept_mean.append(mean_val)
        kept_scale.append(scale_inv)
        kept_total.append(pixel_total)
        finished.append(sent)
    stack_in = jnp.stack(kept_in)
    stack_pre = jnp.stack(kept_pre)
    stack_mean = jnp.stack(kept_mean)
    stack_scale = jnp.stack(kept_scale)
    stack_total = jnp.stack(kept_total)
    returned = jnp.zeros(images.shape[1:], jnp.bfloat16)
    weight_sum = jnp.zeros(conv_weight.shape[1:], jnp.float32)
    gain_sum = jnp.zeros((channels,), jnp.float32)
    bias_sum = jnp.zeros((channels,), jnp.float32)
    input_list = []
    for tick in range(ticks):
        micro_raw = tick - (sections - 1 - section_index)
        valid = ((micro_raw >= 0) & (micro_raw < micro_total)).astype(jnp.float32)
        micro_pos = jnp.clip(micro_raw, 0, micro_total - 1)
        forward_tick = jnp.clip(micro_pos + section_index, 0, ticks - 1)
        inside = inside_all[micro_pos]
        grad_out = jnp.where(
            section_index == sections - 1,
            cotangent[micro_pos].astype(jnp.float32),
            returned.astype(jnp.float32),
        )
        grad_in, weight_term, gain_term, bias_term = layer_backward(
            grad_out,
            stack_in[forward_tick],
            stack_pre[forward_tick],
            stack_mean[forward_tick],
            stack_scale[forward_tick],
            stack_total[forward_tick],
            weight,
            gain_row,
            bias_row,
            inside,
            pool_here,
        )
        weight_sum = weight_sum + valid * weight_term
        gain_sum = gain_sum + valid * gain_term
        bias_sum = bias_sum + valid * bias_term
        if tick < ticks - 1:
            returned = from_behind(grad_in, "section", -1)
        input_list.append((grad_in.astype(jnp.float32) * inside).astype(jnp.bfloat16))
    out_stack = jnp.stack(finished[sections - 1 :], axis=0)
    grad_stack = jnp.stack(input_list[sections - 1 :], axis=0)
    out_back, grad_back = (
        lax.all_to_all(out_stack, "section", split_axis=0, concat_axis=1, tiled=True),
        lax.all_to_all(grad_stack, "section", split_axis=0, concat_axis=1, tiled=True),
    )
    activations = out_back[:, sections - 1 : sections]
    input_grad = grad_back[:, 0:1]
    weight_grad = lax.psum_scatter(weight_sum[None], "dp", scatter_dimension=1, tiled=True)
    share = channels // lax.axis_size("dp")
    gain_grad = lax.dynamic_slice_in_dim(gain_sum, lax.axis_index("dp") * share, share)[None]
    bias_grad = lax.dynamic_slice_in_dim(bias_sum, lax.axis_index("dp") * share, share)[None]
    return (activations, input_grad, weight_grad, gain_grad, bias_grad)


AXES = ("section", "dp")
TAPS = 9
VMEM_LIMIT = 24 * 1024 * 1024
META_ROWS = 16
LANES = 128
ROW_AT, COL_AT, FRAME_AT = 6, 7, 8
NT = (((1,), (1,)), ((), ()))


def place():
    dp_index = lax.axis_index("dp")
    return lax.axis_index("section"), dp_index // 2, dp_index % 2


def peer_order():
    return [(k, j) for j in range(2) for k in range(4)]


def slice_at(section, core, k, j):
    return (core ^ j) * lax.axis_size("section") + (section ^ k)


def send(x, target):
    sections = lax.axis_size("section")
    dps = lax.axis_size("dp")
    pairs = []
    for s in range(sections):
        for d in range(dps):
            ts, tz, tc = target(s, d // 2, d % 2)
            pairs.append((s * dps + d, ts * dps + tz * 2 + tc))
    return lax.ppermute(x, AXES, pairs)


def to_section(x, k):
    return send(x, lambda s, z, c: (s ^ k, z, c))


def to_plane(x, k):
    return send(x, lambda s, z, c: (s, z ^ k, c))


def to_core(x):
    return send(x, lambda s, z, c: (s, z, c ^ 1))


def spread(blocks, move, *beside):
    moved = lax.optimization_barrier(([move(blocks[k], k) for k in (1, 2, 3)], beside))[0]
    return [blocks[0]] + moved


def with_core(blocks):
    return blocks + [to_core(x) for x in blocks]


def after(x, *first):
    return lax.optimization_barrier((x, first))[0]


def grid_facts(frames, rows, cols):
    at = np.arange(frames * rows * cols)
    col = at % cols
    row = (at // cols) % rows
    facts = [row > 0, row < rows - 1, col > 0, col < cols - 1, col % 2 == 0, row % 2 == 0, row, col]
    facts = facts + [at // (rows * cols) == frame for frame in range(frames)]
    return jnp.asarray(np.stack(facts).astype(np.float32))


def shift(x, by):
    length = x.shape[1]
    return pltpu.roll(x, (-by) % length, 1) if by % length else x


def row_ok(facts, d):
    return facts[0:1, :] if d < 0 else facts[1:2, :]


def col_ok(facts, d):
    return facts[2:3, :] if d < 0 else facts[3:4, :]


def sum_taps(taps_ref, facts, cols):
    ch = taps_ref.shape[0] // TAPS
    total = None
    for dx in (-1, 0, 1):
        column = None
        for dy in (-1, 0, 1):
            tap = (dy + 1) * 3 + dx + 1
            piece = taps_ref[tap * ch : (tap + 1) * ch, :]
            if dy:
                piece = shift(piece, dy * cols) * row_ok(facts, dy)
            column = piece if column is None else column + piece
        if dx:
            column = shift(column, dx) * col_ok(facts, dx)
        total = column if total is None else total + column
    return total


def spread_taps(grad, moved_ref, base, facts, cols):
    ch = grad.shape[0]
    for dx in (-1, 0, 1):
        column = shift(grad, -dx) * col_ok(facts, -dx) if dx else grad
        for dy in (-1, 0, 1):
            piece = shift(column, -dy * cols) * row_ok(facts, -dy) if dy else column
            at = base + ((dy + 1) * 3 + dx + 1) * ch
            moved_ref[at : at + ch, :] = piece.astype(jnp.bfloat16)


def corner_sum(x, cols):
    x = x + shift(x, 1)
    return x + shift(x, cols)


def from_corner(x, facts, cols):
    x = jnp.where(facts[4:5, :] > 0.5, x, shift(x, -1))
    return jnp.where(facts[5:6, :] > 0.5, x, shift(x, -cols))


def lane_sum(x):
    return jnp.sum(x, axis=1, keepdims=True)


def normalise(pre, inside):
    count = lane_sum(inside)
    mean = lane_sum(pre * inside) / count
    square = lane_sum(pre * pre * inside) / count
    scale = lax.rsqrt(square - mean * mean + eps)
    return (pre - mean) * scale, scale


def hidden_of(normed, gain, bias, inside, facts, cols, pooling):
    pre_act = normed * gain + bias
    hidden = pre_act * jax.nn.sigmoid(pre_act) * inside
    if pooling:
        raised = jnp.exp(hidden)
        total = corner_sum(raised, cols)
        pooled = corner_sum(raised * hidden, cols) / total
        hidden = raised * from_corner(pooled / total, facts, cols) * inside
    return hidden


def norm_back(grad, normed, scale, gain, bias, inside, facts, cols, pooling):
    pre_act = normed * gain + bias
    gate = jax.nn.sigmoid(pre_act)
    if pooling:
        hidden = pre_act * gate * inside
        raised = jnp.exp(hidden)
        out = grad * inside
        total = 1.0 / corner_sum(raised, cols)
        pooled = corner_sum(raised * hidden, cols) * total
        d_pooled = corner_sum(raised * out, cols) * total
        by_out = from_corner(pooled * total, facts, cols)
        by_hidden = from_corner(d_pooled * total, facts, cols)
        rest = from_corner(d_pooled * total * (1.0 - 2.0 * pooled), facts, cols)
        grad = raised * (out * by_out + hidden * by_hidden + rest)
    grad_act = grad * inside * gate * (1.0 + pre_act * (1.0 - gate))
    count = lane_sum(inside)
    shift_sum = lane_sum(grad_act)
    slope_sum = lane_sum(grad_act * normed)
    grad_pre = inside * (scale * gain) * (grad_act - shift_sum / count - normed * (slope_sum / count))
    return grad_pre.astype(jnp.bfloat16), shift_sum, slope_sum


def assemble(blocks, full_ref):
    section, _, core = place()
    ch = blocks[0].shape[0]
    for (k, j), block in zip(peer_order(), blocks):
        at = pl.multiple_of(slice_at(section, core, k, j) * ch, ch)
        full_ref[pl.ds(at, ch), :] = block[...]


def assemble_frames(blocks, full_ref, rows, lanes):
    _, plane, core = place()
    size = rows.stop - rows.start
    for (k, j), block in zip(peer_order(), blocks):
        frame = (plane ^ k) * 2 + (core ^ j)
        full_ref[pl.ds(pl.multiple_of(frame * size, size), size), :] = block[rows, lanes]


def start_all(copies):
    for copy in copies:
        copy.start()
    return copies


def wait_all(copies):
    for copy in copies:
        copy.wait()


def tap_products(weight, full_ref, taps_ref, by_cells):
    length = taps_ref.shape[1]
    step = 512 if length % 512 == 0 else length
    for at in range(0, length, step):
        if by_cells:
            taps_ref[:, at : at + step] = lax.dot_general(
                weight, full_ref[at : at + step, :], NT, preferred_element_type=jnp.float32
            )
        else:
            taps_ref[:, at : at + step] = jnp.dot(
                weight, full_ref[:, at : at + step], preferred_element_type=jnp.float32
            )


def pick_layer(layer, sources, start, target, sem):
    section, _, _ = place()
    rows = pl.ds(start, target.shape[0])
    for k, source in enumerate(sources):

        @pl.when((section ^ layer) == k)
        def _():
            pltpu.make_async_copy(source.at[rows], target, sem).start()

    return pltpu.make_async_copy(sources[0].at[rows], target, sem)


def affine(meta, ch):
    parts = meta[:, :LANES].astype(jnp.float32).T[:ch]
    return (
        parts[:, 0:1] + parts[:, 1:2] + parts[:, 2:3],
        parts[:, 3:4] + parts[:, 4:5] + parts[:, 5:6],
    )


def plane_inside(metas, facts):
    frames = metas.shape[0] // META_ROWS
    extents = []
    for line in (0, 1):
        total = None
        for f in range(frames):
            at = f * META_ROWS + line
            extent = metas[at : at + 1, 0:1].astype(jnp.float32) * facts[FRAME_AT + f : FRAME_AT + f + 1, :]
            total = extent if total is None else total + extent
        extents.append(total)
    on = (facts[ROW_AT : ROW_AT + 1, :] < extents[0]) & (facts[COL_AT : COL_AT + 1, :] < extents[1])
    return jnp.where(on, 1.0, 0.0)


def frames_kernel(dims, group_table, size_table, images, cots, *refs):
    payloads, (image_in, cot_in, groups, sizes, sems) = refs[:4], refs[4:]
    copies = start_all(
        [
            pltpu.make_async_copy(group_table, groups, sems.at[0]),
            pltpu.make_async_copy(size_table, sizes, sems.at[1]),
            pltpu.make_async_copy(images, image_in, sems.at[2]),
            pltpu.make_async_copy(cots, cot_in, sems.at[3]),
        ]
    )
    section, plane, _ = place()
    rows, cols = dims
    cells = rows * cols
    at = lax.broadcasted_iota(jnp.int32, (cells, LANES), 0).astype(jnp.float32)
    row = jnp.floor((at + 0.5) * (1.0 / cols))
    col = at - row * cols
    channels = images.shape[2]
    half = channels // 2
    wait_all(copies)
    for k in range(4):
        micro = plane ^ k
        group = groups[0, micro]
        height = sizes[0, 0]
        breadth = sizes[1, 0]
        for g in range(1, sizes.shape[1]):
            height = jnp.where(group == g, sizes[0, g], height)
            breadth = jnp.where(group == g, sizes[1, g], breadth)
        height = height.astype(jnp.float32)
        breadth = breadth.astype(jnp.float32)
        on = jnp.where((row < height) & (col < breadth), 1.0, 0.0)
        image = image_in[micro]
        for c in range(0, channels, LANES):
            piece = image[:, c : c + LANES].astype(jnp.float32) * on
            payloads[k][:cells, c : c + LANES] = piece.astype(jnp.bfloat16)
        line = lax.broadcasted_iota(jnp.int32, (META_ROWS, channels + LANES), 0)
        payloads[k][cells:, :] = jnp.where(line == 0, height, breadth).astype(jnp.bfloat16)
        tile = section // 2 * LANES
        low = cot_in[micro, :, pl.ds(pl.multiple_of(tile, LANES), LANES)].astype(jnp.float32)
        high = cot_in[micro, :, pl.ds(pl.multiple_of(half + tile, LANES), LANES)].astype(jnp.float32)
        odd = section % 2 == 1
        low = jnp.where(odd, pltpu.roll(low, LANES // 2, 1), low)
        high = jnp.where(odd, high, pltpu.roll(high, LANES // 2, 1))
        lane = lax.broadcasted_iota(jnp.int32, (cells, LANES), 1)
        both = jnp.where(lane < LANES // 2, low, high).astype(jnp.bfloat16)
        payloads[k][:cells, channels:] = both


def pack_kernel(gain, bias, weight, *refs):
    outs, (own, columns, turned, tables, sems) = refs[:4], refs[4:]
    section, _, core = place()
    width = columns.shape[2]
    ch = width // 4
    start = pl.multiple_of(core * width, width)
    copies = start_all(
        [
            pltpu.make_async_copy(weight.at[tap, :, pl.ds(start, width)], columns.at[tap], sems.at[tap])
            for tap in range(TAPS)
        ]
    )
    table_copies = start_all(
        [
            pltpu.make_async_copy(gain, tables.at[0], sems.at[TAPS]),
            pltpu.make_async_copy(bias, tables.at[1], sems.at[TAPS + 1]),
        ]
    )
    wait_all(table_copies)
    targets = [own, *outs[1:]]
    for k, out in enumerate(targets):
        lines = []
        tile = pl.multiple_of(start + (section ^ k) // 2 * LANES, LANES)
        odd = (section ^ k) % 2 == 1
        for m in range(2):
            line = tables[m, :, pl.ds(tile, LANES)]
            line = jnp.where(odd, pltpu.roll(line, ch, 1), line)
            for _ in range(3):
                part = line.astype(jnp.bfloat16).astype(jnp.float32)
                lines.append(part)
                line = line - part
        lines.append(jnp.zeros((META_ROWS - len(lines), LANES), jnp.float32))
        out[TAPS * ch :, :] = jnp.zeros((META_ROWS, out.shape[1]), jnp.bfloat16)
        out[TAPS * ch :, :LANES] = jnp.concatenate(lines, axis=0).astype(jnp.bfloat16)
    for tap in range(TAPS):
        copies[tap].wait()
        turned[...] = columns[tap].T
        for k, out in enumerate(targets):
            rows = pl.ds(pl.multiple_of((section ^ k) * ch, ch), ch)
            out[tap * ch : (tap + 1) * ch, :] = turned[rows, :]
    own_copy = pltpu.make_async_copy(own, outs[0], sems.at[TAPS])
    own_copy.start()
    own_copy.wait()


def pick_kernel(layer, *refs):
    sources, (out, sem) = refs[:4], refs[4:]
    pick_layer(layer, sources, 0, out, sem.at[0]).wait()


def forward_kernel(dims, layer, first, pooling, *refs):
    blocks, weights, rest = refs[:8], refs[8 : 12 if first else 9], refs[12 if first else 9 :]
    rows, cols = dims
    cells = rows * cols
    if first:
        facts, pick, hidden, kept, full_out, inside_out, cot_out, full, taps, stage, weight, metas, *rest = rest
        cot_full, cot, sems = rest
        copy = pick_layer(layer, weights, 0, weight, sems.at[2])
    else:
        inside, facts, hidden, kept, full_out, full, taps, stage, sems = rest
        (weight,) = weights
    facts_now = facts[...]
    if first:
        channels = full.shape[1]
        assemble_frames(blocks, full, slice(0, cells), slice(0, channels))
    else:
        assemble(blocks, full)
    full_copy = pltpu.make_async_copy(full, full_out, sems.at[0])
    full_copy.start()
    if first:
        assemble_frames(blocks, metas, slice(cells, cells + META_ROWS), slice(0, channels))
        assemble_frames(blocks, cot_full, slice(0, cells), slice(channels, channels + LANES))
        inside_now = plane_inside(metas, facts_now)
        inside_out[...] = inside_now
        copy.wait()
    else:
        inside_now = inside[...]
    ch = hidden.shape[0]
    tap_products(weight[: TAPS * ch, :], full, taps, first)
    if first:
        cot[...] = lax.dot_general(
            pick[...], cot_full[...], NT, preferred_element_type=jnp.float32
        ).astype(jnp.bfloat16)
        cot_copy = pltpu.make_async_copy(cot, cot_out, sems.at[3])
        cot_copy.start()
    pre = sum_taps(taps, facts_now, cols)
    normed, scale = normalise(pre, inside_now)
    length = normed.shape[1]
    stage[:, :length] = normed
    stage[:, length:] = jnp.broadcast_to(scale, (ch, LANES))
    kept_copy = pltpu.make_async_copy(stage, kept, sems.at[1])
    kept_copy.start()
    gain, bias = affine(weight[TAPS * ch :, :], ch)
    hidden[...] = hidden_of(normed, gain, bias, inside_now, facts_now, cols, pooling).astype(jnp.bfloat16)
    if first:
        cot_copy.wait()
    full_copy.wait()
    kept_copy.wait()


def turn_kernel(dims, layer, pooling, *refs):
    blocks, (weight, cot_in, inside, facts) = refs[:8], refs[8:12]
    hidden_out, full_out, grad_pre, sums, full, taps, cot, hidden, sems = refs[12:]
    cols = dims[1]
    cot_copy = pltpu.make_async_copy(cot_in, cot, sems.at[0])
    cot_copy.start()
    assemble(blocks, full)
    full_copy = pltpu.make_async_copy(full, full_out, sems.at[1])
    full_copy.start()
    ch = grad_pre.shape[0]
    tap_products(weight[: TAPS * ch, :], full, taps, False)
    facts_now, inside_now = facts[...], inside[...]
    pre = sum_taps(taps, facts_now, cols)
    normed, scale = normalise(pre, inside_now)
    gain, bias = affine(weight[TAPS * ch :, :], ch)
    hidden[...] = hidden_of(normed, gain, bias, inside_now, facts_now, cols, pooling).astype(jnp.bfloat16)
    hidden_copy = pltpu.make_async_copy(hidden, hidden_out, sems.at[2])
    hidden_copy.start()
    cot_copy.wait()
    grad_pre[...], shift_sum, slope_sum = norm_back(
        cot[...].astype(jnp.float32), normed, scale, gain, bias, inside_now, facts_now, cols, pooling
    )
    keep_sums(sums, shift_sum, slope_sum)
    full_copy.wait()
    hidden_copy.wait()


def keep_sums(sums, shift_sum, slope_sum):
    ch = shift_sum.shape[0]
    sums[:, :LANES] = jnp.broadcast_to(shift_sum, (ch, LANES))
    sums[:, LANES:] = jnp.broadcast_to(slope_sum, (ch, LANES))


def add_blocks(blocks):
    total = blocks[0][...].astype(jnp.float32)
    for block in blocks[1:]:
        total = total + block[...].astype(jnp.float32)
    return total


def fetch_kernel(layer, kept, *refs):
    sources, (kept_out, meta_out, sems) = refs[:4], refs[4:]
    copy = pltpu.make_async_copy(kept, kept_out, sems.at[0])
    copy.start()
    start = sources[0].shape[0] - META_ROWS
    pick_layer(layer, sources, start, meta_out, sems.at[1]).wait()
    copy.wait()


def norm_back_kernel(dims, pooling, *refs):
    blocks, (kept, meta, inside, facts, grad_pre, sums) = refs[:4], refs[4:]
    ch, length = grad_pre.shape
    grad = add_blocks(blocks).astype(jnp.bfloat16).astype(jnp.float32)
    gain, bias = affine(meta[...], ch)
    grad_pre[...], shift_sum, slope_sum = norm_back(
        grad,
        kept[:, :length],
        kept[:, length : length + 1],
        gain,
        bias,
        inside[...],
        facts[...],
        dims[1],
        pooling,
    )
    keep_sums(sums, shift_sum, slope_sum)


def conv_back_kernel(dims, layer, own, other, own_weights, other_weights, facts, *refs):
    outs, (moved, weights, sems) = refs[:4], refs[4:]
    ch = own.shape[0]
    rows = pl.ds(layer * 4 * ch, 4 * ch)
    copies = start_all(
        [
            pltpu.make_async_copy(own_weights.at[rows], weights.at[0], sems.at[0]),
            pltpu.make_async_copy(other_weights.at[rows], weights.at[1], sems.at[1]),
        ]
    )
    facts_now = facts[...]
    spread_taps(own[...].astype(jnp.float32), moved.at[0], 0, facts_now, dims[1])
    spread_taps(other[...].astype(jnp.float32), moved.at[1], 0, facts_now, dims[1])
    wait_all(copies)
    value = jnp.dot(weights[0], moved[0], preferred_element_type=jnp.float32)
    value = value + jnp.dot(weights[1], moved[1], preferred_element_type=jnp.float32)
    for k, out in enumerate(outs):
        out[...] = value[k * ch : (k + 1) * ch, :].astype(jnp.bfloat16)


def turn_weights_kernel(layers, *refs):
    sources, outs, (full, turned, stage, sems) = refs[:4], refs[4:6], refs[6:]
    section, _, core = place()
    rows, channels = full.shape[1:]
    half = channels // 2
    ch = half // 4
    copies = [pick_layer(n, sources, 0, full.at[n], sems.at[n]) for n in range(layers)]
    for n in range(layers):
        copies[n].wait()
        turned[...] = full[n].T
        for j in range(2):
            for k in range(4):
                at = pl.multiple_of((core ^ j) * half + (section ^ k) * ch, ch)
                stage[j, n * half + k * ch : n * half + (k + 1) * ch, :] = turned[pl.ds(at, ch), :]
    wait_all(
        start_all([pltpu.make_async_copy(stage.at[j], outs[j], sems.at[j]) for j in range(2)])
    )


def weight_kernel(dims, first, full_in, grad_pre, sums, facts, *refs):
    outs, (full, moved, sems) = refs[:-3], refs[-3:]
    copy = pltpu.make_async_copy(full_in, full, sems.at[0])
    copy.start()
    cols = dims[1]
    ch = grad_pre.shape[0]
    spread_taps(grad_pre[...].astype(jnp.float32), moved, 0, facts[...], cols)
    copy.wait()
    if first:
        value = jnp.dot(moved[...], full[...], preferred_element_type=jnp.float32)
    else:
        value = lax.dot_general(moved[...], full[...], NT, preferred_element_type=jnp.float32)
    width = outs[0].shape[1]
    lines = []
    for at in (0, LANES):
        turned = sums[:, at : at + LANES].T
        lines.append(jnp.concatenate([turned, jnp.zeros((LANES, width - ch), jnp.float32)], axis=1)[0:1])
    sums_block = jnp.concatenate(lines + [jnp.zeros((META_ROWS - 2, width), jnp.float32)], axis=0)
    if len(outs) == 1:
        size = outs[0].shape[0] // 4
        targets = [outs[0].at[pl.ds(n * size, size)] for n in range(4)]
        for n, target in enumerate(targets):
            target[: TAPS * ch, :] = value[:, n * width : (n + 1) * width].astype(jnp.bfloat16)
            target[TAPS * ch :, :] = sums_block.astype(jnp.bfloat16)
    else:
        _, plane, _ = place()
        for n in range(4):
            piece = value[:, n * width : (n + 1) * width].astype(jnp.bfloat16)
            for k, target in enumerate(outs):

                @pl.when((plane ^ k) == n)
                def _():
                    target[: TAPS * ch, :] = piece

        for target in outs:
            target[TAPS * ch :, :] = sums_block.astype(jnp.bfloat16)


def input_kernel(*refs):
    blocks, (hidden, inside), pieces, (full, sems) = refs[:4], refs[4:6], refs[6:10], refs[10:]
    section, _, _ = place()
    ch = hidden.shape[0]
    copy = pltpu.make_async_copy(hidden, full.at[pl.ds(0, ch)], sems.at[0])
    copy.start()
    full[ch:, :] = (add_blocks(blocks) * inside[...]).astype(jnp.bfloat16)
    copy.wait()
    width = pieces[0].shape[1]
    for k, piece in enumerate(pieces):
        piece[...] = full[:, pl.ds(pl.multiple_of((section ^ k) * width, width), width)]


def maps_out_kernel(*refs):
    blocks, outs, (full,) = refs[:8], refs[8:10], refs[10:]
    _, plane, core = place()
    ch = blocks[0].shape[0] // 2
    cells = outs[0].shape[0]
    for n, out in enumerate(outs):
        for (k, j), block in zip(peer_order(), blocks):
            at = pl.multiple_of(slice_at(plane, core, k, j) * ch, ch)
            full[pl.ds(at, ch), :] = block[n * ch : (n + 1) * ch, :]
        both = full[...].astype(jnp.float32)
        mine = jnp.where(core == 0, both[:, :cells], both[:, cells:])
        out[...] = mine.T.astype(out.dtype)


def grads_out_kernel(*refs):
    blocks, (weight_out, shift_out, slope_out), (full, turned) = refs[:8], refs[8:11], refs[11:]
    section, plane, core = place()
    taps, rows, channels = weight_out.shape
    for tap in range(taps):
        for (k, j), block in zip(peer_order(), blocks):
            at = pl.multiple_of(slice_at(section, core, k, j) * rows, rows)
            full[pl.ds(at, rows), :] = block[tap * rows : (tap + 1) * rows, :].astype(jnp.float32)
        turned[...] = full[...].T
        weight_out[tap] = turned[pl.ds(pl.multiple_of(core * rows, rows), rows), :]
    shift_row = jnp.zeros((1, rows), jnp.float32)
    slope_row = jnp.zeros((1, rows), jnp.float32)
    slot = plane * 2 + core
    for (k, j), block in zip(peer_order(), blocks):
        tail = block[taps * rows :, :].astype(jnp.float32)
        mine = slice_at(section, core, k, j) == slot
        shift_row = shift_row + jnp.where(mine, tail[0:1, :rows], 0.0)
        slope_row = slope_row + jnp.where(mine, tail[1:2, :rows], 0.0)
    shift_out[...] = shift_row
    slope_out[...] = slope_row


def call(kernel, outs, scratch, args, name, held=(), held_outs=(), loose=(), last=False, flops=0, copies=None):
    shapes = [
        (jax.ShapeDtypeStruct if last else pltpu.HBM if n in held_outs else pltpu.VMEM)(shape, dtype)
        for n, (shape, dtype) in enumerate(outs)
    ]
    moved = sum(a.size * a.dtype.itemsize for a in args)
    moved += sum(math.prod(shape) * jnp.dtype(dtype).itemsize for shape, dtype in outs)
    spaces = [pltpu.HBM if n in held else pltpu.VMEM for n in range(len(args))]
    out_spaces = [pltpu.HBM if n in held_outs else pltpu.VMEM for n in range(len(outs))]
    args = [
        a if n in loose else pltpu.with_memory_space_constraint(a, space)
        for n, (a, space) in enumerate(zip(args, spaces))
    ]
    scratch_shapes = [
        pltpu.SMEM(shape, dtype) if dtype == jnp.int32 else pltpu.VMEM(shape, dtype) for shape, dtype in scratch
    ]
    if copies is not None:
        scratch_shapes.append(pltpu.SemaphoreType.DMA((copies,)))
    return pl.pallas_call(
        kernel,
        out_shape=shapes,
        in_specs=[pl.BlockSpec(memory_space=space) for space in spaces],
        out_specs=[pl.BlockSpec(memory_space=space) for space in out_spaces],
        scratch_shapes=scratch_shapes,
        compiler_params=pltpu.CompilerParams(vmem_limit_bytes=VMEM_LIMIT),
        cost_estimate=pl.CostEstimate(flops=flops, bytes_accessed=moved, transcendentals=0),
        name=name,
    )(*args)


def plane_shards(images, image_group, group_size, conv_weight, bn_gain, bn_bias, cotangent):
    section, _, core = place()
    micro_total, _, rows, cols, channels = images.shape
    layers = lax.axis_size("section")
    last = layers - 1
    cells = rows * cols
    frames = 2 * micro_total
    length = frames * cells
    ch = channels // 8
    dims = (rows, cols)
    bf16, f32 = jnp.bfloat16, jnp.float32
    facts = grid_facts(frames, rows, cols)
    conv_flops = 2 * TAPS * ch * channels * length
    slice_rows = TAPS * ch + META_ROWS

    full_map = ((channels, length), bf16)
    full_frames = ((length, channels), bf16)
    tap_scratch = ((TAPS * ch, length), f32)
    weight_slice = ((slice_rows, channels), bf16)
    map_out = ((ch, length), bf16)
    sums_out = ((ch, 2 * LANES), f32)
    kept_out = ((ch, length + LANES), f32)

    taps_first = conv_weight[0].transpose(1, 2, 0, 3).reshape(TAPS, channels, channels)
    packed = call(
        pack_kernel,
        [weight_slice] * 4,
        [
            weight_slice,
            ((TAPS, channels, 4 * ch), bf16),
            ((4 * ch, channels), bf16),
            ((2, 1, channels), f32),
        ],
        [bn_gain, bn_bias, taps_first],
        "weight_pack",
        held=range(3),
        held_outs=(0,),
        copies=TAPS + 2,
    )
    slices = spread(packed, to_section)

    payload = ((cells + META_ROWS, channels + LANES), bf16)
    sent = call(
        partial(frames_kernel, dims),
        [payload] * 4,
        [((micro_total, cells, channels), bf16)] * 2
        + [(image_group.shape[::-1], jnp.int32), (group_size.shape[::-1], jnp.int32)],
        [
            image_group.T,
            group_size.T,
            after(images.reshape(micro_total, cells, channels), packed),
            cotangent.reshape(micro_total, cells, channels),
        ],
        "frames",
        held=range(4),
        copies=4,
    )
    frames_in = with_core(spread(sent, to_plane))

    half = (core * ch + np.arange(ch))[:, None] == np.arange(2 * ch)[None, :]
    hidden, normed, full, inside, cot = call(
        partial(forward_kernel, dims, 0, True, CONVS == 1),
        [map_out, kept_out, full_frames, ((1, length), f32), map_out],
        [
            full_frames,
            tap_scratch,
            kept_out,
            weight_slice,
            ((frames * META_ROWS, channels), bf16),
            ((length, LANES), bf16),
            map_out,
        ],
        [*frames_in, *slices, facts, half.astype(bf16)],
        "forward",
        held=range(8, 12),
        held_outs=(1, 2, 4),
        loose=(12, 13),
        flops=conv_flops,
        copies=4,
    )
    kept, fulls = [normed], [full]
    for layer in range(1, layers):
        (weight,) = call(
            partial(pick_kernel, layer),
            [weight_slice],
            [],
            after(slices, hidden),
            "pick",
            held=range(4),
            copies=1,
        )
        beside = [weight]
        if layer == 1:
            turned = call(
                partial(turn_weights_kernel, layers),
                [((layers * 4 * ch, TAPS * ch), bf16)] * 2,
                [
                    ((layers, TAPS * ch, channels), bf16),
                    ((channels, TAPS * ch), bf16),
                    ((2, layers * 4 * ch, TAPS * ch), bf16),
                ],
                after(slices, hidden),
                "turn_weights",
                held=range(4),
                held_outs=(0, 1),
                copies=layers,
            )
            beside.append(turned)
        if layer == 2:
            turned = [turned[0], to_core(after(turned[1], hidden))]
        blocks = with_core(spread([hidden] * 4, to_section, beside))
        if layer < last:
            hidden, normed, full = call(
                partial(forward_kernel, dims, layer, False, layer == CONVS - 1),
                [map_out, kept_out, full_map],
                [full_map, tap_scratch, kept_out],
                [*blocks, weight, inside, facts],
                "forward",
                held_outs=(1, 2),
                loose=(9, 10),
                flops=conv_flops,
                copies=2,
            )
            kept.append(normed)
        else:
            activation, full, grad_pre, sums = call(
                partial(turn_kernel, dims, last, last == CONVS - 1),
                [map_out, full_map, map_out, sums_out],
                [full_map, tap_scratch, map_out, map_out],
                [*blocks, weight, cot, inside, facts],
                "turn",
                held=(9,),
                held_outs=(0, 1),
                loose=(10, 11),
                flops=conv_flops,
                copies=3,
            )
        fulls.append(full)

    shares = [None] * layers
    same_core = [[2 * z + c for z in range(layers)] for c in range(2)]
    for layer in range(last, -1, -1):
        first = layer == 0
        pieces = call(
            partial(weight_kernel, dims, first),
            [((slice_rows, 2 * ch), bf16)] * 4 if first else [((4 * slice_rows, 2 * ch), bf16)],
            [full_frames if first else full_map, ((TAPS * ch, length), bf16)],
            [fulls[layer], grad_pre, sums, facts],
            "weight_share",
            held=(0,),
            loose=(2, 3),
            flops=conv_flops,
            copies=1,
        )
        if first:
            moved = spread(pieces, to_plane)
            shares[layer] = sum(x.astype(f32) for x in moved).astype(bf16)
        else:
            shares[layer] = lax.psum_scatter(
                pieces[0], "dp", scatter_dimension=0, tiled=True, axis_index_groups=same_core
            )
        own, other = after((grad_pre, to_core(grad_pre)), pieces)
        parts = call(
            partial(conv_back_kernel, dims, layer),
            [map_out] * 4,
            [((2, TAPS * ch, length), bf16), ((2, 4 * ch, TAPS * ch), bf16)],
            [own, other, *turned, facts],
            "conv_back",
            held=(2, 3),
            loose=(4,),
            flops=conv_flops,
            copies=2,
        )
        if layer:
            held = call(
                partial(fetch_kernel, layer - 1),
                [kept_out, ((META_ROWS, channels), bf16)],
                [],
                [after(kept[layer - 1], parts), *slices],
                "fetch",
                held=range(5),
                copies=2,
            )
            blocks = spread(parts, to_section, held)
            grad_pre, sums = call(
                partial(norm_back_kernel, dims, layer - 1 == CONVS - 1),
                [map_out, sums_out],
                [],
                [*blocks, *held, inside, facts],
                "norm_back",
                loose=(6, 7),
            )
    blocks = spread(parts, to_section)
    maps = call(
        input_kernel,
        [((2 * ch, 2 * cells), bf16)] * 4,
        [((2 * ch, length), bf16)],
        [*blocks, activation, inside],
        "input",
        held=(4,),
        loose=(5,),
        copies=1,
    )
    maps = lax.optimization_barrier(
        [send(x, lambda s, z, c, k=k: (z, s ^ k, c)) for k, x in enumerate(maps)]
    )
    activations, input_grad = call(
        maps_out_kernel,
        [((cells, channels), bf16)] * 2,
        [((channels, 2 * cells), bf16)],
        with_core(maps),
        "maps_out",
        last=True,
    )

    chosen = [lax.select_n(section ^ k, *shares) for k in range(4)]
    weight_grad, bias_grad, gain_grad = call(
        grads_out_kernel,
        [((TAPS, ch, channels), f32), ((1, ch), f32), ((1, ch), f32)],
        [((channels, 2 * ch), f32), ((2 * ch, channels), f32)],
        with_core(spread(chosen, to_section)),
        "grads_out",
        last=True,
    )
    weight_grad = weight_grad.reshape(3, 3, ch, channels).transpose(2, 0, 1, 3)[None]
    return (
        activations.reshape(1, 1, rows, cols, channels),
        input_grad.reshape(1, 1, rows, cols, channels),
        weight_grad,
        gain_grad,
        bias_grad,
    )


def fits_plane_plan(images, conv_weight, sections, dps):
    micro_total, images_total, rows, cols, channels = images.shape
    return (
        sections == 4
        and dps == 2 * sections
        and micro_total == sections
        and conv_weight.shape[0] == sections
        and images_total == dps
        and rows % 2 == 0
        and cols % 2 == 0
        and (rows * cols) % 64 == 0
        and channels == 512
    )


def solution(mesh):
    in_specs = (
        P(None, "dp", None, None, None),
        P(None, "dp"),
        P(),
        P("section", None, None, None, None),
        P("section", None),
        P("section", None),
        P(None, "dp", None, None, None),
    )
    out_specs = (
        P("section", "dp", None, None, None),
        P("section", "dp", None, None, None),
        P("section", "dp", None, None, None),
        P("section", "dp"),
        P("section", "dp"),
    )
    sections, dps = mesh.shape["section"], mesh.shape["dp"]

    def program(images, image_group, group_size, conv_weight, bn_gain, bn_bias, cotangent):
        plan = plane_shards if fits_plane_plan(images, conv_weight, sections, dps) else pipeline_shards
        sharded = jax.shard_map(plan, mesh=mesh, in_specs=in_specs, out_specs=out_specs, check_vma=False)
        return sharded(images, image_group, group_size, conv_weight, bn_gain, bn_bias, cotangent)

    return program
```

```python
import math
from functools import partial

import jax
import jax.numpy as jnp
import numpy as np
from jax import lax
from jax.experimental import pallas as pl
from jax.experimental.pallas import tpu as pltpu
from jax.sharding import PartitionSpec as P

CONVS = 2


eps = 1e-05


def from_behind(x, axis, by):
    peers = lax.axis_size(axis)
    pairs = [(i, i + by) for i in range(peers) if 0 <= i + by < peers]
    return lax.ppermute(x, axis, pairs)


def canvas_mask(image_group, group_size, canvas_rows, canvas_cols):
    groups_n = group_size.shape[0]
    onehot = image_group[..., None] == jnp.arange(groups_n, dtype=jnp.int32)
    height = jnp.sum(jnp.where(onehot, group_size[:, 0], 0), axis=-1)
    breadth = jnp.sum(jnp.where(onehot, group_size[:, 1], 0), axis=-1)
    inside_rows = jnp.arange(canvas_rows, dtype=jnp.int32)[:, None] < height[..., None, None]
    inside_cols = jnp.arange(canvas_cols, dtype=jnp.int32)[None, :] < breadth[..., None, None]
    return (inside_rows & inside_cols).astype(jnp.float32)[..., None]


def window_pool(hidden):
    frames, height, breadth, channels = hidden.shape
    blocks = hidden.reshape(frames, height // 2, 2, breadth // 2, 2, channels)
    window_max = jnp.max(blocks, axis=(2, 4), keepdims=True)
    raised = jnp.exp(blocks - window_max)
    weights = raised / jnp.sum(raised, axis=(2, 4), keepdims=True)
    pooled = jnp.sum(weights * blocks, axis=(2, 4), keepdims=True)
    return (weights * pooled).reshape(frames, height, breadth, channels)


def activate(pre_act, inside, pooling):
    hidden = jax.nn.silu(pre_act) * inside
    return jnp.where(pooling, window_pool(hidden) * inside, hidden)


def conv_forward(layer_in, weight):
    return lax.conv_general_dilated(
        layer_in,
        weight,
        (1, 1),
        "SAME",
        dimension_numbers=("NHWC", "IHWO", "NHWC"),
        preferred_element_type=jnp.float32,
    )


def conv_data_back(grad_pre, weight):
    flipped = weight[:, ::-1, ::-1, :]
    return lax.conv_general_dilated(
        grad_pre,
        flipped,
        (1, 1),
        "SAME",
        dimension_numbers=("NHWC", "OHWI", "NHWC"),
        preferred_element_type=jnp.float32,
    )


def weight_back(layer_in, grad_pre):
    height = layer_in.shape[1]
    breadth = layer_in.shape[2]
    padded = jnp.pad(layer_in, ((0, 0), (1, 1), (1, 1), (0, 0)))
    pieces = []
    for tap_row in range(3):
        for tap_col in range(3):
            window = padded[:, tap_row : tap_row + height, tap_col : tap_col + breadth, :]
            pieces.append(
                jnp.einsum("nhwi,nhwo->io", window, grad_pre, preferred_element_type=jnp.float32)
            )
    return jnp.stack(pieces, axis=1).reshape(layer_in.shape[3], 3, 3, grad_pre.shape[3])


def layer_forward(layer_in, weight, gain_row, bias_row, inside, pooling):
    pre_norm = conv_forward(layer_in, weight)
    sums = lax.psum(
        (
            jnp.sum(pre_norm * inside, axis=(0, 1, 2)),
            jnp.sum(pre_norm * pre_norm * inside, axis=(0, 1, 2)),
            jnp.sum(inside),
        ),
        "dp",
    )
    pixel_total = sums[2]
    mean_val = sums[0] / pixel_total
    scale_inv = lax.rsqrt(sums[1] / pixel_total - mean_val * mean_val + eps)
    pre_act = (pre_norm - mean_val) * scale_inv * gain_row + bias_row
    hidden = activate(pre_act, inside, pooling)
    return (pre_norm, mean_val, scale_inv, pixel_total, hidden)


def layer_backward(
    grad_out,
    layer_in,
    pre_norm,
    mean_val,
    scale_inv,
    pixel_total,
    weight,
    gain_row,
    bias_row,
    inside,
    pooling,
):
    normed = (pre_norm - mean_val) * scale_inv
    pre_act = normed * gain_row + bias_row
    hidden_out, pullback = jax.vjp(partial(activate, inside=inside, pooling=pooling), pre_act)
    grad_act = pullback(grad_out)[0]
    sums = lax.psum(
        (jnp.sum(grad_act, axis=(0, 1, 2)), jnp.sum(grad_act * normed, axis=(0, 1, 2))), "dp"
    )
    shift_term = sums[0] / pixel_total
    slope_term = sums[1] / pixel_total
    grad_pre = (
        inside * scale_inv * gain_row * (grad_act - shift_term - normed * slope_term)
    ).astype(jnp.bfloat16)
    weight_term = weight_back(layer_in, grad_pre)
    grad_in = conv_data_back(grad_pre, weight).astype(jnp.bfloat16)
    return (grad_in, weight_term, sums[1], sums[0])


def pipeline_shards(images, image_group, group_size, conv_weight, bn_gain, bn_bias, cotangent):
    section_index = lax.axis_index("section")
    sections = lax.axis_size("section")
    micro_total = images.shape[0]
    channels = conv_weight.shape[1]
    inside_all = canvas_mask(image_group, group_size, images.shape[2], images.shape[3])
    ticks = micro_total + sections - 1
    weight = conv_weight[0]
    gain_row = bn_gain[0]
    bias_row = bn_bias[0]
    pool_here = section_index == CONVS - 1
    received = jnp.zeros(images.shape[1:], jnp.bfloat16)
    kept_in, kept_pre, kept_mean, kept_scale, kept_total, finished = ([], [], [], [], [], [])
    for tick in range(ticks):
        micro_pos = jnp.clip(tick - section_index, 0, micro_total - 1)
        inside = inside_all[micro_pos]
        fresh = (images[micro_pos].astype(jnp.float32) * inside).astype(jnp.bfloat16)
        layer_in = jnp.where(section_index == 0, fresh, received)
        pre_norm, mean_val, scale_inv, pixel_total, hidden = layer_forward(
            layer_in, weight, gain_row, bias_row, inside, pool_here
        )
        sent = hidden.astype(jnp.bfloat16)
        if tick < ticks - 1:
            received = from_behind(sent, "section", 1)
        kept_in.append(layer_in)
        kept_pre.append(pre_norm)
        kept_mean.append(mean_val)
        kept_scale.append(scale_inv)
        kept_total.append(pixel_total)
        finished.append(sent)
    stack_in = jnp.stack(kept_in)
    stack_pre = jnp.stack(kept_pre)
    stack_mean = jnp.stack(kept_mean)
    stack_scale = jnp.stack(kept_scale)
    stack_total = jnp.stack(kept_total)
    returned = jnp.zeros(images.shape[1:], jnp.bfloat16)
    weight_sum = jnp.zeros(conv_weight.shape[1:], jnp.float32)
    gain_sum = jnp.zeros((channels,), jnp.float32)
    bias_sum = jnp.zeros((channels,), jnp.float32)
    input_list = []
    for tick in range(ticks):
        micro_raw = tick - (sections - 1 - section_index)
        valid = ((micro_raw >= 0) & (micro_raw < micro_total)).astype(jnp.float32)
        micro_pos = jnp.clip(micro_raw, 0, micro_total - 1)
        forward_tick = jnp.clip(micro_pos + section_index, 0, ticks - 1)
        inside = inside_all[micro_pos]
        grad_out = jnp.where(
            section_index == sections - 1,
            cotangent[micro_pos].astype(jnp.float32),
            returned.astype(jnp.float32),
        )
        grad_in, weight_term, gain_term, bias_term = layer_backward(
            grad_out,
            stack_in[forward_tick],
            stack_pre[forward_tick],
            stack_mean[forward_tick],
            stack_scale[forward_tick],
            stack_total[forward_tick],
            weight,
            gain_row,
            bias_row,
            inside,
            pool_here,
        )
        weight_sum = weight_sum + valid * weight_term
        gain_sum = gain_sum + valid * gain_term
        bias_sum = bias_sum + valid * bias_term
        if tick < ticks - 1:
            returned = from_behind(grad_in, "section", -1)
        input_list.append((grad_in.astype(jnp.float32) * inside).astype(jnp.bfloat16))
    out_stack = jnp.stack(finished[sections - 1 :], axis=0)
    grad_stack = jnp.stack(input_list[sections - 1 :], axis=0)
    out_back, grad_back = (
        lax.all_to_all(out_stack, "section", split_axis=0, concat_axis=1, tiled=True),
        lax.all_to_all(grad_stack, "section", split_axis=0, concat_axis=1, tiled=True),
    )
    activations = out_back[:, sections - 1 : sections]
    input_grad = grad_back[:, 0:1]
    weight_grad = lax.psum_scatter(weight_sum[None], "dp", scatter_dimension=1, tiled=True)
    share = channels // lax.axis_size("dp")
    gain_grad = lax.dynamic_slice_in_dim(gain_sum, lax.axis_index("dp") * share, share)[None]
    bias_grad = lax.dynamic_slice_in_dim(bias_sum, lax.axis_index("dp") * share, share)[None]
    return (activations, input_grad, weight_grad, gain_grad, bias_grad)


AXES = ("section", "dp")
TAPS = 9
VMEM_LIMIT = 24 * 1024 * 1024
META_ROWS = 16
LANES = 128
ROW_AT, COL_AT, FRAME_AT = 6, 7, 8
NT = (((1,), (1,)), ((), ()))


def place():
    dp_index = lax.axis_index("dp")
    return lax.axis_index("section"), dp_index // 2, dp_index % 2


def peer_order():
    return [(k, j) for j in range(2) for k in range(4)]


def slice_at(section, core, k, j):
    return (core ^ j) * lax.axis_size("section") + (section ^ k)


def send(x, target):
    sections = lax.axis_size("section")
    dps = lax.axis_size("dp")
    pairs = []
    for s in range(sections):
        for d in range(dps):
            ts, tz, tc = target(s, d // 2, d % 2)
            pairs.append((s * dps + d, ts * dps + tz * 2 + tc))
    return lax.ppermute(x, AXES, pairs)


def to_section(x, k):
    return send(x, lambda s, z, c: (s ^ k, z, c))


def to_plane(x, k):
    return send(x, lambda s, z, c: (s, z ^ k, c))


def to_core(x):
    return send(x, lambda s, z, c: (s, z, c ^ 1))


def spread(blocks, move, *beside):
    moved = lax.optimization_barrier(([move(blocks[k], k) for k in (1, 2, 3)], beside))[0]
    return [blocks[0]] + moved


def with_core(blocks):
    return blocks + [to_core(x) for x in blocks]


def after(x, *first):
    return lax.optimization_barrier((x, first))[0]


def grid_facts(frames, rows, cols):
    at = np.arange(frames * rows * cols)
    col = at % cols
    row = (at // cols) % rows
    facts = [row > 0, row < rows - 1, col > 0, col < cols - 1, col % 2 == 0, row % 2 == 0, row, col]
    facts = facts + [at // (rows * cols) == frame for frame in range(frames)]
    return jnp.asarray(np.stack(facts).astype(np.float32))


def shift(x, by):
    length = x.shape[1]
    return pltpu.roll(x, (-by) % length, 1) if by % length else x


def row_ok(facts, d):
    return facts[0:1, :] if d < 0 else facts[1:2, :]


def col_ok(facts, d):
    return facts[2:3, :] if d < 0 else facts[3:4, :]


def sum_taps(taps_ref, facts, cols):
    ch = taps_ref.shape[0] // TAPS
    total = None
    for dx in (-1, 0, 1):
        column = None
        for dy in (-1, 0, 1):
            tap = (dy + 1) * 3 + dx + 1
            piece = taps_ref[tap * ch : (tap + 1) * ch, :]
            if dy:
                piece = shift(piece, dy * cols) * row_ok(facts, dy)
            column = piece if column is None else column + piece
        if dx:
            column = shift(column, dx) * col_ok(facts, dx)
        total = column if total is None else total + column
    return total


def spread_taps(grad, moved_ref, base, facts, cols):
    ch = grad.shape[0]
    facts = facts[:4, :].astype(grad.dtype)
    for dx in (-1, 0, 1):
        column = shift(grad, -dx) * col_ok(facts, -dx) if dx else grad
        for dy in (-1, 0, 1):
            piece = shift(column, -dy * cols) * row_ok(facts, -dy) if dy else column
            at = base + ((dy + 1) * 3 + dx + 1) * ch
            moved_ref[at : at + ch, :] = piece


def corner_sum(x, cols):
    x = x + shift(x, 1)
    return x + shift(x, cols)


def from_corner(x, facts, cols):
    x = jnp.where(facts[4:5, :] > 0.5, x, shift(x, -1))
    return jnp.where(facts[5:6, :] > 0.5, x, shift(x, -cols))


def lane_sum(x):
    return jnp.sum(x, axis=1, keepdims=True)


def normalise(pre, inside):
    count = lane_sum(inside)
    mean = lane_sum(pre * inside) / count
    square = lane_sum(pre * pre * inside) / count
    scale = lax.rsqrt(square - mean * mean + eps)
    return (pre - mean) * scale, scale


def hidden_of(normed, gain, bias, inside, facts, cols, pooling):
    pre_act = normed * gain + bias
    hidden = pre_act * jax.nn.sigmoid(pre_act) * inside
    if pooling:
        raised = jnp.exp(hidden)
        total = corner_sum(raised, cols)
        pooled = corner_sum(raised * hidden, cols) / total
        hidden = raised * from_corner(pooled / total, facts, cols) * inside
    return hidden


def norm_back(grad, normed, scale, gain, bias, inside, facts, cols, pooling):
    pre_act = normed * gain + bias
    gate = jax.nn.sigmoid(pre_act)
    if pooling:
        hidden = pre_act * gate * inside
        raised = jnp.exp(hidden)
        out = grad * inside
        total = 1.0 / corner_sum(raised, cols)
        pooled = corner_sum(raised * hidden, cols) * total
        d_pooled = corner_sum(raised * out, cols) * total
        by_out = from_corner(pooled * total, facts, cols)
        by_hidden = from_corner(d_pooled * total, facts, cols)
        rest = from_corner(d_pooled * total * (1.0 - 2.0 * pooled), facts, cols)
        grad = raised * (out * by_out + hidden * by_hidden + rest)
    grad_act = grad * inside * gate * (1.0 + pre_act * (1.0 - gate))
    count = lane_sum(inside)
    shift_sum = lane_sum(grad_act)
    slope_sum = lane_sum(grad_act * normed)
    grad_pre = inside * (scale * gain) * (grad_act - shift_sum / count - normed * (slope_sum / count))
    return grad_pre.astype(jnp.bfloat16), shift_sum, slope_sum


def assemble(blocks, full_ref):
    section, _, core = place()
    ch = blocks[0].shape[0]
    for (k, j), block in zip(peer_order(), blocks):
        at = pl.multiple_of(slice_at(section, core, k, j) * ch, ch)
        full_ref[pl.ds(at, ch), :] = block[...]


def assemble_frames(blocks, full_ref, rows, lanes):
    _, plane, core = place()
    size = rows.stop - rows.start
    for (k, j), block in zip(peer_order(), blocks):
        frame = (plane ^ k) * 2 + (core ^ j)
        full_ref[pl.ds(pl.multiple_of(frame * size, size), size), :] = block[rows, lanes]


def start_all(copies):
    for copy in copies:
        copy.start()
    return copies


def wait_all(copies):
    for copy in copies:
        copy.wait()


def tap_products(weight, full_ref, taps_ref, by_cells):
    length = taps_ref.shape[1]
    step = 512 if length % 512 == 0 else length
    for at in range(0, length, step):
        if by_cells:
            taps_ref[:, at : at + step] = lax.dot_general(
                weight, full_ref[at : at + step, :], NT, preferred_element_type=jnp.float32
            )
        else:
            taps_ref[:, at : at + step] = jnp.dot(
                weight, full_ref[:, at : at + step], preferred_element_type=jnp.float32
            )


def pick_layer(layer, sources, start, target, sem):
    section, _, _ = place()
    rows = pl.ds(start, target.shape[0])
    for k, source in enumerate(sources):

        @pl.when((section ^ layer) == k)
        def _():
            pltpu.make_async_copy(source.at[rows], target, sem).start()

    return pltpu.make_async_copy(sources[0].at[rows], target, sem)


def affine(meta, ch):
    parts = meta[:, :LANES].astype(jnp.float32).T[:ch]
    return (
        parts[:, 0:1] + parts[:, 1:2] + parts[:, 2:3],
        parts[:, 3:4] + parts[:, 4:5] + parts[:, 5:6],
    )


def plane_inside(metas, facts):
    frames = metas.shape[0] // META_ROWS
    extents = []
    for line in (0, 1):
        total = None
        for f in range(frames):
            at = f * META_ROWS + line
            extent = metas[at : at + 1, 0:1].astype(jnp.float32) * facts[FRAME_AT + f : FRAME_AT + f + 1, :]
            total = extent if total is None else total + extent
        extents.append(total)
    on = (facts[ROW_AT : ROW_AT + 1, :] < extents[0]) & (facts[COL_AT : COL_AT + 1, :] < extents[1])
    return jnp.where(on, 1.0, 0.0)


def frames_kernel(dims, group_table, size_table, images, cots, *refs):
    payloads, (image_in, cot_in, groups, sizes, sems) = refs[:4], refs[4:]
    copies = start_all(
        [
            pltpu.make_async_copy(group_table, groups, sems.at[0]),
            pltpu.make_async_copy(size_table, sizes, sems.at[1]),
            pltpu.make_async_copy(images, image_in, sems.at[2]),
            pltpu.make_async_copy(cots, cot_in, sems.at[3]),
        ]
    )
    section, plane, _ = place()
    rows, cols = dims
    cells = rows * cols
    at = lax.broadcasted_iota(jnp.int32, (cells, LANES), 0).astype(jnp.float32)
    row = jnp.floor((at + 0.5) * (1.0 / cols))
    col = at - row * cols
    channels = images.shape[2]
    half = channels // 2
    wait_all(copies)
    for k in range(4):
        micro = plane ^ k
        group = groups[0, micro]
        height = sizes[0, 0]
        breadth = sizes[1, 0]
        for g in range(1, sizes.shape[1]):
            height = jnp.where(group == g, sizes[0, g], height)
            breadth = jnp.where(group == g, sizes[1, g], breadth)
        height = height.astype(jnp.float32)
        breadth = breadth.astype(jnp.float32)
        on = jnp.where((row < height) & (col < breadth), 1.0, 0.0)
        image = image_in[micro]
        for c in range(0, channels, LANES):
            piece = image[:, c : c + LANES].astype(jnp.float32) * on
            payloads[k][:cells, c : c + LANES] = piece.astype(jnp.bfloat16)
        line = lax.broadcasted_iota(jnp.int32, (META_ROWS, channels + LANES), 0)
        payloads[k][cells:, :] = jnp.where(line == 0, height, breadth).astype(jnp.bfloat16)
        tile = section // 2 * LANES
        low = cot_in[micro, :, pl.ds(pl.multiple_of(tile, LANES), LANES)].astype(jnp.float32)
        high = cot_in[micro, :, pl.ds(pl.multiple_of(half + tile, LANES), LANES)].astype(jnp.float32)
        odd = section % 2 == 1
        low = jnp.where(odd, pltpu.roll(low, LANES // 2, 1), low)
        high = jnp.where(odd, high, pltpu.roll(high, LANES // 2, 1))
        lane = lax.broadcasted_iota(jnp.int32, (cells, LANES), 1)
        both = jnp.where(lane < LANES // 2, low, high).astype(jnp.bfloat16)
        payloads[k][:cells, channels:] = both


def pack_kernel(gain, bias, weight, *refs):
    outs, (own, columns, turned, tables, sems) = refs[:4], refs[4:]
    section, _, core = place()
    width = columns.shape[2]
    ch = width // 4
    start = pl.multiple_of(core * width, width)
    copies = start_all(
        [
            pltpu.make_async_copy(weight.at[tap, :, pl.ds(start, width)], columns.at[tap], sems.at[tap])
            for tap in range(TAPS)
        ]
    )
    table_copies = start_all(
        [
            pltpu.make_async_copy(gain, tables.at[0], sems.at[TAPS]),
            pltpu.make_async_copy(bias, tables.at[1], sems.at[TAPS + 1]),
        ]
    )
    wait_all(table_copies)
    targets = [own, *outs[1:]]
    for k, out in enumerate(targets):
        lines = []
        tile = pl.multiple_of(start + (section ^ k) // 2 * LANES, LANES)
        odd = (section ^ k) % 2 == 1
        for m in range(2):
            line = tables[m, :, pl.ds(tile, LANES)]
            line = jnp.where(odd, pltpu.roll(line, ch, 1), line)
            for _ in range(3):
                part = line.astype(jnp.bfloat16).astype(jnp.float32)
                lines.append(part)
                line = line - part
        lines.append(jnp.zeros((META_ROWS - len(lines), LANES), jnp.float32))
        out[TAPS * ch :, :] = jnp.zeros((META_ROWS, out.shape[1]), jnp.bfloat16)
        out[TAPS * ch :, :LANES] = jnp.concatenate(lines, axis=0).astype(jnp.bfloat16)
    for tap in range(TAPS):
        copies[tap].wait()
        turned[...] = columns[tap].T
        for k, out in enumerate(targets):
            rows = pl.ds(pl.multiple_of((section ^ k) * ch, ch), ch)
            out[tap * ch : (tap + 1) * ch, :] = turned[rows, :]
    own_copy = pltpu.make_async_copy(own, outs[0], sems.at[TAPS])
    own_copy.start()
    own_copy.wait()


def pick_kernel(layer, *refs):
    sources, others, out, targets, sems = refs[:4], refs[4:-2], refs[-2], (), refs[-1]
    if len(others) > 0:
        others, out, targets = refs[4:5], refs[5], refs[6:7]
    copies = [pick_layer(layer, sources, 0, out, sems.at[0])]
    for other, target in zip(others, targets):
        copies += start_all([pltpu.make_async_copy(other, target, sems.at[1])])
    wait_all(copies)


def forward_kernel(dims, layer, first, pooling, *refs):
    blocks, weights, rest = refs[:8], refs[8 : 12 if first else 9], refs[12 if first else 9 :]
    rows, cols = dims
    cells = rows * cols
    if first:
        facts, pick, hidden, kept, full_out, inside_out, cot_out, full, taps, stage, weight, metas, *rest = rest
        cot_full, cot, sems = rest
        copy = pick_layer(layer, weights, 0, weight, sems.at[2])
    else:
        inside, facts, hidden, kept, full_out, full, taps, stage, sems = rest
        (weight,) = weights
    facts_now = facts[...]
    if first:
        channels = full.shape[1]
        assemble_frames(blocks, full, slice(0, cells), slice(0, channels))
    else:
        assemble(blocks, full)
    full_copy = pltpu.make_async_copy(full, full_out, sems.at[0])
    full_copy.start()
    if first:
        assemble_frames(blocks, metas, slice(cells, cells + META_ROWS), slice(0, channels))
        assemble_frames(blocks, cot_full, slice(0, cells), slice(channels, channels + LANES))
        inside_now = plane_inside(metas, facts_now)
        inside_out[...] = inside_now
        copy.wait()
    else:
        inside_now = inside[...]
    ch = hidden.shape[0]
    tap_products(weight[: TAPS * ch, :], full, taps, first)
    if first:
        cot[...] = lax.dot_general(
            pick[...], cot_full[...], NT, preferred_element_type=jnp.float32
        ).astype(jnp.bfloat16)
        cot_copy = pltpu.make_async_copy(cot, cot_out, sems.at[3])
        cot_copy.start()
    pre = sum_taps(taps, facts_now, cols)
    normed, scale = normalise(pre, inside_now)
    length = normed.shape[1]
    stage[:, :length] = normed
    stage[:, length:] = jnp.broadcast_to(scale, (ch, LANES))
    kept_copy = pltpu.make_async_copy(stage, kept, sems.at[1])
    kept_copy.start()
    gain, bias = affine(weight[TAPS * ch :, :], ch)
    hidden[...] = hidden_of(normed, gain, bias, inside_now, facts_now, cols, pooling).astype(jnp.bfloat16)
    if first:
        cot_copy.wait()
    full_copy.wait()
    kept_copy.wait()


def turn_kernel(dims, layer, pooling, *refs):
    blocks, (weight, cot_in, inside, facts) = refs[:8], refs[8:12]
    hidden_out, full_out, grad_pre, sums, full, taps, cot, hidden, sems = refs[12:]
    cols = dims[1]
    cot_copy = pltpu.make_async_copy(cot_in, cot, sems.at[0])
    cot_copy.start()
    assemble(blocks, full)
    full_copy = pltpu.make_async_copy(full, full_out, sems.at[1])
    full_copy.start()
    ch = grad_pre.shape[0]
    tap_products(weight[: TAPS * ch, :], full, taps, False)
    facts_now, inside_now = facts[...], inside[...]
    pre = sum_taps(taps, facts_now, cols)
    normed, scale = normalise(pre, inside_now)
    gain, bias = affine(weight[TAPS * ch :, :], ch)
    hidden[...] = hidden_of(normed, gain, bias, inside_now, facts_now, cols, pooling).astype(jnp.bfloat16)
    hidden_copy = pltpu.make_async_copy(hidden, hidden_out, sems.at[2])
    hidden_copy.start()
    cot_copy.wait()
    grad_pre[...], shift_sum, slope_sum = norm_back(
        cot[...].astype(jnp.float32), normed, scale, gain, bias, inside_now, facts_now, cols, pooling
    )
    keep_sums(sums, shift_sum, slope_sum)
    full_copy.wait()
    hidden_copy.wait()


def keep_sums(sums, shift_sum, slope_sum):
    ch = shift_sum.shape[0]
    sums[:, :LANES] = jnp.broadcast_to(shift_sum, (ch, LANES))
    sums[:, LANES:] = jnp.broadcast_to(slope_sum, (ch, LANES))


def add_blocks(blocks):
    total = blocks[0][...].astype(jnp.float32)
    for block in blocks[1:]:
        total = total + block[...].astype(jnp.float32)
    return total


def fetch_kernel(layer, kept, *refs):
    sources, (kept_out, meta_out, sems) = refs[:4], refs[4:]
    copy = pltpu.make_async_copy(kept, kept_out, sems.at[0])
    copy.start()
    start = sources[0].shape[0] - META_ROWS
    pick_layer(layer, sources, start, meta_out, sems.at[1]).wait()
    copy.wait()


def norm_back_kernel(dims, pooling, *refs):
    blocks, (kept, meta, inside, facts, grad_pre, sums) = refs[:4], refs[4:]
    ch, length = grad_pre.shape
    grad = add_blocks(blocks).astype(jnp.bfloat16).astype(jnp.float32)
    gain, bias = affine(meta[...], ch)
    grad_pre[...], shift_sum, slope_sum = norm_back(
        grad,
        kept[:, :length],
        kept[:, length : length + 1],
        gain,
        bias,
        inside[...],
        facts[...],
        dims[1],
        pooling,
    )
    keep_sums(sums, shift_sum, slope_sum)


def weight_product(moved, full, first):
    if first:
        return jnp.dot(moved, full, preferred_element_type=jnp.float32)
    return lax.dot_general(moved, full, NT, preferred_element_type=jnp.float32)


def sums_rows(sums, ch, width):
    lines = []
    for at in (0, LANES):
        turned = sums[:, at : at + LANES].T
        lines.append(jnp.concatenate([turned, jnp.zeros((LANES, width - ch), jnp.float32)], axis=1)[0:1])
    lines.append(jnp.zeros((META_ROWS - 2, width), jnp.float32))
    return jnp.concatenate(lines, axis=0).astype(jnp.bfloat16)


def store_share(value, sums, pieces):
    rows = value.shape[0]
    width = pieces[0].shape[1]
    for n, piece in enumerate(pieces):
        piece[:rows, :] = value[:, n * width : (n + 1) * width].astype(jnp.bfloat16)
        piece[rows:, :] = sums_rows(sums, rows // TAPS, width)


def conv_back_kernel(dims, layer, own, other, own_weights, other_weights, full_in, sums, facts, *refs):
    outs, shares, (product, moved, weights, full, sems) = refs[:4], refs[4:-5], refs[-5:]
    ch = own.shape[0]
    size = moved.shape[0] // 2
    rows = pl.ds(layer * 4 * ch, 4 * ch)
    copies = start_all(
        [
            pltpu.make_async_copy(own_weights.at[rows], weights.at[:, pl.ds(0, size)], sems.at[0]),
            pltpu.make_async_copy(other_weights.at[rows], weights.at[:, pl.ds(size, size)], sems.at[1]),
        ]
    )
    full_copy = pltpu.make_async_copy(full_in, full, sems.at[2])
    full_copy.start()
    facts_now = facts[...]
    spread_taps(own[...], moved, 0, facts_now, dims[1])
    full_copy.wait()
    value = weight_product(moved[: TAPS * ch, :], full[...], layer == 0)
    if len(shares) == 1:
        piece = product.shape[0] // 4
        store_share(value, sums, [product.at[pl.ds(n * piece, piece)] for n in range(4)])
        share_copy = pltpu.make_async_copy(product, shares[0], sems.at[3])
        share_copy.start()
    else:
        _, plane, _ = place()
        width = shares[0].shape[1]
        product[...] = value.astype(jnp.bfloat16)
        for k, share in enumerate(shares):
            at = pl.multiple_of((plane ^ k) * width, width)
            share[: TAPS * ch, :] = product[:, pl.ds(at, width)]
            share[TAPS * ch :, :] = sums_rows(sums, ch, width)
    spread_taps(other[...], moved, size, facts_now, dims[1])
    for n in range(2):
        moved[n * size + TAPS * ch : (n + 1) * size, :] = jnp.zeros(
            (size - TAPS * ch, moved.shape[1]), jnp.bfloat16
        )
    wait_all(copies)
    value = jnp.dot(weights[...], moved[...], preferred_element_type=jnp.float32)
    for k, out in enumerate(outs):
        out[...] = value[k * ch : (k + 1) * ch, :].astype(jnp.bfloat16)
    if len(shares) == 1:
        share_copy.wait()


def choose_kernel(*refs):
    blocks, others, outs, sem = refs[:4], refs[4:-5], refs[-5:-1], refs[-1]
    section, _, _ = place()
    for layer, other in enumerate(others, 1):
        for k, out in enumerate(outs):

            @pl.when((section ^ k) == layer)
            def _():
                pltpu.make_async_copy(other, out, sem.at[k]).start()

    value = add_blocks(blocks).astype(jnp.bfloat16)
    for k, out in enumerate(outs):
        copy = pltpu.make_async_copy(others[0], out, sem.at[k])

        @pl.when((section ^ k) == 0)
        def _():
            out[...] = value

        @pl.when((section ^ k) != 0)
        def _():
            copy.wait()


def turn_weights_kernel(layers, *refs):
    sources, outs, (full, turned, stage, sems) = refs[:4], refs[4:6], refs[6:]
    section, _, core = place()
    rows, channels = full.shape[1:]
    half = channels // 2
    ch = half // 4
    copies = [pick_layer(n, sources, 0, full.at[n], sems.at[n]) for n in range(layers)]
    stage[:, :, rows:] = jnp.zeros((*stage.shape[:2], stage.shape[2] - rows), jnp.bfloat16)
    for n in range(layers):
        copies[n].wait()
        turned[...] = full[n].T
        for j in range(2):
            for k in range(4):
                at = pl.multiple_of((core ^ j) * half + (section ^ k) * ch, ch)
                stage[j, n * half + k * ch : n * half + (k + 1) * ch, :rows] = turned[pl.ds(at, ch), :]
    wait_all(
        start_all([pltpu.make_async_copy(stage.at[j], outs[j], sems.at[j]) for j in range(2)])
    )


def input_kernel(*refs):
    blocks, (hidden, inside), pieces, (full, sems) = refs[:4], refs[4:6], refs[6:10], refs[10:]
    section, _, _ = place()
    ch = hidden.shape[0]
    copy = pltpu.make_async_copy(hidden, full.at[pl.ds(0, ch)], sems.at[0])
    copy.start()
    full[ch:, :] = (add_blocks(blocks) * inside[...]).astype(jnp.bfloat16)
    copy.wait()
    width = pieces[0].shape[1]
    for k, piece in enumerate(pieces):
        piece[...] = full[:, pl.ds(pl.multiple_of((section ^ k) * width, width), width)]


def maps_out_kernel(*refs):
    blocks, outs, (full,) = refs[:8], refs[8:10], refs[10:]
    _, plane, core = place()
    ch = blocks[0].shape[0] // 2
    cells = outs[0].shape[0]
    for n, out in enumerate(outs):
        for (k, j), block in zip(peer_order(), blocks):
            at = pl.multiple_of(slice_at(plane, core, k, j) * ch, ch)
            full[pl.ds(at, ch), :] = block[n * ch : (n + 1) * ch, :]
        both = full[...].astype(jnp.float32)
        mine = jnp.where(core == 0, both[:, :cells], both[:, cells:])
        out[...] = mine.T.astype(out.dtype)


def grads_out_kernel(*refs):
    blocks, (weight_out, shift_out, slope_out), (full, turned) = refs[:8], refs[8:11], refs[11:]
    section, plane, core = place()
    taps, rows, channels = weight_out.shape
    for tap in range(taps):
        for (k, j), block in zip(peer_order(), blocks):
            at = pl.multiple_of(slice_at(section, core, k, j) * rows, rows)
            full[pl.ds(at, rows), :] = block[tap * rows : (tap + 1) * rows, :].astype(jnp.float32)
        turned[...] = full[...].T
        weight_out[tap] = turned[pl.ds(pl.multiple_of(core * rows, rows), rows), :]
    shift_row = jnp.zeros((1, rows), jnp.float32)
    slope_row = jnp.zeros((1, rows), jnp.float32)
    slot = plane * 2 + core
    for (k, j), block in zip(peer_order(), blocks):
        tail = block[taps * rows :, :].astype(jnp.float32)
        mine = slice_at(section, core, k, j) == slot
        shift_row = shift_row + jnp.where(mine, tail[0:1, :rows], 0.0)
        slope_row = slope_row + jnp.where(mine, tail[1:2, :rows], 0.0)
    shift_out[...] = shift_row
    slope_out[...] = slope_row


def call(kernel, outs, scratch, args, name, held=(), held_outs=(), loose=(), last=False, flops=0, copies=None):
    shapes = [
        (jax.ShapeDtypeStruct if last else pltpu.HBM if n in held_outs else pltpu.VMEM)(shape, dtype)
        for n, (shape, dtype) in enumerate(outs)
    ]
    moved = sum(a.size * a.dtype.itemsize for a in args)
    moved += sum(math.prod(shape) * jnp.dtype(dtype).itemsize for shape, dtype in outs)
    spaces = [pltpu.HBM if n in held else pltpu.VMEM for n in range(len(args))]
    out_spaces = [pltpu.HBM if n in held_outs else pltpu.VMEM for n in range(len(outs))]
    args = [
        a if n in loose else pltpu.with_memory_space_constraint(a, space)
        for n, (a, space) in enumerate(zip(args, spaces))
    ]
    scratch_shapes = [
        pltpu.SMEM(shape, dtype) if dtype == jnp.int32 else pltpu.VMEM(shape, dtype) for shape, dtype in scratch
    ]
    if copies is not None:
        scratch_shapes.append(pltpu.SemaphoreType.DMA((copies,)))
    return pl.pallas_call(
        kernel,
        out_shape=shapes,
        in_specs=[pl.BlockSpec(memory_space=space) for space in spaces],
        out_specs=[pl.BlockSpec(memory_space=space) for space in out_spaces],
        scratch_shapes=scratch_shapes,
        compiler_params=pltpu.CompilerParams(vmem_limit_bytes=VMEM_LIMIT),
        cost_estimate=pl.CostEstimate(flops=flops, bytes_accessed=moved, transcendentals=0),
        name=name,
    )(*args)


def plane_shards(images, image_group, group_size, conv_weight, bn_gain, bn_bias, cotangent):
    _, _, core = place()
    micro_total, _, rows, cols, channels = images.shape
    layers = lax.axis_size("section")
    last = layers - 1
    cells = rows * cols
    frames = 2 * micro_total
    length = frames * cells
    ch = channels // 8
    dims = (rows, cols)
    bf16, f32 = jnp.bfloat16, jnp.float32
    facts = grid_facts(frames, rows, cols)
    conv_flops = 2 * TAPS * ch * channels * length
    slice_rows = TAPS * ch + META_ROWS
    tap_rows = -(-TAPS * ch // LANES) * LANES

    full_map = ((channels, length), bf16)
    full_frames = ((length, channels), bf16)
    tap_scratch = ((TAPS * ch, length), f32)
    weight_slice = ((slice_rows, channels), bf16)
    map_out = ((ch, length), bf16)
    sums_out = ((ch, 2 * LANES), f32)
    kept_out = ((ch, length + LANES), f32)
    share_out = ((4 * slice_rows, 2 * ch), bf16)
    share_piece = ((slice_rows, 2 * ch), bf16)

    taps_first = conv_weight[0].transpose(1, 2, 0, 3).reshape(TAPS, channels, channels)
    packed = call(
        pack_kernel,
        [weight_slice] * 4,
        [
            weight_slice,
            ((TAPS, channels, 4 * ch), bf16),
            ((4 * ch, channels), bf16),
            ((2, 1, channels), f32),
        ],
        [bn_gain, bn_bias, taps_first],
        "weight_pack",
        held=range(3),
        held_outs=(0,),
        copies=TAPS + 2,
    )
    slices = spread(packed, to_section)

    payload = ((cells + META_ROWS, channels + LANES), bf16)
    sent = call(
        partial(frames_kernel, dims),
        [payload] * 4,
        [((micro_total, cells, channels), bf16)] * 2
        + [(image_group.shape[::-1], jnp.int32), (group_size.shape[::-1], jnp.int32)],
        [
            image_group.T,
            group_size.T,
            after(images.reshape(micro_total, cells, channels), packed),
            cotangent.reshape(micro_total, cells, channels),
        ],
        "frames",
        held=range(4),
        copies=4,
    )
    frames_in = with_core(spread(sent, to_plane))

    half = (core * ch + np.arange(ch))[:, None] == np.arange(2 * ch)[None, :]
    hidden, normed, full, inside, cot = call(
        partial(forward_kernel, dims, 0, True, CONVS == 1),
        [map_out, kept_out, full_frames, ((1, length), f32), map_out],
        [
            full_frames,
            tap_scratch,
            kept_out,
            weight_slice,
            ((frames * META_ROWS, channels), bf16),
            ((length, LANES), bf16),
            map_out,
        ],
        [*frames_in, *slices, facts, half.astype(bf16)],
        "forward",
        held=range(8, 12),
        held_outs=(1, 2, 4),
        loose=(12, 13),
        flops=conv_flops,
        copies=4,
    )
    kept, fulls = [normed], [full]
    for layer in range(1, layers):
        stored = [turned[1]] if layer == last else []
        weight, *stored = call(
            partial(pick_kernel, layer),
            [weight_slice] + [((layers * 4 * ch, tap_rows), bf16)] * len(stored),
            [],
            [*after(slices, hidden), *after(stored, hidden)],
            "pick",
            held=range(4),
            held_outs=(1,),
            loose=(4,),
            copies=2,
        )
        if stored:
            turned[1] = stored[0]
        beside = [weight]
        if layer == 1:
            turned = call(
                partial(turn_weights_kernel, layers),
                [((layers * 4 * ch, tap_rows), bf16)] * 2,
                [
                    ((layers, TAPS * ch, channels), bf16),
                    ((channels, TAPS * ch), bf16),
                    ((2, layers * 4 * ch, tap_rows), bf16),
                ],
                after(slices, hidden),
                "turn_weights",
                held=range(4),
                held_outs=(0, 1),
                copies=layers,
            )
            beside.append(turned)
        if layer == 2:
            turned = [turned[0], to_core(after(turned[1], hidden))]
        blocks = [hidden] + [to_section(hidden, k) for k in (1, 2, 3)]
        blocks[3] = after(blocks[3], *beside)
        blocks = with_core(blocks)
        if layer < last:
            hidden, normed, full = call(
                partial(forward_kernel, dims, layer, False, layer == CONVS - 1),
                [map_out, kept_out, full_map],
                [full_map, tap_scratch, kept_out],
                [*blocks, weight, inside, facts],
                "forward",
                held_outs=(1, 2),
                loose=(9, 10),
                flops=conv_flops,
                copies=2,
            )
            kept.append(normed)
        else:
            activation, full, grad_pre, sums = call(
                partial(turn_kernel, dims, last, last == CONVS - 1),
                [map_out, full_map, map_out, sums_out],
                [full_map, tap_scratch, map_out, map_out],
                [*blocks, weight, cot, inside, facts],
                "turn",
                held=(9,),
                held_outs=(0, 1),
                loose=(10, 11),
                flops=conv_flops,
                copies=3,
            )
        fulls.append(full)

    shares = [None] * layers
    same_core = [[2 * z + c for z in range(layers)] for c in range(2)]
    for layer in range(last, -1, -1):
        scattered = layer > 0
        result = call(
            partial(conv_back_kernel, dims, layer),
            [map_out] * 4 + ([share_out] if scattered else [share_piece] * 4),
            [
                share_out if scattered else ((TAPS * ch, channels), bf16),
                ((2 * tap_rows, length), bf16),
                ((4 * ch, 2 * tap_rows), bf16),
                full_map if layer else full_frames,
            ],
            [grad_pre, to_core(grad_pre), *turned, fulls[layer], sums, facts],
            "conv_back",
            held=(2, 3, 4),
            held_outs=(4,) if scattered else (),
            loose=(5, 6),
            copies=4,
        )
        parts = result[:4]
        if scattered:
            shares[layer] = lax.psum_scatter(
                result[4], "dp", scatter_dimension=0, tiled=True, axis_index_groups=same_core
            )
        else:
            shares[layer] = spread(result[4:], to_plane)
        if layer:
            held = call(
                partial(fetch_kernel, layer - 1),
                [kept_out, ((META_ROWS, channels), bf16)],
                [],
                [after(kept[layer - 1], parts), *slices],
                "fetch",
                held=range(5),
                copies=2,
            )
            blocks = spread(parts, to_section, held)
            grad_pre, sums = call(
                partial(norm_back_kernel, dims, layer - 1 == CONVS - 1),
                [map_out, sums_out],
                [],
                [*blocks, *held, inside, facts],
                "norm_back",
                loose=(6, 7),
            )
    blocks = spread(parts, to_section)
    maps = call(
        input_kernel,
        [((2 * ch, 2 * cells), bf16)] * 4,
        [((2 * ch, length), bf16)],
        [*blocks, activation, inside],
        "input",
        held=(4,),
        loose=(5,),
        copies=1,
    )
    maps = lax.optimization_barrier(
        [send(x, lambda s, z, c, k=k: (z, s ^ k, c)) for k, x in enumerate(maps)]
    )
    activations, input_grad = call(
        maps_out_kernel,
        [((cells, channels), bf16)] * 2,
        [((channels, 2 * cells), bf16)],
        with_core(maps),
        "maps_out",
        last=True,
    )

    ready = shares[1:]
    chosen = call(
        choose_kernel,
        [share_piece] * 4,
        [],
        [*shares[0], *ready],
        "choose",
        held=range(4, 4 + len(ready)),
        copies=4,
    )
    weight_grad, bias_grad, gain_grad = call(
        grads_out_kernel,
        [((TAPS, ch, channels), f32), ((1, ch), f32), ((1, ch), f32)],
        [((channels, 2 * ch), f32), ((2 * ch, channels), f32)],
        with_core(spread(chosen, to_section)),
        "grads_out",
        last=True,
    )
    weight_grad = weight_grad.reshape(3, 3, ch, channels).transpose(2, 0, 1, 3)[None]
    return (
        activations.reshape(1, 1, rows, cols, channels),
        input_grad.reshape(1, 1, rows, cols, channels),
        weight_grad,
        gain_grad,
        bias_grad,
    )


def fits_plane_plan(images, conv_weight, sections, dps):
    micro_total, images_total, rows, cols, channels = images.shape
    return (
        sections == 4
        and dps == 2 * sections
        and micro_total == sections
        and conv_weight.shape[0] == sections
        and images_total == dps
        and rows % 2 == 0
        and cols % 2 == 0
        and (rows * cols) % 64 == 0
        and channels == 512
    )


def solution(mesh):
    in_specs = (
        P(None, "dp", None, None, None),
        P(None, "dp"),
        P(),
        P("section", None, None, None, None),
        P("section", None),
        P("section", None),
        P(None, "dp", None, None, None),
    )
    out_specs = (
        P("section", "dp", None, None, None),
        P("section", "dp", None, None, None),
        P("section", "dp", None, None, None),
        P("section", "dp"),
        P("section", "dp"),
    )
    sections, dps = mesh.shape["section"], mesh.shape["dp"]

    def program(images, image_group, group_size, conv_weight, bn_gain, bn_bias, cotangent):
        plan = plane_shards if fits_plane_plan(images, conv_weight, sections, dps) else pipeline_shards
        sharded = jax.shard_map(plan, mesh=mesh, in_specs=in_specs, out_specs=out_specs, check_vma=False)
        return sharded(images, image_group, group_size, conv_weight, bn_gain, bn_bias, cotangent)

    return program
```

```python
import math
from functools import partial

import jax
import jax.numpy as jnp
import numpy as np
from jax import lax
from jax.experimental import pallas as pl
from jax.experimental.pallas import tpu as pltpu
from jax.sharding import PartitionSpec as P

CONVS = 2
BACK_FLOPS = 6000000000


eps = 1e-05


def from_behind(x, axis, by):
    peers = lax.axis_size(axis)
    pairs = [(i, i + by) for i in range(peers) if 0 <= i + by < peers]
    return lax.ppermute(x, axis, pairs)


def canvas_mask(image_group, group_size, canvas_rows, canvas_cols):
    groups_n = group_size.shape[0]
    onehot = image_group[..., None] == jnp.arange(groups_n, dtype=jnp.int32)
    height = jnp.sum(jnp.where(onehot, group_size[:, 0], 0), axis=-1)
    breadth = jnp.sum(jnp.where(onehot, group_size[:, 1], 0), axis=-1)
    inside_rows = jnp.arange(canvas_rows, dtype=jnp.int32)[:, None] < height[..., None, None]
    inside_cols = jnp.arange(canvas_cols, dtype=jnp.int32)[None, :] < breadth[..., None, None]
    return (inside_rows & inside_cols).astype(jnp.float32)[..., None]


def window_pool(hidden):
    frames, height, breadth, channels = hidden.shape
    blocks = hidden.reshape(frames, height // 2, 2, breadth // 2, 2, channels)
    window_max = jnp.max(blocks, axis=(2, 4), keepdims=True)
    raised = jnp.exp(blocks - window_max)
    weights = raised / jnp.sum(raised, axis=(2, 4), keepdims=True)
    pooled = jnp.sum(weights * blocks, axis=(2, 4), keepdims=True)
    return (weights * pooled).reshape(frames, height, breadth, channels)


def activate(pre_act, inside, pooling):
    hidden = jax.nn.silu(pre_act) * inside
    return jnp.where(pooling, window_pool(hidden) * inside, hidden)


def conv_forward(layer_in, weight):
    return lax.conv_general_dilated(
        layer_in,
        weight,
        (1, 1),
        "SAME",
        dimension_numbers=("NHWC", "IHWO", "NHWC"),
        preferred_element_type=jnp.float32,
    )


def conv_data_back(grad_pre, weight):
    flipped = weight[:, ::-1, ::-1, :]
    return lax.conv_general_dilated(
        grad_pre,
        flipped,
        (1, 1),
        "SAME",
        dimension_numbers=("NHWC", "OHWI", "NHWC"),
        preferred_element_type=jnp.float32,
    )


def weight_back(layer_in, grad_pre):
    height = layer_in.shape[1]
    breadth = layer_in.shape[2]
    padded = jnp.pad(layer_in, ((0, 0), (1, 1), (1, 1), (0, 0)))
    pieces = []
    for tap_row in range(3):
        for tap_col in range(3):
            window = padded[:, tap_row : tap_row + height, tap_col : tap_col + breadth, :]
            pieces.append(
                jnp.einsum("nhwi,nhwo->io", window, grad_pre, preferred_element_type=jnp.float32)
            )
    return jnp.stack(pieces, axis=1).reshape(layer_in.shape[3], 3, 3, grad_pre.shape[3])


def layer_forward(layer_in, weight, gain_row, bias_row, inside, pooling):
    pre_norm = conv_forward(layer_in, weight)
    sums = lax.psum(
        (
            jnp.sum(pre_norm * inside, axis=(0, 1, 2)),
            jnp.sum(pre_norm * pre_norm * inside, axis=(0, 1, 2)),
            jnp.sum(inside),
        ),
        "dp",
    )
    pixel_total = sums[2]
    mean_val = sums[0] / pixel_total
    scale_inv = lax.rsqrt(sums[1] / pixel_total - mean_val * mean_val + eps)
    pre_act = (pre_norm - mean_val) * scale_inv * gain_row + bias_row
    hidden = activate(pre_act, inside, pooling)
    return (pre_norm, mean_val, scale_inv, pixel_total, hidden)


def layer_backward(
    grad_out,
    layer_in,
    pre_norm,
    mean_val,
    scale_inv,
    pixel_total,
    weight,
    gain_row,
    bias_row,
    inside,
    pooling,
):
    normed = (pre_norm - mean_val) * scale_inv
    pre_act = normed * gain_row + bias_row
    hidden_out, pullback = jax.vjp(partial(activate, inside=inside, pooling=pooling), pre_act)
    grad_act = pullback(grad_out)[0]
    sums = lax.psum(
        (jnp.sum(grad_act, axis=(0, 1, 2)), jnp.sum(grad_act * normed, axis=(0, 1, 2))), "dp"
    )
    shift_term = sums[0] / pixel_total
    slope_term = sums[1] / pixel_total
    grad_pre = (
        inside * scale_inv * gain_row * (grad_act - shift_term - normed * slope_term)
    ).astype(jnp.bfloat16)
    weight_term = weight_back(layer_in, grad_pre)
    grad_in = conv_data_back(grad_pre, weight).astype(jnp.bfloat16)
    return (grad_in, weight_term, sums[1], sums[0])


def pipeline_shards(images, image_group, group_size, conv_weight, bn_gain, bn_bias, cotangent):
    section_index = lax.axis_index("section")
    sections = lax.axis_size("section")
    micro_total = images.shape[0]
    channels = conv_weight.shape[1]
    inside_all = canvas_mask(image_group, group_size, images.shape[2], images.shape[3])
    ticks = micro_total + sections - 1
    weight = conv_weight[0]
    gain_row = bn_gain[0]
    bias_row = bn_bias[0]
    pool_here = section_index == CONVS - 1
    received = jnp.zeros(images.shape[1:], jnp.bfloat16)
    kept_in, kept_pre, kept_mean, kept_scale, kept_total, finished = ([], [], [], [], [], [])
    for tick in range(ticks):
        micro_pos = jnp.clip(tick - section_index, 0, micro_total - 1)
        inside = inside_all[micro_pos]
        fresh = (images[micro_pos].astype(jnp.float32) * inside).astype(jnp.bfloat16)
        layer_in = jnp.where(section_index == 0, fresh, received)
        pre_norm, mean_val, scale_inv, pixel_total, hidden = layer_forward(
            layer_in, weight, gain_row, bias_row, inside, pool_here
        )
        sent = hidden.astype(jnp.bfloat16)
        if tick < ticks - 1:
            received = from_behind(sent, "section", 1)
        kept_in.append(layer_in)
        kept_pre.append(pre_norm)
        kept_mean.append(mean_val)
        kept_scale.append(scale_inv)
        kept_total.append(pixel_total)
        finished.append(sent)
    stack_in = jnp.stack(kept_in)
    stack_pre = jnp.stack(kept_pre)
    stack_mean = jnp.stack(kept_mean)
    stack_scale = jnp.stack(kept_scale)
    stack_total = jnp.stack(kept_total)
    returned = jnp.zeros(images.shape[1:], jnp.bfloat16)
    weight_sum = jnp.zeros(conv_weight.shape[1:], jnp.float32)
    gain_sum = jnp.zeros((channels,), jnp.float32)
    bias_sum = jnp.zeros((channels,), jnp.float32)
    input_list = []
    for tick in range(ticks):
        micro_raw = tick - (sections - 1 - section_index)
        valid = ((micro_raw >= 0) & (micro_raw < micro_total)).astype(jnp.float32)
        micro_pos = jnp.clip(micro_raw, 0, micro_total - 1)
        forward_tick = jnp.clip(micro_pos + section_index, 0, ticks - 1)
        inside = inside_all[micro_pos]
        grad_out = jnp.where(
            section_index == sections - 1,
            cotangent[micro_pos].astype(jnp.float32),
            returned.astype(jnp.float32),
        )
        grad_in, weight_term, gain_term, bias_term = layer_backward(
            grad_out,
            stack_in[forward_tick],
            stack_pre[forward_tick],
            stack_mean[forward_tick],
            stack_scale[forward_tick],
            stack_total[forward_tick],
            weight,
            gain_row,
            bias_row,
            inside,
            pool_here,
        )
        weight_sum = weight_sum + valid * weight_term
        gain_sum = gain_sum + valid * gain_term
        bias_sum = bias_sum + valid * bias_term
        if tick < ticks - 1:
            returned = from_behind(grad_in, "section", -1)
        input_list.append((grad_in.astype(jnp.float32) * inside).astype(jnp.bfloat16))
    out_stack = jnp.stack(finished[sections - 1 :], axis=0)
    grad_stack = jnp.stack(input_list[sections - 1 :], axis=0)
    out_back, grad_back = (
        lax.all_to_all(out_stack, "section", split_axis=0, concat_axis=1, tiled=True),
        lax.all_to_all(grad_stack, "section", split_axis=0, concat_axis=1, tiled=True),
    )
    activations = out_back[:, sections - 1 : sections]
    input_grad = grad_back[:, 0:1]
    weight_grad = lax.psum_scatter(weight_sum[None], "dp", scatter_dimension=1, tiled=True)
    share = channels // lax.axis_size("dp")
    gain_grad = lax.dynamic_slice_in_dim(gain_sum, lax.axis_index("dp") * share, share)[None]
    bias_grad = lax.dynamic_slice_in_dim(bias_sum, lax.axis_index("dp") * share, share)[None]
    return (activations, input_grad, weight_grad, gain_grad, bias_grad)


AXES = ("section", "dp")
TAPS = 9
VMEM_LIMIT = 24 * 1024 * 1024
META_ROWS = 16
LANES = 128
ROW_AT, COL_AT, FRAME_AT = 6, 7, 8
NT = (((1,), (1,)), ((), ()))


def place():
    dp_index = lax.axis_index("dp")
    return lax.axis_index("section"), dp_index // 2, dp_index % 2


def peer_order():
    return [(k, j) for j in range(2) for k in range(4)]


def slice_at(section, core, k, j):
    return (core ^ j) * lax.axis_size("section") + (section ^ k)


def send(x, target):
    sections = lax.axis_size("section")
    dps = lax.axis_size("dp")
    pairs = []
    for s in range(sections):
        for d in range(dps):
            ts, tz, tc = target(s, d // 2, d % 2)
            pairs.append((s * dps + d, ts * dps + tz * 2 + tc))
    return lax.ppermute(x, AXES, pairs)


def to_section(x, k):
    return send(x, lambda s, z, c: (s ^ k, z, c))


def to_plane(x, k):
    return send(x, lambda s, z, c: (s, z ^ k, c))


def to_core(x):
    return send(x, lambda s, z, c: (s, z, c ^ 1))


def spread(blocks, move, *beside):
    moved = lax.optimization_barrier(([move(blocks[k], k) for k in (1, 2, 3)], beside))[0]
    return [blocks[0]] + moved


def with_core(blocks):
    return blocks + [to_core(x) for x in blocks]


def after(x, *first):
    return lax.optimization_barrier((x, first))[0]


def grid_facts(frames, rows, cols):
    at = np.arange(frames * rows * cols)
    col = at % cols
    row = (at // cols) % rows
    facts = [row > 0, row < rows - 1, col > 0, col < cols - 1, col % 2 == 0, row % 2 == 0, row, col]
    facts = facts + [at // (rows * cols) == frame for frame in range(frames)]
    return jnp.asarray(np.stack(facts).astype(np.float32))


def shift(x, by):
    length = x.shape[1]
    return pltpu.roll(x, (-by) % length, 1) if by % length else x


def row_ok(facts, d):
    return facts[0:1, :] if d < 0 else facts[1:2, :]


def col_ok(facts, d):
    return facts[2:3, :] if d < 0 else facts[3:4, :]


def sum_taps(taps_ref, facts, cols):
    ch = taps_ref.shape[0] // TAPS
    total = None
    for dx in (-1, 0, 1):
        column = None
        for dy in (-1, 0, 1):
            tap = (dy + 1) * 3 + dx + 1
            piece = taps_ref[tap * ch : (tap + 1) * ch, :]
            if dy:
                piece = shift(piece, dy * cols) * row_ok(facts, dy)
            column = piece if column is None else column + piece
        if dx:
            column = shift(column, dx) * col_ok(facts, dx)
        total = column if total is None else total + column
    return total


def spread_taps(grad, moved_ref, base, facts, cols):
    ch = grad.shape[0]
    facts = facts[:4, :].astype(grad.dtype)
    for dx in (-1, 0, 1):
        column = shift(grad, -dx) * col_ok(facts, -dx) if dx else grad
        for dy in (-1, 0, 1):
            piece = shift(column, -dy * cols) * row_ok(facts, -dy) if dy else column
            at = base + ((dy + 1) * 3 + dx + 1) * ch
            moved_ref[at : at + ch, :] = piece


def corner_sum(x, cols):
    x = x + shift(x, 1)
    return x + shift(x, cols)


def from_corner(x, facts, cols):
    x = jnp.where(facts[4:5, :] > 0.5, x, shift(x, -1))
    return jnp.where(facts[5:6, :] > 0.5, x, shift(x, -cols))


def lane_sum(x):
    return jnp.sum(x, axis=1, keepdims=True)


def normalise(pre, inside):
    count = lane_sum(inside)
    mean = lane_sum(pre * inside) / count
    square = lane_sum(pre * pre * inside) / count
    scale = lax.rsqrt(square - mean * mean + eps)
    return (pre - mean) * scale, scale


def hidden_of(normed, gain, bias, inside, facts, cols, pooling):
    pre_act = normed * gain + bias
    hidden = pre_act * jax.nn.sigmoid(pre_act) * inside
    if pooling:
        raised = jnp.exp(hidden)
        total = corner_sum(raised, cols)
        pooled = corner_sum(raised * hidden, cols) / total
        hidden = raised * from_corner(pooled / total, facts, cols) * inside
    return hidden


def norm_back(grad, normed, scale, gain, bias, inside, facts, cols, pooling):
    pre_act = normed * gain + bias
    gate = jax.nn.sigmoid(pre_act)
    if pooling:
        hidden = pre_act * gate * inside
        raised = jnp.exp(hidden)
        out = grad * inside
        total = 1.0 / corner_sum(raised, cols)
        pooled = corner_sum(raised * hidden, cols) * total
        d_pooled = corner_sum(raised * out, cols) * total
        by_out = from_corner(pooled * total, facts, cols)
        by_hidden = from_corner(d_pooled * total, facts, cols)
        rest = from_corner(d_pooled * total * (1.0 - 2.0 * pooled), facts, cols)
        grad = raised * (out * by_out + hidden * by_hidden + rest)
    grad_act = grad * inside * gate * (1.0 + pre_act * (1.0 - gate))
    count = lane_sum(inside)
    shift_sum = lane_sum(grad_act)
    slope_sum = lane_sum(grad_act * normed)
    grad_pre = inside * (scale * gain) * (grad_act - shift_sum / count - normed * (slope_sum / count))
    return grad_pre.astype(jnp.bfloat16), shift_sum, slope_sum


def assemble(blocks, full_ref):
    section, _, core = place()
    ch = blocks[0].shape[0]
    for (k, j), block in zip(peer_order(), blocks):
        at = pl.multiple_of(slice_at(section, core, k, j) * ch, ch)
        full_ref[pl.ds(at, ch), :] = block[...]


def assemble_frames(blocks, full_ref, rows, lanes):
    _, plane, core = place()
    size = rows.stop - rows.start
    for (k, j), block in zip(peer_order(), blocks):
        frame = (plane ^ k) * 2 + (core ^ j)
        full_ref[pl.ds(pl.multiple_of(frame * size, size), size), :] = block[rows, lanes]


def start_all(copies):
    for copy in copies:
        copy.start()
    return copies


def wait_all(copies):
    for copy in copies:
        copy.wait()


def tap_products(weight, full_ref, taps_ref, by_cells):
    length = taps_ref.shape[1]
    step = 512 if length % 512 == 0 else length
    for at in range(0, length, step):
        if by_cells:
            taps_ref[:, at : at + step] = lax.dot_general(
                weight, full_ref[at : at + step, :], NT, preferred_element_type=jnp.float32
            )
        else:
            taps_ref[:, at : at + step] = jnp.dot(
                weight, full_ref[:, at : at + step], preferred_element_type=jnp.float32
            )


def pick_layer(layer, sources, start, target, sem):
    section, _, _ = place()
    rows = pl.ds(start, target.shape[0])
    for k, source in enumerate(sources):

        @pl.when((section ^ layer) == k)
        def _():
            pltpu.make_async_copy(source.at[rows], target, sem).start()

    return pltpu.make_async_copy(sources[0].at[rows], target, sem)


def affine(meta, ch):
    parts = meta[:, :LANES].astype(jnp.float32).T[:ch]
    return (
        parts[:, 0:1] + parts[:, 1:2] + parts[:, 2:3],
        parts[:, 3:4] + parts[:, 4:5] + parts[:, 5:6],
    )


def plane_inside(metas, facts):
    frames = metas.shape[0] // META_ROWS
    extents = []
    for line in (0, 1):
        total = None
        for f in range(frames):
            at = f * META_ROWS + line
            extent = metas[at : at + 1, 0:1].astype(jnp.float32) * facts[FRAME_AT + f : FRAME_AT + f + 1, :]
            total = extent if total is None else total + extent
        extents.append(total)
    on = (facts[ROW_AT : ROW_AT + 1, :] < extents[0]) & (facts[COL_AT : COL_AT + 1, :] < extents[1])
    return jnp.where(on, 1.0, 0.0)


def frames_kernel(dims, group_table, size_table, images, cots, *refs):
    payloads, (image_in, cot_in, groups, sizes, sems) = refs[:4], refs[4:]
    copies = start_all(
        [
            pltpu.make_async_copy(group_table, groups, sems.at[0]),
            pltpu.make_async_copy(size_table, sizes, sems.at[1]),
            pltpu.make_async_copy(images, image_in, sems.at[2]),
            pltpu.make_async_copy(cots, cot_in, sems.at[3]),
        ]
    )
    section, plane, _ = place()
    rows, cols = dims
    cells = rows * cols
    at = lax.broadcasted_iota(jnp.int32, (cells, LANES), 0).astype(jnp.float32)
    row = jnp.floor((at + 0.5) * (1.0 / cols))
    col = at - row * cols
    channels = images.shape[2]
    half = channels // 2
    wait_all(copies)
    for k in range(4):
        micro = plane ^ k
        group = groups[0, micro]
        height = sizes[0, 0]
        breadth = sizes[1, 0]
        for g in range(1, sizes.shape[1]):
            height = jnp.where(group == g, sizes[0, g], height)
            breadth = jnp.where(group == g, sizes[1, g], breadth)
        height = height.astype(jnp.float32)
        breadth = breadth.astype(jnp.float32)
        on = jnp.where((row < height) & (col < breadth), 1.0, 0.0)
        image = image_in[micro]
        for c in range(0, channels, LANES):
            piece = image[:, c : c + LANES].astype(jnp.float32) * on
            payloads[k][:cells, c : c + LANES] = piece.astype(jnp.bfloat16)
        line = lax.broadcasted_iota(jnp.int32, (META_ROWS, channels + LANES), 0)
        payloads[k][cells:, :] = jnp.where(line == 0, height, breadth).astype(jnp.bfloat16)
        tile = section // 2 * LANES
        low = cot_in[micro, :, pl.ds(pl.multiple_of(tile, LANES), LANES)].astype(jnp.float32)
        high = cot_in[micro, :, pl.ds(pl.multiple_of(half + tile, LANES), LANES)].astype(jnp.float32)
        odd = section % 2 == 1
        low = jnp.where(odd, pltpu.roll(low, LANES // 2, 1), low)
        high = jnp.where(odd, high, pltpu.roll(high, LANES // 2, 1))
        lane = lax.broadcasted_iota(jnp.int32, (cells, LANES), 1)
        both = jnp.where(lane < LANES // 2, low, high).astype(jnp.bfloat16)
        payloads[k][:cells, channels:] = both


def pack_kernel(gain, bias, weight, *refs):
    outs, (own, columns, turned, tables, sems) = refs[:4], refs[4:]
    section, _, core = place()
    width = columns.shape[2]
    ch = width // 4
    start = pl.multiple_of(core * width, width)
    copies = start_all(
        [
            pltpu.make_async_copy(weight.at[tap, :, pl.ds(start, width)], columns.at[tap], sems.at[tap])
            for tap in range(TAPS)
        ]
    )
    table_copies = start_all(
        [
            pltpu.make_async_copy(gain, tables.at[0], sems.at[TAPS]),
            pltpu.make_async_copy(bias, tables.at[1], sems.at[TAPS + 1]),
        ]
    )
    wait_all(table_copies)
    targets = [own, *outs[1:]]
    for k, out in enumerate(targets):
        lines = []
        tile = pl.multiple_of(start + (section ^ k) // 2 * LANES, LANES)
        odd = (section ^ k) % 2 == 1
        for m in range(2):
            line = tables[m, :, pl.ds(tile, LANES)]
            line = jnp.where(odd, pltpu.roll(line, ch, 1), line)
            for _ in range(3):
                part = line.astype(jnp.bfloat16).astype(jnp.float32)
                lines.append(part)
                line = line - part
        lines.append(jnp.zeros((META_ROWS - len(lines), LANES), jnp.float32))
        out[TAPS * ch :, :] = jnp.zeros((META_ROWS, out.shape[1]), jnp.bfloat16)
        out[TAPS * ch :, :LANES] = jnp.concatenate(lines, axis=0).astype(jnp.bfloat16)
    tail = pl.ds(TAPS * ch, META_ROWS)
    own_copies = start_all([pltpu.make_async_copy(own.at[tail], outs[0].at[tail], sems.at[2 * TAPS + 2])])
    for tap in range(TAPS):
        copies[tap].wait()
        turned[...] = columns[tap].T
        for k, out in enumerate(targets):
            rows = pl.ds(pl.multiple_of((section ^ k) * ch, ch), ch)
            out[tap * ch : (tap + 1) * ch, :] = turned[rows, :]
        piece = pl.ds(tap * ch, ch)
        own_copies += start_all(
            [pltpu.make_async_copy(own.at[piece], outs[0].at[piece], sems.at[TAPS + 2 + tap])]
        )
    wait_all(own_copies)


def pick_kernel(layer, *refs):
    sources, others, out, targets, sems = refs[:4], refs[4:-2], refs[-2], (), refs[-1]
    if len(others) > 0:
        others, out, targets = refs[4:5], refs[5], refs[6:7]
    copies = [pick_layer(layer, sources, 0, out, sems.at[0])]
    for other, target in zip(others, targets):
        copies += start_all([pltpu.make_async_copy(other, target, sems.at[1])])
    wait_all(copies)


def forward_kernel(dims, layer, first, pooling, *refs):
    blocks, weights, rest = refs[:8], refs[8 : 12 if first else 9], refs[12 if first else 9 :]
    rows, cols = dims
    cells = rows * cols
    if first:
        facts, pick, hidden, kept, full_out, inside_out, cot_out, full, taps, stage, weight, metas, *rest = rest
        cot_full, cot, sems = rest
        copy = pick_layer(layer, weights, 0, weight, sems.at[2])
    else:
        inside, facts, hidden, kept, full_out, full, taps, stage, sems = rest
        (weight,) = weights
    facts_now = facts[...]
    if first:
        channels = full.shape[1]
        assemble_frames(blocks, full, slice(0, cells), slice(0, channels))
    else:
        assemble(blocks, full)
    full_copy = pltpu.make_async_copy(full, full_out, sems.at[0])
    full_copy.start()
    if first:
        assemble_frames(blocks, metas, slice(cells, cells + META_ROWS), slice(0, channels))
        assemble_frames(blocks, cot_full, slice(0, cells), slice(channels, channels + LANES))
        inside_now = plane_inside(metas, facts_now)
        inside_out[...] = inside_now
        copy.wait()
    else:
        inside_now = inside[...]
    ch = hidden.shape[0]
    tap_products(weight[: TAPS * ch, :], full, taps, first)
    if first:
        cot[...] = lax.dot_general(
            pick[...], cot_full[...], NT, preferred_element_type=jnp.float32
        ).astype(jnp.bfloat16)
        cot_copy = pltpu.make_async_copy(cot, cot_out, sems.at[3])
        cot_copy.start()
    pre = sum_taps(taps, facts_now, cols)
    normed, scale = normalise(pre, inside_now)
    length = normed.shape[1]
    stage[:, :length] = normed
    stage[:, length:] = jnp.broadcast_to(scale, (ch, LANES))
    kept_copy = pltpu.make_async_copy(stage, kept, sems.at[1])
    kept_copy.start()
    gain, bias = affine(weight[TAPS * ch :, :], ch)
    hidden[...] = hidden_of(normed, gain, bias, inside_now, facts_now, cols, pooling).astype(jnp.bfloat16)
    if first:
        cot_copy.wait()
    full_copy.wait()
    kept_copy.wait()


def turn_kernel(dims, layer, pooling, *refs):
    blocks, (weight, cot_in, inside, facts) = refs[:8], refs[8:12]
    hidden_out, full_out, grad_pre, sums, full, taps, cot, hidden, sems = refs[12:]
    cols = dims[1]
    cot_copy = pltpu.make_async_copy(cot_in, cot, sems.at[0])
    cot_copy.start()
    assemble(blocks, full)
    full_copy = pltpu.make_async_copy(full, full_out, sems.at[1])
    full_copy.start()
    ch = grad_pre.shape[0]
    tap_products(weight[: TAPS * ch, :], full, taps, False)
    facts_now, inside_now = facts[...], inside[...]
    pre = sum_taps(taps, facts_now, cols)
    normed, scale = normalise(pre, inside_now)
    gain, bias = affine(weight[TAPS * ch :, :], ch)
    hidden[...] = hidden_of(normed, gain, bias, inside_now, facts_now, cols, pooling).astype(jnp.bfloat16)
    hidden_copy = pltpu.make_async_copy(hidden, hidden_out, sems.at[2])
    hidden_copy.start()
    cot_copy.wait()
    grad_pre[...], shift_sum, slope_sum = norm_back(
        cot[...].astype(jnp.float32), normed, scale, gain, bias, inside_now, facts_now, cols, pooling
    )
    keep_sums(sums, shift_sum, slope_sum)
    full_copy.wait()
    hidden_copy.wait()


def keep_sums(sums, shift_sum, slope_sum):
    ch = shift_sum.shape[0]
    sums[:, :LANES] = jnp.broadcast_to(shift_sum, (ch, LANES))
    sums[:, LANES:] = jnp.broadcast_to(slope_sum, (ch, LANES))


def add_blocks(blocks):
    total = blocks[0][...].astype(jnp.float32)
    for block in blocks[1:]:
        total = total + block[...].astype(jnp.float32)
    return total


def fetch_kernel(layer, kept, *refs):
    sources, (kept_out, meta_out, sems) = refs[:4], refs[4:]
    copy = pltpu.make_async_copy(kept, kept_out, sems.at[0])
    copy.start()
    start = sources[0].shape[0] - META_ROWS
    pick_layer(layer, sources, start, meta_out, sems.at[1]).wait()
    copy.wait()


def norm_back_kernel(dims, pooling, *refs):
    blocks, (kept, meta, inside, facts, grad_pre, sums) = refs[:4], refs[4:]
    ch, length = grad_pre.shape
    grad = add_blocks(blocks).astype(jnp.bfloat16).astype(jnp.float32)
    gain, bias = affine(meta[...], ch)
    grad_pre[...], shift_sum, slope_sum = norm_back(
        grad,
        kept[:, :length],
        kept[:, length : length + 1],
        gain,
        bias,
        inside[...],
        facts[...],
        dims[1],
        pooling,
    )
    keep_sums(sums, shift_sum, slope_sum)


def weight_product(moved, full, first):
    if first:
        return jnp.dot(moved, full, preferred_element_type=jnp.float32)
    return lax.dot_general(moved, full, NT, preferred_element_type=jnp.float32)


def sums_rows(sums, ch, width):
    lines = []
    for at in (0, LANES):
        turned = sums[:, at : at + LANES].T
        lines.append(jnp.concatenate([turned, jnp.zeros((LANES, width - ch), jnp.float32)], axis=1)[0:1])
    lines.append(jnp.zeros((META_ROWS - 2, width), jnp.float32))
    return jnp.concatenate(lines, axis=0).astype(jnp.bfloat16)


def store_share(value, sums, pieces):
    rows = value.shape[0]
    width = pieces[0].shape[1]
    for n, piece in enumerate(pieces):
        piece[:rows, :] = value[:, n * width : (n + 1) * width].astype(jnp.bfloat16)
        piece[rows:, :] = sums_rows(sums, rows // TAPS, width)


def form_share(layer, moved, full, sums, product):
    piece = product.shape[0] // 4
    value = weight_product(moved[: piece - META_ROWS, :], full[...], layer == 0)
    store_share(value, sums, [product.at[pl.ds(n * piece, piece)] for n in range(4)])


def conv_back_kernel(dims, layer, own, other, own_weights, other_weights, full_in, sums, facts, *refs):
    *outs, share, product, full, moved, weights, sems = refs
    ch = own.shape[0]
    size = moved.shape[0] // 2
    rows = pl.ds(layer * 4 * ch, 4 * ch)
    copies = start_all(
        [
            pltpu.make_async_copy(own_weights.at[rows], weights.at[:, pl.ds(0, size)], sems.at[0]),
            pltpu.make_async_copy(other_weights.at[rows], weights.at[:, pl.ds(size, size)], sems.at[1]),
        ]
    )
    full_copy = pltpu.make_async_copy(full_in, full, sems.at[2])
    full_copy.start()
    facts_now = facts[...]
    spread_taps(own[...], moved, 0, facts_now, dims[1])
    full_copy.wait()
    form_share(layer, moved, full, sums, product)
    share_copy = pltpu.make_async_copy(product, share, sems.at[3])
    share_copy.start()
    spread_taps(other[...], moved, size, facts_now, dims[1])
    for n in range(2):
        moved[n * size + TAPS * ch : (n + 1) * size, :] = jnp.zeros(
            (size - TAPS * ch, moved.shape[1]), jnp.bfloat16
        )
    wait_all(copies)
    value = jnp.dot(weights[...], moved[...], preferred_element_type=jnp.float32)
    for k, out in enumerate(outs):
        out[...] = value[k * ch : (k + 1) * ch, :].astype(jnp.bfloat16)
    share_copy.wait()


def choose_kernel(*refs):
    shares, outs, (blocks, sems) = refs[:-6], refs[-6:-2], refs[-2:]
    section, _, _ = place()
    rows = outs[0].shape[0]
    copies = start_all(
        [pltpu.make_async_copy(share, blocks.at[layer], sems.at[layer]) for layer, share in enumerate(shares)]
    )
    for layer, copy in enumerate(copies):
        copy.wait()
        value = add_blocks([blocks.at[layer, pl.ds(n * rows, rows)] for n in range(blocks.shape[1] // rows)])
        value = value.astype(jnp.bfloat16)
        for k, out in enumerate(outs):

            @pl.when((section ^ k) == layer)
            def _():
                out[...] = value


def turn_weights_kernel(layers, *refs):
    sources, outs, (full, turned, stage, sems) = refs[:4], refs[4:6], refs[6:]
    section, _, core = place()
    rows, channels = full.shape[1:]
    half = channels // 2
    ch = half // 4
    copies = [pick_layer(n, sources, 0, full.at[n], sems.at[n]) for n in range(layers)]
    stage[:, :, rows:] = jnp.zeros((*stage.shape[:2], stage.shape[2] - rows), jnp.bfloat16)
    for n in range(layers):
        copies[n].wait()
        turned[...] = full[n].T
        for j in range(2):
            for k in range(4):
                at = pl.multiple_of((core ^ j) * half + (section ^ k) * ch, ch)
                stage[j, n * half + k * ch : n * half + (k + 1) * ch, :rows] = turned[pl.ds(at, ch), :]
    wait_all(
        start_all([pltpu.make_async_copy(stage.at[j], outs[j], sems.at[j]) for j in range(2)])
    )


def input_kernel(*refs):
    blocks, (hidden, inside, keep, give, full, sems) = refs[:4], refs[4:]
    section, _, core = place()
    ch = hidden.shape[0]
    copy = pltpu.make_async_copy(hidden, full.at[pl.ds(0, ch)], sems.at[0])
    copy.start()
    full[ch:, :] = (add_blocks(blocks) * inside[...]).astype(jnp.bfloat16)
    copy.wait()
    rows = 2 * ch
    width = keep.shape[1]
    for j, out in enumerate((keep, give)):
        for n in range(2):
            at = pl.multiple_of((section ^ (2 * (core ^ j) + n)) * width, width)
            out[n * rows : (n + 1) * rows, :] = full[:, pl.ds(at, width)]


def pair_kernel(keep, got, *outs):
    rows = keep.shape[0] // 2
    for n, out in enumerate(outs):
        out[:rows, :] = keep[n * rows : (n + 1) * rows, :]
        out[rows:, :] = got[n * rows : (n + 1) * rows, :]


def maps_out_kernel(*refs):
    blocks, pick, outs, full = refs[:4], refs[4], refs[5:7], refs[7]
    _, plane, core = place()
    ch = blocks[0].shape[0] // 4
    for m, out in enumerate(outs):
        for j in range(2):
            for n in range(2):
                for h in range(2):
                    slot = slice_at(plane ^ (2 * (core ^ j) + n), core ^ j, 0, h)
                    at = pl.multiple_of(slot * ch, ch)
                    start = (2 * h + m) * ch
                    full[pl.ds(at, ch), :] = blocks[2 * j + n][start : start + ch, :]
        mine = lax.dot_general(pick[...], full[...], NT, preferred_element_type=jnp.float32)
        out[...] = mine.astype(out.dtype)


def grads_out_kernel(*refs):
    blocks, pick, (weight_out, shift_out, slope_out), (full,) = refs[:8], refs[8], refs[9:12], refs[12:]
    section, plane, core = place()
    taps, rows, channels = weight_out.shape
    for tap in range(taps):
        for (k, j), block in zip(peer_order(), blocks):
            at = pl.multiple_of(slice_at(section, core, k, j) * rows, rows)
            full[tap, pl.ds(at, rows), :] = block[tap * rows : (tap + 1) * rows, :]
        weight_out[tap] = lax.dot_general(pick[...], full[tap], NT, preferred_element_type=jnp.float32)
    shift_row = jnp.zeros((1, rows), jnp.float32)
    slope_row = jnp.zeros((1, rows), jnp.float32)
    slot = plane * 2 + core
    for (k, j), block in zip(peer_order(), blocks):
        tail = block[taps * rows :, :].astype(jnp.float32)
        mine = slice_at(section, core, k, j) == slot
        shift_row = shift_row + jnp.where(mine, tail[0:1, :rows], 0.0)
        slope_row = slope_row + jnp.where(mine, tail[1:2, :rows], 0.0)
    shift_out[...] = shift_row
    slope_out[...] = slope_row


def call(kernel, outs, scratch, args, name, held=(), held_outs=(), loose=(), last=False, flops=0, copies=None):
    shapes = [
        (jax.ShapeDtypeStruct if last else pltpu.HBM if n in held_outs else pltpu.VMEM)(shape, dtype)
        for n, (shape, dtype) in enumerate(outs)
    ]
    moved = sum(a.size * a.dtype.itemsize for a in args)
    moved += sum(math.prod(shape) * jnp.dtype(dtype).itemsize for shape, dtype in outs)
    spaces = [pltpu.HBM if n in held else pltpu.VMEM for n in range(len(args))]
    out_spaces = [pltpu.HBM if n in held_outs else pltpu.VMEM for n in range(len(outs))]
    args = [
        a if n in loose else pltpu.with_memory_space_constraint(a, space)
        for n, (a, space) in enumerate(zip(args, spaces))
    ]
    scratch_shapes = [
        pltpu.SMEM(shape, dtype) if dtype == jnp.int32 else pltpu.VMEM(shape, dtype) for shape, dtype in scratch
    ]
    if copies is not None:
        scratch_shapes.append(pltpu.SemaphoreType.DMA((copies,)))
    return pl.pallas_call(
        kernel,
        out_shape=shapes,
        in_specs=[pl.BlockSpec(memory_space=space) for space in spaces],
        out_specs=[pl.BlockSpec(memory_space=space) for space in out_spaces],
        scratch_shapes=scratch_shapes,
        compiler_params=pltpu.CompilerParams(vmem_limit_bytes=VMEM_LIMIT),
        cost_estimate=pl.CostEstimate(flops=flops, bytes_accessed=moved, transcendentals=0),
        name=name,
    )(*args)


def plane_shards(images, image_group, group_size, conv_weight, bn_gain, bn_bias, cotangent):
    _, _, core = place()
    micro_total, _, rows, cols, channels = images.shape
    layers = lax.axis_size("section")
    last = layers - 1
    cells = rows * cols
    frames = 2 * micro_total
    length = frames * cells
    ch = channels // 8
    dims = (rows, cols)
    bf16, f32 = jnp.bfloat16, jnp.float32
    facts = grid_facts(frames, rows, cols)
    conv_flops = 2 * TAPS * ch * channels * length
    slice_rows = TAPS * ch + META_ROWS
    tap_rows = -(-TAPS * ch // LANES) * LANES

    full_map = ((channels, length), bf16)
    full_frames = ((length, channels), bf16)
    tap_scratch = ((TAPS * ch, length), f32)
    weight_slice = ((slice_rows, channels), bf16)
    map_out = ((ch, length), bf16)
    sums_out = ((ch, 2 * LANES), f32)
    kept_out = ((ch, length + LANES), f32)
    share_out = ((4 * slice_rows, 2 * ch), bf16)
    share_piece = ((slice_rows, 2 * ch), bf16)

    taps_first = conv_weight[0].transpose(1, 2, 0, 3).reshape(TAPS, channels, channels)
    packed = call(
        pack_kernel,
        [weight_slice] * 4,
        [
            weight_slice,
            ((TAPS, channels, 4 * ch), bf16),
            ((4 * ch, channels), bf16),
            ((2, 1, channels), f32),
        ],
        [bn_gain, bn_bias, taps_first],
        "weight_pack",
        held=range(3),
        held_outs=(0,),
        copies=2 * TAPS + 3,
    )
    slices = spread(packed, to_section)

    payload = ((cells + META_ROWS, channels + LANES), bf16)
    sent = call(
        partial(frames_kernel, dims),
        [payload] * 4,
        [((micro_total, cells, channels), bf16)] * 2
        + [(image_group.shape[::-1], jnp.int32), (group_size.shape[::-1], jnp.int32)],
        [
            image_group.T,
            group_size.T,
            after(images.reshape(micro_total, cells, channels), packed),
            cotangent.reshape(micro_total, cells, channels),
        ],
        "frames",
        held=range(4),
        copies=4,
    )
    frames_in = with_core(spread(sent, to_plane))

    half = (core * ch + np.arange(ch))[:, None] == np.arange(2 * ch)[None, :]
    hidden, normed, full, inside, cot = call(
        partial(forward_kernel, dims, 0, True, CONVS == 1),
        [map_out, kept_out, full_frames, ((1, length), f32), map_out],
        [
            full_frames,
            tap_scratch,
            kept_out,
            weight_slice,
            ((frames * META_ROWS, channels), bf16),
            ((length, LANES), bf16),
            map_out,
        ],
        [*frames_in, *slices, facts, half.astype(bf16)],
        "forward",
        held=range(8, 12),
        held_outs=(1, 2, 4),
        loose=(12, 13),
        flops=conv_flops,
        copies=4,
    )
    kept, fulls = [normed], [full]
    for layer in range(1, layers):
        stored = [turned[1]] if layer == last else []
        weight, *stored = call(
            partial(pick_kernel, layer),
            [weight_slice] + [((layers * 4 * ch, tap_rows), bf16)] * len(stored),
            [],
            [*after(slices, hidden), *after(stored, hidden)],
            "pick",
            held=range(4),
            held_outs=(1,),
            loose=(4,),
            copies=2,
        )
        if stored:
            turned[1] = stored[0]
        beside = [weight]
        if layer == 1:
            turned = call(
                partial(turn_weights_kernel, layers),
                [((layers * 4 * ch, tap_rows), bf16)] * 2,
                [
                    ((layers, TAPS * ch, channels), bf16),
                    ((channels, TAPS * ch), bf16),
                    ((2, layers * 4 * ch, tap_rows), bf16),
                ],
                after(slices, hidden),
                "turn_weights",
                held=range(4),
                held_outs=(0, 1),
                copies=layers,
            )
            beside.append(turned)
        if layer == 2:
            turned = [turned[0], to_core(after(turned[1], hidden))]
        blocks = [hidden] + [to_section(hidden, k) for k in (1, 2, 3)]
        blocks[3] = after(blocks[3], *beside)
        blocks = with_core(blocks)
        if layer < last:
            hidden, normed, full = call(
                partial(forward_kernel, dims, layer, False, layer == CONVS - 1),
                [map_out, kept_out, full_map],
                [full_map, tap_scratch, kept_out],
                [*blocks, weight, inside, facts],
                "forward",
                held_outs=(1, 2),
                loose=(9, 10),
                flops=conv_flops,
                copies=2,
            )
            kept.append(normed)
        else:
            activation, full, grad_pre, sums = call(
                partial(turn_kernel, dims, last, last == CONVS - 1),
                [map_out, full_map, map_out, sums_out],
                [full_map, tap_scratch, map_out, map_out],
                [*blocks, weight, cot, inside, facts],
                "turn",
                held=(9,),
                held_outs=(0, 1),
                loose=(10, 11),
                flops=conv_flops,
                copies=3,
            )
        fulls.append(full)

    shares = [None] * layers
    same_core = [[2 * z + c for z in range(layers)] for c in range(2)]
    for layer in range(last, -1, -1):
        *parts, share = call(
            partial(conv_back_kernel, dims, layer),
            [map_out] * 4 + [share_out],
            [
                share_out,
                full_map if layer else full_frames,
                ((2 * tap_rows, length), bf16),
                ((4 * ch, 2 * tap_rows), bf16),
            ],
            [grad_pre, to_core(grad_pre), *turned, fulls[layer], sums, facts],
            "conv_back",
            held=(2, 3, 4),
            held_outs=(4,),
            loose=(5, 6),
            flops=BACK_FLOPS,
            copies=4,
        )
        if layer < last:
            share = after(share, shares[layer + 1])
        shares[layer] = lax.all_to_all(share, "dp", 0, 0, tiled=True, axis_index_groups=same_core)
        if layer:
            held = call(
                partial(fetch_kernel, layer - 1),
                [kept_out, ((META_ROWS, channels), bf16)],
                [],
                [after(kept[layer - 1], parts), *slices],
                "fetch",
                held=range(5),
                copies=2,
            )
            blocks = spread(parts, to_section, held)
            grad_pre, sums = call(
                partial(norm_back_kernel, dims, layer - 1 == CONVS - 1),
                [map_out, sums_out],
                [],
                [*blocks, *held, inside, facts],
                "norm_back",
                loose=(6, 7),
            )
    blocks = spread(parts, to_section)
    keep, give = call(
        input_kernel,
        [((4 * ch, 2 * cells), bf16)] * 2,
        [((2 * ch, length), bf16)],
        [*blocks, activation, inside],
        "input",
        held=(4,),
        loose=(5,),
        copies=1,
    )
    maps = call(pair_kernel, [((4 * ch, 2 * cells), bf16)] * 2, [], [keep, to_core(give)], "pair")
    maps = [send(x, lambda s, z, c, n=n: (z, s ^ (2 * c + n), c)) for n, x in enumerate(maps)]
    chosen = call(
        choose_kernel,
        [share_piece] * 4,
        [((layers, 4 * slice_rows, 2 * ch), bf16)],
        shares,
        "choose",
        held=range(layers),
        copies=layers,
    )
    pick = (core * cells + np.arange(cells))[:, None] == np.arange(2 * cells)[None, :]
    activations, input_grad = call(
        maps_out_kernel,
        [((cells, channels), bf16)] * 2,
        [((channels, 2 * cells), bf16)],
        [*with_core(after(maps, chosen)), pick.astype(bf16)],
        "maps_out",
        loose=(4,),
        last=True,
    )

    pick = (core * ch + np.arange(ch))[:, None] == np.arange(2 * ch)[None, :]
    weight_grad, bias_grad, gain_grad = call(
        grads_out_kernel,
        [((TAPS, ch, channels), f32), ((1, ch), f32), ((1, ch), f32)],
        [((TAPS, channels, 2 * ch), bf16)],
        [*with_core(after(spread(chosen, to_section), activations, input_grad)), pick.astype(bf16)],
        "grads_out",
        loose=(8,),
        last=True,
    )
    weight_grad = weight_grad.reshape(3, 3, ch, channels).transpose(2, 0, 1, 3)[None]
    return (
        activations.reshape(1, 1, rows, cols, channels),
        input_grad.reshape(1, 1, rows, cols, channels),
        weight_grad,
        gain_grad,
        bias_grad,
    )


def fits_plane_plan(images, conv_weight, sections, dps):
    micro_total, images_total, rows, cols, channels = images.shape
    return (
        sections == 4
        and dps == 2 * sections
        and micro_total == sections
        and conv_weight.shape[0] == sections
        and images_total == dps
        and rows % 2 == 0
        and cols % 2 == 0
        and (rows * cols) % 64 == 0
        and channels == 512
    )


def solution(mesh):
    in_specs = (
        P(None, "dp", None, None, None),
        P(None, "dp"),
        P(),
        P("section", None, None, None, None),
        P("section", None),
        P("section", None),
        P(None, "dp", None, None, None),
    )
    out_specs = (
        P("section", "dp", None, None, None),
        P("section", "dp", None, None, None),
        P("section", "dp", None, None, None),
        P("section", "dp"),
        P("section", "dp"),
    )
    sections, dps = mesh.shape["section"], mesh.shape["dp"]

    def program(images, image_group, group_size, conv_weight, bn_gain, bn_bias, cotangent):
        plan = plane_shards if fits_plane_plan(images, conv_weight, sections, dps) else pipeline_shards
        sharded = jax.shard_map(plan, mesh=mesh, in_specs=in_specs, out_specs=out_specs, check_vma=False)
        return sharded(images, image_group, group_size, conv_weight, bn_gain, bn_bias, cotangent)

    return program
```

```python
import math
from functools import partial

import jax
import jax.numpy as jnp
import numpy as np
from jax import lax
from jax.experimental import pallas as pl
from jax.experimental.pallas import tpu as pltpu
from jax.sharding import PartitionSpec as P

CONVS = 2
BACK_FLOPS = 6000000000
INPUT_FLOPS = 4000000000


eps = 1e-05


def from_behind(x, axis, by):
    peers = lax.axis_size(axis)
    pairs = [(i, i + by) for i in range(peers) if 0 <= i + by < peers]
    return lax.ppermute(x, axis, pairs)


def canvas_mask(image_group, group_size, canvas_rows, canvas_cols):
    groups_n = group_size.shape[0]
    onehot = image_group[..., None] == jnp.arange(groups_n, dtype=jnp.int32)
    height = jnp.sum(jnp.where(onehot, group_size[:, 0], 0), axis=-1)
    breadth = jnp.sum(jnp.where(onehot, group_size[:, 1], 0), axis=-1)
    inside_rows = jnp.arange(canvas_rows, dtype=jnp.int32)[:, None] < height[..., None, None]
    inside_cols = jnp.arange(canvas_cols, dtype=jnp.int32)[None, :] < breadth[..., None, None]
    return (inside_rows & inside_cols).astype(jnp.float32)[..., None]


def window_pool(hidden):
    frames, height, breadth, channels = hidden.shape
    blocks = hidden.reshape(frames, height // 2, 2, breadth // 2, 2, channels)
    window_max = jnp.max(blocks, axis=(2, 4), keepdims=True)
    raised = jnp.exp(blocks - window_max)
    weights = raised / jnp.sum(raised, axis=(2, 4), keepdims=True)
    pooled = jnp.sum(weights * blocks, axis=(2, 4), keepdims=True)
    return (weights * pooled).reshape(frames, height, breadth, channels)


def activate(pre_act, inside, pooling):
    hidden = jax.nn.silu(pre_act) * inside
    return jnp.where(pooling, window_pool(hidden) * inside, hidden)


def conv_forward(layer_in, weight):
    return lax.conv_general_dilated(
        layer_in,
        weight,
        (1, 1),
        "SAME",
        dimension_numbers=("NHWC", "IHWO", "NHWC"),
        preferred_element_type=jnp.float32,
    )


def conv_data_back(grad_pre, weight):
    flipped = weight[:, ::-1, ::-1, :]
    return lax.conv_general_dilated(
        grad_pre,
        flipped,
        (1, 1),
        "SAME",
        dimension_numbers=("NHWC", "OHWI", "NHWC"),
        preferred_element_type=jnp.float32,
    )


def weight_back(layer_in, grad_pre):
    height = layer_in.shape[1]
    breadth = layer_in.shape[2]
    padded = jnp.pad(layer_in, ((0, 0), (1, 1), (1, 1), (0, 0)))
    pieces = []
    for tap_row in range(3):
        for tap_col in range(3):
            window = padded[:, tap_row : tap_row + height, tap_col : tap_col + breadth, :]
            pieces.append(
                jnp.einsum("nhwi,nhwo->io", window, grad_pre, preferred_element_type=jnp.float32)
            )
    return jnp.stack(pieces, axis=1).reshape(layer_in.shape[3], 3, 3, grad_pre.shape[3])


def layer_forward(layer_in, weight, gain_row, bias_row, inside, pooling):
    pre_norm = conv_forward(layer_in, weight)
    sums = lax.psum(
        (
            jnp.sum(pre_norm * inside, axis=(0, 1, 2)),
            jnp.sum(pre_norm * pre_norm * inside, axis=(0, 1, 2)),
            jnp.sum(inside),
        ),
        "dp",
    )
    pixel_total = sums[2]
    mean_val = sums[0] / pixel_total
    scale_inv = lax.rsqrt(sums[1] / pixel_total - mean_val * mean_val + eps)
    pre_act = (pre_norm - mean_val) * scale_inv * gain_row + bias_row
    hidden = activate(pre_act, inside, pooling)
    return (pre_norm, mean_val, scale_inv, pixel_total, hidden)


def layer_backward(
    grad_out,
    layer_in,
    pre_norm,
    mean_val,
    scale_inv,
    pixel_total,
    weight,
    gain_row,
    bias_row,
    inside,
    pooling,
):
    normed = (pre_norm - mean_val) * scale_inv
    pre_act = normed * gain_row + bias_row
    hidden_out, pullback = jax.vjp(partial(activate, inside=inside, pooling=pooling), pre_act)
    grad_act = pullback(grad_out)[0]
    sums = lax.psum(
        (jnp.sum(grad_act, axis=(0, 1, 2)), jnp.sum(grad_act * normed, axis=(0, 1, 2))), "dp"
    )
    shift_term = sums[0] / pixel_total
    slope_term = sums[1] / pixel_total
    grad_pre = (
        inside * scale_inv * gain_row * (grad_act - shift_term - normed * slope_term)
    ).astype(jnp.bfloat16)
    weight_term = weight_back(layer_in, grad_pre)
    grad_in = conv_data_back(grad_pre, weight).astype(jnp.bfloat16)
    return (grad_in, weight_term, sums[1], sums[0])


def pipeline_shards(images, image_group, group_size, conv_weight, bn_gain, bn_bias, cotangent):
    section_index = lax.axis_index("section")
    sections = lax.axis_size("section")
    micro_total = images.shape[0]
    channels = conv_weight.shape[1]
    inside_all = canvas_mask(image_group, group_size, images.shape[2], images.shape[3])
    ticks = micro_total + sections - 1
    weight = conv_weight[0]
    gain_row = bn_gain[0]
    bias_row = bn_bias[0]
    pool_here = section_index == CONVS - 1
    received = jnp.zeros(images.shape[1:], jnp.bfloat16)
    kept_in, kept_pre, kept_mean, kept_scale, kept_total, finished = ([], [], [], [], [], [])
    for tick in range(ticks):
        micro_pos = jnp.clip(tick - section_index, 0, micro_total - 1)
        inside = inside_all[micro_pos]
        fresh = (images[micro_pos].astype(jnp.float32) * inside).astype(jnp.bfloat16)
        layer_in = jnp.where(section_index == 0, fresh, received)
        pre_norm, mean_val, scale_inv, pixel_total, hidden = layer_forward(
            layer_in, weight, gain_row, bias_row, inside, pool_here
        )
        sent = hidden.astype(jnp.bfloat16)
        if tick < ticks - 1:
            received = from_behind(sent, "section", 1)
        kept_in.append(layer_in)
        kept_pre.append(pre_norm)
        kept_mean.append(mean_val)
        kept_scale.append(scale_inv)
        kept_total.append(pixel_total)
        finished.append(sent)
    stack_in = jnp.stack(kept_in)
    stack_pre = jnp.stack(kept_pre)
    stack_mean = jnp.stack(kept_mean)
    stack_scale = jnp.stack(kept_scale)
    stack_total = jnp.stack(kept_total)
    returned = jnp.zeros(images.shape[1:], jnp.bfloat16)
    weight_sum = jnp.zeros(conv_weight.shape[1:], jnp.float32)
    gain_sum = jnp.zeros((channels,), jnp.float32)
    bias_sum = jnp.zeros((channels,), jnp.float32)
    input_list = []
    for tick in range(ticks):
        micro_raw = tick - (sections - 1 - section_index)
        valid = ((micro_raw >= 0) & (micro_raw < micro_total)).astype(jnp.float32)
        micro_pos = jnp.clip(micro_raw, 0, micro_total - 1)
        forward_tick = jnp.clip(micro_pos + section_index, 0, ticks - 1)
        inside = inside_all[micro_pos]
        grad_out = jnp.where(
            section_index == sections - 1,
            cotangent[micro_pos].astype(jnp.float32),
            returned.astype(jnp.float32),
        )
        grad_in, weight_term, gain_term, bias_term = layer_backward(
            grad_out,
            stack_in[forward_tick],
            stack_pre[forward_tick],
            stack_mean[forward_tick],
            stack_scale[forward_tick],
            stack_total[forward_tick],
            weight,
            gain_row,
            bias_row,
            inside,
            pool_here,
        )
        weight_sum = weight_sum + valid * weight_term
        gain_sum = gain_sum + valid * gain_term
        bias_sum = bias_sum + valid * bias_term
        if tick < ticks - 1:
            returned = from_behind(grad_in, "section", -1)
        input_list.append((grad_in.astype(jnp.float32) * inside).astype(jnp.bfloat16))
    out_stack = jnp.stack(finished[sections - 1 :], axis=0)
    grad_stack = jnp.stack(input_list[sections - 1 :], axis=0)
    out_back, grad_back = (
        lax.all_to_all(out_stack, "section", split_axis=0, concat_axis=1, tiled=True),
        lax.all_to_all(grad_stack, "section", split_axis=0, concat_axis=1, tiled=True),
    )
    activations = out_back[:, sections - 1 : sections]
    input_grad = grad_back[:, 0:1]
    weight_grad = lax.psum_scatter(weight_sum[None], "dp", scatter_dimension=1, tiled=True)
    share = channels // lax.axis_size("dp")
    gain_grad = lax.dynamic_slice_in_dim(gain_sum, lax.axis_index("dp") * share, share)[None]
    bias_grad = lax.dynamic_slice_in_dim(bias_sum, lax.axis_index("dp") * share, share)[None]
    return (activations, input_grad, weight_grad, gain_grad, bias_grad)


AXES = ("section", "dp")
TAPS = 9
VMEM_LIMIT = 24 * 1024 * 1024
META_ROWS = 16
LANES = 128
ROW_AT, COL_AT, FRAME_AT = 6, 7, 8
NT = (((1,), (1,)), ((), ()))


def place():
    dp_index = lax.axis_index("dp")
    return lax.axis_index("section"), dp_index // 2, dp_index % 2


def peer_order():
    return [(k, j) for j in range(2) for k in range(4)]


def slice_at(section, core, k, j):
    return (core ^ j) * lax.axis_size("section") + (section ^ k)


def send(x, target):
    sections = lax.axis_size("section")
    dps = lax.axis_size("dp")
    pairs = []
    for s in range(sections):
        for d in range(dps):
            ts, tz, tc = target(s, d // 2, d % 2)
            pairs.append((s * dps + d, ts * dps + tz * 2 + tc))
    return lax.ppermute(x, AXES, pairs)


def to_section(x, k):
    return send(x, lambda s, z, c: (s ^ k, z, c))


def to_plane(x, k):
    return send(x, lambda s, z, c: (s, z ^ k, c))


def to_core(x):
    return send(x, lambda s, z, c: (s, z, c ^ 1))


def spread(blocks, move, *beside):
    moved = lax.optimization_barrier(([move(blocks[k], k) for k in (1, 2, 3)], beside))[0]
    return [blocks[0]] + moved


def with_core(blocks):
    return blocks + [to_core(x) for x in blocks]


def after(x, *first):
    return lax.optimization_barrier((x, first))[0]


def grid_facts(frames, rows, cols):
    at = np.arange(frames * rows * cols)
    col = at % cols
    row = (at // cols) % rows
    facts = [row > 0, row < rows - 1, col > 0, col < cols - 1, col % 2 == 0, row % 2 == 0, row, col]
    facts = facts + [at // (rows * cols) == frame for frame in range(frames)]
    return jnp.asarray(np.stack(facts).astype(np.float32))


def shift(x, by):
    length = x.shape[1]
    return pltpu.roll(x, (-by) % length, 1) if by % length else x


def row_ok(facts, d):
    return facts[0:1, :] if d < 0 else facts[1:2, :]


def col_ok(facts, d):
    return facts[2:3, :] if d < 0 else facts[3:4, :]


def sum_taps(taps_ref, facts, cols):
    ch = taps_ref.shape[0] // TAPS
    total = None
    for dx in (-1, 0, 1):
        column = None
        for dy in (-1, 0, 1):
            tap = (dy + 1) * 3 + dx + 1
            piece = taps_ref[tap * ch : (tap + 1) * ch, :]
            if dy:
                piece = shift(piece, dy * cols) * row_ok(facts, dy)
            column = piece if column is None else column + piece
        if dx:
            column = shift(column, dx) * col_ok(facts, dx)
        total = column if total is None else total + column
    return total


def spread_taps(grad, moved_ref, base, facts, cols):
    ch = grad.shape[0]
    facts = facts[:4, :].astype(grad.dtype)
    for dx in (-1, 0, 1):
        column = shift(grad, -dx) * col_ok(facts, -dx) if dx else grad
        for dy in (-1, 0, 1):
            piece = shift(column, -dy * cols) * row_ok(facts, -dy) if dy else column
            at = base + ((dy + 1) * 3 + dx + 1) * ch
            moved_ref[at : at + ch, :] = piece


def corner_sum(x, cols):
    x = x + shift(x, 1)
    return x + shift(x, cols)


def from_corner(x, facts, cols):
    x = jnp.where(facts[4:5, :] > 0.5, x, shift(x, -1))
    return jnp.where(facts[5:6, :] > 0.5, x, shift(x, -cols))


def lane_sum(x):
    return jnp.sum(x, axis=1, keepdims=True)


def normalise(pre, inside):
    count = lane_sum(inside)
    mean = lane_sum(pre * inside) / count
    square = lane_sum(pre * pre * inside) / count
    scale = lax.rsqrt(square - mean * mean + eps)
    return (pre - mean) * scale, scale


def hidden_of(normed, gain, bias, inside, facts, cols, pooling):
    pre_act = normed * gain + bias
    hidden = pre_act * jax.nn.sigmoid(pre_act) * inside
    if pooling:
        raised = jnp.exp(hidden)
        total = corner_sum(raised, cols)
        pooled = corner_sum(raised * hidden, cols) / total
        hidden = raised * from_corner(pooled / total, facts, cols) * inside
    return hidden


def norm_back(grad, normed, scale, gain, bias, inside, facts, cols, pooling):
    pre_act = normed * gain + bias
    gate = jax.nn.sigmoid(pre_act)
    if pooling:
        hidden = pre_act * gate * inside
        raised = jnp.exp(hidden)
        out = grad * inside
        total = 1.0 / corner_sum(raised, cols)
        pooled = corner_sum(raised * hidden, cols) * total
        d_pooled = corner_sum(raised * out, cols) * total
        by_out = from_corner(pooled * total, facts, cols)
        by_hidden = from_corner(d_pooled * total, facts, cols)
        rest = from_corner(d_pooled * total * (1.0 - 2.0 * pooled), facts, cols)
        grad = raised * (out * by_out + hidden * by_hidden + rest)
    grad_act = grad * inside * gate * (1.0 + pre_act * (1.0 - gate))
    count = lane_sum(inside)
    shift_sum = lane_sum(grad_act)
    slope_sum = lane_sum(grad_act * normed)
    grad_pre = inside * (scale * gain) * (grad_act - shift_sum / count - normed * (slope_sum / count))
    return grad_pre.astype(jnp.bfloat16), shift_sum, slope_sum


def assemble(blocks, full_ref):
    section, _, core = place()
    ch = blocks[0].shape[0]
    for (k, j), block in zip(peer_order(), blocks):
        at = pl.multiple_of(slice_at(section, core, k, j) * ch, ch)
        full_ref[pl.ds(at, ch), :] = block[...]


def assemble_frames(blocks, full_ref, rows, lanes):
    _, plane, core = place()
    size = rows.stop - rows.start
    for (k, j), block in zip(peer_order(), blocks):
        frame = (plane ^ k) * 2 + (core ^ j)
        full_ref[pl.ds(pl.multiple_of(frame * size, size), size), :] = block[rows, lanes]


def start_all(copies):
    for copy in copies:
        copy.start()
    return copies


def wait_all(copies):
    for copy in copies:
        copy.wait()


def tap_products(weight, full_ref, taps_ref, by_cells):
    length = taps_ref.shape[1]
    step = 512 if length % 512 == 0 else length
    for at in range(0, length, step):
        if by_cells:
            taps_ref[:, at : at + step] = lax.dot_general(
                weight, full_ref[at : at + step, :], NT, preferred_element_type=jnp.float32
            )
        else:
            taps_ref[:, at : at + step] = jnp.dot(
                weight, full_ref[:, at : at + step], preferred_element_type=jnp.float32
            )


def pick_layer(layer, sources, start, target, sem):
    section, _, _ = place()
    rows = pl.ds(start, target.shape[0])
    for k, source in enumerate(sources):

        @pl.when((section ^ layer) == k)
        def _():
            pltpu.make_async_copy(source.at[rows], target, sem).start()

    return pltpu.make_async_copy(sources[0].at[rows], target, sem)


def affine(meta, ch):
    parts = meta[:, :LANES].astype(jnp.float32).T[:ch]
    return (
        parts[:, 0:1] + parts[:, 1:2] + parts[:, 2:3],
        parts[:, 3:4] + parts[:, 4:5] + parts[:, 5:6],
    )


def plane_inside(metas, facts):
    frames = metas.shape[0] // META_ROWS
    extents = []
    for line in (0, 1):
        total = None
        for f in range(frames):
            at = f * META_ROWS + line
            extent = metas[at : at + 1, 0:1].astype(jnp.float32) * facts[FRAME_AT + f : FRAME_AT + f + 1, :]
            total = extent if total is None else total + extent
        extents.append(total)
    on = (facts[ROW_AT : ROW_AT + 1, :] < extents[0]) & (facts[COL_AT : COL_AT + 1, :] < extents[1])
    return jnp.where(on, 1.0, 0.0)


def frames_kernel(dims, group_table, size_table, images, cots, *refs):
    payloads, (image_in, cot_in, groups, sizes, sems) = refs[:4], refs[4:]
    copies = start_all(
        [
            pltpu.make_async_copy(group_table, groups, sems.at[0]),
            pltpu.make_async_copy(size_table, sizes, sems.at[1]),
            pltpu.make_async_copy(images, image_in, sems.at[2]),
            pltpu.make_async_copy(cots, cot_in, sems.at[3]),
        ]
    )
    section, plane, _ = place()
    rows, cols = dims
    cells = rows * cols
    at = lax.broadcasted_iota(jnp.int32, (cells, LANES), 0).astype(jnp.float32)
    row = jnp.floor((at + 0.5) * (1.0 / cols))
    col = at - row * cols
    channels = images.shape[2]
    half = channels // 2
    wait_all(copies)
    for k in range(4):
        micro = plane ^ k
        group = groups[0, micro]
        height = sizes[0, 0]
        breadth = sizes[1, 0]
        for g in range(1, sizes.shape[1]):
            height = jnp.where(group == g, sizes[0, g], height)
            breadth = jnp.where(group == g, sizes[1, g], breadth)
        height = height.astype(jnp.float32)
        breadth = breadth.astype(jnp.float32)
        on = jnp.where((row < height) & (col < breadth), 1.0, 0.0)
        image = image_in[micro]
        for c in range(0, channels, LANES):
            piece = image[:, c : c + LANES].astype(jnp.float32) * on
            payloads[k][:cells, c : c + LANES] = piece.astype(jnp.bfloat16)
        line = lax.broadcasted_iota(jnp.int32, (META_ROWS, channels + LANES), 0)
        payloads[k][cells:, :] = jnp.where(line == 0, height, breadth).astype(jnp.bfloat16)
        tile = section // 2 * LANES
        low = cot_in[micro, :, pl.ds(pl.multiple_of(tile, LANES), LANES)].astype(jnp.float32)
        high = cot_in[micro, :, pl.ds(pl.multiple_of(half + tile, LANES), LANES)].astype(jnp.float32)
        odd = section % 2 == 1
        low = jnp.where(odd, pltpu.roll(low, LANES // 2, 1), low)
        high = jnp.where(odd, high, pltpu.roll(high, LANES // 2, 1))
        lane = lax.broadcasted_iota(jnp.int32, (cells, LANES), 1)
        both = jnp.where(lane < LANES // 2, low, high).astype(jnp.bfloat16)
        payloads[k][:cells, channels:] = both


def pack_kernel(gain, bias, weight, *refs):
    outs, (own, columns, turned, tables, sems) = refs[:4], refs[4:]
    section, _, core = place()
    width = columns.shape[2]
    ch = width // 4
    start = pl.multiple_of(core * width, width)
    copies = start_all(
        [
            pltpu.make_async_copy(weight.at[tap, :, pl.ds(start, width)], columns.at[tap], sems.at[tap])
            for tap in range(TAPS)
        ]
    )
    table_copies = start_all(
        [
            pltpu.make_async_copy(gain, tables.at[0], sems.at[TAPS]),
            pltpu.make_async_copy(bias, tables.at[1], sems.at[TAPS + 1]),
        ]
    )
    wait_all(table_copies)
    targets = [own, *outs[1:]]
    for k, out in enumerate(targets):
        lines = []
        tile = pl.multiple_of(start + (section ^ k) // 2 * LANES, LANES)
        odd = (section ^ k) % 2 == 1
        for m in range(2):
            line = tables[m, :, pl.ds(tile, LANES)]
            line = jnp.where(odd, pltpu.roll(line, ch, 1), line)
            for _ in range(3):
                part = line.astype(jnp.bfloat16).astype(jnp.float32)
                lines.append(part)
                line = line - part
        lines.append(jnp.zeros((META_ROWS - len(lines), LANES), jnp.float32))
        out[TAPS * ch :, :] = jnp.zeros((META_ROWS, out.shape[1]), jnp.bfloat16)
        out[TAPS * ch :, :LANES] = jnp.concatenate(lines, axis=0).astype(jnp.bfloat16)
    tail = pl.ds(TAPS * ch, META_ROWS)
    own_copies = start_all([pltpu.make_async_copy(own.at[tail], outs[0].at[tail], sems.at[2 * TAPS + 2])])
    for tap in range(TAPS):
        copies[tap].wait()
        turned[...] = columns[tap].T
        for k, out in enumerate(targets):
            rows = pl.ds(pl.multiple_of((section ^ k) * ch, ch), ch)
            out[tap * ch : (tap + 1) * ch, :] = turned[rows, :]
        piece = pl.ds(tap * ch, ch)
        own_copies += start_all(
            [pltpu.make_async_copy(own.at[piece], outs[0].at[piece], sems.at[TAPS + 2 + tap])]
        )
    wait_all(own_copies)


def pick_kernel(layer, *refs):
    sources, others, out, targets, sems = refs[:4], refs[4:-2], refs[-2], (), refs[-1]
    if len(others) > 0:
        others, out, targets = refs[4:5], refs[5], refs[6:7]
    copies = [pick_layer(layer, sources, 0, out, sems.at[0])]
    for other, target in zip(others, targets):
        copies += start_all([pltpu.make_async_copy(other, target, sems.at[1])])
    wait_all(copies)


def forward_kernel(dims, layer, first, pooling, *refs):
    blocks, weights, rest = refs[:8], refs[8 : 12 if first else 9], refs[12 if first else 9 :]
    rows, cols = dims
    cells = rows * cols
    if first:
        facts, pick, hidden, kept, full_out, inside_out, cot_out, full, taps, stage, weight, metas, *rest = rest
        cot_full, cot, sems = rest
        copy = pick_layer(layer, weights, 0, weight, sems.at[2])
    else:
        inside, facts, hidden, kept, full_out, full, taps, stage, sems = rest
        (weight,) = weights
    facts_now = facts[...]
    if first:
        channels = full.shape[1]
        assemble_frames(blocks, full, slice(0, cells), slice(0, channels))
    else:
        assemble(blocks, full)
    full_copy = pltpu.make_async_copy(full, full_out, sems.at[0])
    full_copy.start()
    if first:
        assemble_frames(blocks, metas, slice(cells, cells + META_ROWS), slice(0, channels))
        assemble_frames(blocks, cot_full, slice(0, cells), slice(channels, channels + LANES))
        inside_now = plane_inside(metas, facts_now)
        inside_out[...] = inside_now
        copy.wait()
    else:
        inside_now = inside[...]
    ch = hidden.shape[0]
    tap_products(weight[: TAPS * ch, :], full, taps, first)
    if first:
        cot[...] = lax.dot_general(
            pick[...], cot_full[...], NT, preferred_element_type=jnp.float32
        ).astype(jnp.bfloat16)
        cot_copy = pltpu.make_async_copy(cot, cot_out, sems.at[3])
        cot_copy.start()
    pre = sum_taps(taps, facts_now, cols)
    normed, scale = normalise(pre, inside_now)
    length = normed.shape[1]
    stage[:, :length] = normed
    stage[:, length:] = jnp.broadcast_to(scale, (ch, LANES))
    kept_copy = pltpu.make_async_copy(stage, kept, sems.at[1])
    kept_copy.start()
    gain, bias = affine(weight[TAPS * ch :, :], ch)
    hidden[...] = hidden_of(normed, gain, bias, inside_now, facts_now, cols, pooling).astype(jnp.bfloat16)
    if first:
        cot_copy.wait()
    full_copy.wait()
    kept_copy.wait()


def turn_kernel(dims, layer, pooling, *refs):
    blocks, (weight, cot_in, inside, facts) = refs[:8], refs[8:12]
    hidden_out, full_out, grad_pre, sums, full, taps, cot, hidden, sems = refs[12:]
    cols = dims[1]
    cot_copy = pltpu.make_async_copy(cot_in, cot, sems.at[0])
    cot_copy.start()
    assemble(blocks, full)
    full_copy = pltpu.make_async_copy(full, full_out, sems.at[1])
    full_copy.start()
    ch = grad_pre.shape[0]
    tap_products(weight[: TAPS * ch, :], full, taps, False)
    facts_now, inside_now = facts[...], inside[...]
    pre = sum_taps(taps, facts_now, cols)
    normed, scale = normalise(pre, inside_now)
    gain, bias = affine(weight[TAPS * ch :, :], ch)
    hidden[...] = hidden_of(normed, gain, bias, inside_now, facts_now, cols, pooling).astype(jnp.bfloat16)
    hidden_copy = pltpu.make_async_copy(hidden, hidden_out, sems.at[2])
    hidden_copy.start()
    cot_copy.wait()
    grad_pre[...], shift_sum, slope_sum = norm_back(
        cot[...].astype(jnp.float32), normed, scale, gain, bias, inside_now, facts_now, cols, pooling
    )
    keep_sums(sums, shift_sum, slope_sum)
    full_copy.wait()
    hidden_copy.wait()


def keep_sums(sums, shift_sum, slope_sum):
    ch = shift_sum.shape[0]
    sums[:, :LANES] = jnp.broadcast_to(shift_sum, (ch, LANES))
    sums[:, LANES:] = jnp.broadcast_to(slope_sum, (ch, LANES))


def add_blocks(blocks):
    total = blocks[0][...].astype(jnp.float32)
    for block in blocks[1:]:
        total = total + block[...].astype(jnp.float32)
    return total


def fetch_kernel(layer, kept, *refs):
    sources, (kept_out, meta_out, sems) = refs[:4], refs[4:]
    copy = pltpu.make_async_copy(kept, kept_out, sems.at[0])
    copy.start()
    start = sources[0].shape[0] - META_ROWS
    pick_layer(layer, sources, start, meta_out, sems.at[1]).wait()
    copy.wait()


def norm_back_kernel(dims, pooling, *refs):
    blocks, (kept, meta, inside, facts, grad_pre, sums) = refs[:4], refs[4:]
    ch, length = grad_pre.shape
    grad = add_blocks(blocks).astype(jnp.bfloat16).astype(jnp.float32)
    gain, bias = affine(meta[...], ch)
    grad_pre[...], shift_sum, slope_sum = norm_back(
        grad,
        kept[:, :length],
        kept[:, length : length + 1],
        gain,
        bias,
        inside[...],
        facts[...],
        dims[1],
        pooling,
    )
    keep_sums(sums, shift_sum, slope_sum)


def weight_product(moved, full, first):
    if first:
        return jnp.dot(moved, full, preferred_element_type=jnp.float32)
    return lax.dot_general(moved, full, NT, preferred_element_type=jnp.float32)


def sums_rows(sums, ch, width):
    lines = []
    for at in (0, LANES):
        turned = sums[:, at : at + LANES].T
        lines.append(jnp.concatenate([turned, jnp.zeros((LANES, width - ch), jnp.float32)], axis=1)[0:1])
    lines.append(jnp.zeros((META_ROWS - 2, width), jnp.float32))
    return jnp.concatenate(lines, axis=0).astype(jnp.bfloat16)


def store_share(value, sums, pieces):
    rows = value.shape[0]
    width = pieces[0].shape[1]
    for n, piece in enumerate(pieces):
        piece[:rows, :] = value[:, n * width : (n + 1) * width].astype(jnp.bfloat16)
        piece[rows:, :] = sums_rows(sums, rows // TAPS, width)


def form_share(layer, moved, full, sums, product):
    piece = product.shape[0] // 4
    value = weight_product(moved[: piece - META_ROWS, :], full[...], layer == 0)
    store_share(value, sums, [product.at[pl.ds(n * piece, piece)] for n in range(4)])


def conv_back_kernel(dims, layer, own, other, own_weights, other_weights, full_in, sums, facts, *refs):
    *outs, share, product, full, moved, weights, sems = refs
    ch = own.shape[0]
    size = moved.shape[0] // 2
    rows = pl.ds(layer * 4 * ch, 4 * ch)
    copies = start_all(
        [
            pltpu.make_async_copy(own_weights.at[rows], weights.at[:, pl.ds(0, size)], sems.at[0]),
            pltpu.make_async_copy(other_weights.at[rows], weights.at[:, pl.ds(size, size)], sems.at[1]),
        ]
    )
    full_copy = pltpu.make_async_copy(full_in, full, sems.at[2])
    full_copy.start()
    facts_now = facts[...]
    spread_taps(own[...], moved, 0, facts_now, dims[1])
    full_copy.wait()
    form_share(layer, moved, full, sums, product)
    share_copy = pltpu.make_async_copy(product, share, sems.at[3])
    share_copy.start()
    spread_taps(other[...], moved, size, facts_now, dims[1])
    for n in range(2):
        moved[n * size + TAPS * ch : (n + 1) * size, :] = jnp.zeros(
            (size - TAPS * ch, moved.shape[1]), jnp.bfloat16
        )
    wait_all(copies)
    value = jnp.dot(weights[...], moved[...], preferred_element_type=jnp.float32)
    for k, out in enumerate(outs):
        out[...] = value[k * ch : (k + 1) * ch, :].astype(jnp.bfloat16)
    share_copy.wait()


def fold_kernel(*refs):
    count = (len(refs) - 2) // 2
    shares, outs, (blocks, sems) = refs[:count], refs[count:-2], refs[-2:]
    rows = outs[0].shape[0]
    copies = start_all(
        [pltpu.make_async_copy(share, blocks.at[n], sems.at[n]) for n, share in enumerate(shares)]
    )
    for n, copy in enumerate(copies):
        copy.wait()
        value = add_blocks([blocks.at[n, pl.ds(m * rows, rows)] for m in range(blocks.shape[1] // rows)])
        outs[n][...] = value.astype(jnp.bfloat16)


def choose_kernel(*refs):
    last, others, outs = refs[0], refs[1:-4], refs[-4:]
    section, _, _ = place()
    rows = outs[0].shape[0]
    value = add_blocks([last.at[pl.ds(n * rows, rows)] for n in range(last.shape[0] // rows)])
    value = value.astype(jnp.bfloat16)
    for k, out in enumerate(outs):

        @pl.when((section ^ k) == 0)
        def _():
            out[...] = value

        for layer, other in enumerate(others, 1):

            @pl.when((section ^ k) == layer)
            def _():
                out[...] = other[...]


def turn_weights_kernel(layers, *refs):
    sources, outs, (full, turned, stage, sems) = refs[:4], refs[4:6], refs[6:]
    section, _, core = place()
    rows, channels = full.shape[1:]
    half = channels // 2
    ch = half // 4
    copies = [pick_layer(n, sources, 0, full.at[n], sems.at[n]) for n in range(layers)]
    stage[:, :, rows:] = jnp.zeros((*stage.shape[:2], stage.shape[2] - rows), jnp.bfloat16)
    for n in range(layers):
        copies[n].wait()
        turned[...] = full[n].T
        for j in range(2):
            for k in range(4):
                at = pl.multiple_of((core ^ j) * half + (section ^ k) * ch, ch)
                stage[j, n * half + k * ch : n * half + (k + 1) * ch, :rows] = turned[pl.ds(at, ch), :]
    wait_all(
        start_all([pltpu.make_async_copy(stage.at[j], outs[j], sems.at[j]) for j in range(2)])
    )


def input_kernel(*refs):
    blocks, (hidden, inside, keep, give, full, sems) = refs[:4], refs[4:]
    section, _, core = place()
    ch = hidden.shape[0]
    copy = pltpu.make_async_copy(hidden, full.at[pl.ds(0, ch)], sems.at[0])
    copy.start()
    full[ch:, :] = (add_blocks(blocks) * inside[...]).astype(jnp.bfloat16)
    copy.wait()
    rows = 2 * ch
    width = keep.shape[1]
    for j, out in enumerate((keep, give)):
        for n in range(2):
            at = pl.multiple_of((section ^ (2 * (core ^ j) + n)) * width, width)
            out[n * rows : (n + 1) * rows, :] = full[:, pl.ds(at, width)]


def pair_kernel(keep, got, *outs):
    rows = keep.shape[0] // 2
    for n, out in enumerate(outs):
        out[:rows, :] = keep[n * rows : (n + 1) * rows, :]
        out[rows:, :] = got[n * rows : (n + 1) * rows, :]


def maps_out_kernel(*refs):
    blocks, pick, outs, full = refs[:4], refs[4], refs[5:7], refs[7]
    _, plane, core = place()
    ch = blocks[0].shape[0] // 4
    for m, out in enumerate(outs):
        for j in range(2):
            for n in range(2):
                for h in range(2):
                    slot = slice_at(plane ^ (2 * (core ^ j) + n), core ^ j, 0, h)
                    at = pl.multiple_of(slot * ch, ch)
                    start = (2 * h + m) * ch
                    full[pl.ds(at, ch), :] = blocks[2 * j + n][start : start + ch, :]
        mine = lax.dot_general(pick[...], full[...], NT, preferred_element_type=jnp.float32)
        out[...] = mine.astype(out.dtype)


def grads_out_kernel(*refs):
    blocks, pick, (weight_out, shift_out, slope_out), (full,) = refs[:8], refs[8], refs[9:12], refs[12:]
    section, plane, core = place()
    taps, rows, channels = weight_out.shape
    for tap in range(taps):
        for (k, j), block in zip(peer_order(), blocks):
            at = pl.multiple_of(slice_at(section, core, k, j) * rows, rows)
            full[tap, pl.ds(at, rows), :] = block[tap * rows : (tap + 1) * rows, :]
        weight_out[tap] = lax.dot_general(pick[...], full[tap], NT, preferred_element_type=jnp.float32)
    shift_row = jnp.zeros((1, rows), jnp.float32)
    slope_row = jnp.zeros((1, rows), jnp.float32)
    slot = plane * 2 + core
    for (k, j), block in zip(peer_order(), blocks):
        tail = block[taps * rows :, :].astype(jnp.float32)
        mine = slice_at(section, core, k, j) == slot
        shift_row = shift_row + jnp.where(mine, tail[0:1, :rows], 0.0)
        slope_row = slope_row + jnp.where(mine, tail[1:2, :rows], 0.0)
    shift_out[...] = shift_row
    slope_out[...] = slope_row


def call(kernel, outs, scratch, args, name, held=(), held_outs=(), loose=(), last=False, flops=0, copies=None):
    shapes = [
        (jax.ShapeDtypeStruct if last else pltpu.HBM if n in held_outs else pltpu.VMEM)(shape, dtype)
        for n, (shape, dtype) in enumerate(outs)
    ]
    moved = sum(a.size * a.dtype.itemsize for a in args)
    moved += sum(math.prod(shape) * jnp.dtype(dtype).itemsize for shape, dtype in outs)
    spaces = [pltpu.HBM if n in held else pltpu.VMEM for n in range(len(args))]
    out_spaces = [pltpu.HBM if n in held_outs else pltpu.VMEM for n in range(len(outs))]
    args = [
        a if n in loose else pltpu.with_memory_space_constraint(a, space)
        for n, (a, space) in enumerate(zip(args, spaces))
    ]
    scratch_shapes = [
        pltpu.SMEM(shape, dtype) if dtype == jnp.int32 else pltpu.VMEM(shape, dtype) for shape, dtype in scratch
    ]
    if copies is not None:
        scratch_shapes.append(pltpu.SemaphoreType.DMA((copies,)))
    return pl.pallas_call(
        kernel,
        out_shape=shapes,
        in_specs=[pl.BlockSpec(memory_space=space) for space in spaces],
        out_specs=[pl.BlockSpec(memory_space=space) for space in out_spaces],
        scratch_shapes=scratch_shapes,
        compiler_params=pltpu.CompilerParams(vmem_limit_bytes=VMEM_LIMIT),
        cost_estimate=pl.CostEstimate(flops=flops, bytes_accessed=moved, transcendentals=0),
        name=name,
    )(*args)


def plane_shards(images, image_group, group_size, conv_weight, bn_gain, bn_bias, cotangent):
    _, _, core = place()
    micro_total, _, rows, cols, channels = images.shape
    layers = lax.axis_size("section")
    last = layers - 1
    cells = rows * cols
    frames = 2 * micro_total
    length = frames * cells
    ch = channels // 8
    dims = (rows, cols)
    bf16, f32 = jnp.bfloat16, jnp.float32
    facts = grid_facts(frames, rows, cols)
    conv_flops = 2 * TAPS * ch * channels * length
    slice_rows = TAPS * ch + META_ROWS
    tap_rows = -(-TAPS * ch // LANES) * LANES

    full_map = ((channels, length), bf16)
    full_frames = ((length, channels), bf16)
    tap_scratch = ((TAPS * ch, length), f32)
    weight_slice = ((slice_rows, channels), bf16)
    map_out = ((ch, length), bf16)
    sums_out = ((ch, 2 * LANES), f32)
    kept_out = ((ch, length + LANES), f32)
    share_out = ((4 * slice_rows, 2 * ch), bf16)
    share_piece = ((slice_rows, 2 * ch), bf16)

    taps_first = conv_weight[0].transpose(1, 2, 0, 3).reshape(TAPS, channels, channels)
    packed = call(
        pack_kernel,
        [weight_slice] * 4,
        [
            weight_slice,
            ((TAPS, channels, 4 * ch), bf16),
            ((4 * ch, channels), bf16),
            ((2, 1, channels), f32),
        ],
        [bn_gain, bn_bias, taps_first],
        "weight_pack",
        held=range(3),
        held_outs=(0,),
        copies=2 * TAPS + 3,
    )
    slices = spread(packed, to_section)

    payload = ((cells + META_ROWS, channels + LANES), bf16)
    sent = call(
        partial(frames_kernel, dims),
        [payload] * 4,
        [((micro_total, cells, channels), bf16)] * 2
        + [(image_group.shape[::-1], jnp.int32), (group_size.shape[::-1], jnp.int32)],
        [
            image_group.T,
            group_size.T,
            after(images.reshape(micro_total, cells, channels), packed),
            cotangent.reshape(micro_total, cells, channels),
        ],
        "frames",
        held=range(4),
        copies=4,
    )
    frames_in = with_core(spread(sent, to_plane))

    half = (core * ch + np.arange(ch))[:, None] == np.arange(2 * ch)[None, :]
    hidden, normed, full, inside, cot = call(
        partial(forward_kernel, dims, 0, True, CONVS == 1),
        [map_out, kept_out, full_frames, ((1, length), f32), map_out],
        [
            full_frames,
            tap_scratch,
            kept_out,
            weight_slice,
            ((frames * META_ROWS, channels), bf16),
            ((length, LANES), bf16),
            map_out,
        ],
        [*frames_in, *slices, facts, half.astype(bf16)],
        "forward",
        held=range(8, 12),
        held_outs=(1, 2, 4),
        loose=(12, 13),
        flops=conv_flops,
        copies=4,
    )
    kept, fulls = [normed], [full]
    for layer in range(1, layers):
        stored = [turned[1]] if layer == last else []
        weight, *stored = call(
            partial(pick_kernel, layer),
            [weight_slice] + [((layers * 4 * ch, tap_rows), bf16)] * len(stored),
            [],
            [*after(slices, hidden), *after(stored, hidden)],
            "pick",
            held=range(4),
            held_outs=(1,),
            loose=(4,),
            copies=2,
        )
        if stored:
            turned[1] = stored[0]
        beside = [weight]
        if layer == 1:
            turned = call(
                partial(turn_weights_kernel, layers),
                [((layers * 4 * ch, tap_rows), bf16)] * 2,
                [
                    ((layers, TAPS * ch, channels), bf16),
                    ((channels, TAPS * ch), bf16),
                    ((2, layers * 4 * ch, tap_rows), bf16),
                ],
                after(slices, hidden),
                "turn_weights",
                held=range(4),
                held_outs=(0, 1),
                copies=layers,
            )
            beside.append(turned)
        if layer == 2:
            turned = [turned[0], to_core(after(turned[1], hidden))]
        blocks = [hidden] + [to_section(hidden, k) for k in (1, 2, 3)]
        blocks[3] = after(blocks[3], *beside)
        blocks = with_core(blocks)
        if layer < last:
            hidden, normed, full = call(
                partial(forward_kernel, dims, layer, False, layer == CONVS - 1),
                [map_out, kept_out, full_map],
                [full_map, tap_scratch, kept_out],
                [*blocks, weight, inside, facts],
                "forward",
                held_outs=(1, 2),
                loose=(9, 10),
                flops=conv_flops,
                copies=2,
            )
            kept.append(normed)
        else:
            activation, full, grad_pre, sums = call(
                partial(turn_kernel, dims, last, last == CONVS - 1),
                [map_out, full_map, map_out, sums_out],
                [full_map, tap_scratch, map_out, map_out],
                [*blocks, weight, cot, inside, facts],
                "turn",
                held=(9,),
                held_outs=(0, 1),
                loose=(10, 11),
                flops=conv_flops,
                copies=3,
            )
        fulls.append(full)

    shares = [None] * layers
    same_core = [[2 * z + c for z in range(layers)] for c in range(2)]
    for layer in range(last, -1, -1):
        *parts, share = call(
            partial(conv_back_kernel, dims, layer),
            [map_out] * 4 + [share_out],
            [
                share_out,
                full_map if layer else full_frames,
                ((2 * tap_rows, length), bf16),
                ((4 * ch, 2 * tap_rows), bf16),
            ],
            [grad_pre, to_core(grad_pre), *turned, fulls[layer], sums, facts],
            "conv_back",
            held=(2, 3, 4),
            held_outs=(4,),
            loose=(5, 6),
            flops=BACK_FLOPS,
            copies=4,
        )
        if layer < last:
            share = after(share, shares[layer + 1])
        shares[layer] = lax.all_to_all(share, "dp", 0, 0, tiled=True, axis_index_groups=same_core)
        if layer:
            held = call(
                partial(fetch_kernel, layer - 1),
                [kept_out, ((META_ROWS, channels), bf16)],
                [],
                [after(kept[layer - 1], parts), *slices],
                "fetch",
                held=range(5),
                copies=2,
            )
            blocks = spread(parts, to_section, held)
            grad_pre, sums = call(
                partial(norm_back_kernel, dims, layer - 1 == CONVS - 1),
                [map_out, sums_out],
                [],
                [*blocks, *held, inside, facts],
                "norm_back",
                loose=(6, 7),
            )
    blocks = spread(parts, to_section)
    keep, give = call(
        input_kernel,
        [((4 * ch, 2 * cells), bf16)] * 2,
        [((2 * ch, length), bf16)],
        [*blocks, activation, inside],
        "input",
        flops=INPUT_FLOPS,
        held=(4,),
        loose=(5,),
        copies=1,
    )
    maps = call(pair_kernel, [((4 * ch, 2 * cells), bf16)] * 2, [], [keep, to_core(give)], "pair")
    maps = [send(x, lambda s, z, c, n=n: (z, s ^ (2 * c + n), c)) for n, x in enumerate(maps)]
    folded = call(
        fold_kernel,
        [share_piece] * last,
        [((last, 4 * slice_rows, 2 * ch), bf16)],
        shares[1:],
        "fold",
        held=range(last),
        copies=last,
    )
    chosen = call(
        choose_kernel,
        [share_piece] * 4,
        [],
        [shares[0], *folded],
        "choose",
        loose=(0,),
    )
    pick = (core * cells + np.arange(cells))[:, None] == np.arange(2 * cells)[None, :]
    activations, input_grad = call(
        maps_out_kernel,
        [((cells, channels), bf16)] * 2,
        [((channels, 2 * cells), bf16)],
        [*with_core(after(maps, chosen)), pick.astype(bf16)],
        "maps_out",
        loose=(4,),
        last=True,
    )

    pick = (core * ch + np.arange(ch))[:, None] == np.arange(2 * ch)[None, :]
    weight_grad, bias_grad, gain_grad = call(
        grads_out_kernel,
        [((TAPS, ch, channels), f32), ((1, ch), f32), ((1, ch), f32)],
        [((TAPS, channels, 2 * ch), bf16)],
        [*with_core(after(spread(chosen, to_section), activations, input_grad)), pick.astype(bf16)],
        "grads_out",
        loose=(8,),
        last=True,
    )
    weight_grad = weight_grad.reshape(3, 3, ch, channels).transpose(2, 0, 1, 3)[None]
    return (
        activations.reshape(1, 1, rows, cols, channels),
        input_grad.reshape(1, 1, rows, cols, channels),
        weight_grad,
        gain_grad,
        bias_grad,
    )


def fits_plane_plan(images, conv_weight, sections, dps):
    micro_total, images_total, rows, cols, channels = images.shape
    return (
        sections == 4
        and dps == 2 * sections
        and micro_total == sections
        and conv_weight.shape[0] == sections
        and images_total == dps
        and rows % 2 == 0
        and cols % 2 == 0
        and (rows * cols) % 64 == 0
        and channels == 512
    )


def solution(mesh):
    in_specs = (
        P(None, "dp", None, None, None),
        P(None, "dp"),
        P(),
        P("section", None, None, None, None),
        P("section", None),
        P("section", None),
        P(None, "dp", None, None, None),
    )
    out_specs = (
        P("section", "dp", None, None, None),
        P("section", "dp", None, None, None),
        P("section", "dp", None, None, None),
        P("section", "dp"),
        P("section", "dp"),
    )
    sections, dps = mesh.shape["section"], mesh.shape["dp"]

    def program(images, image_group, group_size, conv_weight, bn_gain, bn_bias, cotangent):
        plan = plane_shards if fits_plane_plan(images, conv_weight, sections, dps) else pipeline_shards
        sharded = jax.shard_map(plan, mesh=mesh, in_specs=in_specs, out_specs=out_specs, check_vma=False)
        return sharded(images, image_group, group_size, conv_weight, bn_gain, bn_bias, cotangent)

    return program
```

```python
import math
from functools import partial

import jax
import jax.numpy as jnp
import numpy as np
from jax import lax
from jax.experimental import pallas as pl
from jax.experimental.pallas import tpu as pltpu
from jax.sharding import PartitionSpec as P

CONVS = 2
BACK_FLOPS = (6 * 10**9, 6 * 10**9, 6 * 10**9, 0)
PICK_FLOPS = 4 * 10**9
COT_LAYER = 2
INPUT_FLOPS = 4000000000


eps = 1e-05


def from_behind(x, axis, by):
    peers = lax.axis_size(axis)
    pairs = [(i, i + by) for i in range(peers) if 0 <= i + by < peers]
    return lax.ppermute(x, axis, pairs)


def canvas_mask(image_group, group_size, canvas_rows, canvas_cols):
    groups_n = group_size.shape[0]
    onehot = image_group[..., None] == jnp.arange(groups_n, dtype=jnp.int32)
    height = jnp.sum(jnp.where(onehot, group_size[:, 0], 0), axis=-1)
    breadth = jnp.sum(jnp.where(onehot, group_size[:, 1], 0), axis=-1)
    inside_rows = jnp.arange(canvas_rows, dtype=jnp.int32)[:, None] < height[..., None, None]
    inside_cols = jnp.arange(canvas_cols, dtype=jnp.int32)[None, :] < breadth[..., None, None]
    return (inside_rows & inside_cols).astype(jnp.float32)[..., None]


def window_pool(hidden):
    frames, height, breadth, channels = hidden.shape
    blocks = hidden.reshape(frames, height // 2, 2, breadth // 2, 2, channels)
    window_max = jnp.max(blocks, axis=(2, 4), keepdims=True)
    raised = jnp.exp(blocks - window_max)
    weights = raised / jnp.sum(raised, axis=(2, 4), keepdims=True)
    pooled = jnp.sum(weights * blocks, axis=(2, 4), keepdims=True)
    return (weights * pooled).reshape(frames, height, breadth, channels)


def activate(pre_act, inside, pooling):
    hidden = jax.nn.silu(pre_act) * inside
    return jnp.where(pooling, window_pool(hidden) * inside, hidden)


def conv_forward(layer_in, weight):
    return lax.conv_general_dilated(
        layer_in,
        weight,
        (1, 1),
        "SAME",
        dimension_numbers=("NHWC", "IHWO", "NHWC"),
        preferred_element_type=jnp.float32,
    )


def conv_data_back(grad_pre, weight):
    flipped = weight[:, ::-1, ::-1, :]
    return lax.conv_general_dilated(
        grad_pre,
        flipped,
        (1, 1),
        "SAME",
        dimension_numbers=("NHWC", "OHWI", "NHWC"),
        preferred_element_type=jnp.float32,
    )


def weight_back(layer_in, grad_pre):
    height = layer_in.shape[1]
    breadth = layer_in.shape[2]
    padded = jnp.pad(layer_in, ((0, 0), (1, 1), (1, 1), (0, 0)))
    pieces = []
    for tap_row in range(3):
        for tap_col in range(3):
            window = padded[:, tap_row : tap_row + height, tap_col : tap_col + breadth, :]
            pieces.append(
                jnp.einsum("nhwi,nhwo->io", window, grad_pre, preferred_element_type=jnp.float32)
            )
    return jnp.stack(pieces, axis=1).reshape(layer_in.shape[3], 3, 3, grad_pre.shape[3])


def layer_forward(layer_in, weight, gain_row, bias_row, inside, pooling):
    pre_norm = conv_forward(layer_in, weight)
    sums = lax.psum(
        (
            jnp.sum(pre_norm * inside, axis=(0, 1, 2)),
            jnp.sum(pre_norm * pre_norm * inside, axis=(0, 1, 2)),
            jnp.sum(inside),
        ),
        "dp",
    )
    pixel_total = sums[2]
    mean_val = sums[0] / pixel_total
    scale_inv = lax.rsqrt(sums[1] / pixel_total - mean_val * mean_val + eps)
    pre_act = (pre_norm - mean_val) * scale_inv * gain_row + bias_row
    hidden = activate(pre_act, inside, pooling)
    return (pre_norm, mean_val, scale_inv, pixel_total, hidden)


def layer_backward(
    grad_out,
    layer_in,
    pre_norm,
    mean_val,
    scale_inv,
    pixel_total,
    weight,
    gain_row,
    bias_row,
    inside,
    pooling,
):
    normed = (pre_norm - mean_val) * scale_inv
    pre_act = normed * gain_row + bias_row
    hidden_out, pullback = jax.vjp(partial(activate, inside=inside, pooling=pooling), pre_act)
    grad_act = pullback(grad_out)[0]
    sums = lax.psum(
        (jnp.sum(grad_act, axis=(0, 1, 2)), jnp.sum(grad_act * normed, axis=(0, 1, 2))), "dp"
    )
    shift_term = sums[0] / pixel_total
    slope_term = sums[1] / pixel_total
    grad_pre = (
        inside * scale_inv * gain_row * (grad_act - shift_term - normed * slope_term)
    ).astype(jnp.bfloat16)
    weight_term = weight_back(layer_in, grad_pre)
    grad_in = conv_data_back(grad_pre, weight).astype(jnp.bfloat16)
    return (grad_in, weight_term, sums[1], sums[0])


def pipeline_shards(images, image_group, group_size, conv_weight, bn_gain, bn_bias, cotangent):
    section_index = lax.axis_index("section")
    sections = lax.axis_size("section")
    micro_total = images.shape[0]
    channels = conv_weight.shape[1]
    inside_all = canvas_mask(image_group, group_size, images.shape[2], images.shape[3])
    ticks = micro_total + sections - 1
    weight = conv_weight[0]
    gain_row = bn_gain[0]
    bias_row = bn_bias[0]
    pool_here = section_index == CONVS - 1
    received = jnp.zeros(images.shape[1:], jnp.bfloat16)
    kept_in, kept_pre, kept_mean, kept_scale, kept_total, finished = ([], [], [], [], [], [])
    for tick in range(ticks):
        micro_pos = jnp.clip(tick - section_index, 0, micro_total - 1)
        inside = inside_all[micro_pos]
        fresh = (images[micro_pos].astype(jnp.float32) * inside).astype(jnp.bfloat16)
        layer_in = jnp.where(section_index == 0, fresh, received)
        pre_norm, mean_val, scale_inv, pixel_total, hidden = layer_forward(
            layer_in, weight, gain_row, bias_row, inside, pool_here
        )
        sent = hidden.astype(jnp.bfloat16)
        if tick < ticks - 1:
            received = from_behind(sent, "section", 1)
        kept_in.append(layer_in)
        kept_pre.append(pre_norm)
        kept_mean.append(mean_val)
        kept_scale.append(scale_inv)
        kept_total.append(pixel_total)
        finished.append(sent)
    stack_in = jnp.stack(kept_in)
    stack_pre = jnp.stack(kept_pre)
    stack_mean = jnp.stack(kept_mean)
    stack_scale = jnp.stack(kept_scale)
    stack_total = jnp.stack(kept_total)
    returned = jnp.zeros(images.shape[1:], jnp.bfloat16)
    weight_sum = jnp.zeros(conv_weight.shape[1:], jnp.float32)
    gain_sum = jnp.zeros((channels,), jnp.float32)
    bias_sum = jnp.zeros((channels,), jnp.float32)
    input_list = []
    for tick in range(ticks):
        micro_raw = tick - (sections - 1 - section_index)
        valid = ((micro_raw >= 0) & (micro_raw < micro_total)).astype(jnp.float32)
        micro_pos = jnp.clip(micro_raw, 0, micro_total - 1)
        forward_tick = jnp.clip(micro_pos + section_index, 0, ticks - 1)
        inside = inside_all[micro_pos]
        grad_out = jnp.where(
            section_index == sections - 1,
            cotangent[micro_pos].astype(jnp.float32),
            returned.astype(jnp.float32),
        )
        grad_in, weight_term, gain_term, bias_term = layer_backward(
            grad_out,
            stack_in[forward_tick],
            stack_pre[forward_tick],
            stack_mean[forward_tick],
            stack_scale[forward_tick],
            stack_total[forward_tick],
            weight,
            gain_row,
            bias_row,
            inside,
            pool_here,
        )
        weight_sum = weight_sum + valid * weight_term
        gain_sum = gain_sum + valid * gain_term
        bias_sum = bias_sum + valid * bias_term
        if tick < ticks - 1:
            returned = from_behind(grad_in, "section", -1)
        input_list.append((grad_in.astype(jnp.float32) * inside).astype(jnp.bfloat16))
    out_stack = jnp.stack(finished[sections - 1 :], axis=0)
    grad_stack = jnp.stack(input_list[sections - 1 :], axis=0)
    out_back, grad_back = (
        lax.all_to_all(out_stack, "section", split_axis=0, concat_axis=1, tiled=True),
        lax.all_to_all(grad_stack, "section", split_axis=0, concat_axis=1, tiled=True),
    )
    activations = out_back[:, sections - 1 : sections]
    input_grad = grad_back[:, 0:1]
    weight_grad = lax.psum_scatter(weight_sum[None], "dp", scatter_dimension=1, tiled=True)
    share = channels // lax.axis_size("dp")
    gain_grad = lax.dynamic_slice_in_dim(gain_sum, lax.axis_index("dp") * share, share)[None]
    bias_grad = lax.dynamic_slice_in_dim(bias_sum, lax.axis_index("dp") * share, share)[None]
    return (activations, input_grad, weight_grad, gain_grad, bias_grad)


AXES = ("section", "dp")
TAPS = 9
VMEM_LIMIT = 24 * 1024 * 1024
META_ROWS = 16
LANES = 128
ROW_AT, COL_AT, FRAME_AT = 6, 7, 8
NT = (((1,), (1,)), ((), ()))


def place():
    dp_index = lax.axis_index("dp")
    return lax.axis_index("section"), dp_index // 2, dp_index % 2


def peer_order():
    return [(k, j) for j in range(2) for k in range(4)]


def slice_at(section, core, k, j):
    return (core ^ j) * lax.axis_size("section") + (section ^ k)


def send(x, target):
    sections = lax.axis_size("section")
    dps = lax.axis_size("dp")
    pairs = []
    for s in range(sections):
        for d in range(dps):
            ts, tz, tc = target(s, d // 2, d % 2)
            pairs.append((s * dps + d, ts * dps + tz * 2 + tc))
    return lax.ppermute(x, AXES, pairs)


def to_section(x, k):
    return send(x, lambda s, z, c: (s ^ k, z, c))


def to_plane(x, k):
    return send(x, lambda s, z, c: (s, z ^ k, c))


def to_core(x):
    return send(x, lambda s, z, c: (s, z, c ^ 1))


def spread(blocks, move, *beside):
    moved = lax.optimization_barrier(([move(blocks[k], k) for k in (1, 2, 3)], beside))[0]
    return [blocks[0]] + moved


def with_core(blocks):
    return blocks + [to_core(x) for x in blocks]


def after(x, *first):
    return lax.optimization_barrier((x, first))[0]


def grid_facts(frames, rows, cols):
    at = np.arange(frames * rows * cols)
    col = at % cols
    row = (at // cols) % rows
    facts = [row > 0, row < rows - 1, col > 0, col < cols - 1, col % 2 == 0, row % 2 == 0, row, col]
    facts = facts + [at // (rows * cols) == frame for frame in range(frames)]
    return jnp.asarray(np.stack(facts).astype(np.float32))


def shift(x, by):
    length = x.shape[1]
    return pltpu.roll(x, (-by) % length, 1) if by % length else x


def row_ok(facts, d):
    return facts[0:1, :] if d < 0 else facts[1:2, :]


def col_ok(facts, d):
    return facts[2:3, :] if d < 0 else facts[3:4, :]


def sum_taps(taps_ref, facts, cols):
    ch = taps_ref.shape[0] // TAPS
    total = None
    for dx in (-1, 0, 1):
        column = None
        for dy in (-1, 0, 1):
            tap = (dy + 1) * 3 + dx + 1
            piece = taps_ref[tap * ch : (tap + 1) * ch, :]
            if dy:
                piece = shift(piece, dy * cols) * row_ok(facts, dy)
            column = piece if column is None else column + piece
        if dx:
            column = shift(column, dx) * col_ok(facts, dx)
        total = column if total is None else total + column
    return total


def spread_taps(grad, moved_ref, base, facts, cols):
    ch = grad.shape[0]
    facts = facts[:4, :].astype(grad.dtype)
    for dx in (-1, 0, 1):
        column = shift(grad, -dx) * col_ok(facts, -dx) if dx else grad
        for dy in (-1, 0, 1):
            piece = shift(column, -dy * cols) * row_ok(facts, -dy) if dy else column
            at = base + ((dy + 1) * 3 + dx + 1) * ch
            moved_ref[at : at + ch, :] = piece


def corner_sum(x, cols):
    x = x + shift(x, 1)
    return x + shift(x, cols)


def from_corner(x, facts, cols):
    x = jnp.where(facts[4:5, :] > 0.5, x, shift(x, -1))
    return jnp.where(facts[5:6, :] > 0.5, x, shift(x, -cols))


def lane_sum(x):
    return jnp.sum(x, axis=1, keepdims=True)


def normalise(pre, inside):
    count = lane_sum(inside)
    mean = lane_sum(pre * inside) / count
    square = lane_sum(pre * pre * inside) / count
    scale = lax.rsqrt(square - mean * mean + eps)
    return (pre - mean) * scale, scale


def hidden_of(normed, gain, bias, inside, facts, cols, pooling):
    pre_act = normed * gain + bias
    hidden = pre_act * jax.nn.sigmoid(pre_act) * inside
    if pooling:
        raised = jnp.exp(hidden)
        total = corner_sum(raised, cols)
        pooled = corner_sum(raised * hidden, cols) / total
        hidden = raised * from_corner(pooled / total, facts, cols) * inside
    return hidden


def norm_back(grad, normed, scale, gain, bias, inside, facts, cols, pooling):
    pre_act = normed * gain + bias
    gate = jax.nn.sigmoid(pre_act)
    if pooling:
        hidden = pre_act * gate * inside
        raised = jnp.exp(hidden)
        out = grad * inside
        total = 1.0 / corner_sum(raised, cols)
        pooled = corner_sum(raised * hidden, cols) * total
        d_pooled = corner_sum(raised * out, cols) * total
        by_out = from_corner(pooled * total, facts, cols)
        by_hidden = from_corner(d_pooled * total, facts, cols)
        rest = from_corner(d_pooled * total * (1.0 - 2.0 * pooled), facts, cols)
        grad = raised * (out * by_out + hidden * by_hidden + rest)
    grad_act = grad * inside * gate * (1.0 + pre_act * (1.0 - gate))
    count = lane_sum(inside)
    shift_sum = lane_sum(grad_act)
    slope_sum = lane_sum(grad_act * normed)
    grad_pre = inside * (scale * gain) * (grad_act - shift_sum / count - normed * (slope_sum / count))
    return grad_pre.astype(jnp.bfloat16), shift_sum, slope_sum


def assemble(blocks, full_ref):
    section, _, core = place()
    ch = blocks[0].shape[0]
    for (k, j), block in zip(peer_order(), blocks):
        at = pl.multiple_of(slice_at(section, core, k, j) * ch, ch)
        full_ref[pl.ds(at, ch), :] = block[...]


def assemble_frames(blocks, full_ref, rows, lanes):
    _, plane, core = place()
    size = rows.stop - rows.start
    for (k, j), block in zip(peer_order(), blocks):
        frame = (plane ^ k) * 2 + (core ^ j)
        full_ref[pl.ds(pl.multiple_of(frame * size, size), size), :] = block[rows, lanes]


def start_all(copies):
    for copy in copies:
        copy.start()
    return copies


def wait_all(copies):
    for copy in copies:
        copy.wait()


def tap_products(weight, full_ref, taps_ref, by_cells):
    length = taps_ref.shape[1]
    step = 512 if length % 512 == 0 else length
    for at in range(0, length, step):
        if by_cells:
            taps_ref[:, at : at + step] = lax.dot_general(
                weight, full_ref[at : at + step, :], NT, preferred_element_type=jnp.float32
            )
        else:
            taps_ref[:, at : at + step] = jnp.dot(
                weight, full_ref[:, at : at + step], preferred_element_type=jnp.float32
            )


def pick_layer(layer, sources, start, target, sem):
    section, _, _ = place()
    rows = pl.ds(start, target.shape[0])
    for k, source in enumerate(sources):

        @pl.when((section ^ layer) == k)
        def _():
            pltpu.make_async_copy(source.at[rows], target, sem).start()

    return pltpu.make_async_copy(sources[0].at[rows], target, sem)


def affine(meta, ch):
    parts = meta[:, :LANES].astype(jnp.float32).T[:ch]
    return (
        parts[:, 0:1] + parts[:, 1:2] + parts[:, 2:3],
        parts[:, 3:4] + parts[:, 4:5] + parts[:, 5:6],
    )


def plane_inside(metas, facts):
    frames = metas.shape[0] // META_ROWS
    extents = []
    for line in (0, 1):
        total = None
        for f in range(frames):
            at = f * META_ROWS + line
            extent = metas[at : at + 1, 0:1].astype(jnp.float32) * facts[FRAME_AT + f : FRAME_AT + f + 1, :]
            total = extent if total is None else total + extent
        extents.append(total)
    on = (facts[ROW_AT : ROW_AT + 1, :] < extents[0]) & (facts[COL_AT : COL_AT + 1, :] < extents[1])
    return jnp.where(on, 1.0, 0.0)


def frames_kernel(dims, group_table, size_table, images, *refs):
    payloads, (image_in, groups, sizes, sems) = refs[:4], refs[4:]
    copies = start_all(
        [
            pltpu.make_async_copy(group_table, groups, sems.at[0]),
            pltpu.make_async_copy(size_table, sizes, sems.at[1]),
            pltpu.make_async_copy(images, image_in, sems.at[2]),
        ]
    )
    _, plane, _ = place()
    rows, cols = dims
    cells = rows * cols
    at = lax.broadcasted_iota(jnp.int32, (cells, LANES), 0).astype(jnp.float32)
    row = jnp.floor((at + 0.5) * (1.0 / cols))
    col = at - row * cols
    channels = images.shape[2]
    line = lax.broadcasted_iota(jnp.int32, (META_ROWS, channels), 0)
    wait_all(copies)
    for k in range(4):
        micro = plane ^ k
        group = groups[0, micro]
        height = sizes[0, 0]
        breadth = sizes[1, 0]
        for g in range(1, sizes.shape[1]):
            height = jnp.where(group == g, sizes[0, g], height)
            breadth = jnp.where(group == g, sizes[1, g], breadth)
        height = height.astype(jnp.float32)
        breadth = breadth.astype(jnp.float32)
        on = jnp.where((row < height) & (col < breadth), 1.0, 0.0)
        image = image_in[micro]
        for c in range(0, channels, LANES):
            piece = image[:, c : c + LANES].astype(jnp.float32) * on
            payloads[k][:cells, c : c + LANES] = piece.astype(jnp.bfloat16)
        payloads[k][cells:, :] = jnp.where(line == 0, height, breadth).astype(jnp.bfloat16)


def cot_slice_kernel(cots, out, cot_in, sems):
    copy = pltpu.make_async_copy(cots, cot_in, sems.at[0])
    copy.start()
    section, _, _ = place()
    micros, cells, channels = cots.shape
    half = channels // 2
    tile = section // 2 * LANES
    odd = section % 2 == 1
    lane = lax.broadcasted_iota(jnp.int32, (cells, LANES), 1)
    copy.wait()
    for micro in range(micros):
        low = cot_in[micro, :, pl.ds(pl.multiple_of(tile, LANES), LANES)].astype(jnp.float32)
        high = cot_in[micro, :, pl.ds(pl.multiple_of(half + tile, LANES), LANES)].astype(jnp.float32)
        low = jnp.where(odd, pltpu.roll(low, LANES // 2, 1), low)
        high = jnp.where(odd, high, pltpu.roll(high, LANES // 2, 1))
        both = jnp.where(lane < LANES // 2, low, high).astype(jnp.bfloat16)
        out[micro * cells : (micro + 1) * cells, :] = both


def cot_kernel(own, other, pick, out, full):
    _, _, core = place()
    cells = full.shape[0] // 8
    for n in range(4):
        for j, block in enumerate((own, other)):
            at = pl.multiple_of((2 * n + (core ^ j)) * cells, cells)
            full[pl.ds(at, cells), :] = block[n * cells : (n + 1) * cells, :]
    out[...] = lax.dot_general(pick[...], full[...], NT, preferred_element_type=jnp.float32).astype(
        jnp.bfloat16
    )


def pack_kernel(gain, bias, weight, *refs):
    outs, (own, columns, turned, tables, sems) = refs[:4], refs[4:]
    section, _, core = place()
    width = columns.shape[2]
    ch = width // 4
    start = pl.multiple_of(core * width, width)
    copies = start_all(
        [
            pltpu.make_async_copy(weight.at[tap, :, pl.ds(start, width)], columns.at[tap], sems.at[tap])
            for tap in range(TAPS)
        ]
    )
    table_copies = start_all(
        [
            pltpu.make_async_copy(gain, tables.at[0], sems.at[TAPS]),
            pltpu.make_async_copy(bias, tables.at[1], sems.at[TAPS + 1]),
        ]
    )
    targets = [own, *outs[1:]]
    own_copies = []
    for tap in range(TAPS):
        copies[tap].wait()
        turned[tap % 2] = columns[tap].T
        for k, out in enumerate(targets):
            rows = pl.ds(pl.multiple_of((section ^ k) * ch, ch), ch)
            out[tap * ch : (tap + 1) * ch, :] = turned[tap % 2, rows, :]
        piece = pl.ds(tap * ch, ch)
        own_copies += start_all(
            [pltpu.make_async_copy(own.at[piece], outs[0].at[piece], sems.at[TAPS + 2 + tap])]
        )
    wait_all(table_copies)
    for k, out in enumerate(targets):
        lines = []
        tile = pl.multiple_of(start + (section ^ k) // 2 * LANES, LANES)
        odd = (section ^ k) % 2 == 1
        for m in range(2):
            line = tables[m, :, pl.ds(tile, LANES)]
            line = jnp.where(odd, pltpu.roll(line, ch, 1), line)
            for _ in range(3):
                part = line.astype(jnp.bfloat16).astype(jnp.float32)
                lines.append(part)
                line = line - part
        lines.append(jnp.zeros((META_ROWS - len(lines), LANES), jnp.float32))
        out[TAPS * ch :, :] = jnp.zeros((META_ROWS, out.shape[1]), jnp.bfloat16)
        out[TAPS * ch :, :LANES] = jnp.concatenate(lines, axis=0).astype(jnp.bfloat16)
    tail = pl.ds(TAPS * ch, META_ROWS)
    own_copies += start_all([pltpu.make_async_copy(own.at[tail], outs[0].at[tail], sems.at[2 * TAPS + 2])])
    wait_all(own_copies)


def pick_kernel(layer, *refs):
    sources, (out, sems) = refs[:4], refs[4:]
    pick_layer(layer, sources, 0, out, sems.at[0]).wait()


def forward_kernel(dims, layer, first, picks, pooling, *refs):
    blocks, weights, rest = refs[:8], refs[8 : 12 if picks else 9], refs[12 if picks else 9 :]
    rows, cols = dims
    cells = rows * cols
    if first:
        facts, hidden, kept, full_out, inside_out, full, taps, stage, weight, metas, sems = rest
    elif picks:
        inside, facts, hidden, kept, full_out, full, taps, stage, weight, sems = rest
    else:
        inside, facts, hidden, kept, full_out, full, taps, stage, sems = rest
        (weight,) = weights
    if picks:
        copy = pick_layer(layer, weights, 0, weight, sems.at[2])
    facts_now = facts[...]
    if first:
        channels = full.shape[1]
        assemble_frames(blocks, full, slice(0, cells), slice(0, channels))
    else:
        assemble(blocks, full)
    full_copy = pltpu.make_async_copy(full, full_out, sems.at[0])
    full_copy.start()
    if first:
        assemble_frames(blocks, metas, slice(cells, cells + META_ROWS), slice(0, channels))
        inside_now = plane_inside(metas, facts_now)
        inside_out[...] = inside_now
    else:
        inside_now = inside[...]
    if picks:
        copy.wait()
    ch = hidden.shape[0]
    tap_products(weight[: TAPS * ch, :], full, taps, first)
    pre = sum_taps(taps, facts_now, cols)
    normed, scale = normalise(pre, inside_now)
    length = normed.shape[1]
    stage[:, :length] = normed
    stage[:, length:] = jnp.broadcast_to(scale, (ch, LANES))
    kept_copy = pltpu.make_async_copy(stage, kept, sems.at[1])
    kept_copy.start()
    gain, bias = affine(weight[TAPS * ch :, :], ch)
    hidden[...] = hidden_of(normed, gain, bias, inside_now, facts_now, cols, pooling).astype(jnp.bfloat16)
    full_copy.wait()
    kept_copy.wait()


def turn_kernel(dims, layer, pooling, *refs):
    blocks, (weight, cot_in, inside, facts) = refs[:8], refs[8:12]
    hidden_out, full_out, grad_pre, sums, full, taps, hidden, sems = refs[12:]
    cols = dims[1]
    assemble(blocks, full)
    full_copy = pltpu.make_async_copy(full, full_out, sems.at[1])
    full_copy.start()
    ch = grad_pre.shape[0]
    tap_products(weight[: TAPS * ch, :], full, taps, False)
    facts_now, inside_now = facts[...], inside[...]
    pre = sum_taps(taps, facts_now, cols)
    normed, scale = normalise(pre, inside_now)
    gain, bias = affine(weight[TAPS * ch :, :], ch)
    hidden[...] = hidden_of(normed, gain, bias, inside_now, facts_now, cols, pooling).astype(jnp.bfloat16)
    hidden_copy = pltpu.make_async_copy(hidden, hidden_out, sems.at[2])
    hidden_copy.start()
    grad_pre[...], shift_sum, slope_sum = norm_back(
        cot_in[...].astype(jnp.float32), normed, scale, gain, bias, inside_now, facts_now, cols, pooling
    )
    keep_sums(sums, shift_sum, slope_sum)
    full_copy.wait()
    hidden_copy.wait()


def keep_sums(sums, shift_sum, slope_sum):
    ch = shift_sum.shape[0]
    sums[:, :LANES] = jnp.broadcast_to(shift_sum, (ch, LANES))
    sums[:, LANES:] = jnp.broadcast_to(slope_sum, (ch, LANES))


def add_blocks(blocks):
    total = blocks[0][...].astype(jnp.float32)
    for block in blocks[1:]:
        total = total + block[...].astype(jnp.float32)
    return total


def fetch_kernel(layer, kept, *refs):
    sources, (kept_out, meta_out, sems) = refs[:4], refs[4:]
    copy = pltpu.make_async_copy(kept, kept_out, sems.at[0])
    copy.start()
    start = sources[0].shape[0] - META_ROWS
    pick_layer(layer, sources, start, meta_out, sems.at[1]).wait()
    copy.wait()


def norm_back_kernel(dims, pooling, *refs):
    blocks, (kept, meta, inside, facts, grad_pre, sums) = refs[:4], refs[4:]
    ch, length = grad_pre.shape
    grad = add_blocks(blocks).astype(jnp.bfloat16).astype(jnp.float32)
    gain, bias = affine(meta[...], ch)
    grad_pre[...], shift_sum, slope_sum = norm_back(
        grad,
        kept[:, :length],
        kept[:, length : length + 1],
        gain,
        bias,
        inside[...],
        facts[...],
        dims[1],
        pooling,
    )
    keep_sums(sums, shift_sum, slope_sum)


def weight_product(moved, full, first):
    if first:
        return jnp.dot(moved, full, preferred_element_type=jnp.float32)
    return lax.dot_general(moved, full, NT, preferred_element_type=jnp.float32)


def sums_rows(sums, ch, width):
    lines = []
    for at in (0, LANES):
        turned = sums[:, at : at + LANES].T
        lines.append(jnp.concatenate([turned, jnp.zeros((LANES, width - ch), jnp.float32)], axis=1)[0:1])
    lines.append(jnp.zeros((META_ROWS - 2, width), jnp.float32))
    return jnp.concatenate(lines, axis=0).astype(jnp.bfloat16)


def store_share(value, sums, pieces):
    rows = value.shape[0]
    width = pieces[0].shape[1]
    below = sums_rows(sums, rows // TAPS, width)
    for n, piece in enumerate(pieces):
        piece[:rows, :] = value[:, n * width : (n + 1) * width].astype(jnp.bfloat16)
        piece[rows:, :] = below


def form_share(layer, moved, full, sums, product):
    piece = product.shape[0] // 4
    value = weight_product(moved[: piece - META_ROWS, :], full[...], layer == 0)
    store_share(value, sums, [product.at[pl.ds(n * piece, piece)] for n in range(4)])


def conv_back_kernel(dims, layer, own, other, own_weights, other_weights, full_in, sums, facts, *refs):
    *outs, share, product, full, moved, weights, sems = refs
    ch = own.shape[0]
    size = moved.shape[0] // 2
    rows = pl.ds(layer * 4 * ch, 4 * ch)
    copies = start_all(
        [
            pltpu.make_async_copy(own_weights.at[rows], weights.at[:, pl.ds(0, size)], sems.at[0]),
            pltpu.make_async_copy(other_weights.at[rows], weights.at[:, pl.ds(size, size)], sems.at[1]),
        ]
    )
    full_copy = pltpu.make_async_copy(full_in, full, sems.at[2])
    full_copy.start()
    facts_now = facts[...]
    spread_taps(own[...], moved, 0, facts_now, dims[1])
    full_copy.wait()
    form_share(layer, moved, full, sums, product)
    share_copy = pltpu.make_async_copy(product, share, sems.at[3])
    share_copy.start()
    spread_taps(other[...], moved, size, facts_now, dims[1])
    for n in range(2):
        moved[n * size + TAPS * ch : (n + 1) * size, :] = jnp.zeros(
            (size - TAPS * ch, moved.shape[1]), jnp.bfloat16
        )
    wait_all(copies)
    value = jnp.dot(weights[...], moved[...], preferred_element_type=jnp.float32)
    for k, out in enumerate(outs):
        out[...] = value[k * ch : (k + 1) * ch, :].astype(jnp.bfloat16)
    share_copy.wait()


def fold_kernel(*refs):
    count = (len(refs) - 2) // 2
    shares, outs, (blocks, sems) = refs[:count], refs[count:-2], refs[-2:]
    rows = outs[0].shape[0]
    copies = start_all(
        [pltpu.make_async_copy(share, blocks.at[n], sems.at[n]) for n, share in enumerate(shares)]
    )
    for n, copy in enumerate(copies):
        copy.wait()
        value = add_blocks([blocks.at[n, pl.ds(m * rows, rows)] for m in range(blocks.shape[1] // rows)])
        outs[n][...] = value.astype(jnp.bfloat16)


def choose_kernel(*refs):
    last, others, outs = refs[0], refs[1:-4], refs[-4:]
    section, _, _ = place()
    rows = outs[0].shape[0]
    value = add_blocks([last.at[pl.ds(n * rows, rows)] for n in range(last.shape[0] // rows)])
    value = value.astype(jnp.bfloat16)
    for k, out in enumerate(outs):

        @pl.when((section ^ k) == 0)
        def _():
            out[...] = value

        for layer, other in enumerate(others, 1):

            @pl.when((section ^ k) == layer)
            def _():
                out[...] = other[...]


def turn_weights_kernel(layers, *refs):
    sources, outs, (full, turned, stage, sems) = refs[:4], refs[4:6], refs[6:]
    section, _, core = place()
    rows, channels = full.shape[1:]
    half = channels // 2
    ch = half // 4
    copies = [pick_layer(n, sources, 0, full.at[n], sems.at[n]) for n in range(layers)]
    stage[:, :, rows:] = jnp.zeros((*stage.shape[:2], stage.shape[2] - rows), jnp.bfloat16)
    for n in range(layers):
        copies[n].wait()
        turned[...] = full[n].T
        for j in range(2):
            for k in range(4):
                at = pl.multiple_of((core ^ j) * half + (section ^ k) * ch, ch)
                stage[j, n * half + k * ch : n * half + (k + 1) * ch, :rows] = turned[pl.ds(at, ch), :]
    wait_all(
        start_all([pltpu.make_async_copy(stage.at[j], outs[j], sems.at[j]) for j in range(2)])
    )


def input_kernel(*refs):
    blocks, (hidden, inside, keep, give, full, sems) = refs[:4], refs[4:]
    section, _, core = place()
    ch = hidden.shape[0]
    copy = pltpu.make_async_copy(hidden, full.at[pl.ds(0, ch)], sems.at[0])
    copy.start()
    full[ch:, :] = (add_blocks(blocks) * inside[...]).astype(jnp.bfloat16)
    copy.wait()
    rows = 2 * ch
    width = keep.shape[1]
    for j, out in enumerate((keep, give)):
        for n in range(2):
            at = pl.multiple_of((section ^ (2 * (core ^ j) + n)) * width, width)
            out[n * rows : (n + 1) * rows, :] = full[:, pl.ds(at, width)]


def pair_kernel(keep, got, *outs):
    rows = keep.shape[0] // 2
    for n, out in enumerate(outs):
        out[:rows, :] = keep[n * rows : (n + 1) * rows, :]
        out[rows:, :] = got[n * rows : (n + 1) * rows, :]


def store_maps(blocks, pick, outs, full):
    _, plane, core = place()
    ch = blocks[0].shape[0] // 4
    for m, out in enumerate(outs):
        for j in range(2):
            for n in range(2):
                for h in range(2):
                    slot = slice_at(plane ^ (2 * (core ^ j) + n), core ^ j, 0, h)
                    at = pl.multiple_of(slot * ch, ch)
                    start = (2 * h + m) * ch
                    full[m, pl.ds(at, ch), :] = blocks[2 * j + n][start : start + ch, :]
        mine = lax.dot_general(pick[...], full[m], NT, preferred_element_type=jnp.float32)
        out[...] = mine.astype(out.dtype)


def outputs_kernel(*refs):
    blocks, pick, map_blocks, map_pick, refs = refs[:8], refs[8], refs[9:13], refs[13], refs[14:]
    (weight_out, shift_out, slope_out), map_outs, (full, maps_full) = refs[:3], refs[3:5], refs[5:]
    store_maps(map_blocks, map_pick, map_outs, maps_full)
    section, plane, core = place()
    taps, rows, channels = weight_out.shape
    for tap in range(taps):
        for (k, j), block in zip(peer_order(), blocks):
            at = pl.multiple_of(slice_at(section, core, k, j) * rows, rows)
            full[tap, pl.ds(at, rows), :] = block[tap * rows : (tap + 1) * rows, :]
        weight_out[tap] = lax.dot_general(pick[...], full[tap], NT, preferred_element_type=jnp.float32)
    shift_row = jnp.zeros((1, rows), jnp.float32)
    slope_row = jnp.zeros((1, rows), jnp.float32)
    slot = plane * 2 + core
    for (k, j), block in zip(peer_order(), blocks):
        tail = block[taps * rows :, :].astype(jnp.float32)
        mine = slice_at(section, core, k, j) == slot
        shift_row = shift_row + jnp.where(mine, tail[0:1, :rows], 0.0)
        slope_row = slope_row + jnp.where(mine, tail[1:2, :rows], 0.0)
    shift_out[...] = shift_row
    slope_out[...] = slope_row


def call(
    kernel, outs, scratch, args, name, held=(), free=(), held_outs=(), loose=(), last=False, flops=0, copies=None
):
    shapes = [
        (jax.ShapeDtypeStruct if last else pltpu.HBM if n in held_outs else pltpu.VMEM)(shape, dtype)
        for n, (shape, dtype) in enumerate(outs)
    ]
    moved = sum(a.size * a.dtype.itemsize for a in args)
    moved += sum(math.prod(shape) * jnp.dtype(dtype).itemsize for shape, dtype in outs)
    spaces = [pl.ANY if n in free else pltpu.HBM if n in held else pltpu.VMEM for n in range(len(args))]
    out_spaces = [pltpu.HBM if n in held_outs else pltpu.VMEM for n in range(len(outs))]
    args = [
        a if n in loose or n in free else pltpu.with_memory_space_constraint(a, space)
        for n, (a, space) in enumerate(zip(args, spaces))
    ]
    scratch_shapes = [
        pltpu.SMEM(shape, dtype) if dtype == jnp.int32 else pltpu.VMEM(shape, dtype) for shape, dtype in scratch
    ]
    if copies is not None:
        scratch_shapes.append(pltpu.SemaphoreType.DMA((copies,)))
    return pl.pallas_call(
        kernel,
        out_shape=shapes,
        in_specs=[pl.BlockSpec(memory_space=space) for space in spaces],
        out_specs=[pl.BlockSpec(memory_space=space) for space in out_spaces],
        scratch_shapes=scratch_shapes,
        compiler_params=pltpu.CompilerParams(vmem_limit_bytes=VMEM_LIMIT),
        cost_estimate=pl.CostEstimate(flops=flops, bytes_accessed=moved, transcendentals=0),
        name=name,
    )(*args)


def plane_shards(images, image_group, group_size, conv_weight, bn_gain, bn_bias, cotangent):
    _, _, core = place()
    micro_total, _, rows, cols, channels = images.shape
    layers = lax.axis_size("section")
    last = layers - 1
    cells = rows * cols
    frames = 2 * micro_total
    length = frames * cells
    ch = channels // 8
    dims = (rows, cols)
    bf16, f32 = jnp.bfloat16, jnp.float32
    facts = grid_facts(frames, rows, cols)
    conv_flops = 2 * TAPS * ch * channels * length
    slice_rows = TAPS * ch + META_ROWS
    tap_rows = -(-TAPS * ch // LANES) * LANES

    full_map = ((channels, length), bf16)
    full_frames = ((length, channels), bf16)
    tap_scratch = ((TAPS * ch, length), f32)
    weight_slice = ((slice_rows, channels), bf16)
    map_out = ((ch, length), bf16)
    sums_out = ((ch, 2 * LANES), f32)
    kept_out = ((ch, length + LANES), f32)
    share_out = ((4 * slice_rows, 2 * ch), bf16)
    share_piece = ((slice_rows, 2 * ch), bf16)

    taps_first = conv_weight[0].transpose(1, 2, 0, 3).reshape(TAPS, channels, channels)
    packed = call(
        pack_kernel,
        [weight_slice] * 4,
        [
            weight_slice,
            ((TAPS, channels, 4 * ch), bf16),
            ((2, 4 * ch, channels), bf16),
            ((2, 1, channels), f32),
        ],
        [bn_gain, bn_bias, taps_first],
        "weight_pack",
        held=range(3),
        held_outs=(0,),
        copies=2 * TAPS + 3,
    )
    slices = spread(packed, to_section)

    payload = ((cells + META_ROWS, channels), bf16)
    sent = call(
        partial(frames_kernel, dims),
        [payload] * 4,
        [
            ((micro_total, cells, channels), bf16),
            (image_group.shape[::-1], jnp.int32),
            (group_size.shape[::-1], jnp.int32),
        ],
        [image_group.T, group_size.T, after(images.reshape(micro_total, cells, channels), packed)],
        "frames",
        held=range(3),
        copies=3,
    )
    frames_in = with_core(spread(sent, to_plane))

    half = (core * ch + np.arange(ch))[:, None] == np.arange(2 * ch)[None, :]
    hidden, normed, full, inside = call(
        partial(forward_kernel, dims, 0, True, True, CONVS == 1),
        [map_out, kept_out, full_frames, ((1, length), f32)],
        [
            full_frames,
            tap_scratch,
            kept_out,
            weight_slice,
            ((frames * META_ROWS, channels), bf16),
        ],
        [*frames_in, *slices, facts],
        "forward",
        held=range(8, 12),
        held_outs=(1, 2),
        loose=(12,),
        flops=conv_flops,
        copies=4,
    )
    kept, fulls = [normed], [full]
    same_core = [[2 * z + c for z in range(layers)] for c in range(2)]
    for layer in range(1, layers):
        picks = layer == COT_LAYER
        weights = slices if picks else call(
            partial(pick_kernel, layer),
            [weight_slice],
            [],
            after(slices, hidden),
            "pick",
            flops=PICK_FLOPS,
            held=range(4),
            copies=1,
        )
        beside = [] if picks else [*weights]
        if layer == 1:
            turned = call(
                partial(turn_weights_kernel, layers),
                [((layers * 4 * ch, tap_rows), bf16)] * 2,
                [
                    ((layers, TAPS * ch, channels), bf16),
                    ((channels, TAPS * ch), bf16),
                    ((2, layers * 4 * ch, tap_rows), bf16),
                ],
                after(slices, hidden),
                "turn_weights",
                held=range(4),
                held_outs=(0, 1),
                copies=layers,
            )
            beside.append(turned)
        if layer == COT_LAYER - 1:
            (cot_slots,) = call(
                cot_slice_kernel,
                [((micro_total * cells, LANES), bf16)],
                [((micro_total, cells, channels), bf16)],
                [after(cotangent.reshape(micro_total, cells, channels), hidden)],
                "cot_slices",
                held=(0,),
                copies=1,
            )
            beside.append(cot_slots)
        if layer == COT_LAYER:
            cot_slots = after(cot_slots, hidden)
            cots = lax.all_to_all(cot_slots, "dp", 0, 0, tiled=True, axis_index_groups=same_core)
        if layer == 2:
            turned = [turned[0], to_core(after(turned[1], hidden))]
        if layer == last:
            cots = after(cots, hidden)
            (cot,) = call(
                cot_kernel,
                [map_out],
                [((length, LANES), bf16)],
                [cots, to_core(cots), half.astype(bf16)],
                "cotangent",
                loose=(0, 1, 2),
            )
            beside.append(cot)
        blocks = [hidden] + [to_section(hidden, k) for k in (1, 2, 3)]
        blocks[3] = after(blocks[3], *beside)
        blocks = with_core(blocks)
        if layer < last:
            hidden, normed, full = call(
                partial(forward_kernel, dims, layer, False, picks, layer == CONVS - 1),
                [map_out, kept_out, full_map],
                [full_map, tap_scratch, kept_out] + [weight_slice] * picks,
                [*blocks, *weights, inside, facts],
                "forward",
                held=range(8, 12) if picks else (),
                held_outs=(1, 2),
                loose=(12, 13) if picks else (9, 10),
                flops=conv_flops,
                copies=3,
            )
            kept.append(normed)
        else:
            activation, full, grad_pre, sums = call(
                partial(turn_kernel, dims, last, last == CONVS - 1),
                [map_out, full_map, map_out, sums_out],
                [full_map, tap_scratch, map_out],
                [*blocks, *weights, cot, inside, facts],
                "turn",
                held_outs=(0, 1),
                loose=(10, 11),
                flops=conv_flops,
                copies=3,
            )
        fulls.append(full)

    shares = [None] * layers
    for layer in range(last, -1, -1):
        *parts, share = call(
            partial(conv_back_kernel, dims, layer),
            [map_out] * 4 + [share_out],
            [
                share_out,
                full_map if layer else full_frames,
                ((2 * tap_rows, length), bf16),
                ((4 * ch, 2 * tap_rows), bf16),
            ],
            [grad_pre, to_core(grad_pre), *turned, fulls[layer], sums, facts],
            "conv_back",
            held=(2, 4),
            free=(3,),
            held_outs=(4,),
            loose=(5, 6),
            flops=BACK_FLOPS[layer],
            copies=4,
        )
        if layer < last:
            share = after(share, shares[layer + 1])
        shares[layer] = lax.all_to_all(share, "dp", 0, 0, tiled=True, axis_index_groups=same_core)
        if layer:
            held = call(
                partial(fetch_kernel, layer - 1),
                [kept_out, ((META_ROWS, channels), bf16)],
                [],
                [after(kept[layer - 1], parts), *slices],
                "fetch",
                held=range(5),
                copies=2,
            )
            blocks = spread(parts, to_section, held)
            grad_pre, sums = call(
                partial(norm_back_kernel, dims, layer - 1 == CONVS - 1),
                [map_out, sums_out],
                [],
                [*blocks, *held, inside, facts],
                "norm_back",
                loose=(6, 7),
            )
    blocks = spread(parts, to_section)
    keep, give = call(
        input_kernel,
        [((4 * ch, 2 * cells), bf16)] * 2,
        [((2 * ch, length), bf16)],
        [*blocks, activation, inside],
        "input",
        flops=INPUT_FLOPS,
        held=(4,),
        loose=(5,),
        copies=1,
    )
    maps = call(pair_kernel, [((4 * ch, 2 * cells), bf16)] * 2, [], [keep, to_core(give)], "pair")
    maps = [send(x, lambda s, z, c, n=n: (z, s ^ (2 * c + n), c)) for n, x in enumerate(maps)]
    folded = call(
        fold_kernel,
        [share_piece] * last,
        [((last, 4 * slice_rows, 2 * ch), bf16)],
        shares[1:],
        "fold",
        held=range(last),
        copies=last,
    )
    chosen = call(
        choose_kernel,
        [share_piece] * 4,
        [],
        [shares[0], *folded],
        "choose",
        loose=(0,),
    )
    pick = (core * cells + np.arange(cells))[:, None] == np.arange(2 * cells)[None, :]
    map_pick = pick.astype(bf16)
    pick = (core * ch + np.arange(ch))[:, None] == np.arange(2 * ch)[None, :]
    weight_grad, bias_grad, gain_grad, activations, input_grad = call(
        outputs_kernel,
        [((TAPS, ch, channels), f32), ((1, ch), f32), ((1, ch), f32)] + [((cells, channels), bf16)] * 2,
        [((TAPS, channels, 2 * ch), bf16), ((2, channels, 2 * cells), bf16)],
        [
            *with_core([chosen[0]] + [to_section(chosen[k], k) for k in (1, 2, 3)]),
            pick.astype(bf16),
            *with_core(after(maps, chosen)),
            map_pick,
        ],
        "outputs",
        loose=(8, 13),
        last=True,
    )
    weight_grad = weight_grad.reshape(3, 3, ch, channels).transpose(2, 0, 1, 3)[None]
    return (
        activations.reshape(1, 1, rows, cols, channels),
        input_grad.reshape(1, 1, rows, cols, channels),
        weight_grad,
        gain_grad,
        bias_grad,
    )


def fits_plane_plan(images, conv_weight, sections, dps):
    micro_total, images_total, rows, cols, channels = images.shape
    return (
        sections == 4
        and dps == 2 * sections
        and micro_total == sections
        and conv_weight.shape[0] == sections
        and images_total == dps
        and rows % 2 == 0
        and cols % 2 == 0
        and (rows * cols) % 64 == 0
        and channels == 512
    )


def solution(mesh):
    in_specs = (
        P(None, "dp", None, None, None),
        P(None, "dp"),
        P(),
        P("section", None, None, None, None),
        P("section", None),
        P("section", None),
        P(None, "dp", None, None, None),
    )
    out_specs = (
        P("section", "dp", None, None, None),
        P("section", "dp", None, None, None),
        P("section", "dp", None, None, None),
        P("section", "dp"),
        P("section", "dp"),
    )
    sections, dps = mesh.shape["section"], mesh.shape["dp"]

    def program(images, image_group, group_size, conv_weight, bn_gain, bn_bias, cotangent):
        plan = plane_shards if fits_plane_plan(images, conv_weight, sections, dps) else pipeline_shards
        sharded = jax.shard_map(plan, mesh=mesh, in_specs=in_specs, out_specs=out_specs, check_vma=False)
        return sharded(images, image_group, group_size, conv_weight, bn_gain, bn_bias, cotangent)

    return program
```

```python
import math
from functools import partial

import jax
import jax.numpy as jnp
import numpy as np
from jax import lax
from jax.experimental import pallas as pl
from jax.experimental.pallas import tpu as pltpu
from jax.sharding import PartitionSpec as P

CONVS = 2
BACK_FLOPS = (6 * 10**9, 6 * 10**9, 6 * 10**9, 0)
PICK_FLOPS = 4 * 10**9
COT_LAYER = 2
INPUT_FLOPS = 4000000000


eps = 1e-05


def from_behind(x, axis, by):
    peers = lax.axis_size(axis)
    pairs = [(i, i + by) for i in range(peers) if 0 <= i + by < peers]
    return lax.ppermute(x, axis, pairs)


def canvas_mask(image_group, group_size, canvas_rows, canvas_cols):
    groups_n = group_size.shape[0]
    onehot = image_group[..., None] == jnp.arange(groups_n, dtype=jnp.int32)
    height = jnp.sum(jnp.where(onehot, group_size[:, 0], 0), axis=-1)
    breadth = jnp.sum(jnp.where(onehot, group_size[:, 1], 0), axis=-1)
    inside_rows = jnp.arange(canvas_rows, dtype=jnp.int32)[:, None] < height[..., None, None]
    inside_cols = jnp.arange(canvas_cols, dtype=jnp.int32)[None, :] < breadth[..., None, None]
    return (inside_rows & inside_cols).astype(jnp.float32)[..., None]


def window_pool(hidden):
    frames, height, breadth, channels = hidden.shape
    blocks = hidden.reshape(frames, height // 2, 2, breadth // 2, 2, channels)
    window_max = jnp.max(blocks, axis=(2, 4), keepdims=True)
    raised = jnp.exp(blocks - window_max)
    weights = raised / jnp.sum(raised, axis=(2, 4), keepdims=True)
    pooled = jnp.sum(weights * blocks, axis=(2, 4), keepdims=True)
    return (weights * pooled).reshape(frames, height, breadth, channels)


def activate(pre_act, inside, pooling):
    hidden = jax.nn.silu(pre_act) * inside
    return jnp.where(pooling, window_pool(hidden) * inside, hidden)


def conv_forward(layer_in, weight):
    return lax.conv_general_dilated(
        layer_in,
        weight,
        (1, 1),
        "SAME",
        dimension_numbers=("NHWC", "IHWO", "NHWC"),
        preferred_element_type=jnp.float32,
    )


def conv_data_back(grad_pre, weight):
    flipped = weight[:, ::-1, ::-1, :]
    return lax.conv_general_dilated(
        grad_pre,
        flipped,
        (1, 1),
        "SAME",
        dimension_numbers=("NHWC", "OHWI", "NHWC"),
        preferred_element_type=jnp.float32,
    )


def weight_back(layer_in, grad_pre):
    height = layer_in.shape[1]
    breadth = layer_in.shape[2]
    padded = jnp.pad(layer_in, ((0, 0), (1, 1), (1, 1), (0, 0)))
    pieces = []
    for tap_row in range(3):
        for tap_col in range(3):
            window = padded[:, tap_row : tap_row + height, tap_col : tap_col + breadth, :]
            pieces.append(
                jnp.einsum("nhwi,nhwo->io", window, grad_pre, preferred_element_type=jnp.float32)
            )
    return jnp.stack(pieces, axis=1).reshape(layer_in.shape[3], 3, 3, grad_pre.shape[3])


def layer_forward(layer_in, weight, gain_row, bias_row, inside, pooling):
    pre_norm = conv_forward(layer_in, weight)
    sums = lax.psum(
        (
            jnp.sum(pre_norm * inside, axis=(0, 1, 2)),
            jnp.sum(pre_norm * pre_norm * inside, axis=(0, 1, 2)),
            jnp.sum(inside),
        ),
        "dp",
    )
    pixel_total = sums[2]
    mean_val = sums[0] / pixel_total
    scale_inv = lax.rsqrt(sums[1] / pixel_total - mean_val * mean_val + eps)
    pre_act = (pre_norm - mean_val) * scale_inv * gain_row + bias_row
    hidden = activate(pre_act, inside, pooling)
    return (pre_norm, mean_val, scale_inv, pixel_total, hidden)


def layer_backward(
    grad_out,
    layer_in,
    pre_norm,
    mean_val,
    scale_inv,
    pixel_total,
    weight,
    gain_row,
    bias_row,
    inside,
    pooling,
):
    normed = (pre_norm - mean_val) * scale_inv
    pre_act = normed * gain_row + bias_row
    hidden_out, pullback = jax.vjp(partial(activate, inside=inside, pooling=pooling), pre_act)
    grad_act = pullback(grad_out)[0]
    sums = lax.psum(
        (jnp.sum(grad_act, axis=(0, 1, 2)), jnp.sum(grad_act * normed, axis=(0, 1, 2))), "dp"
    )
    shift_term = sums[0] / pixel_total
    slope_term = sums[1] / pixel_total
    grad_pre = (
        inside * scale_inv * gain_row * (grad_act - shift_term - normed * slope_term)
    ).astype(jnp.bfloat16)
    weight_term = weight_back(layer_in, grad_pre)
    grad_in = conv_data_back(grad_pre, weight).astype(jnp.bfloat16)
    return (grad_in, weight_term, sums[1], sums[0])


def pipeline_shards(images, image_group, group_size, conv_weight, bn_gain, bn_bias, cotangent):
    section_index = lax.axis_index("section")
    sections = lax.axis_size("section")
    micro_total = images.shape[0]
    channels = conv_weight.shape[1]
    inside_all = canvas_mask(image_group, group_size, images.shape[2], images.shape[3])
    ticks = micro_total + sections - 1
    weight = conv_weight[0]
    gain_row = bn_gain[0]
    bias_row = bn_bias[0]
    pool_here = section_index == CONVS - 1
    received = jnp.zeros(images.shape[1:], jnp.bfloat16)
    kept_in, kept_pre, kept_mean, kept_scale, kept_total, finished = ([], [], [], [], [], [])
    for tick in range(ticks):
        micro_pos = jnp.clip(tick - section_index, 0, micro_total - 1)
        inside = inside_all[micro_pos]
        fresh = (images[micro_pos].astype(jnp.float32) * inside).astype(jnp.bfloat16)
        layer_in = jnp.where(section_index == 0, fresh, received)
        pre_norm, mean_val, scale_inv, pixel_total, hidden = layer_forward(
            layer_in, weight, gain_row, bias_row, inside, pool_here
        )
        sent = hidden.astype(jnp.bfloat16)
        if tick < ticks - 1:
            received = from_behind(sent, "section", 1)
        kept_in.append(layer_in)
        kept_pre.append(pre_norm)
        kept_mean.append(mean_val)
        kept_scale.append(scale_inv)
        kept_total.append(pixel_total)
        finished.append(sent)
    stack_in = jnp.stack(kept_in)
    stack_pre = jnp.stack(kept_pre)
    stack_mean = jnp.stack(kept_mean)
    stack_scale = jnp.stack(kept_scale)
    stack_total = jnp.stack(kept_total)
    returned = jnp.zeros(images.shape[1:], jnp.bfloat16)
    weight_sum = jnp.zeros(conv_weight.shape[1:], jnp.float32)
    gain_sum = jnp.zeros((channels,), jnp.float32)
    bias_sum = jnp.zeros((channels,), jnp.float32)
    input_list = []
    for tick in range(ticks):
        micro_raw = tick - (sections - 1 - section_index)
        valid = ((micro_raw >= 0) & (micro_raw < micro_total)).astype(jnp.float32)
        micro_pos = jnp.clip(micro_raw, 0, micro_total - 1)
        forward_tick = jnp.clip(micro_pos + section_index, 0, ticks - 1)
        inside = inside_all[micro_pos]
        grad_out = jnp.where(
            section_index == sections - 1,
            cotangent[micro_pos].astype(jnp.float32),
            returned.astype(jnp.float32),
        )
        grad_in, weight_term, gain_term, bias_term = layer_backward(
            grad_out,
            stack_in[forward_tick],
            stack_pre[forward_tick],
            stack_mean[forward_tick],
            stack_scale[forward_tick],
            stack_total[forward_tick],
            weight,
            gain_row,
            bias_row,
            inside,
            pool_here,
        )
        weight_sum = weight_sum + valid * weight_term
        gain_sum = gain_sum + valid * gain_term
        bias_sum = bias_sum + valid * bias_term
        if tick < ticks - 1:
            returned = from_behind(grad_in, "section", -1)
        input_list.append((grad_in.astype(jnp.float32) * inside).astype(jnp.bfloat16))
    out_stack = jnp.stack(finished[sections - 1 :], axis=0)
    grad_stack = jnp.stack(input_list[sections - 1 :], axis=0)
    out_back, grad_back = (
        lax.all_to_all(out_stack, "section", split_axis=0, concat_axis=1, tiled=True),
        lax.all_to_all(grad_stack, "section", split_axis=0, concat_axis=1, tiled=True),
    )
    activations = out_back[:, sections - 1 : sections]
    input_grad = grad_back[:, 0:1]
    weight_grad = lax.psum_scatter(weight_sum[None], "dp", scatter_dimension=1, tiled=True)
    share = channels // lax.axis_size("dp")
    gain_grad = lax.dynamic_slice_in_dim(gain_sum, lax.axis_index("dp") * share, share)[None]
    bias_grad = lax.dynamic_slice_in_dim(bias_sum, lax.axis_index("dp") * share, share)[None]
    return (activations, input_grad, weight_grad, gain_grad, bias_grad)


AXES = ("section", "dp")
TAPS = 9
VMEM_LIMIT = 24 * 1024 * 1024
META_ROWS = 16
LANES = 128
ROW_AT, COL_AT, FRAME_AT = 6, 7, 8
NT = (((1,), (1,)), ((), ()))


def place():
    dp_index = lax.axis_index("dp")
    return lax.axis_index("section"), dp_index // 2, dp_index % 2


def peer_order():
    return [(k, j) for j in range(2) for k in range(4)]


def slice_at(section, core, k, j):
    return (core ^ j) * lax.axis_size("section") + (section ^ k)


def send(x, target):
    sections = lax.axis_size("section")
    dps = lax.axis_size("dp")
    pairs = []
    for s in range(sections):
        for d in range(dps):
            ts, tz, tc = target(s, d // 2, d % 2)
            pairs.append((s * dps + d, ts * dps + tz * 2 + tc))
    return lax.ppermute(x, AXES, pairs)


def to_section(x, k):
    return send(x, lambda s, z, c: (s ^ k, z, c))


def to_plane(x, k):
    return send(x, lambda s, z, c: (s, z ^ k, c))


def to_core(x):
    return send(x, lambda s, z, c: (s, z, c ^ 1))


def spread(blocks, move, *beside):
    moved = lax.optimization_barrier(([move(blocks[k], k) for k in (1, 2, 3)], beside))[0]
    return [blocks[0]] + moved


def with_core(blocks):
    return blocks + [to_core(x) for x in blocks]


def after(x, *first):
    return lax.optimization_barrier((x, first))[0]


def grid_facts(frames, rows, cols):
    at = np.arange(frames * rows * cols)
    col = at % cols
    row = (at // cols) % rows
    facts = [row > 0, row < rows - 1, col > 0, col < cols - 1, col % 2 == 0, row % 2 == 0, row, col]
    facts = facts + [at // (rows * cols) == frame for frame in range(frames)]
    return jnp.asarray(np.stack(facts).astype(np.float32))


def shift(x, by):
    length = x.shape[1]
    return pltpu.roll(x, (-by) % length, 1) if by % length else x


def row_ok(facts, d):
    return facts[0:1, :] if d < 0 else facts[1:2, :]


def col_ok(facts, d):
    return facts[2:3, :] if d < 0 else facts[3:4, :]


def sum_taps(taps_ref, facts, cols):
    ch = taps_ref.shape[0] // TAPS
    total = None
    for dx in (-1, 0, 1):
        column = None
        for dy in (-1, 0, 1):
            tap = (dy + 1) * 3 + dx + 1
            piece = taps_ref[tap * ch : (tap + 1) * ch, :]
            if dy:
                piece = shift(piece, dy * cols) * row_ok(facts, dy)
            column = piece if column is None else column + piece
        if dx:
            column = shift(column, dx) * col_ok(facts, dx)
        total = column if total is None else total + column
    return total


def spread_taps(grad, moved_ref, base, facts, cols):
    ch = grad.shape[0]
    facts = facts[:4, :].astype(grad.dtype)
    for dx in (-1, 0, 1):
        column = shift(grad, -dx) * col_ok(facts, -dx) if dx else grad
        for dy in (-1, 0, 1):
            piece = shift(column, -dy * cols) * row_ok(facts, -dy) if dy else column
            at = base + ((dy + 1) * 3 + dx + 1) * ch
            moved_ref[at : at + ch, :] = piece


def corner_sum(x, cols):
    x = x + shift(x, 1)
    return x + shift(x, cols)


def from_corner(x, facts, cols):
    x = jnp.where(facts[4:5, :] > 0.5, x, shift(x, -1))
    return jnp.where(facts[5:6, :] > 0.5, x, shift(x, -cols))


def lane_sum(x):
    return jnp.sum(x, axis=1, keepdims=True)


def normalise(pre, inside):
    count = lane_sum(inside)
    mean = lane_sum(pre * inside) / count
    square = lane_sum(pre * pre * inside) / count
    scale = lax.rsqrt(square - mean * mean + eps)
    return (pre - mean) * scale, scale


def hidden_of(normed, gain, bias, inside, facts, cols, pooling):
    pre_act = normed * gain + bias
    hidden = pre_act * jax.nn.sigmoid(pre_act) * inside
    if pooling:
        raised = jnp.exp(hidden)
        total = corner_sum(raised, cols)
        pooled = corner_sum(raised * hidden, cols) / total
        hidden = raised * from_corner(pooled / total, facts, cols) * inside
    return hidden


def norm_back(grad, normed, scale, gain, bias, inside, facts, cols, pooling):
    pre_act = normed * gain + bias
    gate = jax.nn.sigmoid(pre_act)
    if pooling:
        hidden = pre_act * gate * inside
        raised = jnp.exp(hidden)
        out = grad * inside
        total = 1.0 / corner_sum(raised, cols)
        pooled = corner_sum(raised * hidden, cols) * total
        d_pooled = corner_sum(raised * out, cols) * total
        by_out = from_corner(pooled * total, facts, cols)
        by_hidden = from_corner(d_pooled * total, facts, cols)
        rest = from_corner(d_pooled * total * (1.0 - 2.0 * pooled), facts, cols)
        grad = raised * (out * by_out + hidden * by_hidden + rest)
    grad_act = grad * inside * gate * (1.0 + pre_act * (1.0 - gate))
    count = lane_sum(inside)
    shift_sum = lane_sum(grad_act)
    slope_sum = lane_sum(grad_act * normed)
    grad_pre = inside * (scale * gain) * (grad_act - shift_sum / count - normed * (slope_sum / count))
    return grad_pre.astype(jnp.bfloat16), shift_sum, slope_sum


def assemble(blocks, full_ref):
    section, _, core = place()
    ch = blocks[0].shape[0]
    for (k, j), block in zip(peer_order(), blocks):
        at = pl.multiple_of(slice_at(section, core, k, j) * ch, ch)
        full_ref[pl.ds(at, ch), :] = block[...]


def assemble_frames(blocks, full_ref, rows, lanes):
    _, plane, core = place()
    size = rows.stop - rows.start
    for (k, j), block in zip(peer_order(), blocks):
        frame = (plane ^ k) * 2 + (core ^ j)
        full_ref[pl.ds(pl.multiple_of(frame * size, size), size), :] = block[rows, lanes]


def start_all(copies):
    for copy in copies:
        copy.start()
    return copies


def wait_all(copies):
    for copy in copies:
        copy.wait()


def tap_products(weight, full_ref, taps_ref, by_cells):
    length = taps_ref.shape[1]
    step = 512 if length % 512 == 0 else length
    for at in range(0, length, step):
        if by_cells:
            taps_ref[:, at : at + step] = lax.dot_general(
                weight, full_ref[at : at + step, :], NT, preferred_element_type=jnp.float32
            )
        else:
            taps_ref[:, at : at + step] = jnp.dot(
                weight, full_ref[:, at : at + step], preferred_element_type=jnp.float32
            )


def pick_layer(layer, sources, start, target, sem):
    section, _, _ = place()
    rows = pl.ds(start, target.shape[0])
    for k, source in enumerate(sources):

        @pl.when((section ^ layer) == k)
        def _():
            pltpu.make_async_copy(source.at[rows], target, sem).start()

    return pltpu.make_async_copy(sources[0].at[rows], target, sem)


def take_layer(layer, sources, target):
    section, _, _ = place()
    for k, source in enumerate(sources):

        @pl.when((section ^ layer) == k)
        def _():
            target[...] = source[...]


def affine(meta, ch):
    parts = meta[:, :LANES].astype(jnp.float32).T[:ch]
    return (
        parts[:, 0:1] + parts[:, 1:2] + parts[:, 2:3],
        parts[:, 3:4] + parts[:, 4:5] + parts[:, 5:6],
    )


def plane_inside(metas, facts):
    frames = metas.shape[0] // META_ROWS
    extents = []
    for line in (0, 1):
        total = None
        for f in range(frames):
            at = f * META_ROWS + line
            extent = metas[at : at + 1, 0:1].astype(jnp.float32) * facts[FRAME_AT + f : FRAME_AT + f + 1, :]
            total = extent if total is None else total + extent
        extents.append(total)
    on = (facts[ROW_AT : ROW_AT + 1, :] < extents[0]) & (facts[COL_AT : COL_AT + 1, :] < extents[1])
    return jnp.where(on, 1.0, 0.0)


def frames_kernel(dims, group_table, size_table, images, *refs):
    payloads, (image_in, groups, sizes, sems) = refs[:4], refs[4:]
    copies = start_all(
        [
            pltpu.make_async_copy(group_table, groups, sems.at[0]),
            pltpu.make_async_copy(size_table, sizes, sems.at[1]),
            pltpu.make_async_copy(images, image_in, sems.at[2]),
        ]
    )
    _, plane, _ = place()
    rows, cols = dims
    cells = rows * cols
    at = lax.broadcasted_iota(jnp.int32, (cells, LANES), 0).astype(jnp.float32)
    row = jnp.floor((at + 0.5) * (1.0 / cols))
    col = at - row * cols
    channels = images.shape[2]
    line = lax.broadcasted_iota(jnp.int32, (META_ROWS, channels), 0)
    wait_all(copies)
    for k in range(4):
        micro = plane ^ k
        group = groups[0, micro]
        height = sizes[0, 0]
        breadth = sizes[1, 0]
        for g in range(1, sizes.shape[1]):
            height = jnp.where(group == g, sizes[0, g], height)
            breadth = jnp.where(group == g, sizes[1, g], breadth)
        height = height.astype(jnp.float32)
        breadth = breadth.astype(jnp.float32)
        on = jnp.where((row < height) & (col < breadth), 1.0, 0.0)
        image = image_in[micro]
        for c in range(0, channels, LANES):
            piece = image[:, c : c + LANES].astype(jnp.float32) * on
            payloads[k][:cells, c : c + LANES] = piece.astype(jnp.bfloat16)
        payloads[k][cells:, :] = jnp.where(line == 0, height, breadth).astype(jnp.bfloat16)


def cot_slice_kernel(cots, out, cot_in, sems):
    copy = pltpu.make_async_copy(cots, cot_in, sems.at[0])
    copy.start()
    section, _, _ = place()
    micros, cells, channels = cots.shape
    half = channels // 2
    tile = section // 2 * LANES
    odd = section % 2 == 1
    lane = lax.broadcasted_iota(jnp.int32, (cells, LANES), 1)
    copy.wait()
    for micro in range(micros):
        low = cot_in[micro, :, pl.ds(pl.multiple_of(tile, LANES), LANES)].astype(jnp.float32)
        high = cot_in[micro, :, pl.ds(pl.multiple_of(half + tile, LANES), LANES)].astype(jnp.float32)
        low = jnp.where(odd, pltpu.roll(low, LANES // 2, 1), low)
        high = jnp.where(odd, high, pltpu.roll(high, LANES // 2, 1))
        both = jnp.where(lane < LANES // 2, low, high).astype(jnp.bfloat16)
        out[micro * cells : (micro + 1) * cells, :] = both


def cot_kernel(own, other, pick, out, full):
    _, _, core = place()
    cells = full.shape[0] // 8
    for n in range(4):
        for j, block in enumerate((own, other)):
            at = pl.multiple_of((2 * n + (core ^ j)) * cells, cells)
            full[pl.ds(at, cells), :] = block[n * cells : (n + 1) * cells, :]
    out[...] = lax.dot_general(pick[...], full[...], NT, preferred_element_type=jnp.float32).astype(
        jnp.bfloat16
    )


def pack_kernel(gain, bias, weight, *refs):
    outs, (columns, turned, tables, sems) = refs[:4], refs[4:]
    section, _, core = place()
    width = columns.shape[2]
    ch = width // 4
    start = pl.multiple_of(core * width, width)
    copies = start_all(
        [
            pltpu.make_async_copy(weight.at[tap, :, pl.ds(start, width)], columns.at[tap], sems.at[tap])
            for tap in range(TAPS)
        ]
    )
    table_copies = start_all(
        [
            pltpu.make_async_copy(gain, tables.at[0], sems.at[TAPS]),
            pltpu.make_async_copy(bias, tables.at[1], sems.at[TAPS + 1]),
        ]
    )
    for tap in range(TAPS):
        copies[tap].wait()
        turned[tap % 2] = columns[tap].T
        for k, out in enumerate(outs):
            rows = pl.ds(pl.multiple_of((section ^ k) * ch, ch), ch)
            out[tap * ch : (tap + 1) * ch, :] = turned[tap % 2, rows, :]
    wait_all(table_copies)
    for k, out in enumerate(outs):
        lines = []
        tile = pl.multiple_of(start + (section ^ k) // 2 * LANES, LANES)
        odd = (section ^ k) % 2 == 1
        for m in range(2):
            line = tables[m, :, pl.ds(tile, LANES)]
            line = jnp.where(odd, pltpu.roll(line, ch, 1), line)
            for _ in range(3):
                part = line.astype(jnp.bfloat16).astype(jnp.float32)
                lines.append(part)
                line = line - part
        lines.append(jnp.zeros((META_ROWS - len(lines), LANES), jnp.float32))
        out[TAPS * ch :, :] = jnp.zeros((META_ROWS, out.shape[1]), jnp.bfloat16)
        out[TAPS * ch :, :LANES] = jnp.concatenate(lines, axis=0).astype(jnp.bfloat16)


def pick_kernel(layer, *refs):
    sources, (out, sems) = refs[:4], refs[4:]
    pick_layer(layer, sources, 0, out, sems.at[0]).wait()


def forward_kernel(dims, layer, first, picks, pooling, *refs):
    blocks, weights, rest = refs[:8], refs[8 : 12 if picks else 9], refs[12 if picks else 9 :]
    rows, cols = dims
    cells = rows * cols
    if first:
        facts, hidden, kept, full_out, inside_out, full, taps, stage, weight, metas, sems = rest
    elif picks:
        inside, facts, hidden, kept, full_out, full, taps, stage, weight, sems = rest
    else:
        inside, facts, hidden, kept, full_out, full, taps, stage, sems = rest
        (weight,) = weights
    if first:
        take_layer(layer, weights, weight)
    elif picks:
        copy = pick_layer(layer, weights, 0, weight, sems.at[2])
    facts_now = facts[...]
    if first:
        channels = full.shape[1]
        assemble_frames(blocks, full, slice(0, cells), slice(0, channels))
    else:
        assemble(blocks, full)
    full_copy = pltpu.make_async_copy(full, full_out, sems.at[0])
    full_copy.start()
    if first:
        assemble_frames(blocks, metas, slice(cells, cells + META_ROWS), slice(0, channels))
        inside_now = plane_inside(metas, facts_now)
        inside_out[...] = inside_now
    else:
        inside_now = inside[...]
    if picks and not first:
        copy.wait()
    ch = hidden.shape[0]
    tap_products(weight[: TAPS * ch, :], full, taps, first)
    pre = sum_taps(taps, facts_now, cols)
    normed, scale = normalise(pre, inside_now)
    length = normed.shape[1]
    stage[:, :length] = normed
    stage[:, length:] = jnp.broadcast_to(scale, (ch, LANES))
    kept_copy = pltpu.make_async_copy(stage, kept, sems.at[1])
    kept_copy.start()
    gain, bias = affine(weight[TAPS * ch :, :], ch)
    hidden[...] = hidden_of(normed, gain, bias, inside_now, facts_now, cols, pooling).astype(jnp.bfloat16)
    full_copy.wait()
    kept_copy.wait()


def turn_kernel(dims, layer, pooling, *refs):
    blocks, (weight, cot_in, inside, facts) = refs[:8], refs[8:12]
    hidden_out, full_out, grad_pre, sums, full, taps, hidden, sems = refs[12:]
    cols = dims[1]
    assemble(blocks, full)
    full_copy = pltpu.make_async_copy(full, full_out, sems.at[1])
    full_copy.start()
    ch = grad_pre.shape[0]
    tap_products(weight[: TAPS * ch, :], full, taps, False)
    facts_now, inside_now = facts[...], inside[...]
    pre = sum_taps(taps, facts_now, cols)
    normed, scale = normalise(pre, inside_now)
    gain, bias = affine(weight[TAPS * ch :, :], ch)
    hidden[...] = hidden_of(normed, gain, bias, inside_now, facts_now, cols, pooling).astype(jnp.bfloat16)
    hidden_copy = pltpu.make_async_copy(hidden, hidden_out, sems.at[2])
    hidden_copy.start()
    grad_pre[...], shift_sum, slope_sum = norm_back(
        cot_in[...].astype(jnp.float32), normed, scale, gain, bias, inside_now, facts_now, cols, pooling
    )
    keep_sums(sums, shift_sum, slope_sum)
    full_copy.wait()
    hidden_copy.wait()


def keep_sums(sums, shift_sum, slope_sum):
    ch = shift_sum.shape[0]
    sums[:, :LANES] = jnp.broadcast_to(shift_sum, (ch, LANES))
    sums[:, LANES:] = jnp.broadcast_to(slope_sum, (ch, LANES))


def add_blocks(blocks):
    total = blocks[0][...].astype(jnp.float32)
    for block in blocks[1:]:
        total = total + block[...].astype(jnp.float32)
    return total


def fetch_kernel(layer, kept, *refs):
    sources, (kept_out, meta_out, sems) = refs[:4], refs[4:]
    copy = pltpu.make_async_copy(kept, kept_out, sems.at[0])
    copy.start()
    start = sources[0].shape[0] - META_ROWS
    pick_layer(layer, sources, start, meta_out, sems.at[1]).wait()
    copy.wait()


def norm_back_kernel(dims, pooling, *refs):
    blocks, (kept, meta, inside, facts, grad_pre, sums) = refs[:4], refs[4:]
    ch, length = grad_pre.shape
    grad = add_blocks(blocks).astype(jnp.bfloat16).astype(jnp.float32)
    gain, bias = affine(meta[...], ch)
    grad_pre[...], shift_sum, slope_sum = norm_back(
        grad,
        kept[:, :length],
        kept[:, length : length + 1],
        gain,
        bias,
        inside[...],
        facts[...],
        dims[1],
        pooling,
    )
    keep_sums(sums, shift_sum, slope_sum)


def weight_product(moved, full, first):
    if first:
        return jnp.dot(moved, full, preferred_element_type=jnp.float32)
    return lax.dot_general(moved, full, NT, preferred_element_type=jnp.float32)


def sums_rows(sums, ch, width):
    lines = []
    for at in (0, LANES):
        turned = sums[:, at : at + LANES].T
        lines.append(jnp.concatenate([turned, jnp.zeros((LANES, width - ch), jnp.float32)], axis=1)[0:1])
    lines.append(jnp.zeros((META_ROWS - 2, width), jnp.float32))
    return jnp.concatenate(lines, axis=0).astype(jnp.bfloat16)


def store_share(value, sums, pieces):
    rows = value.shape[0]
    width = pieces[0].shape[1]
    below = sums_rows(sums, rows // TAPS, width)
    for n, piece in enumerate(pieces):
        piece[:rows, :] = value[:, n * width : (n + 1) * width].astype(jnp.bfloat16)
        piece[rows:, :] = below


def form_share(layer, moved, full, sums, product):
    piece = product.shape[0] // 4
    value = weight_product(moved[: piece - META_ROWS, :], full[...], layer == 0)
    store_share(value, sums, [product.at[pl.ds(n * piece, piece)] for n in range(4)])


def conv_back_kernel(dims, layer, own, other, own_weights, other_weights, full_in, sums, facts, *refs):
    *outs, share, product, full, moved, weights, sems = refs
    ch = own.shape[0]
    size = moved.shape[0] // 2
    rows = pl.ds(layer * 4 * ch, 4 * ch)
    copies = start_all(
        [
            pltpu.make_async_copy(own_weights.at[rows], weights.at[:, pl.ds(0, size)], sems.at[0]),
            pltpu.make_async_copy(other_weights.at[rows], weights.at[:, pl.ds(size, size)], sems.at[1]),
        ]
    )
    full_copy = pltpu.make_async_copy(full_in, full, sems.at[2])
    full_copy.start()
    facts_now = facts[...]
    spread_taps(own[...], moved, 0, facts_now, dims[1])
    full_copy.wait()
    form_share(layer, moved, full, sums, product)
    share_copy = pltpu.make_async_copy(product, share, sems.at[3])
    share_copy.start()
    spread_taps(other[...], moved, size, facts_now, dims[1])
    for n in range(2):
        moved[n * size + TAPS * ch : (n + 1) * size, :] = jnp.zeros(
            (size - TAPS * ch, moved.shape[1]), jnp.bfloat16
        )
    wait_all(copies)
    value = jnp.dot(weights[...], moved[...], preferred_element_type=jnp.float32)
    for k, out in enumerate(outs):
        out[...] = value[k * ch : (k + 1) * ch, :].astype(jnp.bfloat16)
    share_copy.wait()


def fold_kernel(*refs):
    count = (len(refs) - 2) // 2
    shares, outs, (blocks, sems) = refs[:count], refs[count:-2], refs[-2:]
    rows = outs[0].shape[0]
    copies = start_all(
        [pltpu.make_async_copy(share, blocks.at[n], sems.at[n]) for n, share in enumerate(shares)]
    )
    for n, copy in enumerate(copies):
        copy.wait()
        value = add_blocks([blocks.at[n, pl.ds(m * rows, rows)] for m in range(blocks.shape[1] // rows)])
        outs[n][...] = value.astype(jnp.bfloat16)


def choose_kernel(*refs):
    last, others, outs = refs[0], refs[1:-4], refs[-4:]
    section, _, _ = place()
    rows = outs[0].shape[0]
    value = add_blocks([last.at[pl.ds(n * rows, rows)] for n in range(last.shape[0] // rows)])
    value = value.astype(jnp.bfloat16)
    for k, out in enumerate(outs):

        @pl.when((section ^ k) == 0)
        def _():
            out[...] = value

        for layer, other in enumerate(others, 1):

            @pl.when((section ^ k) == layer)
            def _():
                out[...] = other[...]


def turn_weights_kernel(layers, *refs):
    sources, outs, (full, turned, stage, sems) = refs[:4], refs[4:6], refs[6:]
    section, _, core = place()
    rows, channels = full.shape[1:]
    half = channels // 2
    ch = half // 4
    copies = [pick_layer(n, sources, 0, full.at[n], sems.at[n]) for n in range(layers)]
    stage[:, :, rows:] = jnp.zeros((*stage.shape[:2], stage.shape[2] - rows), jnp.bfloat16)
    for n in range(layers):
        copies[n].wait()
        turned[...] = full[n].T
        for j in range(2):
            for k in range(4):
                at = pl.multiple_of((core ^ j) * half + (section ^ k) * ch, ch)
                stage[j, n * half + k * ch : n * half + (k + 1) * ch, :rows] = turned[pl.ds(at, ch), :]
    wait_all(
        start_all([pltpu.make_async_copy(stage.at[j], outs[j], sems.at[j]) for j in range(2)])
    )


def input_kernel(*refs):
    blocks, (hidden, inside, keep, give, full, sems) = refs[:4], refs[4:]
    section, _, core = place()
    ch = hidden.shape[0]
    copy = pltpu.make_async_copy(hidden, full.at[pl.ds(0, ch)], sems.at[0])
    copy.start()
    full[ch:, :] = (add_blocks(blocks) * inside[...]).astype(jnp.bfloat16)
    copy.wait()
    rows = 2 * ch
    width = keep.shape[1]
    for j, out in enumerate((keep, give)):
        for n in range(2):
            at = pl.multiple_of((section ^ (2 * (core ^ j) + n)) * width, width)
            out[n * rows : (n + 1) * rows, :] = full[:, pl.ds(at, width)]


def pair_kernel(keep, got, *outs):
    rows = keep.shape[0] // 2
    for n, out in enumerate(outs):
        out[:rows, :] = keep[n * rows : (n + 1) * rows, :]
        out[rows:, :] = got[n * rows : (n + 1) * rows, :]


def store_maps(blocks, pick, outs, full):
    _, plane, core = place()
    ch = blocks[0].shape[0] // 4
    for m, out in enumerate(outs):
        for j in range(2):
            for n in range(2):
                for h in range(2):
                    slot = slice_at(plane ^ (2 * (core ^ j) + n), core ^ j, 0, h)
                    at = pl.multiple_of(slot * ch, ch)
                    start = (2 * h + m) * ch
                    full[m, pl.ds(at, ch), :] = blocks[2 * j + n][start : start + ch, :]
        mine = lax.dot_general(pick[...], full[m], NT, preferred_element_type=jnp.float32)
        out[...] = mine.astype(out.dtype)


def outputs_kernel(*refs):
    blocks, pick, map_blocks, map_pick, refs = refs[:8], refs[8], refs[9:13], refs[13], refs[14:]
    (weight_out, shift_out, slope_out), map_outs, (full, maps_full) = refs[:3], refs[3:5], refs[5:]
    store_maps(map_blocks, map_pick, map_outs, maps_full)
    section, plane, core = place()
    taps, rows, channels = weight_out.shape
    for tap in range(taps):
        for (k, j), block in zip(peer_order(), blocks):
            at = pl.multiple_of(slice_at(section, core, k, j) * rows, rows)
            full[tap, pl.ds(at, rows), :] = block[tap * rows : (tap + 1) * rows, :]
        weight_out[tap] = lax.dot_general(pick[...], full[tap], NT, preferred_element_type=jnp.float32)
    shift_row = jnp.zeros((1, rows), jnp.float32)
    slope_row = jnp.zeros((1, rows), jnp.float32)
    slot = plane * 2 + core
    for (k, j), block in zip(peer_order(), blocks):
        tail = block[taps * rows :, :].astype(jnp.float32)
        mine = slice_at(section, core, k, j) == slot
        shift_row = shift_row + jnp.where(mine, tail[0:1, :rows], 0.0)
        slope_row = slope_row + jnp.where(mine, tail[1:2, :rows], 0.0)
    shift_out[...] = shift_row
    slope_out[...] = slope_row


def call(
    kernel, outs, scratch, args, name, held=(), free=(), held_outs=(), loose=(), last=False, flops=0, copies=None
):
    shapes = [
        (jax.ShapeDtypeStruct if last else pltpu.HBM if n in held_outs else pltpu.VMEM)(shape, dtype)
        for n, (shape, dtype) in enumerate(outs)
    ]
    moved = sum(a.size * a.dtype.itemsize for a in args)
    moved += sum(math.prod(shape) * jnp.dtype(dtype).itemsize for shape, dtype in outs)
    spaces = [pl.ANY if n in free else pltpu.HBM if n in held else pltpu.VMEM for n in range(len(args))]
    out_spaces = [pltpu.HBM if n in held_outs else pltpu.VMEM for n in range(len(outs))]
    args = [
        a if n in loose or n in free else pltpu.with_memory_space_constraint(a, space)
        for n, (a, space) in enumerate(zip(args, spaces))
    ]
    scratch_shapes = [
        pltpu.SMEM(shape, dtype) if dtype == jnp.int32 else pltpu.VMEM(shape, dtype) for shape, dtype in scratch
    ]
    if copies is not None:
        scratch_shapes.append(pltpu.SemaphoreType.DMA((copies,)))
    return pl.pallas_call(
        kernel,
        out_shape=shapes,
        in_specs=[pl.BlockSpec(memory_space=space) for space in spaces],
        out_specs=[pl.BlockSpec(memory_space=space) for space in out_spaces],
        scratch_shapes=scratch_shapes,
        compiler_params=pltpu.CompilerParams(vmem_limit_bytes=VMEM_LIMIT),
        cost_estimate=pl.CostEstimate(flops=flops, bytes_accessed=moved, transcendentals=0),
        name=name,
    )(*args)


def plane_shards(images, image_group, group_size, conv_weight, bn_gain, bn_bias, cotangent):
    _, _, core = place()
    micro_total, _, rows, cols, channels = images.shape
    layers = lax.axis_size("section")
    last = layers - 1
    cells = rows * cols
    frames = 2 * micro_total
    length = frames * cells
    ch = channels // 8
    dims = (rows, cols)
    bf16, f32 = jnp.bfloat16, jnp.float32
    facts = grid_facts(frames, rows, cols)
    conv_flops = 2 * TAPS * ch * channels * length
    slice_rows = TAPS * ch + META_ROWS
    tap_rows = -(-TAPS * ch // LANES) * LANES

    full_map = ((channels, length), bf16)
    full_frames = ((length, channels), bf16)
    tap_scratch = ((TAPS * ch, length), f32)
    weight_slice = ((slice_rows, channels), bf16)
    map_out = ((ch, length), bf16)
    sums_out = ((ch, 2 * LANES), f32)
    kept_out = ((ch, length + LANES), f32)
    share_out = ((4 * slice_rows, 2 * ch), bf16)
    share_piece = ((slice_rows, 2 * ch), bf16)

    taps_first = conv_weight[0].transpose(1, 2, 0, 3).reshape(TAPS, channels, channels)
    packed = call(
        pack_kernel,
        [weight_slice] * 4,
        [
            ((TAPS, channels, 4 * ch), bf16),
            ((2, 4 * ch, channels), bf16),
            ((2, 1, channels), f32),
        ],
        [bn_gain, bn_bias, taps_first],
        "weight_pack",
        held=range(3),
        copies=TAPS + 2,
    )
    slices = spread(packed, to_section)

    payload = ((cells + META_ROWS, channels), bf16)
    sent = call(
        partial(frames_kernel, dims),
        [payload] * 4,
        [
            ((micro_total, cells, channels), bf16),
            (image_group.shape[::-1], jnp.int32),
            (group_size.shape[::-1], jnp.int32),
        ],
        [image_group.T, group_size.T, after(images.reshape(micro_total, cells, channels), packed)],
        "frames",
        held=range(3),
        copies=3,
    )
    frames_in = with_core(spread(sent, to_plane))

    half = (core * ch + np.arange(ch))[:, None] == np.arange(2 * ch)[None, :]
    hidden, normed, full, inside = call(
        partial(forward_kernel, dims, 0, True, True, CONVS == 1),
        [map_out, kept_out, full_frames, ((1, length), f32)],
        [
            full_frames,
            tap_scratch,
            kept_out,
            weight_slice,
            ((frames * META_ROWS, channels), bf16),
        ],
        [*frames_in, *slices, facts],
        "forward",
        held_outs=(1, 2),
        loose=(8, 9, 10, 11, 12),
        flops=conv_flops,
        copies=4,
    )
    kept, fulls = [normed], [full]
    same_core = [[2 * z + c for z in range(layers)] for c in range(2)]
    for layer in range(1, layers):
        picks = layer == COT_LAYER
        weights = slices if picks else call(
            partial(pick_kernel, layer),
            [weight_slice],
            [],
            after(slices, hidden),
            "pick",
            flops=PICK_FLOPS,
            held=range(4),
            copies=1,
        )
        beside = [] if picks else [*weights]
        if layer == 1:
            turned = call(
                partial(turn_weights_kernel, layers),
                [((layers * 4 * ch, tap_rows), bf16)] * 2,
                [
                    ((layers, TAPS * ch, channels), bf16),
                    ((channels, TAPS * ch), bf16),
                    ((2, layers * 4 * ch, tap_rows), bf16),
                ],
                after(slices, hidden),
                "turn_weights",
                held=range(4),
                held_outs=(0, 1),
                copies=layers,
            )
            beside.append(turned)
        if layer == COT_LAYER - 1:
            (cot_slots,) = call(
                cot_slice_kernel,
                [((micro_total * cells, LANES), bf16)],
                [((micro_total, cells, channels), bf16)],
                [after(cotangent.reshape(micro_total, cells, channels), hidden)],
                "cot_slices",
                held=(0,),
                copies=1,
            )
            beside.append(cot_slots)
        if layer == COT_LAYER:
            cot_slots = after(cot_slots, hidden)
            cots = lax.all_to_all(cot_slots, "dp", 0, 0, tiled=True, axis_index_groups=same_core)
        if layer == 2:
            turned = [turned[0], to_core(after(turned[1], hidden))]
        if layer == last:
            cots = after(cots, hidden)
            (cot,) = call(
                cot_kernel,
                [map_out],
                [((length, LANES), bf16)],
                [cots, to_core(cots), half.astype(bf16)],
                "cotangent",
                loose=(0, 1, 2),
            )
            beside.append(cot)
        blocks = [hidden] + [to_section(hidden, k) for k in (1, 2, 3)]
        blocks[3] = after(blocks[3], *beside)
        blocks = with_core(blocks)
        if layer < last:
            hidden, normed, full = call(
                partial(forward_kernel, dims, layer, False, picks, layer == CONVS - 1),
                [map_out, kept_out, full_map],
                [full_map, tap_scratch, kept_out] + [weight_slice] * picks,
                [*blocks, *weights, inside, facts],
                "forward",
                held=range(8, 12) if picks else (),
                held_outs=(1, 2),
                loose=(12, 13) if picks else (9, 10),
                flops=conv_flops,
                copies=3,
            )
            kept.append(normed)
        else:
            activation, full, grad_pre, sums = call(
                partial(turn_kernel, dims, last, last == CONVS - 1),
                [map_out, full_map, map_out, sums_out],
                [full_map, tap_scratch, map_out],
                [*blocks, *weights, cot, inside, facts],
                "turn",
                held_outs=(0, 1),
                loose=(10, 11),
                flops=conv_flops,
                copies=3,
            )
        fulls.append(full)

    shares = [None] * layers
    for layer in range(last, -1, -1):
        *parts, share = call(
            partial(conv_back_kernel, dims, layer),
            [map_out] * 4 + [share_out],
            [
                share_out,
                full_map if layer else full_frames,
                ((2 * tap_rows, length), bf16),
                ((4 * ch, 2 * tap_rows), bf16),
            ],
            [grad_pre, to_core(grad_pre), *turned, fulls[layer], sums, facts],
            "conv_back",
            held=(2, 4),
            free=(3,),
            held_outs=(4,),
            loose=(5, 6),
            flops=BACK_FLOPS[layer],
            copies=4,
        )
        if layer < last:
            share = after(share, shares[layer + 1])
        shares[layer] = lax.all_to_all(share, "dp", 0, 0, tiled=True, axis_index_groups=same_core)
        if layer:
            held = call(
                partial(fetch_kernel, layer - 1),
                [kept_out, ((META_ROWS, channels), bf16)],
                [],
                [after(kept[layer - 1], parts), *slices],
                "fetch",
                held=range(5),
                copies=2,
            )
            blocks = spread(parts, to_section, held)
            grad_pre, sums = call(
                partial(norm_back_kernel, dims, layer - 1 == CONVS - 1),
                [map_out, sums_out],
                [],
                [*blocks, *held, inside, facts],
                "norm_back",
                loose=(6, 7),
            )
    blocks = spread(parts, to_section)
    keep, give = call(
        input_kernel,
        [((4 * ch, 2 * cells), bf16)] * 2,
        [((2 * ch, length), bf16)],
        [*blocks, activation, inside],
        "input",
        flops=INPUT_FLOPS,
        held=(4,),
        loose=(5,),
        copies=1,
    )
    maps = call(pair_kernel, [((4 * ch, 2 * cells), bf16)] * 2, [], [keep, to_core(give)], "pair")
    maps = [send(x, lambda s, z, c, n=n: (z, s ^ (2 * c + n), c)) for n, x in enumerate(maps)]
    folded = call(
        fold_kernel,
        [share_piece] * last,
        [((last, 4 * slice_rows, 2 * ch), bf16)],
        shares[1:],
        "fold",
        held=range(last),
        copies=last,
    )
    chosen = call(
        choose_kernel,
        [share_piece] * 4,
        [],
        [shares[0], *folded],
        "choose",
        loose=(0,),
    )
    pick = (core * cells + np.arange(cells))[:, None] == np.arange(2 * cells)[None, :]
    map_pick = pick.astype(bf16)
    pick = (core * ch + np.arange(ch))[:, None] == np.arange(2 * ch)[None, :]
    weight_grad, bias_grad, gain_grad, activations, input_grad = call(
        outputs_kernel,
        [((TAPS, ch, channels), f32), ((1, ch), f32), ((1, ch), f32)] + [((cells, channels), bf16)] * 2,
        [((TAPS, channels, 2 * ch), bf16), ((2, channels, 2 * cells), bf16)],
        [
            *with_core([chosen[0]] + [to_section(chosen[k], k) for k in (1, 2, 3)]),
            pick.astype(bf16),
            *with_core(after(maps, chosen)),
            map_pick,
        ],
        "outputs",
        loose=(8, 13),
        last=True,
    )
    weight_grad = weight_grad.reshape(3, 3, ch, channels).transpose(2, 0, 1, 3)[None]
    return (
        activations.reshape(1, 1, rows, cols, channels),
        input_grad.reshape(1, 1, rows, cols, channels),
        weight_grad,
        gain_grad,
        bias_grad,
    )


def fits_plane_plan(images, conv_weight, sections, dps):
    micro_total, images_total, rows, cols, channels = images.shape
    return (
        sections == 4
        and dps == 2 * sections
        and micro_total == sections
        and conv_weight.shape[0] == sections
        and images_total == dps
        and rows % 2 == 0
        and cols % 2 == 0
        and (rows * cols) % 64 == 0
        and channels == 512
    )


def solution(mesh):
    in_specs = (
        P(None, "dp", None, None, None),
        P(None, "dp"),
        P(),
        P("section", None, None, None, None),
        P("section", None),
        P("section", None),
        P(None, "dp", None, None, None),
    )
    out_specs = (
        P("section", "dp", None, None, None),
        P("section", "dp", None, None, None),
        P("section", "dp", None, None, None),
        P("section", "dp"),
        P("section", "dp"),
    )
    sections, dps = mesh.shape["section"], mesh.shape["dp"]

    def program(images, image_group, group_size, conv_weight, bn_gain, bn_bias, cotangent):
        plan = plane_shards if fits_plane_plan(images, conv_weight, sections, dps) else pipeline_shards
        sharded = jax.shard_map(plan, mesh=mesh, in_specs=in_specs, out_specs=out_specs, check_vma=False)
        return sharded(images, image_group, group_size, conv_weight, bn_gain, bn_bias, cotangent)

    return program
```

```python
import math
from functools import partial

import jax
import jax.numpy as jnp
import numpy as np
from jax import lax
from jax.experimental import pallas as pl
from jax.experimental.pallas import tpu as pltpu
from jax.sharding import PartitionSpec as P

CONVS = 2
BACK_FLOPS = (6 * 10**9, 6 * 10**9, 6 * 10**9, 0)
PICK_FLOPS = 2 * 10**9
COT_LAYER = 2
INPUT_FLOPS = 4000000000


eps = 1e-05


def from_behind(x, axis, by):
    peers = lax.axis_size(axis)
    pairs = [(i, i + by) for i in range(peers) if 0 <= i + by < peers]
    return lax.ppermute(x, axis, pairs)


def canvas_mask(image_group, group_size, canvas_rows, canvas_cols):
    groups_n = group_size.shape[0]
    onehot = image_group[..., None] == jnp.arange(groups_n, dtype=jnp.int32)
    height = jnp.sum(jnp.where(onehot, group_size[:, 0], 0), axis=-1)
    breadth = jnp.sum(jnp.where(onehot, group_size[:, 1], 0), axis=-1)
    inside_rows = jnp.arange(canvas_rows, dtype=jnp.int32)[:, None] < height[..., None, None]
    inside_cols = jnp.arange(canvas_cols, dtype=jnp.int32)[None, :] < breadth[..., None, None]
    return (inside_rows & inside_cols).astype(jnp.float32)[..., None]


def window_pool(hidden):
    frames, height, breadth, channels = hidden.shape
    blocks = hidden.reshape(frames, height // 2, 2, breadth // 2, 2, channels)
    window_max = jnp.max(blocks, axis=(2, 4), keepdims=True)
    raised = jnp.exp(blocks - window_max)
    weights = raised / jnp.sum(raised, axis=(2, 4), keepdims=True)
    pooled = jnp.sum(weights * blocks, axis=(2, 4), keepdims=True)
    return (weights * pooled).reshape(frames, height, breadth, channels)


def activate(pre_act, inside, pooling):
    hidden = jax.nn.silu(pre_act) * inside
    return jnp.where(pooling, window_pool(hidden) * inside, hidden)


def conv_forward(layer_in, weight):
    return lax.conv_general_dilated(
        layer_in,
        weight,
        (1, 1),
        "SAME",
        dimension_numbers=("NHWC", "IHWO", "NHWC"),
        preferred_element_type=jnp.float32,
    )


def conv_data_back(grad_pre, weight):
    flipped = weight[:, ::-1, ::-1, :]
    return lax.conv_general_dilated(
        grad_pre,
        flipped,
        (1, 1),
        "SAME",
        dimension_numbers=("NHWC", "OHWI", "NHWC"),
        preferred_element_type=jnp.float32,
    )


def weight_back(layer_in, grad_pre):
    height = layer_in.shape[1]
    breadth = layer_in.shape[2]
    padded = jnp.pad(layer_in, ((0, 0), (1, 1), (1, 1), (0, 0)))
    pieces = []
    for tap_row in range(3):
        for tap_col in range(3):
            window = padded[:, tap_row : tap_row + height, tap_col : tap_col + breadth, :]
            pieces.append(
                jnp.einsum("nhwi,nhwo->io", window, grad_pre, preferred_element_type=jnp.float32)
            )
    return jnp.stack(pieces, axis=1).reshape(layer_in.shape[3], 3, 3, grad_pre.shape[3])


def layer_forward(layer_in, weight, gain_row, bias_row, inside, pooling):
    pre_norm = conv_forward(layer_in, weight)
    sums = lax.psum(
        (
            jnp.sum(pre_norm * inside, axis=(0, 1, 2)),
            jnp.sum(pre_norm * pre_norm * inside, axis=(0, 1, 2)),
            jnp.sum(inside),
        ),
        "dp",
    )
    pixel_total = sums[2]
    mean_val = sums[0] / pixel_total
    scale_inv = lax.rsqrt(sums[1] / pixel_total - mean_val * mean_val + eps)
    pre_act = (pre_norm - mean_val) * scale_inv * gain_row + bias_row
    hidden = activate(pre_act, inside, pooling)
    return (pre_norm, mean_val, scale_inv, pixel_total, hidden)


def layer_backward(
    grad_out,
    layer_in,
    pre_norm,
    mean_val,
    scale_inv,
    pixel_total,
    weight,
    gain_row,
    bias_row,
    inside,
    pooling,
):
    normed = (pre_norm - mean_val) * scale_inv
    pre_act = normed * gain_row + bias_row
    hidden_out, pullback = jax.vjp(partial(activate, inside=inside, pooling=pooling), pre_act)
    grad_act = pullback(grad_out)[0]
    sums = lax.psum(
        (jnp.sum(grad_act, axis=(0, 1, 2)), jnp.sum(grad_act * normed, axis=(0, 1, 2))), "dp"
    )
    shift_term = sums[0] / pixel_total
    slope_term = sums[1] / pixel_total
    grad_pre = (
        inside * scale_inv * gain_row * (grad_act - shift_term - normed * slope_term)
    ).astype(jnp.bfloat16)
    weight_term = weight_back(layer_in, grad_pre)
    grad_in = conv_data_back(grad_pre, weight).astype(jnp.bfloat16)
    return (grad_in, weight_term, sums[1], sums[0])


def pipeline_shards(images, image_group, group_size, conv_weight, bn_gain, bn_bias, cotangent):
    section_index = lax.axis_index("section")
    sections = lax.axis_size("section")
    micro_total = images.shape[0]
    channels = conv_weight.shape[1]
    inside_all = canvas_mask(image_group, group_size, images.shape[2], images.shape[3])
    ticks = micro_total + sections - 1
    weight = conv_weight[0]
    gain_row = bn_gain[0]
    bias_row = bn_bias[0]
    pool_here = section_index == CONVS - 1
    received = jnp.zeros(images.shape[1:], jnp.bfloat16)
    kept_in, kept_pre, kept_mean, kept_scale, kept_total, finished = ([], [], [], [], [], [])
    for tick in range(ticks):
        micro_pos = jnp.clip(tick - section_index, 0, micro_total - 1)
        inside = inside_all[micro_pos]
        fresh = (images[micro_pos].astype(jnp.float32) * inside).astype(jnp.bfloat16)
        layer_in = jnp.where(section_index == 0, fresh, received)
        pre_norm, mean_val, scale_inv, pixel_total, hidden = layer_forward(
            layer_in, weight, gain_row, bias_row, inside, pool_here
        )
        sent = hidden.astype(jnp.bfloat16)
        if tick < ticks - 1:
            received = from_behind(sent, "section", 1)
        kept_in.append(layer_in)
        kept_pre.append(pre_norm)
        kept_mean.append(mean_val)
        kept_scale.append(scale_inv)
        kept_total.append(pixel_total)
        finished.append(sent)
    stack_in = jnp.stack(kept_in)
    stack_pre = jnp.stack(kept_pre)
    stack_mean = jnp.stack(kept_mean)
    stack_scale = jnp.stack(kept_scale)
    stack_total = jnp.stack(kept_total)
    returned = jnp.zeros(images.shape[1:], jnp.bfloat16)
    weight_sum = jnp.zeros(conv_weight.shape[1:], jnp.float32)
    gain_sum = jnp.zeros((channels,), jnp.float32)
    bias_sum = jnp.zeros((channels,), jnp.float32)
    input_list = []
    for tick in range(ticks):
        micro_raw = tick - (sections - 1 - section_index)
        valid = ((micro_raw >= 0) & (micro_raw < micro_total)).astype(jnp.float32)
        micro_pos = jnp.clip(micro_raw, 0, micro_total - 1)
        forward_tick = jnp.clip(micro_pos + section_index, 0, ticks - 1)
        inside = inside_all[micro_pos]
        grad_out = jnp.where(
            section_index == sections - 1,
            cotangent[micro_pos].astype(jnp.float32),
            returned.astype(jnp.float32),
        )
        grad_in, weight_term, gain_term, bias_term = layer_backward(
            grad_out,
            stack_in[forward_tick],
            stack_pre[forward_tick],
            stack_mean[forward_tick],
            stack_scale[forward_tick],
            stack_total[forward_tick],
            weight,
            gain_row,
            bias_row,
            inside,
            pool_here,
        )
        weight_sum = weight_sum + valid * weight_term
        gain_sum = gain_sum + valid * gain_term
        bias_sum = bias_sum + valid * bias_term
        if tick < ticks - 1:
            returned = from_behind(grad_in, "section", -1)
        input_list.append((grad_in.astype(jnp.float32) * inside).astype(jnp.bfloat16))
    out_stack = jnp.stack(finished[sections - 1 :], axis=0)
    grad_stack = jnp.stack(input_list[sections - 1 :], axis=0)
    out_back, grad_back = (
        lax.all_to_all(out_stack, "section", split_axis=0, concat_axis=1, tiled=True),
        lax.all_to_all(grad_stack, "section", split_axis=0, concat_axis=1, tiled=True),
    )
    activations = out_back[:, sections - 1 : sections]
    input_grad = grad_back[:, 0:1]
    weight_grad = lax.psum_scatter(weight_sum[None], "dp", scatter_dimension=1, tiled=True)
    share = channels // lax.axis_size("dp")
    gain_grad = lax.dynamic_slice_in_dim(gain_sum, lax.axis_index("dp") * share, share)[None]
    bias_grad = lax.dynamic_slice_in_dim(bias_sum, lax.axis_index("dp") * share, share)[None]
    return (activations, input_grad, weight_grad, gain_grad, bias_grad)


AXES = ("section", "dp")
TAPS = 9
VMEM_LIMIT = 24 * 1024 * 1024
META_ROWS = 16
LANES = 128
ROW_AT, COL_AT, FRAME_AT = 6, 7, 8
NT = (((1,), (1,)), ((), ()))


def place():
    dp_index = lax.axis_index("dp")
    return lax.axis_index("section"), dp_index // 2, dp_index % 2


def peer_order():
    return [(k, j) for j in range(2) for k in range(4)]


def slice_at(section, core, k, j):
    return (core ^ j) * lax.axis_size("section") + (section ^ k)


def send(x, target):
    sections = lax.axis_size("section")
    dps = lax.axis_size("dp")
    pairs = []
    for s in range(sections):
        for d in range(dps):
            ts, tz, tc = target(s, d // 2, d % 2)
            pairs.append((s * dps + d, ts * dps + tz * 2 + tc))
    return lax.ppermute(x, AXES, pairs)


def to_section(x, k):
    return send(x, lambda s, z, c: (s ^ k, z, c))


def to_plane(x, k):
    return send(x, lambda s, z, c: (s, z ^ k, c))


def to_core(x):
    return send(x, lambda s, z, c: (s, z, c ^ 1))


def spread(blocks, move, *beside):
    moved = lax.optimization_barrier(([move(blocks[k], k) for k in (1, 2, 3)], beside))[0]
    return [blocks[0]] + moved


def with_core(blocks):
    return blocks + [to_core(x) for x in blocks]


def after(x, *first):
    return lax.optimization_barrier((x, first))[0]


def grid_facts(frames, rows, cols):
    at = np.arange(frames * rows * cols)
    col = at % cols
    row = (at // cols) % rows
    facts = [row > 0, row < rows - 1, col > 0, col < cols - 1, col % 2 == 0, row % 2 == 0, row, col]
    facts = facts + [at // (rows * cols) == frame for frame in range(frames)]
    return jnp.asarray(np.stack(facts).astype(np.float32))


def shift(x, by):
    length = x.shape[1]
    return pltpu.roll(x, (-by) % length, 1) if by % length else x


def row_ok(facts, d):
    return facts[0:1, :] if d < 0 else facts[1:2, :]


def col_ok(facts, d):
    return facts[2:3, :] if d < 0 else facts[3:4, :]


def sum_taps(taps_ref, facts, cols):
    ch = taps_ref.shape[0] // TAPS
    total = None
    for dx in (-1, 0, 1):
        column = None
        for dy in (-1, 0, 1):
            tap = (dy + 1) * 3 + dx + 1
            piece = taps_ref[tap * ch : (tap + 1) * ch, :]
            if dy:
                piece = shift(piece, dy * cols) * row_ok(facts, dy)
            column = piece if column is None else column + piece
        if dx:
            column = shift(column, dx) * col_ok(facts, dx)
        total = column if total is None else total + column
    return total


def spread_taps(grad, moved_ref, base, facts, cols):
    ch = grad.shape[0]
    facts = facts[:4, :].astype(grad.dtype)
    for dx in (-1, 0, 1):
        column = shift(grad, -dx) * col_ok(facts, -dx) if dx else grad
        for dy in (-1, 0, 1):
            piece = shift(column, -dy * cols) * row_ok(facts, -dy) if dy else column
            at = base + ((dy + 1) * 3 + dx + 1) * ch
            moved_ref[at : at + ch, :] = piece


def corner_sum(x, cols):
    x = x + shift(x, 1)
    return x + shift(x, cols)


def from_corner(x, facts, cols):
    x = jnp.where(facts[4:5, :] > 0.5, x, shift(x, -1))
    return jnp.where(facts[5:6, :] > 0.5, x, shift(x, -cols))


def lane_sum(x):
    return jnp.sum(x, axis=1, keepdims=True)


def normalise(pre, inside):
    count = lane_sum(inside)
    mean = lane_sum(pre * inside) / count
    square = lane_sum(pre * pre * inside) / count
    scale = lax.rsqrt(square - mean * mean + eps)
    return (pre - mean) * scale, scale


def hidden_of(normed, gain, bias, inside, facts, cols, pooling):
    pre_act = normed * gain + bias
    hidden = pre_act * jax.nn.sigmoid(pre_act) * inside
    if pooling:
        raised = jnp.exp(hidden)
        total = corner_sum(raised, cols)
        pooled = corner_sum(raised * hidden, cols) / total
        hidden = raised * from_corner(pooled / total, facts, cols) * inside
    return hidden


def norm_back(grad, normed, scale, gain, bias, inside, facts, cols, pooling):
    pre_act = normed * gain + bias
    gate = jax.nn.sigmoid(pre_act)
    if pooling:
        hidden = pre_act * gate * inside
        raised = jnp.exp(hidden)
        out = grad * inside
        total = 1.0 / corner_sum(raised, cols)
        pooled = corner_sum(raised * hidden, cols) * total
        d_pooled = corner_sum(raised * out, cols) * total
        by_out = from_corner(pooled * total, facts, cols)
        by_hidden = from_corner(d_pooled * total, facts, cols)
        rest = from_corner(d_pooled * total * (1.0 - 2.0 * pooled), facts, cols)
        grad = raised * (out * by_out + hidden * by_hidden + rest)
    grad_act = grad * inside * gate * (1.0 + pre_act * (1.0 - gate))
    count = lane_sum(inside)
    shift_sum = lane_sum(grad_act)
    slope_sum = lane_sum(grad_act * normed)
    grad_pre = inside * (scale * gain) * (grad_act - shift_sum / count - normed * (slope_sum / count))
    return grad_pre.astype(jnp.bfloat16), shift_sum, slope_sum


def assemble(blocks, full_ref):
    section, _, core = place()
    ch = blocks[0].shape[0]
    for (k, j), block in zip(peer_order(), blocks):
        at = pl.multiple_of(slice_at(section, core, k, j) * ch, ch)
        full_ref[pl.ds(at, ch), :] = block[...]


def assemble_frames(blocks, full_ref, rows, lanes):
    _, plane, core = place()
    size = rows.stop - rows.start
    for (k, j), block in zip(peer_order(), blocks):
        frame = (plane ^ k) * 2 + (core ^ j)
        full_ref[pl.ds(pl.multiple_of(frame * size, size), size), :] = block[rows, lanes]


def start_all(copies):
    for copy in copies:
        copy.start()
    return copies


def wait_all(copies):
    for copy in copies:
        copy.wait()


def tap_products(weight, full_ref, taps_ref, by_cells):
    length = taps_ref.shape[1]
    step = 512 if length % 512 == 0 else length
    for at in range(0, length, step):
        if by_cells:
            taps_ref[:, at : at + step] = lax.dot_general(
                weight, full_ref[at : at + step, :], NT, preferred_element_type=jnp.float32
            )
        else:
            taps_ref[:, at : at + step] = jnp.dot(
                weight, full_ref[:, at : at + step], preferred_element_type=jnp.float32
            )


def pick_layer(layer, sources, start, target, sem):
    section, _, _ = place()
    rows = pl.ds(start, target.shape[0])
    for k, source in enumerate(sources):

        @pl.when((section ^ layer) == k)
        def _():
            pltpu.make_async_copy(source.at[rows], target, sem).start()

    return pltpu.make_async_copy(sources[0].at[rows], target, sem)


def take_layer(layer, sources, target):
    section, _, _ = place()
    for k, source in enumerate(sources):

        @pl.when((section ^ layer) == k)
        def _():
            target[...] = source[...]


def affine(meta, ch):
    parts = meta[:, :LANES].astype(jnp.float32).T[:ch]
    return (
        parts[:, 0:1] + parts[:, 1:2] + parts[:, 2:3],
        parts[:, 3:4] + parts[:, 4:5] + parts[:, 5:6],
    )


def plane_inside(metas, facts):
    frames = metas.shape[0] // META_ROWS
    extents = []
    for line in (0, 1):
        total = None
        for f in range(frames):
            at = f * META_ROWS + line
            extent = metas[at : at + 1, 0:1].astype(jnp.float32) * facts[FRAME_AT + f : FRAME_AT + f + 1, :]
            total = extent if total is None else total + extent
        extents.append(total)
    on = (facts[ROW_AT : ROW_AT + 1, :] < extents[0]) & (facts[COL_AT : COL_AT + 1, :] < extents[1])
    return jnp.where(on, 1.0, 0.0)


def frames_kernel(dims, group_table, size_table, images, *refs):
    payloads, (image_in, groups, sizes, sems) = refs[:4], refs[4:]
    copies = start_all(
        [
            pltpu.make_async_copy(group_table, groups, sems.at[0]),
            pltpu.make_async_copy(size_table, sizes, sems.at[1]),
            pltpu.make_async_copy(images, image_in, sems.at[2]),
        ]
    )
    _, plane, _ = place()
    rows, cols = dims
    cells = rows * cols
    at = lax.broadcasted_iota(jnp.int32, (cells, LANES), 0).astype(jnp.float32)
    row = jnp.floor((at + 0.5) * (1.0 / cols))
    col = at - row * cols
    channels = images.shape[2]
    line = lax.broadcasted_iota(jnp.int32, (META_ROWS, channels), 0)
    wait_all(copies)
    for k in range(4):
        micro = plane ^ k
        group = groups[0, micro]
        height = sizes[0, 0]
        breadth = sizes[1, 0]
        for g in range(1, sizes.shape[1]):
            height = jnp.where(group == g, sizes[0, g], height)
            breadth = jnp.where(group == g, sizes[1, g], breadth)
        height = height.astype(jnp.float32)
        breadth = breadth.astype(jnp.float32)
        on = jnp.where((row < height) & (col < breadth), 1.0, 0.0)
        image = image_in[micro]
        for c in range(0, channels, LANES):
            piece = image[:, c : c + LANES].astype(jnp.float32) * on
            payloads[k][:cells, c : c + LANES] = piece.astype(jnp.bfloat16)
        payloads[k][cells:, :] = jnp.where(line == 0, height, breadth).astype(jnp.bfloat16)


def cot_slice_kernel(cots, out, cot_in, sems):
    copy = pltpu.make_async_copy(cots, cot_in, sems.at[0])
    copy.start()
    section, _, _ = place()
    micros, cells, channels = cots.shape
    half = channels // 2
    tile = section // 2 * LANES
    odd = section % 2 == 1
    lane = lax.broadcasted_iota(jnp.int32, (cells, LANES), 1)
    copy.wait()
    for micro in range(micros):
        low = cot_in[micro, :, pl.ds(pl.multiple_of(tile, LANES), LANES)].astype(jnp.float32)
        high = cot_in[micro, :, pl.ds(pl.multiple_of(half + tile, LANES), LANES)].astype(jnp.float32)
        low = jnp.where(odd, pltpu.roll(low, LANES // 2, 1), low)
        high = jnp.where(odd, high, pltpu.roll(high, LANES // 2, 1))
        both = jnp.where(lane < LANES // 2, low, high).astype(jnp.bfloat16)
        out[micro * cells : (micro + 1) * cells, :] = both


def cot_kernel(own, other, pick, out, full):
    _, _, core = place()
    cells = full.shape[0] // 8
    for n in range(4):
        for j, block in enumerate((own, other)):
            at = pl.multiple_of((2 * n + (core ^ j)) * cells, cells)
            full[pl.ds(at, cells), :] = block[n * cells : (n + 1) * cells, :]
    out[...] = lax.dot_general(pick[...], full[...], NT, preferred_element_type=jnp.float32).astype(
        jnp.bfloat16
    )


def pack_kernel(gain, bias, weight, *refs):
    outs, (columns, turned, tables, sems) = refs[:4], refs[4:]
    section, _, core = place()
    width = columns.shape[2]
    ch = width // 4
    start = pl.multiple_of(core * width, width)
    copies = start_all(
        [
            pltpu.make_async_copy(weight.at[tap, :, pl.ds(start, width)], columns.at[tap], sems.at[tap])
            for tap in range(TAPS)
        ]
    )
    table_copies = start_all(
        [
            pltpu.make_async_copy(gain, tables.at[0], sems.at[TAPS]),
            pltpu.make_async_copy(bias, tables.at[1], sems.at[TAPS + 1]),
        ]
    )
    for tap in range(TAPS):
        copies[tap].wait()
        turned[tap % 2] = columns[tap].T
        for k, out in enumerate(outs):
            rows = pl.ds(pl.multiple_of((section ^ k) * ch, ch), ch)
            out[tap * ch : (tap + 1) * ch, :] = turned[tap % 2, rows, :]
    wait_all(table_copies)
    for k, out in enumerate(outs):
        lines = []
        tile = pl.multiple_of(start + (section ^ k) // 2 * LANES, LANES)
        odd = (section ^ k) % 2 == 1
        for m in range(2):
            line = tables[m, :, pl.ds(tile, LANES)]
            line = jnp.where(odd, pltpu.roll(line, ch, 1), line)
            for _ in range(3):
                part = line.astype(jnp.bfloat16).astype(jnp.float32)
                lines.append(part)
                line = line - part
        lines.append(jnp.zeros((META_ROWS - len(lines), LANES), jnp.float32))
        out[TAPS * ch :, :] = jnp.zeros((META_ROWS, out.shape[1]), jnp.bfloat16)
        out[TAPS * ch :, :LANES] = jnp.concatenate(lines, axis=0).astype(jnp.bfloat16)


def pick_kernel(layer, *refs):
    sources, (out, sems) = refs[:4], refs[4:]
    pick_layer(layer, sources, 0, out, sems.at[0]).wait()


def forward_kernel(dims, layer, first, picks, pooling, *refs):
    blocks, weights, rest = refs[:8], refs[8 : 12 if picks else 9], refs[12 if picks else 9 :]
    rows, cols = dims
    cells = rows * cols
    if first:
        facts, hidden, kept, full_out, inside_out, full, taps, stage, weight, metas, sems = rest
    elif picks:
        inside, facts, hidden, kept, full_out, full, taps, stage, weight, sems = rest
    else:
        inside, facts, hidden, kept, full_out, full, taps, stage, sems = rest
        (weight,) = weights
    if first:
        take_layer(layer, weights, weight)
    elif picks:
        copy = pick_layer(layer, weights, 0, weight, sems.at[2])
    facts_now = facts[...]
    if first:
        channels = full.shape[1]
        assemble_frames(blocks, full, slice(0, cells), slice(0, channels))
    else:
        assemble(blocks, full)
    full_copy = pltpu.make_async_copy(full, full_out, sems.at[0])
    full_copy.start()
    if first:
        assemble_frames(blocks, metas, slice(cells, cells + META_ROWS), slice(0, channels))
        inside_now = plane_inside(metas, facts_now)
        inside_out[...] = inside_now
    else:
        inside_now = inside[...]
    if picks and not first:
        copy.wait()
    ch = hidden.shape[0]
    tap_products(weight[: TAPS * ch, :], full, taps, first)
    pre = sum_taps(taps, facts_now, cols)
    normed, scale = normalise(pre, inside_now)
    length = normed.shape[1]
    stage[:, :length] = normed
    stage[:, length:] = jnp.broadcast_to(scale, (ch, LANES))
    kept_copy = pltpu.make_async_copy(stage, kept, sems.at[1])
    kept_copy.start()
    gain, bias = affine(weight[TAPS * ch :, :], ch)
    hidden[...] = hidden_of(normed, gain, bias, inside_now, facts_now, cols, pooling).astype(jnp.bfloat16)
    full_copy.wait()
    kept_copy.wait()


def turn_kernel(dims, layer, pooling, *refs):
    blocks, (weight, cot_in, inside, facts) = refs[:8], refs[8:12]
    hidden_out, full_out, grad_pre, sums, full, taps, hidden, sems = refs[12:]
    cols = dims[1]
    assemble(blocks, full)
    full_copy = pltpu.make_async_copy(full, full_out, sems.at[1])
    full_copy.start()
    ch = grad_pre.shape[0]
    tap_products(weight[: TAPS * ch, :], full, taps, False)
    facts_now, inside_now = facts[...], inside[...]
    pre = sum_taps(taps, facts_now, cols)
    normed, scale = normalise(pre, inside_now)
    gain, bias = affine(weight[TAPS * ch :, :], ch)
    hidden[...] = hidden_of(normed, gain, bias, inside_now, facts_now, cols, pooling).astype(jnp.bfloat16)
    hidden_copy = pltpu.make_async_copy(hidden, hidden_out, sems.at[2])
    hidden_copy.start()
    grad_pre[...], shift_sum, slope_sum = norm_back(
        cot_in[...].astype(jnp.float32), normed, scale, gain, bias, inside_now, facts_now, cols, pooling
    )
    keep_sums(sums, shift_sum, slope_sum)
    full_copy.wait()
    hidden_copy.wait()


def keep_sums(sums, shift_sum, slope_sum):
    ch = shift_sum.shape[0]
    sums[:, :LANES] = jnp.broadcast_to(shift_sum, (ch, LANES))
    sums[:, LANES:] = jnp.broadcast_to(slope_sum, (ch, LANES))


def add_blocks(blocks):
    total = blocks[0][...].astype(jnp.float32)
    for block in blocks[1:]:
        total = total + block[...].astype(jnp.float32)
    return total


def fetch_kernel(layer, kept, *refs):
    sources, (kept_out, meta_out, sems) = refs[:4], refs[4:]
    copy = pltpu.make_async_copy(kept, kept_out, sems.at[0])
    copy.start()
    start = sources[0].shape[0] - META_ROWS
    pick_layer(layer, sources, start, meta_out, sems.at[1]).wait()
    copy.wait()


def norm_back_kernel(dims, pooling, *refs):
    blocks, (kept, meta, inside, facts, grad_pre, sums) = refs[:4], refs[4:]
    ch, length = grad_pre.shape
    grad = add_blocks(blocks).astype(jnp.bfloat16).astype(jnp.float32)
    gain, bias = affine(meta[...], ch)
    grad_pre[...], shift_sum, slope_sum = norm_back(
        grad,
        kept[:, :length],
        kept[:, length : length + 1],
        gain,
        bias,
        inside[...],
        facts[...],
        dims[1],
        pooling,
    )
    keep_sums(sums, shift_sum, slope_sum)


def weight_product(moved, full, first):
    if first:
        return jnp.dot(moved, full, preferred_element_type=jnp.float32)
    return lax.dot_general(moved, full, NT, preferred_element_type=jnp.float32)


def sums_rows(sums, ch, width):
    lines = []
    for at in (0, LANES):
        turned = sums[:, at : at + LANES].T
        lines.append(jnp.concatenate([turned, jnp.zeros((LANES, width - ch), jnp.float32)], axis=1)[0:1])
    lines.append(jnp.zeros((META_ROWS - 2, width), jnp.float32))
    return jnp.concatenate(lines, axis=0).astype(jnp.bfloat16)


def store_share(value, sums, pieces):
    rows = value.shape[0]
    width = pieces[0].shape[1]
    below = sums_rows(sums, rows // TAPS, width)
    for n, piece in enumerate(pieces):
        piece[:rows, :] = value[:, n * width : (n + 1) * width].astype(jnp.bfloat16)
        piece[rows:, :] = below


def form_share(layer, moved, full, sums, product):
    piece = product.shape[0] // 4
    value = weight_product(moved[: piece - META_ROWS, :], full[...], layer == 0)
    store_share(value, sums, [product.at[pl.ds(n * piece, piece)] for n in range(4)])


def conv_back_kernel(dims, layer, own, other, own_weights, other_weights, full_in, sums, facts, *refs):
    *outs, share, product, full, moved, weights, sems = refs
    ch = own.shape[0]
    size = moved.shape[0] // 2
    rows = pl.ds(layer * 4 * ch, 4 * ch)
    copies = start_all(
        [
            pltpu.make_async_copy(own_weights.at[rows], weights.at[:, pl.ds(0, size)], sems.at[0]),
            pltpu.make_async_copy(other_weights, weights.at[:, pl.ds(size, size)], sems.at[1]),
        ]
    )
    full_copy = pltpu.make_async_copy(full_in, full, sems.at[2])
    full_copy.start()
    facts_now = facts[...]
    spread_taps(own[...], moved, 0, facts_now, dims[1])
    full_copy.wait()
    form_share(layer, moved, full, sums, product)
    share_copy = pltpu.make_async_copy(product, share, sems.at[3])
    share_copy.start()
    spread_taps(other[...], moved, size, facts_now, dims[1])
    for n in range(2):
        moved[n * size + TAPS * ch : (n + 1) * size, :] = jnp.zeros(
            (size - TAPS * ch, moved.shape[1]), jnp.bfloat16
        )
    wait_all(copies)
    value = jnp.dot(weights[...], moved[...], preferred_element_type=jnp.float32)
    for k, out in enumerate(outs):
        out[...] = value[k * ch : (k + 1) * ch, :].astype(jnp.bfloat16)
    share_copy.wait()


def fold_kernel(*refs):
    count = (len(refs) - 2) // 2
    shares, outs, (blocks, sems) = refs[:count], refs[count:-2], refs[-2:]
    rows = outs[0].shape[0]
    copies = start_all(
        [pltpu.make_async_copy(share, blocks.at[n], sems.at[n]) for n, share in enumerate(shares)]
    )
    for n, copy in enumerate(copies):
        copy.wait()
        value = add_blocks([blocks.at[n, pl.ds(m * rows, rows)] for m in range(blocks.shape[1] // rows)])
        outs[n][...] = value.astype(jnp.bfloat16)


def choose_kernel(*refs):
    last, others, outs = refs[0], refs[1:-4], refs[-4:]
    section, _, _ = place()
    rows = outs[0].shape[0]
    value = add_blocks([last.at[pl.ds(n * rows, rows)] for n in range(last.shape[0] // rows)])
    value = value.astype(jnp.bfloat16)
    for k, out in enumerate(outs):

        @pl.when((section ^ k) == 0)
        def _():
            out[...] = value

        for layer, other in enumerate(others, 1):

            @pl.when((section ^ k) == layer)
            def _():
                out[...] = other[...]


def turn_weights_kernel(layers, *refs):
    sources, own, others, (full, turned, stage, sems) = refs[:4], refs[4], refs[5:-4], refs[-4:]
    section, _, core = place()
    rows, channels = full.shape[1:]
    half = channels // 2
    ch = half // 4
    copies = [pick_layer(n, sources, 0, full.at[n], sems.at[n]) for n in range(layers)]
    stage[:, :, rows:] = jnp.zeros((*stage.shape[:2], stage.shape[2] - rows), jnp.bfloat16)
    for n in range(layers):
        copies[n].wait()
        turned[...] = full[n].T
        for j in range(2):
            for k in range(4):
                at = pl.multiple_of((core ^ j) * half + (section ^ k) * ch, ch)
                stage[j, n * half + k * ch : n * half + (k + 1) * ch, :rows] = turned[pl.ds(at, ch), :]
    copies = [pltpu.make_async_copy(stage.at[0], own, sems.at[0])]
    for n, other in enumerate(others):
        source = stage.at[1, pl.ds(n * half, half)]
        copies.append(pltpu.make_async_copy(source, other, sems.at[1 + n]))
    wait_all(start_all(copies))


def input_kernel(*refs):
    blocks, (hidden, inside, keep, give, full, sems) = refs[:4], refs[4:]
    section, _, core = place()
    ch = hidden.shape[0]
    copy = pltpu.make_async_copy(hidden, full.at[pl.ds(0, ch)], sems.at[0])
    copy.start()
    full[ch:, :] = (add_blocks(blocks) * inside[...]).astype(jnp.bfloat16)
    copy.wait()
    rows = 2 * ch
    width = keep.shape[1]
    for j, out in enumerate((keep, give)):
        for n in range(2):
            at = pl.multiple_of((section ^ (2 * (core ^ j) + n)) * width, width)
            out[n * rows : (n + 1) * rows, :] = full[:, pl.ds(at, width)]


def pair_kernel(keep, got, *outs):
    rows = keep.shape[0] // 2
    for n, out in enumerate(outs):
        out[:rows, :] = keep[n * rows : (n + 1) * rows, :]
        out[rows:, :] = got[n * rows : (n + 1) * rows, :]


def store_maps(blocks, pick, outs, full):
    _, plane, core = place()
    ch = blocks[0].shape[0] // 4
    for m, out in enumerate(outs):
        for j in range(2):
            for n in range(2):
                for h in range(2):
                    slot = slice_at(plane ^ (2 * (core ^ j) + n), core ^ j, 0, h)
                    at = pl.multiple_of(slot * ch, ch)
                    start = (2 * h + m) * ch
                    full[m, pl.ds(at, ch), :] = blocks[2 * j + n][start : start + ch, :]
        mine = lax.dot_general(pick[...], full[m], NT, preferred_element_type=jnp.float32)
        out[...] = mine.astype(out.dtype)


def outputs_kernel(*refs):
    blocks, pick, map_blocks, map_pick, refs = refs[:8], refs[8], refs[9:13], refs[13], refs[14:]
    (weight_out, shift_out, slope_out), map_outs, (full, maps_full) = refs[:3], refs[3:5], refs[5:]
    store_maps(map_blocks, map_pick, map_outs, maps_full)
    section, plane, core = place()
    taps, rows, channels = weight_out.shape
    for tap in range(taps):
        for (k, j), block in zip(peer_order(), blocks):
            at = pl.multiple_of(slice_at(section, core, k, j) * rows, rows)
            full[tap, pl.ds(at, rows), :] = block[tap * rows : (tap + 1) * rows, :]
        weight_out[tap] = lax.dot_general(pick[...], full[tap], NT, preferred_element_type=jnp.float32)
    shift_row = jnp.zeros((1, rows), jnp.float32)
    slope_row = jnp.zeros((1, rows), jnp.float32)
    slot = plane * 2 + core
    for (k, j), block in zip(peer_order(), blocks):
        tail = block[taps * rows :, :].astype(jnp.float32)
        mine = slice_at(section, core, k, j) == slot
        shift_row = shift_row + jnp.where(mine, tail[0:1, :rows], 0.0)
        slope_row = slope_row + jnp.where(mine, tail[1:2, :rows], 0.0)
    shift_out[...] = shift_row
    slope_out[...] = slope_row


def call(
    kernel, outs, scratch, args, name, held=(), free=(), held_outs=(), loose=(), last=False, flops=0, copies=None
):
    shapes = [
        (jax.ShapeDtypeStruct if last else pltpu.HBM if n in held_outs else pltpu.VMEM)(shape, dtype)
        for n, (shape, dtype) in enumerate(outs)
    ]
    moved = sum(a.size * a.dtype.itemsize for a in args)
    moved += sum(math.prod(shape) * jnp.dtype(dtype).itemsize for shape, dtype in outs)
    spaces = [pl.ANY if n in free else pltpu.HBM if n in held else pltpu.VMEM for n in range(len(args))]
    out_spaces = [pltpu.HBM if n in held_outs else pltpu.VMEM for n in range(len(outs))]
    args = [
        a if n in loose or n in free else pltpu.with_memory_space_constraint(a, space)
        for n, (a, space) in enumerate(zip(args, spaces))
    ]
    scratch_shapes = [
        pltpu.SMEM(shape, dtype) if dtype == jnp.int32 else pltpu.VMEM(shape, dtype) for shape, dtype in scratch
    ]
    if copies is not None:
        scratch_shapes.append(pltpu.SemaphoreType.DMA((copies,)))
    return pl.pallas_call(
        kernel,
        out_shape=shapes,
        in_specs=[pl.BlockSpec(memory_space=space) for space in spaces],
        out_specs=[pl.BlockSpec(memory_space=space) for space in out_spaces],
        scratch_shapes=scratch_shapes,
        compiler_params=pltpu.CompilerParams(vmem_limit_bytes=VMEM_LIMIT),
        cost_estimate=pl.CostEstimate(flops=flops, bytes_accessed=moved, transcendentals=0),
        name=name,
    )(*args)


def plane_shards(images, image_group, group_size, conv_weight, bn_gain, bn_bias, cotangent):
    _, _, core = place()
    micro_total, _, rows, cols, channels = images.shape
    layers = lax.axis_size("section")
    last = layers - 1
    cells = rows * cols
    frames = 2 * micro_total
    length = frames * cells
    ch = channels // 8
    dims = (rows, cols)
    bf16, f32 = jnp.bfloat16, jnp.float32
    facts = grid_facts(frames, rows, cols)
    conv_flops = 2 * TAPS * ch * channels * length
    slice_rows = TAPS * ch + META_ROWS
    tap_rows = -(-TAPS * ch // LANES) * LANES

    full_map = ((channels, length), bf16)
    full_frames = ((length, channels), bf16)
    tap_scratch = ((TAPS * ch, length), f32)
    weight_slice = ((slice_rows, channels), bf16)
    map_out = ((ch, length), bf16)
    sums_out = ((ch, 2 * LANES), f32)
    kept_out = ((ch, length + LANES), f32)
    share_out = ((4 * slice_rows, 2 * ch), bf16)
    share_piece = ((slice_rows, 2 * ch), bf16)

    taps_first = conv_weight[0].transpose(1, 2, 0, 3).reshape(TAPS, channels, channels)
    packed = call(
        pack_kernel,
        [weight_slice] * 4,
        [
            ((TAPS, channels, 4 * ch), bf16),
            ((2, 4 * ch, channels), bf16),
            ((2, 1, channels), f32),
        ],
        [bn_gain, bn_bias, taps_first],
        "weight_pack",
        held=range(3),
        copies=TAPS + 2,
    )
    slices = spread(packed, to_section)

    payload = ((cells + META_ROWS, channels), bf16)
    sent = call(
        partial(frames_kernel, dims),
        [payload] * 4,
        [
            ((micro_total, cells, channels), bf16),
            (image_group.shape[::-1], jnp.int32),
            (group_size.shape[::-1], jnp.int32),
        ],
        [image_group.T, group_size.T, after(images.reshape(micro_total, cells, channels), packed)],
        "frames",
        held=range(3),
        copies=3,
    )
    frames_in = with_core(spread(sent, to_plane))

    half = (core * ch + np.arange(ch))[:, None] == np.arange(2 * ch)[None, :]
    hidden, normed, full, inside = call(
        partial(forward_kernel, dims, 0, True, True, CONVS == 1),
        [map_out, kept_out, full_frames, ((1, length), f32)],
        [
            full_frames,
            tap_scratch,
            kept_out,
            weight_slice,
            ((frames * META_ROWS, channels), bf16),
        ],
        [*frames_in, *slices, facts],
        "forward",
        held_outs=(1, 2),
        loose=(8, 9, 10, 11, 12),
        flops=conv_flops,
        copies=4,
    )
    kept, fulls = [normed], [full]
    same_core = [[2 * z + c for z in range(layers)] for c in range(2)]
    for layer in range(1, layers):
        weights = call(
            partial(pick_kernel, layer),
            [weight_slice],
            [],
            after(slices, hidden),
            "pick",
            flops=PICK_FLOPS,
            held=range(4),
            copies=1,
        )
        beside = [*weights]
        if layer == 1:
            turned, *crossing = call(
                partial(turn_weights_kernel, layers),
                [((layers * 4 * ch, tap_rows), bf16)] + [((4 * ch, tap_rows), bf16)] * layers,
                [
                    ((layers, TAPS * ch, channels), bf16),
                    ((channels, TAPS * ch), bf16),
                    ((2, layers * 4 * ch, tap_rows), bf16),
                ],
                after(slices, hidden),
                "turn_weights",
                held=range(4),
                held_outs=range(1 + layers),
                copies=1 + layers,
            )
            beside.append((turned, crossing))
        if layer == COT_LAYER - 1:
            (cot_slots,) = call(
                cot_slice_kernel,
                [((micro_total * cells, LANES), bf16)],
                [((micro_total, cells, channels), bf16)],
                [after(cotangent.reshape(micro_total, cells, channels), hidden)],
                "cot_slices",
                held=(0,),
                copies=1,
            )
            beside.append(cot_slots)
        if layer == COT_LAYER:
            cot_slots = after(cot_slots, hidden)
            cots = lax.all_to_all(cot_slots, "dp", 0, 0, tiled=True, axis_index_groups=same_core)
        if layer == last:
            crossing[last] = to_core(after(crossing[last], hidden))
            cots = after(cots, hidden)
            (cot,) = call(
                cot_kernel,
                [map_out],
                [((length, LANES), bf16)],
                [cots, to_core(cots), half.astype(bf16)],
                "cotangent",
                loose=(0, 1, 2),
            )
            beside.append(cot)
        blocks = [hidden] + [to_section(hidden, k) for k in (1, 2, 3)]
        blocks[3] = after(blocks[3], *beside)
        blocks = with_core(blocks)
        if layer < last:
            hidden, normed, full = call(
                partial(forward_kernel, dims, layer, False, False, layer == CONVS - 1),
                [map_out, kept_out, full_map],
                [full_map, tap_scratch, kept_out],
                [*blocks, *weights, inside, facts],
                "forward",
                held_outs=(1, 2),
                loose=(9, 10),
                flops=conv_flops,
                copies=3,
            )
            kept.append(normed)
        else:
            activation, full, grad_pre, sums = call(
                partial(turn_kernel, dims, last, last == CONVS - 1),
                [map_out, full_map, map_out, sums_out],
                [full_map, tap_scratch, map_out],
                [*blocks, *weights, cot, inside, facts],
                "turn",
                held_outs=(0, 1),
                loose=(10, 11),
                flops=conv_flops,
                copies=3,
            )
        fulls.append(full)

    shares = [None] * layers
    for layer in range(last, -1, -1):
        *parts, share = call(
            partial(conv_back_kernel, dims, layer),
            [map_out] * 4 + [share_out],
            [
                share_out,
                full_map if layer else full_frames,
                ((2 * tap_rows, length), bf16),
                ((4 * ch, 2 * tap_rows), bf16),
            ],
            [grad_pre, to_core(grad_pre), turned, crossing[layer], fulls[layer], sums, facts],
            "conv_back",
            held=(2, 4),
            free=(3,),
            held_outs=(4,),
            loose=(5, 6),
            flops=BACK_FLOPS[layer],
            copies=4,
        )
        if layer < last:
            share = after(share, shares[layer + 1])
        shares[layer] = lax.all_to_all(share, "dp", 0, 0, tiled=True, axis_index_groups=same_core)
        if layer:
            crossing[layer - 1] = to_core(after(crossing[layer - 1], parts))
            held = call(
                partial(fetch_kernel, layer - 1),
                [kept_out, ((META_ROWS, channels), bf16)],
                [],
                [after(kept[layer - 1], parts), *slices],
                "fetch",
                held=range(5),
                copies=2,
            )
            blocks = spread(parts, to_section, held)
            grad_pre, sums = call(
                partial(norm_back_kernel, dims, layer - 1 == CONVS - 1),
                [map_out, sums_out],
                [],
                [*blocks, *held, inside, facts],
                "norm_back",
                loose=(6, 7),
            )
    blocks = spread(parts, to_section)
    keep, give = call(
        input_kernel,
        [((4 * ch, 2 * cells), bf16)] * 2,
        [((2 * ch, length), bf16)],
        [*blocks, activation, inside],
        "input",
        flops=INPUT_FLOPS,
        held=(4,),
        loose=(5,),
        copies=1,
    )
    maps = call(pair_kernel, [((4 * ch, 2 * cells), bf16)] * 2, [], [keep, to_core(give)], "pair")
    maps = [send(x, lambda s, z, c, n=n: (z, s ^ (2 * c + n), c)) for n, x in enumerate(maps)]
    folded = call(
        fold_kernel,
        [share_piece] * last,
        [((last, 4 * slice_rows, 2 * ch), bf16)],
        shares[1:],
        "fold",
        held=range(last),
        copies=last,
    )
    chosen = call(
        choose_kernel,
        [share_piece] * 4,
        [],
        [shares[0], *folded],
        "choose",
        loose=(0,),
    )
    pick = (core * cells + np.arange(cells))[:, None] == np.arange(2 * cells)[None, :]
    map_pick = pick.astype(bf16)
    pick = (core * ch + np.arange(ch))[:, None] == np.arange(2 * ch)[None, :]
    weight_grad, bias_grad, gain_grad, activations, input_grad = call(
        outputs_kernel,
        [((TAPS, ch, channels), f32), ((1, ch), f32), ((1, ch), f32)] + [((cells, channels), bf16)] * 2,
        [((TAPS, channels, 2 * ch), bf16), ((2, channels, 2 * cells), bf16)],
        [
            *with_core([chosen[0]] + [to_section(chosen[k], k) for k in (1, 2, 3)]),
            pick.astype(bf16),
            *with_core(after(maps, chosen)),
            map_pick,
        ],
        "outputs",
        loose=(8, 13),
        last=True,
    )
    weight_grad = weight_grad.reshape(3, 3, ch, channels).transpose(2, 0, 1, 3)[None]
    return (
        activations.reshape(1, 1, rows, cols, channels),
        input_grad.reshape(1, 1, rows, cols, channels),
        weight_grad,
        gain_grad,
        bias_grad,
    )


def fits_plane_plan(images, conv_weight, sections, dps):
    micro_total, images_total, rows, cols, channels = images.shape
    return (
        sections == 4
        and dps == 2 * sections
        and micro_total == sections
        and conv_weight.shape[0] == sections
        and images_total == dps
        and rows % 2 == 0
        and cols % 2 == 0
        and (rows * cols) % 64 == 0
        and channels == 512
    )


def solution(mesh):
    in_specs = (
        P(None, "dp", None, None, None),
        P(None, "dp"),
        P(),
        P("section", None, None, None, None),
        P("section", None),
        P("section", None),
        P(None, "dp", None, None, None),
    )
    out_specs = (
        P("section", "dp", None, None, None),
        P("section", "dp", None, None, None),
        P("section", "dp", None, None, None),
        P("section", "dp"),
        P("section", "dp"),
    )
    sections, dps = mesh.shape["section"], mesh.shape["dp"]

    def program(images, image_group, group_size, conv_weight, bn_gain, bn_bias, cotangent):
        plan = plane_shards if fits_plane_plan(images, conv_weight, sections, dps) else pipeline_shards
        sharded = jax.shard_map(plan, mesh=mesh, in_specs=in_specs, out_specs=out_specs, check_vma=False)
        return sharded(images, image_group, group_size, conv_weight, bn_gain, bn_bias, cotangent)

    return program
```

```python
import math
from functools import partial

import jax
import jax.numpy as jnp
import numpy as np
from jax import lax
from jax.experimental import pallas as pl
from jax.experimental.pallas import tpu as pltpu
from jax.sharding import PartitionSpec as P

CONVS = 2
BACK_FLOPS = (6 * 10**9, 52 * 10**8, 52 * 10**8, 0)
PICK_FLOPS = 2 * 10**9
COT_LAYER = 2
INPUT_FLOPS = 4000000000


eps = 1e-05


def from_behind(x, axis, by):
    peers = lax.axis_size(axis)
    pairs = [(i, i + by) for i in range(peers) if 0 <= i + by < peers]
    return lax.ppermute(x, axis, pairs)


def canvas_mask(image_group, group_size, canvas_rows, canvas_cols):
    groups_n = group_size.shape[0]
    onehot = image_group[..., None] == jnp.arange(groups_n, dtype=jnp.int32)
    height = jnp.sum(jnp.where(onehot, group_size[:, 0], 0), axis=-1)
    breadth = jnp.sum(jnp.where(onehot, group_size[:, 1], 0), axis=-1)
    inside_rows = jnp.arange(canvas_rows, dtype=jnp.int32)[:, None] < height[..., None, None]
    inside_cols = jnp.arange(canvas_cols, dtype=jnp.int32)[None, :] < breadth[..., None, None]
    return (inside_rows & inside_cols).astype(jnp.float32)[..., None]


def window_pool(hidden):
    frames, height, breadth, channels = hidden.shape
    blocks = hidden.reshape(frames, height // 2, 2, breadth // 2, 2, channels)
    window_max = jnp.max(blocks, axis=(2, 4), keepdims=True)
    raised = jnp.exp(blocks - window_max)
    weights = raised / jnp.sum(raised, axis=(2, 4), keepdims=True)
    pooled = jnp.sum(weights * blocks, axis=(2, 4), keepdims=True)
    return (weights * pooled).reshape(frames, height, breadth, channels)


def activate(pre_act, inside, pooling):
    hidden = jax.nn.silu(pre_act) * inside
    return jnp.where(pooling, window_pool(hidden) * inside, hidden)


def conv_forward(layer_in, weight):
    return lax.conv_general_dilated(
        layer_in,
        weight,
        (1, 1),
        "SAME",
        dimension_numbers=("NHWC", "IHWO", "NHWC"),
        preferred_element_type=jnp.float32,
    )


def conv_data_back(grad_pre, weight):
    flipped = weight[:, ::-1, ::-1, :]
    return lax.conv_general_dilated(
        grad_pre,
        flipped,
        (1, 1),
        "SAME",
        dimension_numbers=("NHWC", "OHWI", "NHWC"),
        preferred_element_type=jnp.float32,
    )


def weight_back(layer_in, grad_pre):
    height = layer_in.shape[1]
    breadth = layer_in.shape[2]
    padded = jnp.pad(layer_in, ((0, 0), (1, 1), (1, 1), (0, 0)))
    pieces = []
    for tap_row in range(3):
        for tap_col in range(3):
            window = padded[:, tap_row : tap_row + height, tap_col : tap_col + breadth, :]
            pieces.append(
                jnp.einsum("nhwi,nhwo->io", window, grad_pre, preferred_element_type=jnp.float32)
            )
    return jnp.stack(pieces, axis=1).reshape(layer_in.shape[3], 3, 3, grad_pre.shape[3])


def layer_forward(layer_in, weight, gain_row, bias_row, inside, pooling):
    pre_norm = conv_forward(layer_in, weight)
    sums = lax.psum(
        (
            jnp.sum(pre_norm * inside, axis=(0, 1, 2)),
            jnp.sum(pre_norm * pre_norm * inside, axis=(0, 1, 2)),
            jnp.sum(inside),
        ),
        "dp",
    )
    pixel_total = sums[2]
    mean_val = sums[0] / pixel_total
    scale_inv = lax.rsqrt(sums[1] / pixel_total - mean_val * mean_val + eps)
    pre_act = (pre_norm - mean_val) * scale_inv * gain_row + bias_row
    hidden = activate(pre_act, inside, pooling)
    return (pre_norm, mean_val, scale_inv, pixel_total, hidden)


def layer_backward(
    grad_out,
    layer_in,
    pre_norm,
    mean_val,
    scale_inv,
    pixel_total,
    weight,
    gain_row,
    bias_row,
    inside,
    pooling,
):
    normed = (pre_norm - mean_val) * scale_inv
    pre_act = normed * gain_row + bias_row
    hidden_out, pullback = jax.vjp(partial(activate, inside=inside, pooling=pooling), pre_act)
    grad_act = pullback(grad_out)[0]
    sums = lax.psum(
        (jnp.sum(grad_act, axis=(0, 1, 2)), jnp.sum(grad_act * normed, axis=(0, 1, 2))), "dp"
    )
    shift_term = sums[0] / pixel_total
    slope_term = sums[1] / pixel_total
    grad_pre = (
        inside * scale_inv * gain_row * (grad_act - shift_term - normed * slope_term)
    ).astype(jnp.bfloat16)
    weight_term = weight_back(layer_in, grad_pre)
    grad_in = conv_data_back(grad_pre, weight).astype(jnp.bfloat16)
    return (grad_in, weight_term, sums[1], sums[0])


def pipeline_shards(images, image_group, group_size, conv_weight, bn_gain, bn_bias, cotangent):
    section_index = lax.axis_index("section")
    sections = lax.axis_size("section")
    micro_total = images.shape[0]
    channels = conv_weight.shape[1]
    inside_all = canvas_mask(image_group, group_size, images.shape[2], images.shape[3])
    ticks = micro_total + sections - 1
    weight = conv_weight[0]
    gain_row = bn_gain[0]
    bias_row = bn_bias[0]
    pool_here = section_index == CONVS - 1
    received = jnp.zeros(images.shape[1:], jnp.bfloat16)
    kept_in, kept_pre, kept_mean, kept_scale, kept_total, finished = ([], [], [], [], [], [])
    for tick in range(ticks):
        micro_pos = jnp.clip(tick - section_index, 0, micro_total - 1)
        inside = inside_all[micro_pos]
        fresh = (images[micro_pos].astype(jnp.float32) * inside).astype(jnp.bfloat16)
        layer_in = jnp.where(section_index == 0, fresh, received)
        pre_norm, mean_val, scale_inv, pixel_total, hidden = layer_forward(
            layer_in, weight, gain_row, bias_row, inside, pool_here
        )
        sent = hidden.astype(jnp.bfloat16)
        if tick < ticks - 1:
            received = from_behind(sent, "section", 1)
        kept_in.append(layer_in)
        kept_pre.append(pre_norm)
        kept_mean.append(mean_val)
        kept_scale.append(scale_inv)
        kept_total.append(pixel_total)
        finished.append(sent)
    stack_in = jnp.stack(kept_in)
    stack_pre = jnp.stack(kept_pre)
    stack_mean = jnp.stack(kept_mean)
    stack_scale = jnp.stack(kept_scale)
    stack_total = jnp.stack(kept_total)
    returned = jnp.zeros(images.shape[1:], jnp.bfloat16)
    weight_sum = jnp.zeros(conv_weight.shape[1:], jnp.float32)
    gain_sum = jnp.zeros((channels,), jnp.float32)
    bias_sum = jnp.zeros((channels,), jnp.float32)
    input_list = []
    for tick in range(ticks):
        micro_raw = tick - (sections - 1 - section_index)
        valid = ((micro_raw >= 0) & (micro_raw < micro_total)).astype(jnp.float32)
        micro_pos = jnp.clip(micro_raw, 0, micro_total - 1)
        forward_tick = jnp.clip(micro_pos + section_index, 0, ticks - 1)
        inside = inside_all[micro_pos]
        grad_out = jnp.where(
            section_index == sections - 1,
            cotangent[micro_pos].astype(jnp.float32),
            returned.astype(jnp.float32),
        )
        grad_in, weight_term, gain_term, bias_term = layer_backward(
            grad_out,
            stack_in[forward_tick],
            stack_pre[forward_tick],
            stack_mean[forward_tick],
            stack_scale[forward_tick],
            stack_total[forward_tick],
            weight,
            gain_row,
            bias_row,
            inside,
            pool_here,
        )
        weight_sum = weight_sum + valid * weight_term
        gain_sum = gain_sum + valid * gain_term
        bias_sum = bias_sum + valid * bias_term
        if tick < ticks - 1:
            returned = from_behind(grad_in, "section", -1)
        input_list.append((grad_in.astype(jnp.float32) * inside).astype(jnp.bfloat16))
    out_stack = jnp.stack(finished[sections - 1 :], axis=0)
    grad_stack = jnp.stack(input_list[sections - 1 :], axis=0)
    out_back, grad_back = (
        lax.all_to_all(out_stack, "section", split_axis=0, concat_axis=1, tiled=True),
        lax.all_to_all(grad_stack, "section", split_axis=0, concat_axis=1, tiled=True),
    )
    activations = out_back[:, sections - 1 : sections]
    input_grad = grad_back[:, 0:1]
    weight_grad = lax.psum_scatter(weight_sum[None], "dp", scatter_dimension=1, tiled=True)
    share = channels // lax.axis_size("dp")
    gain_grad = lax.dynamic_slice_in_dim(gain_sum, lax.axis_index("dp") * share, share)[None]
    bias_grad = lax.dynamic_slice_in_dim(bias_sum, lax.axis_index("dp") * share, share)[None]
    return (activations, input_grad, weight_grad, gain_grad, bias_grad)


AXES = ("section", "dp")
TAPS = 9
VMEM_LIMIT = 24 * 1024 * 1024
META_ROWS = 16
LANES = 128
ROW_AT, COL_AT, FRAME_AT = 6, 7, 8
NT = (((1,), (1,)), ((), ()))


def place():
    dp_index = lax.axis_index("dp")
    return lax.axis_index("section"), dp_index // 2, dp_index % 2


def peer_order():
    return [(k, j) for j in range(2) for k in range(4)]


def slice_at(section, core, k, j):
    return (core ^ j) * lax.axis_size("section") + (section ^ k)


def send(x, target):
    sections = lax.axis_size("section")
    dps = lax.axis_size("dp")
    pairs = []
    for s in range(sections):
        for d in range(dps):
            ts, tz, tc = target(s, d // 2, d % 2)
            pairs.append((s * dps + d, ts * dps + tz * 2 + tc))
    return lax.ppermute(x, AXES, pairs)


def to_section(x, k):
    return send(x, lambda s, z, c: (s ^ k, z, c))


def to_plane(x, k):
    return send(x, lambda s, z, c: (s, z ^ k, c))


def to_core(x):
    return send(x, lambda s, z, c: (s, z, c ^ 1))


def spread(blocks, move, *beside):
    moved = lax.optimization_barrier(([move(blocks[k], k) for k in (1, 2, 3)], beside))[0]
    return [blocks[0]] + moved


def with_core(blocks):
    return blocks + [to_core(x) for x in blocks]


def after(x, *first):
    return lax.optimization_barrier((x, first))[0]


def grid_facts(frames, rows, cols):
    at = np.arange(frames * rows * cols)
    col = at % cols
    row = (at // cols) % rows
    facts = [row > 0, row < rows - 1, col > 0, col < cols - 1, col % 2 == 0, row % 2 == 0, row, col]
    facts = facts + [at // (rows * cols) == frame for frame in range(frames)]
    return jnp.asarray(np.stack(facts).astype(np.float32))


def shift(x, by):
    length = x.shape[1]
    return pltpu.roll(x, (-by) % length, 1) if by % length else x


def row_ok(facts, d):
    return facts[0:1, :] if d < 0 else facts[1:2, :]


def col_ok(facts, d):
    return facts[2:3, :] if d < 0 else facts[3:4, :]


def sum_taps(taps_ref, facts, cols):
    ch = taps_ref.shape[0] // TAPS
    total = None
    for dx in (-1, 0, 1):
        column = None
        for dy in (-1, 0, 1):
            tap = (dy + 1) * 3 + dx + 1
            piece = taps_ref[tap * ch : (tap + 1) * ch, :]
            if dy:
                piece = shift(piece, dy * cols) * row_ok(facts, dy)
            column = piece if column is None else column + piece
        if dx:
            column = shift(column, dx) * col_ok(facts, dx)
        total = column if total is None else total + column
    return total


def spread_taps(grad, moved_ref, base, facts, cols):
    ch = grad.shape[0]
    facts = facts[:4, :].astype(grad.dtype)
    for dx in (-1, 0, 1):
        column = shift(grad, -dx) * col_ok(facts, -dx) if dx else grad
        for dy in (-1, 0, 1):
            piece = shift(column, -dy * cols) * row_ok(facts, -dy) if dy else column
            at = base + ((dy + 1) * 3 + dx + 1) * ch
            moved_ref[at : at + ch, :] = piece


def corner_sum(x, cols):
    x = x + shift(x, 1)
    return x + shift(x, cols)


def from_corner(x, facts, cols):
    x = jnp.where(facts[4:5, :] > 0.5, x, shift(x, -1))
    return jnp.where(facts[5:6, :] > 0.5, x, shift(x, -cols))


def lane_sum(x):
    return jnp.sum(x, axis=1, keepdims=True)


def normalise(pre, inside):
    count = lane_sum(inside)
    mean = lane_sum(pre * inside) / count
    square = lane_sum(pre * pre * inside) / count
    scale = lax.rsqrt(square - mean * mean + eps)
    return (pre - mean) * scale, scale


def hidden_of(normed, gain, bias, inside, facts, cols, pooling):
    pre_act = normed * gain + bias
    hidden = pre_act * jax.nn.sigmoid(pre_act) * inside
    if pooling:
        raised = jnp.exp(hidden)
        total = corner_sum(raised, cols)
        pooled = corner_sum(raised * hidden, cols) / total
        hidden = raised * from_corner(pooled / total, facts, cols) * inside
    return hidden


def norm_back(grad, normed, scale, gain, bias, inside, facts, cols, pooling):
    pre_act = normed * gain + bias
    gate = jax.nn.sigmoid(pre_act)
    if pooling:
        hidden = pre_act * gate * inside
        raised = jnp.exp(hidden)
        out = grad * inside
        total = 1.0 / corner_sum(raised, cols)
        pooled = corner_sum(raised * hidden, cols) * total
        d_pooled = corner_sum(raised * out, cols) * total
        by_out = from_corner(pooled * total, facts, cols)
        by_hidden = from_corner(d_pooled * total, facts, cols)
        rest = from_corner(d_pooled * total * (1.0 - 2.0 * pooled), facts, cols)
        grad = raised * (out * by_out + hidden * by_hidden + rest)
    grad_act = grad * inside * gate * (1.0 + pre_act * (1.0 - gate))
    count = lane_sum(inside)
    shift_sum = lane_sum(grad_act)
    slope_sum = lane_sum(grad_act * normed)
    grad_pre = inside * (scale * gain) * (grad_act - shift_sum / count - normed * (slope_sum / count))
    return grad_pre.astype(jnp.bfloat16), shift_sum, slope_sum


def assemble(blocks, full_ref):
    section, _, core = place()
    ch = blocks[0].shape[0]
    for (k, j), block in zip(peer_order(), blocks):
        at = pl.multiple_of(slice_at(section, core, k, j) * ch, ch)
        full_ref[pl.ds(at, ch), :] = block[...]


def assemble_frames(blocks, full_ref, rows, lanes):
    _, plane, core = place()
    size = rows.stop - rows.start
    for (k, j), block in zip(peer_order(), blocks):
        frame = (plane ^ k) * 2 + (core ^ j)
        full_ref[pl.ds(pl.multiple_of(frame * size, size), size), :] = block[rows, lanes]


def start_all(copies):
    for copy in copies:
        copy.start()
    return copies


def wait_all(copies):
    for copy in copies:
        copy.wait()


def tap_products(weight, full_ref, taps_ref, by_cells):
    length = taps_ref.shape[1]
    step = 512 if length % 512 == 0 else length
    for at in range(0, length, step):
        if by_cells:
            taps_ref[:, at : at + step] = lax.dot_general(
                weight, full_ref[at : at + step, :], NT, preferred_element_type=jnp.float32
            )
        else:
            taps_ref[:, at : at + step] = jnp.dot(
                weight, full_ref[:, at : at + step], preferred_element_type=jnp.float32
            )


def pick_layer(layer, sources, start, target, sem):
    section, _, _ = place()
    rows = pl.ds(start, target.shape[0])
    for k, source in enumerate(sources):

        @pl.when((section ^ layer) == k)
        def _():
            pltpu.make_async_copy(source.at[rows], target, sem).start()

    return pltpu.make_async_copy(sources[0].at[rows], target, sem)


def take_layer(layer, sources, target):
    section, _, _ = place()
    for k, source in enumerate(sources):

        @pl.when((section ^ layer) == k)
        def _():
            target[...] = source[...]


def affine(meta, ch):
    parts = meta[:, :LANES].astype(jnp.float32).T[:ch]
    return (
        parts[:, 0:1] + parts[:, 1:2] + parts[:, 2:3],
        parts[:, 3:4] + parts[:, 4:5] + parts[:, 5:6],
    )


def plane_inside(metas, facts):
    frames = metas.shape[0] // META_ROWS
    extents = []
    for line in (0, 1):
        total = None
        for f in range(frames):
            at = f * META_ROWS + line
            extent = metas[at : at + 1, 0:1].astype(jnp.float32) * facts[FRAME_AT + f : FRAME_AT + f + 1, :]
            total = extent if total is None else total + extent
        extents.append(total)
    on = (facts[ROW_AT : ROW_AT + 1, :] < extents[0]) & (facts[COL_AT : COL_AT + 1, :] < extents[1])
    return jnp.where(on, 1.0, 0.0)


def frames_kernel(dims, group_table, size_table, images, *refs):
    payloads, (image_in, groups, sizes, sems) = refs[:4], refs[4:]
    copies = start_all(
        [
            pltpu.make_async_copy(group_table, groups, sems.at[0]),
            pltpu.make_async_copy(size_table, sizes, sems.at[1]),
            pltpu.make_async_copy(images, image_in, sems.at[2]),
        ]
    )
    _, plane, _ = place()
    rows, cols = dims
    cells = rows * cols
    at = lax.broadcasted_iota(jnp.int32, (cells, LANES), 0).astype(jnp.float32)
    row = jnp.floor((at + 0.5) * (1.0 / cols))
    col = at - row * cols
    channels = images.shape[2]
    line = lax.broadcasted_iota(jnp.int32, (META_ROWS, channels), 0)
    wait_all(copies)
    for k in range(4):
        micro = plane ^ k
        group = groups[0, micro]
        height = sizes[0, 0]
        breadth = sizes[1, 0]
        for g in range(1, sizes.shape[1]):
            height = jnp.where(group == g, sizes[0, g], height)
            breadth = jnp.where(group == g, sizes[1, g], breadth)
        height = height.astype(jnp.float32)
        breadth = breadth.astype(jnp.float32)
        on = jnp.where((row < height) & (col < breadth), 1.0, 0.0)
        image = image_in[micro]
        for c in range(0, channels, LANES):
            piece = image[:, c : c + LANES].astype(jnp.float32) * on
            payloads[k][:cells, c : c + LANES] = piece.astype(jnp.bfloat16)
        payloads[k][cells:, :] = jnp.where(line == 0, height, breadth).astype(jnp.bfloat16)


def cot_slice_kernel(cots, out, cot_in, sems):
    copy = pltpu.make_async_copy(cots, cot_in, sems.at[0])
    copy.start()
    section, _, _ = place()
    micros, cells, channels = cots.shape
    half = channels // 2
    tile = section // 2 * LANES
    odd = section % 2 == 1
    lane = lax.broadcasted_iota(jnp.int32, (cells, LANES), 1)
    copy.wait()
    for micro in range(micros):
        low = cot_in[micro, :, pl.ds(pl.multiple_of(tile, LANES), LANES)].astype(jnp.float32)
        high = cot_in[micro, :, pl.ds(pl.multiple_of(half + tile, LANES), LANES)].astype(jnp.float32)
        low = jnp.where(odd, pltpu.roll(low, LANES // 2, 1), low)
        high = jnp.where(odd, high, pltpu.roll(high, LANES // 2, 1))
        both = jnp.where(lane < LANES // 2, low, high).astype(jnp.bfloat16)
        out[micro * cells : (micro + 1) * cells, :] = both


def cot_kernel(own, other, pick, out, full):
    _, _, core = place()
    cells = full.shape[0] // 8
    for n in range(4):
        for j, block in enumerate((own, other)):
            at = pl.multiple_of((2 * n + (core ^ j)) * cells, cells)
            full[pl.ds(at, cells), :] = block[n * cells : (n + 1) * cells, :]
    out[...] = lax.dot_general(pick[...], full[...], NT, preferred_element_type=jnp.float32).astype(
        jnp.bfloat16
    )


def pack_kernel(gain, bias, weight, *refs):
    outs, (columns, turned, tables, sems) = refs[:4], refs[4:]
    section, _, core = place()
    width = columns.shape[2]
    ch = width // 4
    start = pl.multiple_of(core * width, width)
    copies = start_all(
        [
            pltpu.make_async_copy(weight.at[tap, :, pl.ds(start, width)], columns.at[tap], sems.at[tap])
            for tap in range(TAPS)
        ]
    )
    table_copies = start_all(
        [
            pltpu.make_async_copy(gain, tables.at[0], sems.at[TAPS]),
            pltpu.make_async_copy(bias, tables.at[1], sems.at[TAPS + 1]),
        ]
    )
    for tap in range(TAPS):
        copies[tap].wait()
        turned[tap % 2] = columns[tap].T
        for k, out in enumerate(outs):
            rows = pl.ds(pl.multiple_of((section ^ k) * ch, ch), ch)
            out[tap * ch : (tap + 1) * ch, :] = turned[tap % 2, rows, :]
    wait_all(table_copies)
    for k, out in enumerate(outs):
        lines = []
        tile = pl.multiple_of(start + (section ^ k) // 2 * LANES, LANES)
        odd = (section ^ k) % 2 == 1
        for m in range(2):
            line = tables[m, :, pl.ds(tile, LANES)]
            line = jnp.where(odd, pltpu.roll(line, ch, 1), line)
            for _ in range(3):
                part = line.astype(jnp.bfloat16).astype(jnp.float32)
                lines.append(part)
                line = line - part
        lines.append(jnp.zeros((META_ROWS - len(lines), LANES), jnp.float32))
        out[TAPS * ch :, :] = jnp.zeros((META_ROWS, out.shape[1]), jnp.bfloat16)
        out[TAPS * ch :, :LANES] = jnp.concatenate(lines, axis=0).astype(jnp.bfloat16)


def pick_kernel(layer, *refs):
    sources, (out, sems) = refs[:4], refs[4:]
    pick_layer(layer, sources, 0, out, sems.at[0]).wait()


def forward_kernel(dims, layer, first, picks, pooling, *refs):
    blocks, weights, rest = refs[:8], refs[8 : 12 if picks else 9], refs[12 if picks else 9 :]
    rows, cols = dims
    cells = rows * cols
    if first:
        facts, hidden, kept, full_out, inside_out, full, taps, stage, weight, metas, sems = rest
    elif picks:
        inside, facts, hidden, kept, full_out, full, taps, stage, weight, sems = rest
    else:
        inside, facts, hidden, kept, full_out, full, taps, stage, sems = rest
        (weight,) = weights
    if first:
        take_layer(layer, weights, weight)
    elif picks:
        copy = pick_layer(layer, weights, 0, weight, sems.at[2])
    facts_now = facts[...]
    if first:
        channels = full.shape[1]
        assemble_frames(blocks, full, slice(0, cells), slice(0, channels))
    else:
        assemble(blocks, full)
    full_copy = pltpu.make_async_copy(full, full_out, sems.at[0])
    full_copy.start()
    if first:
        assemble_frames(blocks, metas, slice(cells, cells + META_ROWS), slice(0, channels))
        inside_now = plane_inside(metas, facts_now)
        inside_out[...] = inside_now
    else:
        inside_now = inside[...]
    if picks and not first:
        copy.wait()
    ch = hidden.shape[0]
    tap_products(weight[: TAPS * ch, :], full, taps, first)
    pre = sum_taps(taps, facts_now, cols)
    normed, scale = normalise(pre, inside_now)
    length = normed.shape[1]
    stage[:, :length] = normed
    stage[:, length:] = jnp.broadcast_to(scale, (ch, LANES))
    kept_copy = pltpu.make_async_copy(stage, kept, sems.at[1])
    kept_copy.start()
    gain, bias = affine(weight[TAPS * ch :, :], ch)
    hidden[...] = hidden_of(normed, gain, bias, inside_now, facts_now, cols, pooling).astype(jnp.bfloat16)
    full_copy.wait()
    kept_copy.wait()


def turn_kernel(dims, layer, pooling, *refs):
    blocks, (weight, cot_in, inside, facts) = refs[:8], refs[8:12]
    hidden_out, full_out, grad_pre, sums, full, taps, hidden, sems = refs[12:]
    cols = dims[1]
    assemble(blocks, full)
    full_copy = pltpu.make_async_copy(full, full_out, sems.at[1])
    full_copy.start()
    ch = grad_pre.shape[0]
    tap_products(weight[: TAPS * ch, :], full, taps, False)
    facts_now, inside_now = facts[...], inside[...]
    pre = sum_taps(taps, facts_now, cols)
    normed, scale = normalise(pre, inside_now)
    gain, bias = affine(weight[TAPS * ch :, :], ch)
    hidden[...] = hidden_of(normed, gain, bias, inside_now, facts_now, cols, pooling).astype(jnp.bfloat16)
    hidden_copy = pltpu.make_async_copy(hidden, hidden_out, sems.at[2])
    hidden_copy.start()
    grad_pre[...], shift_sum, slope_sum = norm_back(
        cot_in[...].astype(jnp.float32), normed, scale, gain, bias, inside_now, facts_now, cols, pooling
    )
    sums[...] = with_sums(layer, shift_sum, slope_sum, 0.0)
    full_copy.wait()
    hidden_copy.wait()


def with_sums(layer, shift_sum, slope_sum, others):
    at = lax.broadcasted_iota(jnp.int32, (shift_sum.shape[0], LANES), 1)
    return jnp.where(at == 2 * layer, shift_sum, jnp.where(at == 2 * layer + 1, slope_sum, others))


def add_blocks(blocks):
    total = blocks[0][...].astype(jnp.float32)
    for block in blocks[1:]:
        total = total + block[...].astype(jnp.float32)
    return total


def fetch_kernel(layer, kept, *refs):
    sources, (kept_out, meta_out, sems) = refs[:4], refs[4:]
    copy = pltpu.make_async_copy(kept, kept_out, sems.at[0])
    copy.start()
    start = sources[0].shape[0] - META_ROWS
    pick_layer(layer, sources, start, meta_out, sems.at[1]).wait()
    copy.wait()


def norm_back_kernel(dims, layer, pooling, *refs):
    blocks, (kept, meta, inside, facts, sums_in, grad_pre, sums) = refs[:4], refs[4:]
    ch, length = grad_pre.shape
    grad = add_blocks(blocks).astype(jnp.bfloat16).astype(jnp.float32)
    gain, bias = affine(meta[...], ch)
    grad_pre[...], shift_sum, slope_sum = norm_back(
        grad,
        kept[:, :length],
        kept[:, length : length + 1],
        gain,
        bias,
        inside[...],
        facts[...],
        dims[1],
        pooling,
    )
    sums[...] = with_sums(layer, shift_sum, slope_sum, sums_in[...])


def weight_product(moved, full, first):
    if first:
        return jnp.dot(moved, full, preferred_element_type=jnp.float32)
    return lax.dot_general(moved, full, NT, preferred_element_type=jnp.float32)


def sums_rows(sums, width):
    ch = sums.shape[0]
    turned = jnp.concatenate([sums[...].T, jnp.zeros((LANES, width - ch), jnp.float32)], axis=1)
    return turned[:META_ROWS].astype(jnp.bfloat16)


def form_share(layer, moved, full, sums, product):
    piece = product.shape[0] // 4
    rows = piece - META_ROWS * len(sums)
    width = product.shape[1]
    value = weight_product(moved[:rows, :], full[...], layer == 0)
    for n in range(4):
        product[n * piece : n * piece + rows, :] = value[:, n * width : (n + 1) * width].astype(jnp.bfloat16)
        for ref in sums:
            product[n * piece + rows : (n + 1) * piece, :] = sums_rows(ref, width)


def conv_back_kernel(dims, layer, own, other, own_weights, other_weights, full_in, facts, *refs):
    sums, outs, (share, product, full, moved, weights, sems) = refs[:-10], refs[-10:-6], refs[-6:]
    ch = own.shape[0]
    size = moved.shape[0] // 2
    rows = pl.ds(layer * 4 * ch, 4 * ch)
    copies = start_all(
        [
            pltpu.make_async_copy(own_weights.at[rows], weights.at[:, pl.ds(0, size)], sems.at[0]),
            pltpu.make_async_copy(other_weights, weights.at[:, pl.ds(size, size)], sems.at[1]),
        ]
    )
    full_copy = pltpu.make_async_copy(full_in, full, sems.at[2])
    full_copy.start()
    facts_now = facts[...]
    spread_taps(own[...], moved, 0, facts_now, dims[1])
    full_copy.wait()
    form_share(layer, moved, full, sums, product)
    share_copy = pltpu.make_async_copy(product, share, sems.at[3])
    share_copy.start()
    spread_taps(other[...], moved, size, facts_now, dims[1])
    for n in range(2):
        moved[n * size + TAPS * ch : (n + 1) * size, :] = jnp.zeros(
            (size - TAPS * ch, moved.shape[1]), jnp.bfloat16
        )
    wait_all(copies)
    value = jnp.dot(weights[...], moved[...], preferred_element_type=jnp.float32)
    for k, out in enumerate(outs):
        out[...] = value[k * ch : (k + 1) * ch, :].astype(jnp.bfloat16)
    share_copy.wait()


def fold_kernel(*refs):
    count = (len(refs) - 2) // 2
    shares, outs, (blocks, sems) = refs[:count], refs[count:-2], refs[-2:]
    rows = outs[0].shape[0]
    copies = start_all(
        [pltpu.make_async_copy(share, blocks.at[n], sems.at[n]) for n, share in enumerate(shares)]
    )
    for n, copy in enumerate(copies):
        copy.wait()
        value = add_blocks([blocks.at[n, pl.ds(m * rows, rows)] for m in range(blocks.shape[1] // rows)])
        outs[n][...] = value.astype(jnp.bfloat16)


def choose_kernel(*refs):
    last, others, outs = refs[0], refs[1:-4], refs[-4:]
    section, _, _ = place()
    rows = outs[0].shape[0]
    value = add_blocks([last.at[pl.ds(n * rows, rows)] for n in range(last.shape[0] // rows)])
    value = value.astype(jnp.bfloat16)
    for k, out in enumerate(outs):

        @pl.when((section ^ k) == 0)
        def _():
            out[...] = value

        for layer, other in enumerate(others, 1):

            @pl.when((section ^ k) == layer)
            def _():
                out[: other.shape[0], :] = other[...]
                out[other.shape[0] :, :] = value[other.shape[0] :, :]


def turn_weights_kernel(layers, *refs):
    sources, own, others, (full, turned, stage, sems) = refs[:4], refs[4], refs[5:-4], refs[-4:]
    section, _, core = place()
    rows, channels = full.shape[1:]
    half = channels // 2
    ch = half // 4
    copies = [pick_layer(n, sources, 0, full.at[n], sems.at[n]) for n in range(layers)]
    stage[:, :, rows:] = jnp.zeros((*stage.shape[:2], stage.shape[2] - rows), jnp.bfloat16)
    for n in range(layers):
        copies[n].wait()
        turned[...] = full[n].T
        for j in range(2):
            for k in range(4):
                at = pl.multiple_of((core ^ j) * half + (section ^ k) * ch, ch)
                stage[j, n * half + k * ch : n * half + (k + 1) * ch, :rows] = turned[pl.ds(at, ch), :]
    copies = [pltpu.make_async_copy(stage.at[0], own, sems.at[0])]
    for n, other in enumerate(others):
        source = stage.at[1, pl.ds(n * half, half)]
        copies.append(pltpu.make_async_copy(source, other, sems.at[1 + n]))
    wait_all(start_all(copies))


def input_kernel(*refs):
    blocks, (hidden, inside, keep, give, full, sems) = refs[:4], refs[4:]
    section, _, core = place()
    ch = hidden.shape[0]
    copy = pltpu.make_async_copy(hidden, full.at[pl.ds(0, ch)], sems.at[0])
    copy.start()
    full[ch:, :] = (add_blocks(blocks) * inside[...]).astype(jnp.bfloat16)
    copy.wait()
    rows = 2 * ch
    width = keep.shape[1]
    for j, out in enumerate((keep, give)):
        for n in range(2):
            at = pl.multiple_of((section ^ (2 * (core ^ j) + n)) * width, width)
            out[n * rows : (n + 1) * rows, :] = full[:, pl.ds(at, width)]


def pair_kernel(keep, got, *outs):
    rows = keep.shape[0] // 2
    for n, out in enumerate(outs):
        out[:rows, :] = keep[n * rows : (n + 1) * rows, :]
        out[rows:, :] = got[n * rows : (n + 1) * rows, :]


def store_maps(blocks, pick, outs, full):
    _, plane, core = place()
    ch = blocks[0].shape[0] // 4
    for m, out in enumerate(outs):
        for j in range(2):
            for n in range(2):
                for h in range(2):
                    slot = slice_at(plane ^ (2 * (core ^ j) + n), core ^ j, 0, h)
                    at = pl.multiple_of(slot * ch, ch)
                    start = (2 * h + m) * ch
                    full[m, pl.ds(at, ch), :] = blocks[2 * j + n][start : start + ch, :]
        mine = lax.dot_general(pick[...], full[m], NT, preferred_element_type=jnp.float32)
        out[...] = mine.astype(out.dtype)


def outputs_kernel(*refs):
    blocks, pick, map_blocks, map_pick, refs = refs[:8], refs[8], refs[9:13], refs[13], refs[14:]
    (weight_out, shift_out, slope_out), map_outs, (full, maps_full) = refs[:3], refs[3:5], refs[5:]
    store_maps(map_blocks, map_pick, map_outs, maps_full)
    section, plane, core = place()
    taps, rows, channels = weight_out.shape
    for tap in range(taps):
        for (k, j), block in zip(peer_order(), blocks):
            at = pl.multiple_of(slice_at(section, core, k, j) * rows, rows)
            full[tap, pl.ds(at, rows), :] = block[tap * rows : (tap + 1) * rows, :]
        weight_out[tap] = lax.dot_general(pick[...], full[tap], NT, preferred_element_type=jnp.float32)
    shift_row = jnp.zeros((1, rows), jnp.float32)
    slope_row = jnp.zeros((1, rows), jnp.float32)
    slot = plane * 2 + core
    for (k, j), block in zip(peer_order(), blocks):
        tail = block[taps * rows :, :rows].astype(jnp.float32)
        at = lax.broadcasted_iota(jnp.int32, tail.shape, 0)
        mine = slice_at(section, core, k, j) == slot
        shift_row = shift_row + jnp.sum(jnp.where(mine & (at == 2 * section), tail, 0.0), axis=0, keepdims=True)
        slope_row = slope_row + jnp.sum(jnp.where(mine & (at == 2 * section + 1), tail, 0.0), axis=0, keepdims=True)
    shift_out[...] = shift_row
    slope_out[...] = slope_row


def call(
    kernel, outs, scratch, args, name, held=(), free=(), held_outs=(), loose=(), last=False, flops=0, copies=None
):
    shapes = [
        (jax.ShapeDtypeStruct if last else pltpu.HBM if n in held_outs else pltpu.VMEM)(shape, dtype)
        for n, (shape, dtype) in enumerate(outs)
    ]
    moved = sum(a.size * a.dtype.itemsize for a in args)
    moved += sum(math.prod(shape) * jnp.dtype(dtype).itemsize for shape, dtype in outs)
    spaces = [pl.ANY if n in free else pltpu.HBM if n in held else pltpu.VMEM for n in range(len(args))]
    out_spaces = [pltpu.HBM if n in held_outs else pltpu.VMEM for n in range(len(outs))]
    args = [
        a if n in loose or n in free else pltpu.with_memory_space_constraint(a, space)
        for n, (a, space) in enumerate(zip(args, spaces))
    ]
    scratch_shapes = [
        pltpu.SMEM(shape, dtype) if dtype == jnp.int32 else pltpu.VMEM(shape, dtype) for shape, dtype in scratch
    ]
    if copies is not None:
        scratch_shapes.append(pltpu.SemaphoreType.DMA((copies,)))
    return pl.pallas_call(
        kernel,
        out_shape=shapes,
        in_specs=[pl.BlockSpec(memory_space=space) for space in spaces],
        out_specs=[pl.BlockSpec(memory_space=space) for space in out_spaces],
        scratch_shapes=scratch_shapes,
        compiler_params=pltpu.CompilerParams(vmem_limit_bytes=VMEM_LIMIT),
        cost_estimate=pl.CostEstimate(flops=flops, bytes_accessed=moved, transcendentals=0),
        name=name,
    )(*args)


def plane_shards(images, image_group, group_size, conv_weight, bn_gain, bn_bias, cotangent):
    _, _, core = place()
    micro_total, _, rows, cols, channels = images.shape
    layers = lax.axis_size("section")
    last = layers - 1
    cells = rows * cols
    frames = 2 * micro_total
    length = frames * cells
    ch = channels // 8
    dims = (rows, cols)
    bf16, f32 = jnp.bfloat16, jnp.float32
    facts = grid_facts(frames, rows, cols)
    conv_flops = 2 * TAPS * ch * channels * length
    slice_rows = TAPS * ch + META_ROWS
    tap_rows = -(-TAPS * ch // LANES) * LANES

    full_map = ((channels, length), bf16)
    full_frames = ((length, channels), bf16)
    tap_scratch = ((TAPS * ch, length), f32)
    weight_slice = ((slice_rows, channels), bf16)
    map_out = ((ch, length), bf16)
    sums_out = ((ch, LANES), f32)
    kept_out = ((ch, length + LANES), f32)
    piece_rows = [slice_rows] + [TAPS * ch] * last

    taps_first = conv_weight[0].transpose(1, 2, 0, 3).reshape(TAPS, channels, channels)
    packed = call(
        pack_kernel,
        [weight_slice] * 4,
        [
            ((TAPS, channels, 4 * ch), bf16),
            ((2, 4 * ch, channels), bf16),
            ((2, 1, channels), f32),
        ],
        [bn_gain, bn_bias, taps_first],
        "weight_pack",
        held=range(3),
        copies=TAPS + 2,
    )
    slices = spread(packed, to_section)

    payload = ((cells + META_ROWS, channels), bf16)
    sent = call(
        partial(frames_kernel, dims),
        [payload] * 4,
        [
            ((micro_total, cells, channels), bf16),
            (image_group.shape[::-1], jnp.int32),
            (group_size.shape[::-1], jnp.int32),
        ],
        [image_group.T, group_size.T, after(images.reshape(micro_total, cells, channels), packed)],
        "frames",
        held=range(3),
        copies=3,
    )
    frames_in = with_core(spread(sent, to_plane))

    half = (core * ch + np.arange(ch))[:, None] == np.arange(2 * ch)[None, :]
    hidden, normed, full, inside = call(
        partial(forward_kernel, dims, 0, True, True, CONVS == 1),
        [map_out, kept_out, full_frames, ((1, length), f32)],
        [
            full_frames,
            tap_scratch,
            kept_out,
            weight_slice,
            ((frames * META_ROWS, channels), bf16),
        ],
        [*frames_in, *slices, facts],
        "forward",
        held_outs=(1, 2),
        loose=(8, 9, 10, 11, 12),
        flops=conv_flops,
        copies=4,
    )
    kept, fulls = [normed], [full]
    same_core = [[2 * z + c for z in range(layers)] for c in range(2)]
    for layer in range(1, layers):
        weights = call(
            partial(pick_kernel, layer),
            [weight_slice],
            [],
            after(slices, hidden),
            "pick",
            flops=PICK_FLOPS,
            held=range(4),
            copies=1,
        )
        beside = [*weights]
        if layer == 1:
            turned, *crossing = call(
                partial(turn_weights_kernel, layers),
                [((layers * 4 * ch, tap_rows), bf16)] + [((4 * ch, tap_rows), bf16)] * layers,
                [
                    ((layers, TAPS * ch, channels), bf16),
                    ((channels, TAPS * ch), bf16),
                    ((2, layers * 4 * ch, tap_rows), bf16),
                ],
                after(slices, hidden),
                "turn_weights",
                held=range(4),
                held_outs=range(1 + layers),
                copies=1 + layers,
            )
            beside.append((turned, crossing))
        if layer == COT_LAYER - 1:
            (cot_slots,) = call(
                cot_slice_kernel,
                [((micro_total * cells, LANES), bf16)],
                [((micro_total, cells, channels), bf16)],
                [after(cotangent.reshape(micro_total, cells, channels), hidden)],
                "cot_slices",
                held=(0,),
                copies=1,
            )
            beside.append(cot_slots)
        if layer == COT_LAYER:
            cot_slots = after(cot_slots, hidden)
            cots = lax.all_to_all(cot_slots, "dp", 0, 0, tiled=True, axis_index_groups=same_core)
        if layer == last:
            crossing[last] = to_core(after(crossing[last], hidden))
            cots = after(cots, hidden)
            (cot,) = call(
                cot_kernel,
                [map_out],
                [((length, LANES), bf16)],
                [cots, to_core(cots), half.astype(bf16)],
                "cotangent",
                loose=(0, 1, 2),
            )
            beside.append(cot)
        blocks = [hidden] + [to_section(hidden, k) for k in (1, 2, 3)]
        blocks[3] = after(blocks[3], *beside)
        blocks = with_core(blocks)
        if layer < last:
            hidden, normed, full = call(
                partial(forward_kernel, dims, layer, False, False, layer == CONVS - 1),
                [map_out, kept_out, full_map],
                [full_map, tap_scratch, kept_out],
                [*blocks, *weights, inside, facts],
                "forward",
                held_outs=(1, 2),
                loose=(9, 10),
                flops=conv_flops,
                copies=3,
            )
            kept.append(normed)
        else:
            activation, full, grad_pre, sums = call(
                partial(turn_kernel, dims, last, last == CONVS - 1),
                [map_out, full_map, map_out, sums_out],
                [full_map, tap_scratch, map_out],
                [*blocks, *weights, cot, inside, facts],
                "turn",
                held_outs=(0, 1),
                loose=(10, 11),
                flops=conv_flops,
                copies=3,
            )
        fulls.append(full)

    shares = [None] * layers
    for layer in range(last, -1, -1):
        share_out = ((4 * piece_rows[layer], 2 * ch), bf16)
        *parts, share = call(
            partial(conv_back_kernel, dims, layer),
            [map_out] * 4 + [share_out],
            [
                share_out,
                full_map if layer else full_frames,
                ((2 * tap_rows, length), bf16),
                ((4 * ch, 2 * tap_rows), bf16),
            ],
            [grad_pre, to_core(grad_pre), turned, crossing[layer], fulls[layer], facts]
            + ([] if layer else [sums]),
            "conv_back",
            held=(2, 4),
            free=(3,),
            held_outs=(4,),
            loose=(5,) if layer else (5, 6),
            flops=BACK_FLOPS[layer],
            copies=4,
        )
        if layer < last:
            share = after(share, shares[layer + 1])
        shares[layer] = lax.all_to_all(share, "dp", 0, 0, tiled=True, axis_index_groups=same_core)
        if layer:
            crossing[layer - 1] = to_core(after(crossing[layer - 1], parts))
            held = call(
                partial(fetch_kernel, layer - 1),
                [kept_out, ((META_ROWS, channels), bf16)],
                [],
                [after(kept[layer - 1], parts), *slices],
                "fetch",
                held=range(5),
                copies=2,
            )
            blocks = spread(parts, to_section, held)
            grad_pre, sums = call(
                partial(norm_back_kernel, dims, layer - 1, layer - 1 == CONVS - 1),
                [map_out, sums_out],
                [],
                [*blocks, *held, inside, facts, sums],
                "norm_back",
                loose=(6, 7, 8),
            )
    blocks = spread(parts, to_section)
    keep, give = call(
        input_kernel,
        [((4 * ch, 2 * cells), bf16)] * 2,
        [((2 * ch, length), bf16)],
        [*blocks, activation, inside],
        "input",
        flops=INPUT_FLOPS,
        held=(4,),
        loose=(5,),
        copies=1,
    )
    maps = call(pair_kernel, [((4 * ch, 2 * cells), bf16)] * 2, [], [keep, to_core(give)], "pair")
    maps = [send(x, lambda s, z, c, n=n: (z, s ^ (2 * c + n), c)) for n, x in enumerate(maps)]
    folded = call(
        fold_kernel,
        [((rows, 2 * ch), bf16) for rows in piece_rows[1:]],
        [((last, 4 * TAPS * ch, 2 * ch), bf16)],
        shares[1:],
        "fold",
        held=range(last),
        copies=last,
    )
    chosen = call(
        choose_kernel,
        [((slice_rows, 2 * ch), bf16)] * 4,
        [],
        [shares[0], *folded],
        "choose",
        loose=(0,),
    )
    pick = (core * cells + np.arange(cells))[:, None] == np.arange(2 * cells)[None, :]
    map_pick = pick.astype(bf16)
    pick = (core * ch + np.arange(ch))[:, None] == np.arange(2 * ch)[None, :]
    weight_grad, bias_grad, gain_grad, activations, input_grad = call(
        outputs_kernel,
        [((TAPS, ch, channels), f32), ((1, ch), f32), ((1, ch), f32)] + [((cells, channels), bf16)] * 2,
        [((TAPS, channels, 2 * ch), bf16), ((2, channels, 2 * cells), bf16)],
        [
            *with_core([chosen[0]] + [to_section(chosen[k], k) for k in (1, 2, 3)]),
            pick.astype(bf16),
            *with_core(after(maps, chosen)),
            map_pick,
        ],
        "outputs",
        loose=(8, 13),
        last=True,
    )
    weight_grad = weight_grad.reshape(3, 3, ch, channels).transpose(2, 0, 1, 3)[None]
    return (
        activations.reshape(1, 1, rows, cols, channels),
        input_grad.reshape(1, 1, rows, cols, channels),
        weight_grad,
        gain_grad,
        bias_grad,
    )


def fits_plane_plan(images, conv_weight, sections, dps):
    micro_total, images_total, rows, cols, channels = images.shape
    return (
        sections == 4
        and dps == 2 * sections
        and micro_total == sections
        and conv_weight.shape[0] == sections
        and images_total == dps
        and rows % 2 == 0
        and cols % 2 == 0
        and (rows * cols) % 64 == 0
        and channels == 512
    )


def solution(mesh):
    in_specs = (
        P(None, "dp", None, None, None),
        P(None, "dp"),
        P(),
        P("section", None, None, None, None),
        P("section", None),
        P("section", None),
        P(None, "dp", None, None, None),
    )
    out_specs = (
        P("section", "dp", None, None, None),
        P("section", "dp", None, None, None),
        P("section", "dp", None, None, None),
        P("section", "dp"),
        P("section", "dp"),
    )
    sections, dps = mesh.shape["section"], mesh.shape["dp"]

    def program(images, image_group, group_size, conv_weight, bn_gain, bn_bias, cotangent):
        plan = plane_shards if fits_plane_plan(images, conv_weight, sections, dps) else pipeline_shards
        sharded = jax.shard_map(plan, mesh=mesh, in_specs=in_specs, out_specs=out_specs, check_vma=False)
        return sharded(images, image_group, group_size, conv_weight, bn_gain, bn_bias, cotangent)

    return program
```

```python
import math
from functools import partial

import jax
import jax.numpy as jnp
import numpy as np
from jax import lax
from jax.experimental import pallas as pl
from jax.experimental.pallas import tpu as pltpu
from jax.sharding import PartitionSpec as P

CONVS = 2
BACK_FLOPS = (3 * 10**9, 52 * 10**8, 52 * 10**8, 0)
PICK_FLOPS = 2 * 10**9
COT_LAYER = 2
INPUT_FLOPS = 0 * 10**9


eps = 1e-05


def from_behind(x, axis, by):
    peers = lax.axis_size(axis)
    pairs = [(i, i + by) for i in range(peers) if 0 <= i + by < peers]
    return lax.ppermute(x, axis, pairs)


def canvas_mask(image_group, group_size, canvas_rows, canvas_cols):
    groups_n = group_size.shape[0]
    onehot = image_group[..., None] == jnp.arange(groups_n, dtype=jnp.int32)
    height = jnp.sum(jnp.where(onehot, group_size[:, 0], 0), axis=-1)
    breadth = jnp.sum(jnp.where(onehot, group_size[:, 1], 0), axis=-1)
    inside_rows = jnp.arange(canvas_rows, dtype=jnp.int32)[:, None] < height[..., None, None]
    inside_cols = jnp.arange(canvas_cols, dtype=jnp.int32)[None, :] < breadth[..., None, None]
    return (inside_rows & inside_cols).astype(jnp.float32)[..., None]


def window_pool(hidden):
    frames, height, breadth, channels = hidden.shape
    blocks = hidden.reshape(frames, height // 2, 2, breadth // 2, 2, channels)
    window_max = jnp.max(blocks, axis=(2, 4), keepdims=True)
    raised = jnp.exp(blocks - window_max)
    weights = raised / jnp.sum(raised, axis=(2, 4), keepdims=True)
    pooled = jnp.sum(weights * blocks, axis=(2, 4), keepdims=True)
    return (weights * pooled).reshape(frames, height, breadth, channels)


def activate(pre_act, inside, pooling):
    hidden = jax.nn.silu(pre_act) * inside
    return jnp.where(pooling, window_pool(hidden) * inside, hidden)


def conv_forward(layer_in, weight):
    return lax.conv_general_dilated(
        layer_in,
        weight,
        (1, 1),
        "SAME",
        dimension_numbers=("NHWC", "IHWO", "NHWC"),
        preferred_element_type=jnp.float32,
    )


def conv_data_back(grad_pre, weight):
    flipped = weight[:, ::-1, ::-1, :]
    return lax.conv_general_dilated(
        grad_pre,
        flipped,
        (1, 1),
        "SAME",
        dimension_numbers=("NHWC", "OHWI", "NHWC"),
        preferred_element_type=jnp.float32,
    )


def weight_back(layer_in, grad_pre):
    height = layer_in.shape[1]
    breadth = layer_in.shape[2]
    padded = jnp.pad(layer_in, ((0, 0), (1, 1), (1, 1), (0, 0)))
    pieces = []
    for tap_row in range(3):
        for tap_col in range(3):
            window = padded[:, tap_row : tap_row + height, tap_col : tap_col + breadth, :]
            pieces.append(
                jnp.einsum("nhwi,nhwo->io", window, grad_pre, preferred_element_type=jnp.float32)
            )
    return jnp.stack(pieces, axis=1).reshape(layer_in.shape[3], 3, 3, grad_pre.shape[3])


def layer_forward(layer_in, weight, gain_row, bias_row, inside, pooling):
    pre_norm = conv_forward(layer_in, weight)
    sums = lax.psum(
        (
            jnp.sum(pre_norm * inside, axis=(0, 1, 2)),
            jnp.sum(pre_norm * pre_norm * inside, axis=(0, 1, 2)),
            jnp.sum(inside),
        ),
        "dp",
    )
    pixel_total = sums[2]
    mean_val = sums[0] / pixel_total
    scale_inv = lax.rsqrt(sums[1] / pixel_total - mean_val * mean_val + eps)
    pre_act = (pre_norm - mean_val) * scale_inv * gain_row + bias_row
    hidden = activate(pre_act, inside, pooling)
    return (pre_norm, mean_val, scale_inv, pixel_total, hidden)


def layer_backward(
    grad_out,
    layer_in,
    pre_norm,
    mean_val,
    scale_inv,
    pixel_total,
    weight,
    gain_row,
    bias_row,
    inside,
    pooling,
):
    normed = (pre_norm - mean_val) * scale_inv
    pre_act = normed * gain_row + bias_row
    hidden_out, pullback = jax.vjp(partial(activate, inside=inside, pooling=pooling), pre_act)
    grad_act = pullback(grad_out)[0]
    sums = lax.psum(
        (jnp.sum(grad_act, axis=(0, 1, 2)), jnp.sum(grad_act * normed, axis=(0, 1, 2))), "dp"
    )
    shift_term = sums[0] / pixel_total
    slope_term = sums[1] / pixel_total
    grad_pre = (
        inside * scale_inv * gain_row * (grad_act - shift_term - normed * slope_term)
    ).astype(jnp.bfloat16)
    weight_term = weight_back(layer_in, grad_pre)
    grad_in = conv_data_back(grad_pre, weight).astype(jnp.bfloat16)
    return (grad_in, weight_term, sums[1], sums[0])


def pipeline_shards(images, image_group, group_size, conv_weight, bn_gain, bn_bias, cotangent):
    section_index = lax.axis_index("section")
    sections = lax.axis_size("section")
    micro_total = images.shape[0]
    channels = conv_weight.shape[1]
    inside_all = canvas_mask(image_group, group_size, images.shape[2], images.shape[3])
    ticks = micro_total + sections - 1
    weight = conv_weight[0]
    gain_row = bn_gain[0]
    bias_row = bn_bias[0]
    pool_here = section_index == CONVS - 1
    received = jnp.zeros(images.shape[1:], jnp.bfloat16)
    kept_in, kept_pre, kept_mean, kept_scale, kept_total, finished = ([], [], [], [], [], [])
    for tick in range(ticks):
        micro_pos = jnp.clip(tick - section_index, 0, micro_total - 1)
        inside = inside_all[micro_pos]
        fresh = (images[micro_pos].astype(jnp.float32) * inside).astype(jnp.bfloat16)
        layer_in = jnp.where(section_index == 0, fresh, received)
        pre_norm, mean_val, scale_inv, pixel_total, hidden = layer_forward(
            layer_in, weight, gain_row, bias_row, inside, pool_here
        )
        sent = hidden.astype(jnp.bfloat16)
        if tick < ticks - 1:
            received = from_behind(sent, "section", 1)
        kept_in.append(layer_in)
        kept_pre.append(pre_norm)
        kept_mean.append(mean_val)
        kept_scale.append(scale_inv)
        kept_total.append(pixel_total)
        finished.append(sent)
    stack_in = jnp.stack(kept_in)
    stack_pre = jnp.stack(kept_pre)
    stack_mean = jnp.stack(kept_mean)
    stack_scale = jnp.stack(kept_scale)
    stack_total = jnp.stack(kept_total)
    returned = jnp.zeros(images.shape[1:], jnp.bfloat16)
    weight_sum = jnp.zeros(conv_weight.shape[1:], jnp.float32)
    gain_sum = jnp.zeros((channels,), jnp.float32)
    bias_sum = jnp.zeros((channels,), jnp.float32)
    input_list = []
    for tick in range(ticks):
        micro_raw = tick - (sections - 1 - section_index)
        valid = ((micro_raw >= 0) & (micro_raw < micro_total)).astype(jnp.float32)
        micro_pos = jnp.clip(micro_raw, 0, micro_total - 1)
        forward_tick = jnp.clip(micro_pos + section_index, 0, ticks - 1)
        inside = inside_all[micro_pos]
        grad_out = jnp.where(
            section_index == sections - 1,
            cotangent[micro_pos].astype(jnp.float32),
            returned.astype(jnp.float32),
        )
        grad_in, weight_term, gain_term, bias_term = layer_backward(
            grad_out,
            stack_in[forward_tick],
            stack_pre[forward_tick],
            stack_mean[forward_tick],
            stack_scale[forward_tick],
            stack_total[forward_tick],
            weight,
            gain_row,
            bias_row,
            inside,
            pool_here,
        )
        weight_sum = weight_sum + valid * weight_term
        gain_sum = gain_sum + valid * gain_term
        bias_sum = bias_sum + valid * bias_term
        if tick < ticks - 1:
            returned = from_behind(grad_in, "section", -1)
        input_list.append((grad_in.astype(jnp.float32) * inside).astype(jnp.bfloat16))
    out_stack = jnp.stack(finished[sections - 1 :], axis=0)
    grad_stack = jnp.stack(input_list[sections - 1 :], axis=0)
    out_back, grad_back = (
        lax.all_to_all(out_stack, "section", split_axis=0, concat_axis=1, tiled=True),
        lax.all_to_all(grad_stack, "section", split_axis=0, concat_axis=1, tiled=True),
    )
    activations = out_back[:, sections - 1 : sections]
    input_grad = grad_back[:, 0:1]
    weight_grad = lax.psum_scatter(weight_sum[None], "dp", scatter_dimension=1, tiled=True)
    share = channels // lax.axis_size("dp")
    gain_grad = lax.dynamic_slice_in_dim(gain_sum, lax.axis_index("dp") * share, share)[None]
    bias_grad = lax.dynamic_slice_in_dim(bias_sum, lax.axis_index("dp") * share, share)[None]
    return (activations, input_grad, weight_grad, gain_grad, bias_grad)


AXES = ("section", "dp")
TAPS = 9
VMEM_LIMIT = 24 * 1024 * 1024
META_ROWS = 16
LANES = 128
ROW_AT, COL_AT, FRAME_AT = 6, 7, 8
NT = (((1,), (1,)), ((), ()))


def place():
    dp_index = lax.axis_index("dp")
    return lax.axis_index("section"), dp_index // 2, dp_index % 2


def peer_order():
    return [(k, j) for j in range(2) for k in range(4)]


def slice_at(section, core, k, j):
    return (core ^ j) * lax.axis_size("section") + (section ^ k)


def send(x, target):
    sections = lax.axis_size("section")
    dps = lax.axis_size("dp")
    pairs = []
    for s in range(sections):
        for d in range(dps):
            ts, tz, tc = target(s, d // 2, d % 2)
            pairs.append((s * dps + d, ts * dps + tz * 2 + tc))
    return lax.ppermute(x, AXES, pairs)


def to_section(x, k):
    return send(x, lambda s, z, c: (s ^ k, z, c))


def to_plane(x, k):
    return send(x, lambda s, z, c: (s, z ^ k, c))


def to_core(x):
    return send(x, lambda s, z, c: (s, z, c ^ 1))


def spread(blocks, move, *beside):
    moved = lax.optimization_barrier(([move(blocks[k], k) for k in (1, 2, 3)], beside))[0]
    return [blocks[0]] + moved


def with_core(blocks):
    return blocks + [to_core(x) for x in blocks]


def after(x, *first):
    return lax.optimization_barrier((x, first))[0]


def grid_facts(frames, rows, cols):
    at = np.arange(frames * rows * cols)
    col = at % cols
    row = (at // cols) % rows
    facts = [row > 0, row < rows - 1, col > 0, col < cols - 1, col % 2 == 0, row % 2 == 0, row, col]
    facts = facts + [at // (rows * cols) == frame for frame in range(frames)]
    return jnp.asarray(np.stack(facts).astype(np.float32))


def shift(x, by):
    length = x.shape[1]
    return pltpu.roll(x, (-by) % length, 1) if by % length else x


def row_ok(facts, d):
    return facts[0:1, :] if d < 0 else facts[1:2, :]


def col_ok(facts, d):
    return facts[2:3, :] if d < 0 else facts[3:4, :]


def sum_taps(taps_ref, facts, cols):
    ch = taps_ref.shape[0] // TAPS
    total = None
    for dx in (-1, 0, 1):
        column = None
        for dy in (-1, 0, 1):
            tap = (dy + 1) * 3 + dx + 1
            piece = taps_ref[tap * ch : (tap + 1) * ch, :]
            if dy:
                piece = shift(piece, dy * cols) * row_ok(facts, dy)
            column = piece if column is None else column + piece
        if dx:
            column = shift(column, dx) * col_ok(facts, dx)
        total = column if total is None else total + column
    return total


def spread_taps(grad, moved_ref, base, facts, cols):
    ch = grad.shape[0]
    facts = facts[:4, :].astype(grad.dtype)
    for dx in (-1, 0, 1):
        column = shift(grad, -dx) * col_ok(facts, -dx) if dx else grad
        for dy in (-1, 0, 1):
            piece = shift(column, -dy * cols) * row_ok(facts, -dy) if dy else column
            at = base + ((dy + 1) * 3 + dx + 1) * ch
            moved_ref[at : at + ch, :] = piece


def corner_sum(x, cols):
    x = x + shift(x, 1)
    return x + shift(x, cols)


def from_corner(x, facts, cols):
    x = jnp.where(facts[4:5, :] > 0.5, x, shift(x, -1))
    return jnp.where(facts[5:6, :] > 0.5, x, shift(x, -cols))


def lane_sum(x):
    return jnp.sum(x, axis=1, keepdims=True)


def normalise(pre, inside):
    count = lane_sum(inside)
    mean = lane_sum(pre * inside) / count
    square = lane_sum(pre * pre * inside) / count
    scale = lax.rsqrt(square - mean * mean + eps)
    return (pre - mean) * scale, scale


def hidden_of(normed, gain, bias, inside, facts, cols, pooling):
    pre_act = normed * gain + bias
    hidden = pre_act * jax.nn.sigmoid(pre_act) * inside
    if pooling:
        raised = jnp.exp(hidden)
        total = corner_sum(raised, cols)
        pooled = corner_sum(raised * hidden, cols) / total
        hidden = raised * from_corner(pooled / total, facts, cols) * inside
    return hidden


def norm_back(grad, normed, scale, gain, bias, inside, facts, cols, pooling):
    pre_act = normed * gain + bias
    gate = jax.nn.sigmoid(pre_act)
    if pooling:
        hidden = pre_act * gate * inside
        raised = jnp.exp(hidden)
        out = grad * inside
        total = 1.0 / corner_sum(raised, cols)
        pooled = corner_sum(raised * hidden, cols) * total
        d_pooled = corner_sum(raised * out, cols) * total
        by_out = from_corner(pooled * total, facts, cols)
        by_hidden = from_corner(d_pooled * total, facts, cols)
        rest = from_corner(d_pooled * total * (1.0 - 2.0 * pooled), facts, cols)
        grad = raised * (out * by_out + hidden * by_hidden + rest)
    grad_act = grad * inside * gate * (1.0 + pre_act * (1.0 - gate))
    count = lane_sum(inside)
    shift_sum = lane_sum(grad_act)
    slope_sum = lane_sum(grad_act * normed)
    grad_pre = inside * (scale * gain) * (grad_act - shift_sum / count - normed * (slope_sum / count))
    return grad_pre.astype(jnp.bfloat16), shift_sum, slope_sum


def assemble(blocks, full_ref):
    section, _, core = place()
    ch = blocks[0].shape[0]
    for (k, j), block in zip(peer_order(), blocks):
        at = pl.multiple_of(slice_at(section, core, k, j) * ch, ch)
        full_ref[pl.ds(at, ch), :] = block[...]


def assemble_frames(blocks, full_ref, rows, lanes):
    _, plane, core = place()
    size = rows.stop - rows.start
    for (k, j), block in zip(peer_order(), blocks):
        frame = (plane ^ k) * 2 + (core ^ j)
        full_ref[pl.ds(pl.multiple_of(frame * size, size), size), :] = block[rows, lanes]


def start_all(copies):
    for copy in copies:
        copy.start()
    return copies


def wait_all(copies):
    for copy in copies:
        copy.wait()


def tap_products(weight, full_ref, taps_ref, by_cells):
    length = taps_ref.shape[1]
    step = 512 if length % 512 == 0 else length
    for at in range(0, length, step):
        if by_cells:
            taps_ref[:, at : at + step] = lax.dot_general(
                weight, full_ref[at : at + step, :], NT, preferred_element_type=jnp.float32
            )
        else:
            taps_ref[:, at : at + step] = jnp.dot(
                weight, full_ref[:, at : at + step], preferred_element_type=jnp.float32
            )


def pick_layer(layer, sources, start, target, sem):
    section, _, _ = place()
    rows = pl.ds(start, target.shape[0])
    for k, source in enumerate(sources):

        @pl.when((section ^ layer) == k)
        def _():
            pltpu.make_async_copy(source.at[rows], target, sem).start()

    return pltpu.make_async_copy(sources[0].at[rows], target, sem)


def take_layer(layer, sources, target):
    section, _, _ = place()
    for k, source in enumerate(sources):

        @pl.when((section ^ layer) == k)
        def _():
            target[...] = source[...]


def affine(meta, ch):
    parts = meta[:, :LANES].astype(jnp.float32).T[:ch]
    return (
        parts[:, 0:1] + parts[:, 1:2] + parts[:, 2:3],
        parts[:, 3:4] + parts[:, 4:5] + parts[:, 5:6],
    )


def plane_inside(metas, facts):
    frames = metas.shape[0] // META_ROWS
    extents = []
    for line in (0, 1):
        total = None
        for f in range(frames):
            at = f * META_ROWS + line
            extent = metas[at : at + 1, 0:1].astype(jnp.float32) * facts[FRAME_AT + f : FRAME_AT + f + 1, :]
            total = extent if total is None else total + extent
        extents.append(total)
    on = (facts[ROW_AT : ROW_AT + 1, :] < extents[0]) & (facts[COL_AT : COL_AT + 1, :] < extents[1])
    return jnp.where(on, 1.0, 0.0)


def frames_kernel(dims, group_table, size_table, images, *refs):
    payloads, (image_in, groups, sizes, sems) = refs[:4], refs[4:]
    copies = start_all(
        [
            pltpu.make_async_copy(group_table, groups, sems.at[0]),
            pltpu.make_async_copy(size_table, sizes, sems.at[1]),
            pltpu.make_async_copy(images, image_in, sems.at[2]),
        ]
    )
    _, plane, _ = place()
    rows, cols = dims
    cells = rows * cols
    at = lax.broadcasted_iota(jnp.int32, (cells, LANES), 0).astype(jnp.float32)
    row = jnp.floor((at + 0.5) * (1.0 / cols))
    col = at - row * cols
    channels = images.shape[2]
    line = lax.broadcasted_iota(jnp.int32, (META_ROWS, channels), 0)
    wait_all(copies)
    for k in range(4):
        micro = plane ^ k
        group = groups[0, micro]
        height = sizes[0, 0]
        breadth = sizes[1, 0]
        for g in range(1, sizes.shape[1]):
            height = jnp.where(group == g, sizes[0, g], height)
            breadth = jnp.where(group == g, sizes[1, g], breadth)
        height = height.astype(jnp.float32)
        breadth = breadth.astype(jnp.float32)
        on = jnp.where((row < height) & (col < breadth), 1.0, 0.0)
        image = image_in[micro]
        for c in range(0, channels, LANES):
            piece = image[:, c : c + LANES].astype(jnp.float32) * on
            payloads[k][:cells, c : c + LANES] = piece.astype(jnp.bfloat16)
        payloads[k][cells:, :] = jnp.where(line == 0, height, breadth).astype(jnp.bfloat16)


def cot_slice_kernel(cots, out, cot_in, sems):
    copy = pltpu.make_async_copy(cots, cot_in, sems.at[0])
    copy.start()
    section, _, _ = place()
    micros, cells, channels = cots.shape
    half = channels // 2
    tile = section // 2 * LANES
    odd = section % 2 == 1
    lane = lax.broadcasted_iota(jnp.int32, (cells, LANES), 1)
    copy.wait()
    for micro in range(micros):
        low = cot_in[micro, :, pl.ds(pl.multiple_of(tile, LANES), LANES)].astype(jnp.float32)
        high = cot_in[micro, :, pl.ds(pl.multiple_of(half + tile, LANES), LANES)].astype(jnp.float32)
        low = jnp.where(odd, pltpu.roll(low, LANES // 2, 1), low)
        high = jnp.where(odd, high, pltpu.roll(high, LANES // 2, 1))
        both = jnp.where(lane < LANES // 2, low, high).astype(jnp.bfloat16)
        out[micro * cells : (micro + 1) * cells, :] = both


def cot_kernel(own, other, pick, out, full):
    _, _, core = place()
    cells = full.shape[0] // 8
    for n in range(4):
        for j, block in enumerate((own, other)):
            at = pl.multiple_of((2 * n + (core ^ j)) * cells, cells)
            full[pl.ds(at, cells), :] = block[n * cells : (n + 1) * cells, :]
    out[...] = lax.dot_general(pick[...], full[...], NT, preferred_element_type=jnp.float32).astype(
        jnp.bfloat16
    )


def pack_kernel(gain, bias, weight, *refs):
    outs, (columns, turned, tables, sems) = refs[:4], refs[4:]
    section, _, core = place()
    width = columns.shape[2]
    ch = width // 4
    start = pl.multiple_of(core * width, width)
    copies = start_all(
        [
            pltpu.make_async_copy(weight.at[tap, :, pl.ds(start, width)], columns.at[tap], sems.at[tap])
            for tap in range(TAPS)
        ]
    )
    table_copies = start_all(
        [
            pltpu.make_async_copy(gain, tables.at[0], sems.at[TAPS]),
            pltpu.make_async_copy(bias, tables.at[1], sems.at[TAPS + 1]),
        ]
    )
    for tap in range(TAPS):
        copies[tap].wait()
        turned[tap % 2] = columns[tap].T
        for k, out in enumerate(outs):
            rows = pl.ds(pl.multiple_of((section ^ k) * ch, ch), ch)
            out[tap * ch : (tap + 1) * ch, :] = turned[tap % 2, rows, :]
    wait_all(table_copies)
    for k, out in enumerate(outs):
        lines = []
        tile = pl.multiple_of(start + (section ^ k) // 2 * LANES, LANES)
        odd = (section ^ k) % 2 == 1
        for m in range(2):
            line = tables[m, :, pl.ds(tile, LANES)]
            line = jnp.where(odd, pltpu.roll(line, ch, 1), line)
            for _ in range(3):
                part = line.astype(jnp.bfloat16).astype(jnp.float32)
                lines.append(part)
                line = line - part
        lines.append(jnp.zeros((META_ROWS - len(lines), LANES), jnp.float32))
        out[TAPS * ch :, :] = jnp.zeros((META_ROWS, out.shape[1]), jnp.bfloat16)
        out[TAPS * ch :, :LANES] = jnp.concatenate(lines, axis=0).astype(jnp.bfloat16)


def pick_kernel(layer, *refs):
    sources, (out, sems) = refs[:4], refs[4:]
    pick_layer(layer, sources, 0, out, sems.at[0]).wait()


def forward_kernel(dims, layer, first, picks, pooling, *refs):
    blocks, weights, rest = refs[:8], refs[8 : 12 if picks else 9], refs[12 if picks else 9 :]
    rows, cols = dims
    cells = rows * cols
    if first:
        facts, hidden, kept, full_out, inside_out, full, taps, stage, weight, metas, sems = rest
    elif picks:
        inside, facts, hidden, kept, full_out, full, taps, stage, weight, sems = rest
    else:
        inside, facts, hidden, kept, full_out, full, taps, stage, sems = rest
        (weight,) = weights
    if first:
        take_layer(layer, weights, weight)
    elif picks:
        copy = pick_layer(layer, weights, 0, weight, sems.at[2])
    facts_now = facts[...]
    if first:
        channels = full.shape[1]
        assemble_frames(blocks, full, slice(0, cells), slice(0, channels))
    else:
        assemble(blocks, full)
    full_copy = pltpu.make_async_copy(full, full_out, sems.at[0])
    full_copy.start()
    if first:
        assemble_frames(blocks, metas, slice(cells, cells + META_ROWS), slice(0, channels))
        inside_now = plane_inside(metas, facts_now)
        inside_out[...] = inside_now
    else:
        inside_now = inside[...]
    if picks and not first:
        copy.wait()
    ch = hidden.shape[0]
    tap_products(weight[: TAPS * ch, :], full, taps, first)
    pre = sum_taps(taps, facts_now, cols)
    normed, scale = normalise(pre, inside_now)
    length = normed.shape[1]
    stage[:, :length] = normed
    stage[:, length:] = jnp.broadcast_to(scale, (ch, LANES))
    kept_copy = pltpu.make_async_copy(stage, kept, sems.at[1])
    kept_copy.start()
    gain, bias = affine(weight[TAPS * ch :, :], ch)
    hidden[...] = hidden_of(normed, gain, bias, inside_now, facts_now, cols, pooling).astype(jnp.bfloat16)
    full_copy.wait()
    kept_copy.wait()


def turn_kernel(dims, layer, pooling, *refs):
    blocks, (weight, cot_in, inside, facts) = refs[:8], refs[8:12]
    hidden_out, full_out, grad_pre, sums, full, taps, hidden, sems = refs[12:]
    cols = dims[1]
    assemble(blocks, full)
    full_copy = pltpu.make_async_copy(full, full_out, sems.at[1])
    full_copy.start()
    ch = grad_pre.shape[0]
    tap_products(weight[: TAPS * ch, :], full, taps, False)
    facts_now, inside_now = facts[...], inside[...]
    pre = sum_taps(taps, facts_now, cols)
    normed, scale = normalise(pre, inside_now)
    gain, bias = affine(weight[TAPS * ch :, :], ch)
    hidden[...] = hidden_of(normed, gain, bias, inside_now, facts_now, cols, pooling).astype(jnp.bfloat16)
    hidden_copy = pltpu.make_async_copy(hidden, hidden_out, sems.at[2])
    hidden_copy.start()
    grad_pre[...], shift_sum, slope_sum = norm_back(
        cot_in[...].astype(jnp.float32), normed, scale, gain, bias, inside_now, facts_now, cols, pooling
    )
    sums[...] = with_sums(layer, shift_sum, slope_sum, 0.0)
    full_copy.wait()
    hidden_copy.wait()


def with_sums(layer, shift_sum, slope_sum, others):
    at = lax.broadcasted_iota(jnp.int32, (shift_sum.shape[0], LANES), 1)
    return jnp.where(at == 2 * layer, shift_sum, jnp.where(at == 2 * layer + 1, slope_sum, others))


def add_blocks(blocks):
    total = blocks[0][...].astype(jnp.float32)
    for block in blocks[1:]:
        total = total + block[...].astype(jnp.float32)
    return total


def fetch_kernel(layer, kept, *refs):
    sources, (kept_out, meta_out, sems) = refs[:4], refs[4:]
    copy = pltpu.make_async_copy(kept, kept_out, sems.at[0])
    copy.start()
    start = sources[0].shape[0] - META_ROWS
    pick_layer(layer, sources, start, meta_out, sems.at[1]).wait()
    copy.wait()


def norm_back_kernel(dims, layer, pooling, *refs):
    blocks, (kept, meta, inside, facts, sums_in, grad_pre, sums) = refs[:4], refs[4:]
    ch, length = grad_pre.shape
    grad = add_blocks(blocks).astype(jnp.bfloat16).astype(jnp.float32)
    gain, bias = affine(meta[...], ch)
    grad_pre[...], shift_sum, slope_sum = norm_back(
        grad,
        kept[:, :length],
        kept[:, length : length + 1],
        gain,
        bias,
        inside[...],
        facts[...],
        dims[1],
        pooling,
    )
    sums[...] = with_sums(layer, shift_sum, slope_sum, sums_in[...])


def weight_product(moved, full, first):
    if first:
        return jnp.dot(moved, full, preferred_element_type=jnp.float32)
    return lax.dot_general(moved, full, NT, preferred_element_type=jnp.float32)


def sums_rows(sums, width):
    ch = sums.shape[0]
    turned = jnp.concatenate([sums[...].T, jnp.zeros((LANES, width - ch), jnp.float32)], axis=1)
    return turned[:META_ROWS].astype(jnp.bfloat16)


def form_share(layer, moved, full, sums, product):
    piece = product.shape[0] // 4
    rows = piece - META_ROWS * len(sums)
    width = product.shape[1]
    value = weight_product(moved[:rows, :], full[...], layer == 0)
    for n in range(4):
        product[n * piece : n * piece + rows, :] = value[:, n * width : (n + 1) * width].astype(jnp.bfloat16)
        for ref in sums:
            product[n * piece + rows : (n + 1) * piece, :] = sums_rows(ref, width)


def copy_pieces(product, shares, sems):
    if len(shares) == 1:
        return start_all([pltpu.make_async_copy(product, shares[0], sems.at[3])])
    _, plane, _ = place()
    piece = shares[0].shape[0]
    copies = []
    for k, share in enumerate(shares):
        at = pl.multiple_of((plane ^ k) * piece, META_ROWS)
        copies.append(pltpu.make_async_copy(product.at[pl.ds(at, piece)], share, sems.at[3 + k]))
    return start_all(copies)


def conv_back_kernel(dims, layer, own, other, own_weights, other_weights, full_in, facts, *refs):
    refs, (product, full, moved, weights, sems) = refs[:-5], refs[-5:]
    sums, outs, shares = (refs[:1], refs[1:5], refs[5:]) if layer == 0 else ((), refs[:4], refs[4:])
    ch = own.shape[0]
    size = moved.shape[0] // 2
    rows = pl.ds(layer * 4 * ch, 4 * ch)
    copies = start_all(
        [
            pltpu.make_async_copy(own_weights.at[rows], weights.at[:, pl.ds(0, size)], sems.at[0]),
            pltpu.make_async_copy(other_weights, weights.at[:, pl.ds(size, size)], sems.at[1]),
        ]
    )
    full_copy = pltpu.make_async_copy(full_in, full, sems.at[2])
    full_copy.start()
    facts_now = facts[...]
    spread_taps(own[...], moved, 0, facts_now, dims[1])
    full_copy.wait()
    form_share(layer, moved, full, sums, product)
    share_copies = copy_pieces(product, shares, sems)
    spread_taps(other[...], moved, size, facts_now, dims[1])
    for n in range(2):
        moved[n * size + TAPS * ch : (n + 1) * size, :] = jnp.zeros(
            (size - TAPS * ch, moved.shape[1]), jnp.bfloat16
        )
    wait_all(copies)
    value = jnp.dot(weights[...], moved[...], preferred_element_type=jnp.float32)
    for k, out in enumerate(outs):
        out[...] = value[k * ch : (k + 1) * ch, :].astype(jnp.bfloat16)
    wait_all(share_copies)


def fold_kernel(*refs):
    count = (len(refs) - 2) // 2
    shares, outs, (blocks, sems) = refs[:count], refs[count:-2], refs[-2:]
    rows = outs[0].shape[0]
    copies = start_all(
        [pltpu.make_async_copy(share, blocks.at[n], sems.at[n]) for n, share in enumerate(shares)]
    )
    for n, copy in enumerate(copies):
        copy.wait()
        value = add_blocks([blocks.at[n, pl.ds(m * rows, rows)] for m in range(blocks.shape[1] // rows)])
        outs[n][...] = value.astype(jnp.bfloat16)


def choose_kernel(*refs):
    lasts, others, outs = refs[:4], refs[4:-4], refs[-4:]
    section, _, _ = place()
    value = add_blocks(lasts)
    value = value.astype(jnp.bfloat16)
    for k, out in enumerate(outs):

        @pl.when((section ^ k) == 0)
        def _():
            out[...] = value

        for layer, other in enumerate(others, 1):

            @pl.when((section ^ k) == layer)
            def _():
                out[: other.shape[0], :] = other[...]
                out[other.shape[0] :, :] = value[other.shape[0] :, :]


def turn_weights_kernel(layers, *refs):
    sources, own, others, (full, turned, stage, sems) = refs[:4], refs[4], refs[5:-4], refs[-4:]
    section, _, core = place()
    rows, channels = full.shape[1:]
    half = channels // 2
    ch = half // 4
    copies = [pick_layer(n, sources, 0, full.at[n], sems.at[n]) for n in range(layers)]
    stage[:, :, rows:] = jnp.zeros((*stage.shape[:2], stage.shape[2] - rows), jnp.bfloat16)
    for n in range(layers):
        copies[n].wait()
        turned[...] = full[n].T
        for j in range(2):
            for k in range(4):
                at = pl.multiple_of((core ^ j) * half + (section ^ k) * ch, ch)
                stage[j, n * half + k * ch : n * half + (k + 1) * ch, :rows] = turned[pl.ds(at, ch), :]
    copies = [pltpu.make_async_copy(stage.at[0], own, sems.at[0])]
    for n, other in enumerate(others):
        source = stage.at[1, pl.ds(n * half, half)]
        copies.append(pltpu.make_async_copy(source, other, sems.at[1 + n]))
    wait_all(start_all(copies))


def input_kernel(*refs):
    blocks, (hidden, inside, keep, give, full, sems) = refs[:4], refs[4:]
    section, _, core = place()
    ch = hidden.shape[0]
    copy = pltpu.make_async_copy(hidden, full.at[pl.ds(0, ch)], sems.at[0])
    copy.start()
    full[ch:, :] = (add_blocks(blocks) * inside[...]).astype(jnp.bfloat16)
    copy.wait()
    rows = 2 * ch
    width = keep.shape[1]
    for j, out in enumerate((keep, give)):
        for n in range(2):
            at = pl.multiple_of((section ^ (2 * (core ^ j) + n)) * width, width)
            out[n * rows : (n + 1) * rows, :] = full[:, pl.ds(at, width)]


def pair_kernel(keep, got, *outs):
    rows = keep.shape[0] // 2
    for n, out in enumerate(outs):
        out[:rows, :] = keep[n * rows : (n + 1) * rows, :]
        out[rows:, :] = got[n * rows : (n + 1) * rows, :]


def store_maps(blocks, pick, outs, full):
    _, plane, core = place()
    ch = blocks[0].shape[0] // 4
    for m, out in enumerate(outs):
        for j in range(2):
            for n in range(2):
                for h in range(2):
                    slot = slice_at(plane ^ (2 * (core ^ j) + n), core ^ j, 0, h)
                    at = pl.multiple_of(slot * ch, ch)
                    start = (2 * h + m) * ch
                    full[m, pl.ds(at, ch), :] = blocks[2 * j + n][start : start + ch, :]
        mine = lax.dot_general(pick[...], full[m], NT, preferred_element_type=jnp.float32)
        out[...] = mine.astype(out.dtype)


def outputs_kernel(*refs):
    blocks, pick, map_blocks, map_pick, refs = refs[:8], refs[8], refs[9:13], refs[13], refs[14:]
    (weight_out, shift_out, slope_out), map_outs, (full, maps_full) = refs[:3], refs[3:5], refs[5:]
    store_maps(map_blocks, map_pick, map_outs, maps_full)
    section, plane, core = place()
    taps, rows, channels = weight_out.shape
    for tap in range(taps):
        for (k, j), block in zip(peer_order(), blocks):
            at = pl.multiple_of(slice_at(section, core, k, j) * rows, rows)
            full[tap, pl.ds(at, rows), :] = block[tap * rows : (tap + 1) * rows, :]
        weight_out[tap] = lax.dot_general(pick[...], full[tap], NT, preferred_element_type=jnp.float32)
    shift_row = jnp.zeros((1, rows), jnp.float32)
    slope_row = jnp.zeros((1, rows), jnp.float32)
    slot = plane * 2 + core
    for (k, j), block in zip(peer_order(), blocks):
        tail = block[taps * rows :, :rows].astype(jnp.float32)
        at = lax.broadcasted_iota(jnp.int32, tail.shape, 0)
        mine = slice_at(section, core, k, j) == slot
        shift_row = shift_row + jnp.sum(jnp.where(mine & (at == 2 * section), tail, 0.0), axis=0, keepdims=True)
        slope_row = slope_row + jnp.sum(jnp.where(mine & (at == 2 * section + 1), tail, 0.0), axis=0, keepdims=True)
    shift_out[...] = shift_row
    slope_out[...] = slope_row


def call(
    kernel, outs, scratch, args, name, held=(), free=(), held_outs=(), loose=(), last=False, flops=0, copies=None
):
    shapes = [
        (jax.ShapeDtypeStruct if last else pltpu.HBM if n in held_outs else pltpu.VMEM)(shape, dtype)
        for n, (shape, dtype) in enumerate(outs)
    ]
    moved = sum(a.size * a.dtype.itemsize for a in args)
    moved += sum(math.prod(shape) * jnp.dtype(dtype).itemsize for shape, dtype in outs)
    spaces = [pl.ANY if n in free else pltpu.HBM if n in held else pltpu.VMEM for n in range(len(args))]
    out_spaces = [pltpu.HBM if n in held_outs else pltpu.VMEM for n in range(len(outs))]
    args = [
        a if n in loose or n in free else pltpu.with_memory_space_constraint(a, space)
        for n, (a, space) in enumerate(zip(args, spaces))
    ]
    scratch_shapes = [
        pltpu.SMEM(shape, dtype) if dtype == jnp.int32 else pltpu.VMEM(shape, dtype) for shape, dtype in scratch
    ]
    if copies is not None:
        scratch_shapes.append(pltpu.SemaphoreType.DMA((copies,)))
    return pl.pallas_call(
        kernel,
        out_shape=shapes,
        in_specs=[pl.BlockSpec(memory_space=space) for space in spaces],
        out_specs=[pl.BlockSpec(memory_space=space) for space in out_spaces],
        scratch_shapes=scratch_shapes,
        compiler_params=pltpu.CompilerParams(vmem_limit_bytes=VMEM_LIMIT),
        cost_estimate=pl.CostEstimate(flops=flops, bytes_accessed=moved, transcendentals=0),
        name=name,
    )(*args)


def plane_shards(images, image_group, group_size, conv_weight, bn_gain, bn_bias, cotangent):
    _, _, core = place()
    micro_total, _, rows, cols, channels = images.shape
    layers = lax.axis_size("section")
    last = layers - 1
    cells = rows * cols
    frames = 2 * micro_total
    length = frames * cells
    ch = channels // 8
    dims = (rows, cols)
    bf16, f32 = jnp.bfloat16, jnp.float32
    facts = grid_facts(frames, rows, cols)
    conv_flops = 2 * TAPS * ch * channels * length
    slice_rows = TAPS * ch + META_ROWS
    tap_rows = -(-TAPS * ch // LANES) * LANES

    full_map = ((channels, length), bf16)
    full_frames = ((length, channels), bf16)
    tap_scratch = ((TAPS * ch, length), f32)
    weight_slice = ((slice_rows, channels), bf16)
    map_out = ((ch, length), bf16)
    sums_out = ((ch, LANES), f32)
    kept_out = ((ch, length + LANES), f32)
    piece_rows = [slice_rows] + [TAPS * ch] * last

    taps_first = conv_weight[0].transpose(1, 2, 0, 3).reshape(TAPS, channels, channels)
    packed = call(
        pack_kernel,
        [weight_slice] * 4,
        [
            ((TAPS, channels, 4 * ch), bf16),
            ((2, 4 * ch, channels), bf16),
            ((2, 1, channels), f32),
        ],
        [bn_gain, bn_bias, taps_first],
        "weight_pack",
        held=range(3),
        copies=TAPS + 2,
    )
    slices = spread(packed, to_section)

    payload = ((cells + META_ROWS, channels), bf16)
    sent = call(
        partial(frames_kernel, dims),
        [payload] * 4,
        [
            ((micro_total, cells, channels), bf16),
            (image_group.shape[::-1], jnp.int32),
            (group_size.shape[::-1], jnp.int32),
        ],
        [image_group.T, group_size.T, after(images.reshape(micro_total, cells, channels), packed)],
        "frames",
        held=range(3),
        copies=3,
    )
    frames_in = with_core(spread(sent, to_plane))

    half = (core * ch + np.arange(ch))[:, None] == np.arange(2 * ch)[None, :]
    hidden, normed, full, inside = call(
        partial(forward_kernel, dims, 0, True, True, CONVS == 1),
        [map_out, kept_out, full_frames, ((1, length), f32)],
        [
            full_frames,
            tap_scratch,
            kept_out,
            weight_slice,
            ((frames * META_ROWS, channels), bf16),
        ],
        [*frames_in, *slices, facts],
        "forward",
        held_outs=(1, 2),
        loose=(8, 9, 10, 11, 12),
        flops=conv_flops,
        copies=4,
    )
    kept, fulls = [normed], [full]
    same_core = [[2 * z + c for z in range(layers)] for c in range(2)]
    for layer in range(1, layers):
        weights = call(
            partial(pick_kernel, layer),
            [weight_slice],
            [],
            after(slices, hidden),
            "pick",
            flops=PICK_FLOPS,
            held=range(4),
            copies=1,
        )
        beside = [*weights]
        if layer == 1:
            turned, *crossing = call(
                partial(turn_weights_kernel, layers),
                [((layers * 4 * ch, tap_rows), bf16)] + [((4 * ch, tap_rows), bf16)] * layers,
                [
                    ((layers, TAPS * ch, channels), bf16),
                    ((channels, TAPS * ch), bf16),
                    ((2, layers * 4 * ch, tap_rows), bf16),
                ],
                after(slices, hidden),
                "turn_weights",
                held=range(4),
                held_outs=range(1 + layers),
                copies=1 + layers,
            )
            beside.append((turned, crossing))
        if layer == COT_LAYER - 1:
            (cot_slots,) = call(
                cot_slice_kernel,
                [((micro_total * cells, LANES), bf16)],
                [((micro_total, cells, channels), bf16)],
                [after(cotangent.reshape(micro_total, cells, channels), hidden)],
                "cot_slices",
                held=(0,),
                copies=1,
            )
            beside.append(cot_slots)
        if layer == COT_LAYER:
            cot_slots = after(cot_slots, hidden)
            cots = lax.all_to_all(cot_slots, "dp", 0, 0, tiled=True, axis_index_groups=same_core)
        if layer == last:
            crossing[last] = to_core(after(crossing[last], hidden))
            cots = after(cots, hidden)
            (cot,) = call(
                cot_kernel,
                [map_out],
                [((length, LANES), bf16)],
                [cots, to_core(cots), half.astype(bf16)],
                "cotangent",
                loose=(0, 1, 2),
            )
            beside.append(cot)
        blocks = [hidden] + [to_section(hidden, k) for k in (1, 2, 3)]
        blocks[3] = after(blocks[3], *beside)
        blocks = with_core(blocks)
        if layer < last:
            hidden, normed, full = call(
                partial(forward_kernel, dims, layer, False, False, layer == CONVS - 1),
                [map_out, kept_out, full_map],
                [full_map, tap_scratch, kept_out],
                [*blocks, *weights, inside, facts],
                "forward",
                held_outs=(1, 2),
                loose=(9, 10),
                flops=conv_flops,
                copies=3,
            )
            kept.append(normed)
        else:
            activation, full, grad_pre, sums = call(
                partial(turn_kernel, dims, last, last == CONVS - 1),
                [map_out, full_map, map_out, sums_out],
                [full_map, tap_scratch, map_out],
                [*blocks, *weights, cot, inside, facts],
                "turn",
                held_outs=(0, 1),
                loose=(10, 11),
                flops=conv_flops,
                copies=3,
            )
        fulls.append(full)

    shares = [None] * layers
    for layer in range(last, -1, -1):
        share_out = ((4 * piece_rows[layer], 2 * ch), bf16)
        pieces = [share_out] if layer else [((slice_rows, 2 * ch), bf16)] * 4
        outs = call(
            partial(conv_back_kernel, dims, layer),
            [map_out] * 4 + pieces,
            [
                share_out,
                full_map if layer else full_frames,
                ((2 * tap_rows, length), bf16),
                ((4 * ch, 2 * tap_rows), bf16),
            ],
            [grad_pre, to_core(grad_pre), turned, crossing[layer], fulls[layer], facts]
            + ([] if layer else [sums]),
            "conv_back",
            held=(2, 4),
            free=(3,),
            held_outs=range(4, 8),
            loose=(5,) if layer else (5, 6),
            flops=BACK_FLOPS[layer],
            copies=7,
        )
        parts, share = outs[:4], outs[4:]
        if layer == 0:
            shares[0] = [share[0]] + [None] + [to_plane(share[k], k) for k in (2, 3)]
            break
        if layer < last:
            share = after(share, shares[layer + 1])
        shares[layer] = lax.all_to_all(share[0], "dp", 0, 0, tiled=True, axis_index_groups=same_core)
        if layer:
            crossing[layer - 1] = to_core(after(crossing[layer - 1], parts))
            held = call(
                partial(fetch_kernel, layer - 1),
                [kept_out, ((META_ROWS, channels), bf16)],
                [],
                [after(kept[layer - 1], parts), *slices],
                "fetch",
                held=range(5),
                copies=2,
            )
            blocks = spread(parts, to_section, held)
            grad_pre, sums = call(
                partial(norm_back_kernel, dims, layer - 1, layer - 1 == CONVS - 1),
                [map_out, sums_out],
                [],
                [*blocks, *held, inside, facts, sums],
                "norm_back",
                loose=(6, 7, 8),
            )
    blocks = [parts[0]] + [to_section(parts[k], k) for k in (1, 2, 3)]
    shares[0][1] = to_plane(after(share[1], blocks[1]), 1)
    blocks = after(blocks, shares[1])
    keep, give = call(
        input_kernel,
        [((4 * ch, 2 * cells), bf16)] * 2,
        [((2 * ch, length), bf16)],
        [*blocks, activation, inside],
        "input",
        flops=INPUT_FLOPS,
        held=(4,),
        loose=(5,),
        copies=1,
    )
    maps = call(pair_kernel, [((4 * ch, 2 * cells), bf16)] * 2, [], [keep, to_core(give)], "pair")
    maps = [send(x, lambda s, z, c, n=n: (z, s ^ (2 * c + n), c)) for n, x in enumerate(maps)]
    folded = call(
        fold_kernel,
        [((rows, 2 * ch), bf16) for rows in piece_rows[1:]],
        [((last, 4 * TAPS * ch, 2 * ch), bf16)],
        shares[1:],
        "fold",
        held=range(last),
        copies=last,
    )
    chosen = call(
        choose_kernel,
        [((slice_rows, 2 * ch), bf16)] * 4,
        [],
        [*shares[0], *folded],
        "choose",
        loose=range(4),
    )
    pick = (core * cells + np.arange(cells))[:, None] == np.arange(2 * cells)[None, :]
    map_pick = pick.astype(bf16)
    pick = (core * ch + np.arange(ch))[:, None] == np.arange(2 * ch)[None, :]
    weight_grad, bias_grad, gain_grad, activations, input_grad = call(
        outputs_kernel,
        [((TAPS, ch, channels), f32), ((1, ch), f32), ((1, ch), f32)] + [((cells, channels), bf16)] * 2,
        [((TAPS, channels, 2 * ch), bf16), ((2, channels, 2 * cells), bf16)],
        [
            *with_core([chosen[0]] + [to_section(chosen[k], k) for k in (1, 2, 3)]),
            pick.astype(bf16),
            *with_core(after(maps, chosen)),
            map_pick,
        ],
        "outputs",
        loose=(8, 13),
        last=True,
    )
    weight_grad = weight_grad.reshape(3, 3, ch, channels).transpose(2, 0, 1, 3)[None]
    return (
        activations.reshape(1, 1, rows, cols, channels),
        input_grad.reshape(1, 1, rows, cols, channels),
        weight_grad,
        gain_grad,
        bias_grad,
    )


def fits_plane_plan(images, conv_weight, sections, dps):
    micro_total, images_total, rows, cols, channels = images.shape
    return (
        sections == 4
        and dps == 2 * sections
        and micro_total == sections
        and conv_weight.shape[0] == sections
        and images_total == dps
        and rows % 2 == 0
        and cols % 2 == 0
        and (rows * cols) % 64 == 0
        and channels == 512
    )


def solution(mesh):
    in_specs = (
        P(None, "dp", None, None, None),
        P(None, "dp"),
        P(),
        P("section", None, None, None, None),
        P("section", None),
        P("section", None),
        P(None, "dp", None, None, None),
    )
    out_specs = (
        P("section", "dp", None, None, None),
        P("section", "dp", None, None, None),
        P("section", "dp", None, None, None),
        P("section", "dp"),
        P("section", "dp"),
    )
    sections, dps = mesh.shape["section"], mesh.shape["dp"]

    def program(images, image_group, group_size, conv_weight, bn_gain, bn_bias, cotangent):
        plan = plane_shards if fits_plane_plan(images, conv_weight, sections, dps) else pipeline_shards
        sharded = jax.shard_map(plan, mesh=mesh, in_specs=in_specs, out_specs=out_specs, check_vma=False)
        return sharded(images, image_group, group_size, conv_weight, bn_gain, bn_bias, cotangent)

    return program
```

```python
import math
from functools import partial

import jax
import jax.numpy as jnp
import numpy as np
from jax import lax
from jax.experimental import pallas as pl
from jax.experimental.pallas import tpu as pltpu
from jax.sharding import PartitionSpec as P

CONVS = 2
BACK_FLOPS = (4 * 10**9, 52 * 10**8, 52 * 10**8, 0)
PICK_FLOPS = 2 * 10**9
COT_LAYER = 2
INPUT_FLOPS = 0 * 10**9


eps = 1e-05


def from_behind(x, axis, by):
    peers = lax.axis_size(axis)
    pairs = [(i, i + by) for i in range(peers) if 0 <= i + by < peers]
    return lax.ppermute(x, axis, pairs)


def canvas_mask(image_group, group_size, canvas_rows, canvas_cols):
    groups_n = group_size.shape[0]
    onehot = image_group[..., None] == jnp.arange(groups_n, dtype=jnp.int32)
    height = jnp.sum(jnp.where(onehot, group_size[:, 0], 0), axis=-1)
    breadth = jnp.sum(jnp.where(onehot, group_size[:, 1], 0), axis=-1)
    inside_rows = jnp.arange(canvas_rows, dtype=jnp.int32)[:, None] < height[..., None, None]
    inside_cols = jnp.arange(canvas_cols, dtype=jnp.int32)[None, :] < breadth[..., None, None]
    return (inside_rows & inside_cols).astype(jnp.float32)[..., None]


def window_pool(hidden):
    frames, height, breadth, channels = hidden.shape
    blocks = hidden.reshape(frames, height // 2, 2, breadth // 2, 2, channels)
    window_max = jnp.max(blocks, axis=(2, 4), keepdims=True)
    raised = jnp.exp(blocks - window_max)
    weights = raised / jnp.sum(raised, axis=(2, 4), keepdims=True)
    pooled = jnp.sum(weights * blocks, axis=(2, 4), keepdims=True)
    return (weights * pooled).reshape(frames, height, breadth, channels)


def activate(pre_act, inside, pooling):
    hidden = jax.nn.silu(pre_act) * inside
    return jnp.where(pooling, window_pool(hidden) * inside, hidden)


def conv_forward(layer_in, weight):
    return lax.conv_general_dilated(
        layer_in,
        weight,
        (1, 1),
        "SAME",
        dimension_numbers=("NHWC", "IHWO", "NHWC"),
        preferred_element_type=jnp.float32,
    )


def conv_data_back(grad_pre, weight):
    flipped = weight[:, ::-1, ::-1, :]
    return lax.conv_general_dilated(
        grad_pre,
        flipped,
        (1, 1),
        "SAME",
        dimension_numbers=("NHWC", "OHWI", "NHWC"),
        preferred_element_type=jnp.float32,
    )


def weight_back(layer_in, grad_pre):
    height = layer_in.shape[1]
    breadth = layer_in.shape[2]
    padded = jnp.pad(layer_in, ((0, 0), (1, 1), (1, 1), (0, 0)))
    pieces = []
    for tap_row in range(3):
        for tap_col in range(3):
            window = padded[:, tap_row : tap_row + height, tap_col : tap_col + breadth, :]
            pieces.append(
                jnp.einsum("nhwi,nhwo->io", window, grad_pre, preferred_element_type=jnp.float32)
            )
    return jnp.stack(pieces, axis=1).reshape(layer_in.shape[3], 3, 3, grad_pre.shape[3])


def layer_forward(layer_in, weight, gain_row, bias_row, inside, pooling):
    pre_norm = conv_forward(layer_in, weight)
    sums = lax.psum(
        (
            jnp.sum(pre_norm * inside, axis=(0, 1, 2)),
            jnp.sum(pre_norm * pre_norm * inside, axis=(0, 1, 2)),
            jnp.sum(inside),
        ),
        "dp",
    )
    pixel_total = sums[2]
    mean_val = sums[0] / pixel_total
    scale_inv = lax.rsqrt(sums[1] / pixel_total - mean_val * mean_val + eps)
    pre_act = (pre_norm - mean_val) * scale_inv * gain_row + bias_row
    hidden = activate(pre_act, inside, pooling)
    return (pre_norm, mean_val, scale_inv, pixel_total, hidden)


def layer_backward(
    grad_out,
    layer_in,
    pre_norm,
    mean_val,
    scale_inv,
    pixel_total,
    weight,
    gain_row,
    bias_row,
    inside,
    pooling,
):
    normed = (pre_norm - mean_val) * scale_inv
    pre_act = normed * gain_row + bias_row
    hidden_out, pullback = jax.vjp(partial(activate, inside=inside, pooling=pooling), pre_act)
    grad_act = pullback(grad_out)[0]
    sums = lax.psum(
        (jnp.sum(grad_act, axis=(0, 1, 2)), jnp.sum(grad_act * normed, axis=(0, 1, 2))), "dp"
    )
    shift_term = sums[0] / pixel_total
    slope_term = sums[1] / pixel_total
    grad_pre = (
        inside * scale_inv * gain_row * (grad_act - shift_term - normed * slope_term)
    ).astype(jnp.bfloat16)
    weight_term = weight_back(layer_in, grad_pre)
    grad_in = conv_data_back(grad_pre, weight).astype(jnp.bfloat16)
    return (grad_in, weight_term, sums[1], sums[0])


def pipeline_shards(images, image_group, group_size, conv_weight, bn_gain, bn_bias, cotangent):
    section_index = lax.axis_index("section")
    sections = lax.axis_size("section")
    micro_total = images.shape[0]
    channels = conv_weight.shape[1]
    inside_all = canvas_mask(image_group, group_size, images.shape[2], images.shape[3])
    ticks = micro_total + sections - 1
    weight = conv_weight[0]
    gain_row = bn_gain[0]
    bias_row = bn_bias[0]
    pool_here = section_index == CONVS - 1
    received = jnp.zeros(images.shape[1:], jnp.bfloat16)
    kept_in, kept_pre, kept_mean, kept_scale, kept_total, finished = ([], [], [], [], [], [])
    for tick in range(ticks):
        micro_pos = jnp.clip(tick - section_index, 0, micro_total - 1)
        inside = inside_all[micro_pos]
        fresh = (images[micro_pos].astype(jnp.float32) * inside).astype(jnp.bfloat16)
        layer_in = jnp.where(section_index == 0, fresh, received)
        pre_norm, mean_val, scale_inv, pixel_total, hidden = layer_forward(
            layer_in, weight, gain_row, bias_row, inside, pool_here
        )
        sent = hidden.astype(jnp.bfloat16)
        if tick < ticks - 1:
            received = from_behind(sent, "section", 1)
        kept_in.append(layer_in)
        kept_pre.append(pre_norm)
        kept_mean.append(mean_val)
        kept_scale.append(scale_inv)
        kept_total.append(pixel_total)
        finished.append(sent)
    stack_in = jnp.stack(kept_in)
    stack_pre = jnp.stack(kept_pre)
    stack_mean = jnp.stack(kept_mean)
    stack_scale = jnp.stack(kept_scale)
    stack_total = jnp.stack(kept_total)
    returned = jnp.zeros(images.shape[1:], jnp.bfloat16)
    weight_sum = jnp.zeros(conv_weight.shape[1:], jnp.float32)
    gain_sum = jnp.zeros((channels,), jnp.float32)
    bias_sum = jnp.zeros((channels,), jnp.float32)
    input_list = []
    for tick in range(ticks):
        micro_raw = tick - (sections - 1 - section_index)
        valid = ((micro_raw >= 0) & (micro_raw < micro_total)).astype(jnp.float32)
        micro_pos = jnp.clip(micro_raw, 0, micro_total - 1)
        forward_tick = jnp.clip(micro_pos + section_index, 0, ticks - 1)
        inside = inside_all[micro_pos]
        grad_out = jnp.where(
            section_index == sections - 1,
            cotangent[micro_pos].astype(jnp.float32),
            returned.astype(jnp.float32),
        )
        grad_in, weight_term, gain_term, bias_term = layer_backward(
            grad_out,
            stack_in[forward_tick],
            stack_pre[forward_tick],
            stack_mean[forward_tick],
            stack_scale[forward_tick],
            stack_total[forward_tick],
            weight,
            gain_row,
            bias_row,
            inside,
            pool_here,
        )
        weight_sum = weight_sum + valid * weight_term
        gain_sum = gain_sum + valid * gain_term
        bias_sum = bias_sum + valid * bias_term
        if tick < ticks - 1:
            returned = from_behind(grad_in, "section", -1)
        input_list.append((grad_in.astype(jnp.float32) * inside).astype(jnp.bfloat16))
    out_stack = jnp.stack(finished[sections - 1 :], axis=0)
    grad_stack = jnp.stack(input_list[sections - 1 :], axis=0)
    out_back, grad_back = (
        lax.all_to_all(out_stack, "section", split_axis=0, concat_axis=1, tiled=True),
        lax.all_to_all(grad_stack, "section", split_axis=0, concat_axis=1, tiled=True),
    )
    activations = out_back[:, sections - 1 : sections]
    input_grad = grad_back[:, 0:1]
    weight_grad = lax.psum_scatter(weight_sum[None], "dp", scatter_dimension=1, tiled=True)
    share = channels // lax.axis_size("dp")
    gain_grad = lax.dynamic_slice_in_dim(gain_sum, lax.axis_index("dp") * share, share)[None]
    bias_grad = lax.dynamic_slice_in_dim(bias_sum, lax.axis_index("dp") * share, share)[None]
    return (activations, input_grad, weight_grad, gain_grad, bias_grad)


AXES = ("section", "dp")
TAPS = 9
VMEM_LIMIT = 24 * 1024 * 1024
META_ROWS = 16
LANES = 128
ROW_AT, COL_AT, FRAME_AT = 6, 7, 8
NT = (((1,), (1,)), ((), ()))


def place():
    dp_index = lax.axis_index("dp")
    return lax.axis_index("section"), dp_index // 2, dp_index % 2


def peer_order():
    return [(k, j) for j in range(2) for k in range(4)]


def slice_at(section, core, k, j):
    return (core ^ j) * lax.axis_size("section") + (section ^ k)


def send(x, target):
    sections = lax.axis_size("section")
    dps = lax.axis_size("dp")
    pairs = []
    for s in range(sections):
        for d in range(dps):
            ts, tz, tc = target(s, d // 2, d % 2)
            pairs.append((s * dps + d, ts * dps + tz * 2 + tc))
    return lax.ppermute(x, AXES, pairs)


def to_section(x, k):
    return send(x, lambda s, z, c: (s ^ k, z, c))


def to_plane(x, k):
    return send(x, lambda s, z, c: (s, z ^ k, c))


def to_core(x):
    return send(x, lambda s, z, c: (s, z, c ^ 1))


def spread(blocks, move, *beside):
    moved = lax.optimization_barrier(([move(blocks[k], k) for k in (1, 2, 3)], beside))[0]
    return [blocks[0]] + moved


def with_core(blocks):
    return blocks + [to_core(x) for x in blocks]


def after(x, *first):
    return lax.optimization_barrier((x, first))[0]


def grid_facts(frames, rows, cols):
    at = np.arange(frames * rows * cols)
    col = at % cols
    row = (at // cols) % rows
    facts = [row > 0, row < rows - 1, col > 0, col < cols - 1, col % 2 == 0, row % 2 == 0, row, col]
    facts = facts + [at // (rows * cols) == frame for frame in range(frames)]
    return jnp.asarray(np.stack(facts).astype(np.float32))


def shift(x, by):
    length = x.shape[1]
    return pltpu.roll(x, (-by) % length, 1) if by % length else x


def row_ok(facts, d):
    return facts[0:1, :] if d < 0 else facts[1:2, :]


def col_ok(facts, d):
    return facts[2:3, :] if d < 0 else facts[3:4, :]


def sum_taps(taps_ref, facts, cols):
    ch = taps_ref.shape[0] // TAPS
    total = None
    for dx in (-1, 0, 1):
        column = None
        for dy in (-1, 0, 1):
            tap = (dy + 1) * 3 + dx + 1
            piece = taps_ref[tap * ch : (tap + 1) * ch, :]
            if dy:
                piece = shift(piece, dy * cols) * row_ok(facts, dy)
            column = piece if column is None else column + piece
        if dx:
            column = shift(column, dx) * col_ok(facts, dx)
        total = column if total is None else total + column
    return total


def spread_taps(grad, moved_ref, base, facts, cols):
    ch = grad.shape[0]
    facts = facts[:4, :].astype(grad.dtype)
    for dx in (-1, 0, 1):
        column = shift(grad, -dx) * col_ok(facts, -dx) if dx else grad
        for dy in (-1, 0, 1):
            piece = shift(column, -dy * cols) * row_ok(facts, -dy) if dy else column
            at = base + ((dy + 1) * 3 + dx + 1) * ch
            moved_ref[at : at + ch, :] = piece


def corner_sum(x, cols):
    x = x + shift(x, 1)
    return x + shift(x, cols)


def from_corner(x, facts, cols):
    x = jnp.where(facts[4:5, :] > 0.5, x, shift(x, -1))
    return jnp.where(facts[5:6, :] > 0.5, x, shift(x, -cols))


def lane_sum(x):
    return jnp.sum(x, axis=1, keepdims=True)


def normalise(pre, inside):
    count = lane_sum(inside)
    mean = lane_sum(pre * inside) / count
    square = lane_sum(pre * pre * inside) / count
    scale = lax.rsqrt(square - mean * mean + eps)
    return (pre - mean) * scale, scale


def hidden_of(normed, gain, bias, inside, facts, cols, pooling):
    pre_act = normed * gain + bias
    hidden = pre_act * jax.nn.sigmoid(pre_act) * inside
    if pooling:
        raised = jnp.exp(hidden)
        total = corner_sum(raised, cols)
        pooled = corner_sum(raised * hidden, cols) / total
        hidden = raised * from_corner(pooled / total, facts, cols) * inside
    return hidden


def norm_back(grad, normed, scale, gain, bias, inside, facts, cols, pooling):
    pre_act = normed * gain + bias
    gate = jax.nn.sigmoid(pre_act)
    if pooling:
        hidden = pre_act * gate * inside
        raised = jnp.exp(hidden)
        out = grad * inside
        total = 1.0 / corner_sum(raised, cols)
        pooled = corner_sum(raised * hidden, cols) * total
        d_pooled = corner_sum(raised * out, cols) * total
        by_out = from_corner(pooled * total, facts, cols)
        by_hidden = from_corner(d_pooled * total, facts, cols)
        rest = from_corner(d_pooled * total * (1.0 - 2.0 * pooled), facts, cols)
        grad = raised * (out * by_out + hidden * by_hidden + rest)
    grad_act = grad * inside * gate * (1.0 + pre_act * (1.0 - gate))
    count = lane_sum(inside)
    shift_sum = lane_sum(grad_act)
    slope_sum = lane_sum(grad_act * normed)
    grad_pre = inside * (scale * gain) * (grad_act - shift_sum / count - normed * (slope_sum / count))
    return grad_pre.astype(jnp.bfloat16), shift_sum, slope_sum


def assemble(blocks, full_ref):
    section, _, core = place()
    ch = blocks[0].shape[0]
    for (k, j), block in zip(peer_order(), blocks):
        at = pl.multiple_of(slice_at(section, core, k, j) * ch, ch)
        full_ref[pl.ds(at, ch), :] = block[...]


def assemble_frames(blocks, full_ref, rows, lanes):
    _, plane, core = place()
    size = rows.stop - rows.start
    for (k, j), block in zip(peer_order(), blocks):
        frame = (plane ^ k) * 2 + (core ^ j)
        full_ref[pl.ds(pl.multiple_of(frame * size, size), size), :] = block[rows, lanes]


def start_all(copies):
    for copy in copies:
        copy.start()
    return copies


def wait_all(copies):
    for copy in copies:
        copy.wait()


def tap_products(weight, full_ref, taps_ref, by_cells):
    length = taps_ref.shape[1]
    step = 512 if length % 512 == 0 else length
    for at in range(0, length, step):
        if by_cells:
            taps_ref[:, at : at + step] = lax.dot_general(
                weight, full_ref[at : at + step, :], NT, preferred_element_type=jnp.float32
            )
        else:
            taps_ref[:, at : at + step] = jnp.dot(
                weight, full_ref[:, at : at + step], preferred_element_type=jnp.float32
            )


def pick_layer(layer, sources, start, target, sem):
    section, _, _ = place()
    rows = pl.ds(start, target.shape[0])
    for k, source in enumerate(sources):

        @pl.when((section ^ layer) == k)
        def _():
            pltpu.make_async_copy(source.at[rows], target, sem).start()

    return pltpu.make_async_copy(sources[0].at[rows], target, sem)


def take_layer(layer, sources, target):
    section, _, _ = place()
    for k, source in enumerate(sources):

        @pl.when((section ^ layer) == k)
        def _():
            target[...] = source[...]


def affine(meta, ch):
    parts = meta[:, :LANES].astype(jnp.float32).T[:ch]
    return (
        parts[:, 0:1] + parts[:, 1:2] + parts[:, 2:3],
        parts[:, 3:4] + parts[:, 4:5] + parts[:, 5:6],
    )


def plane_inside(metas, facts):
    frames = metas.shape[0] // META_ROWS
    extents = []
    for line in (0, 1):
        total = None
        for f in range(frames):
            at = f * META_ROWS + line
            extent = metas[at : at + 1, 0:1].astype(jnp.float32) * facts[FRAME_AT + f : FRAME_AT + f + 1, :]
            total = extent if total is None else total + extent
        extents.append(total)
    on = (facts[ROW_AT : ROW_AT + 1, :] < extents[0]) & (facts[COL_AT : COL_AT + 1, :] < extents[1])
    return jnp.where(on, 1.0, 0.0)


def frames_kernel(dims, group_table, size_table, images, *refs):
    payloads, (image_in, groups, sizes, sems) = refs[:4], refs[4:]
    copies = start_all(
        [
            pltpu.make_async_copy(group_table, groups, sems.at[0]),
            pltpu.make_async_copy(size_table, sizes, sems.at[1]),
            pltpu.make_async_copy(images, image_in, sems.at[2]),
        ]
    )
    _, plane, _ = place()
    rows, cols = dims
    cells = rows * cols
    at = lax.broadcasted_iota(jnp.int32, (cells, LANES), 0).astype(jnp.float32)
    row = jnp.floor((at + 0.5) * (1.0 / cols))
    col = at - row * cols
    channels = images.shape[2]
    line = lax.broadcasted_iota(jnp.int32, (META_ROWS, channels), 0)
    wait_all(copies)
    for k in range(4):
        micro = plane ^ k
        group = groups[0, micro]
        height = sizes[0, 0]
        breadth = sizes[1, 0]
        for g in range(1, sizes.shape[1]):
            height = jnp.where(group == g, sizes[0, g], height)
            breadth = jnp.where(group == g, sizes[1, g], breadth)
        height = height.astype(jnp.float32)
        breadth = breadth.astype(jnp.float32)
        on = jnp.where((row < height) & (col < breadth), 1.0, 0.0)
        image = image_in[micro]
        for c in range(0, channels, LANES):
            piece = image[:, c : c + LANES].astype(jnp.float32) * on
            payloads[k][:cells, c : c + LANES] = piece.astype(jnp.bfloat16)
        payloads[k][cells:, :] = jnp.where(line == 0, height, breadth).astype(jnp.bfloat16)


def cot_slice_kernel(cots, out, cot_in, sems):
    copy = pltpu.make_async_copy(cots, cot_in, sems.at[0])
    copy.start()
    section, _, _ = place()
    micros, cells, channels = cots.shape
    half = channels // 2
    tile = section // 2 * LANES
    odd = section % 2 == 1
    lane = lax.broadcasted_iota(jnp.int32, (cells, LANES), 1)
    copy.wait()
    for micro in range(micros):
        low = cot_in[micro, :, pl.ds(pl.multiple_of(tile, LANES), LANES)].astype(jnp.float32)
        high = cot_in[micro, :, pl.ds(pl.multiple_of(half + tile, LANES), LANES)].astype(jnp.float32)
        low = jnp.where(odd, pltpu.roll(low, LANES // 2, 1), low)
        high = jnp.where(odd, high, pltpu.roll(high, LANES // 2, 1))
        both = jnp.where(lane < LANES // 2, low, high).astype(jnp.bfloat16)
        out[micro * cells : (micro + 1) * cells, :] = both


def cot_kernel(own, other, pick, out, full):
    _, _, core = place()
    cells = full.shape[0] // 8
    for n in range(4):
        for j, block in enumerate((own, other)):
            at = pl.multiple_of((2 * n + (core ^ j)) * cells, cells)
            full[pl.ds(at, cells), :] = block[n * cells : (n + 1) * cells, :]
    out[...] = lax.dot_general(pick[...], full[...], NT, preferred_element_type=jnp.float32).astype(
        jnp.bfloat16
    )


def pack_kernel(gain, bias, weight, *refs):
    outs, (columns, turned, tables, sems) = refs[:4], refs[4:]
    section, _, core = place()
    width = columns.shape[2]
    ch = width // 4
    start = pl.multiple_of(core * width, width)
    copies = start_all(
        [
            pltpu.make_async_copy(weight.at[tap, :, pl.ds(start, width)], columns.at[tap], sems.at[tap])
            for tap in range(TAPS)
        ]
    )
    table_copies = start_all(
        [
            pltpu.make_async_copy(gain, tables.at[0], sems.at[TAPS]),
            pltpu.make_async_copy(bias, tables.at[1], sems.at[TAPS + 1]),
        ]
    )
    for tap in range(TAPS):
        copies[tap].wait()
        turned[tap % 2] = columns[tap].T
        for k, out in enumerate(outs):
            rows = pl.ds(pl.multiple_of((section ^ k) * ch, ch), ch)
            out[tap * ch : (tap + 1) * ch, :] = turned[tap % 2, rows, :]
    wait_all(table_copies)
    for k, out in enumerate(outs):
        lines = []
        tile = pl.multiple_of(start + (section ^ k) // 2 * LANES, LANES)
        odd = (section ^ k) % 2 == 1
        for m in range(2):
            line = tables[m, :, pl.ds(tile, LANES)]
            line = jnp.where(odd, pltpu.roll(line, ch, 1), line)
            for _ in range(3):
                part = line.astype(jnp.bfloat16).astype(jnp.float32)
                lines.append(part)
                line = line - part
        lines.append(jnp.zeros((META_ROWS - len(lines), LANES), jnp.float32))
        out[TAPS * ch :, :] = jnp.zeros((META_ROWS, out.shape[1]), jnp.bfloat16)
        out[TAPS * ch :, :LANES] = jnp.concatenate(lines, axis=0).astype(jnp.bfloat16)


def pick_kernel(layer, *refs):
    sources, (out, sems) = refs[:4], refs[4:]
    pick_layer(layer, sources, 0, out, sems.at[0]).wait()


def forward_kernel(dims, layer, first, picks, pooling, *refs):
    blocks, weights, rest = refs[:8], refs[8 : 12 if picks else 9], refs[12 if picks else 9 :]
    rows, cols = dims
    cells = rows * cols
    if first:
        facts, hidden, kept, full_out, inside_out, full, taps, stage, weight, metas, sems = rest
    elif picks:
        inside, facts, hidden, kept, full_out, full, taps, stage, weight, sems = rest
    else:
        inside, facts, hidden, kept, full_out, full, taps, stage, sems = rest
        (weight,) = weights
    if first:
        take_layer(layer, weights, weight)
    elif picks:
        copy = pick_layer(layer, weights, 0, weight, sems.at[2])
    facts_now = facts[...]
    if first:
        channels = full.shape[1]
        assemble_frames(blocks, full, slice(0, cells), slice(0, channels))
    else:
        assemble(blocks, full)
    full_copy = pltpu.make_async_copy(full, full_out, sems.at[0])
    full_copy.start()
    if first:
        assemble_frames(blocks, metas, slice(cells, cells + META_ROWS), slice(0, channels))
        inside_now = plane_inside(metas, facts_now)
        inside_out[...] = inside_now
    else:
        inside_now = inside[...]
    if picks and not first:
        copy.wait()
    ch = hidden.shape[0]
    tap_products(weight[: TAPS * ch, :], full, taps, first)
    pre = sum_taps(taps, facts_now, cols)
    normed, scale = normalise(pre, inside_now)
    length = normed.shape[1]
    stage[:, :length] = normed
    stage[:, length:] = jnp.broadcast_to(scale, (ch, LANES))
    kept_copy = pltpu.make_async_copy(stage, kept, sems.at[1])
    kept_copy.start()
    gain, bias = affine(weight[TAPS * ch :, :], ch)
    hidden[...] = hidden_of(normed, gain, bias, inside_now, facts_now, cols, pooling).astype(jnp.bfloat16)
    full_copy.wait()
    kept_copy.wait()


def turn_kernel(dims, layer, pooling, *refs):
    blocks, (weight, cot_in, inside, facts) = refs[:8], refs[8:12]
    hidden_out, full_out, grad_pre, sums, full, taps, hidden, sems = refs[12:]
    cols = dims[1]
    assemble(blocks, full)
    full_copy = pltpu.make_async_copy(full, full_out, sems.at[1])
    full_copy.start()
    ch = grad_pre.shape[0]
    tap_products(weight[: TAPS * ch, :], full, taps, False)
    facts_now, inside_now = facts[...], inside[...]
    pre = sum_taps(taps, facts_now, cols)
    normed, scale = normalise(pre, inside_now)
    gain, bias = affine(weight[TAPS * ch :, :], ch)
    hidden[...] = hidden_of(normed, gain, bias, inside_now, facts_now, cols, pooling).astype(jnp.bfloat16)
    hidden_copy = pltpu.make_async_copy(hidden, hidden_out, sems.at[2])
    hidden_copy.start()
    grad_pre[...], shift_sum, slope_sum = norm_back(
        cot_in[...].astype(jnp.float32), normed, scale, gain, bias, inside_now, facts_now, cols, pooling
    )
    sums[...] = with_sums(layer, shift_sum, slope_sum, 0.0)
    full_copy.wait()
    hidden_copy.wait()


def with_sums(layer, shift_sum, slope_sum, others):
    at = lax.broadcasted_iota(jnp.int32, (shift_sum.shape[0], LANES), 1)
    return jnp.where(at == 2 * layer, shift_sum, jnp.where(at == 2 * layer + 1, slope_sum, others))


def add_blocks(blocks):
    total = blocks[0][...].astype(jnp.float32)
    for block in blocks[1:]:
        total = total + block[...].astype(jnp.float32)
    return total


def fetch_kernel(layer, kept, *refs):
    sources, (kept_out, meta_out, sems) = refs[:4], refs[4:]
    copy = pltpu.make_async_copy(kept, kept_out, sems.at[0])
    copy.start()
    start = sources[0].shape[0] - META_ROWS
    pick_layer(layer, sources, start, meta_out, sems.at[1]).wait()
    copy.wait()


def norm_back_kernel(dims, layer, pooling, *refs):
    blocks, (kept, meta, inside, facts, sums_in, grad_pre, sums) = refs[:4], refs[4:]
    ch, length = grad_pre.shape
    grad = add_blocks(blocks).astype(jnp.bfloat16).astype(jnp.float32)
    gain, bias = affine(meta[...], ch)
    grad_pre[...], shift_sum, slope_sum = norm_back(
        grad,
        kept[:, :length],
        kept[:, length : length + 1],
        gain,
        bias,
        inside[...],
        facts[...],
        dims[1],
        pooling,
    )
    sums[...] = with_sums(layer, shift_sum, slope_sum, sums_in[...])


def weight_product(moved, full, first):
    if first:
        return jnp.dot(moved, full, preferred_element_type=jnp.float32)
    return lax.dot_general(moved, full, NT, preferred_element_type=jnp.float32)


def sums_rows(sums, width):
    ch = sums.shape[0]
    turned = jnp.concatenate([sums[...].T, jnp.zeros((LANES, width - ch), jnp.float32)], axis=1)
    return turned[:META_ROWS].astype(jnp.bfloat16)


def form_share(layer, moved, full, sums, product):
    piece = product.shape[0] // 4
    rows = piece - META_ROWS * len(sums)
    width = product.shape[1]
    value = weight_product(moved[:rows, :], full[...], layer == 0)
    for n in range(4):
        product[n * piece : n * piece + rows, :] = value[:, n * width : (n + 1) * width].astype(jnp.bfloat16)
        for ref in sums:
            product[n * piece + rows : (n + 1) * piece, :] = sums_rows(ref, width)


def copy_pieces(product, shares, sems):
    if len(shares) == 1:
        return start_all([pltpu.make_async_copy(product, shares[0], sems.at[3])])
    _, plane, _ = place()
    piece = shares[0].shape[0]
    copies = []
    for k, share in enumerate(shares):
        at = pl.multiple_of((plane ^ k) * piece, META_ROWS)
        copies.append(pltpu.make_async_copy(product.at[pl.ds(at, piece)], share, sems.at[3 + k]))
    return start_all(copies)


def conv_back_kernel(dims, layer, own, other, own_weights, other_weights, full_in, facts, *refs):
    refs, (product, full, moved, weights, sems) = refs[:-5], refs[-5:]
    sums, outs, shares = (refs[:1], refs[1:5], refs[5:]) if layer == 0 else ((), refs[:4], refs[4:])
    ch = own.shape[0]
    size = moved.shape[0] // 2
    rows = pl.ds(layer * 4 * ch, 4 * ch)
    copies = start_all(
        [
            pltpu.make_async_copy(own_weights.at[rows], weights.at[:, pl.ds(0, size)], sems.at[0]),
            pltpu.make_async_copy(other_weights, weights.at[:, pl.ds(size, size)], sems.at[1]),
        ]
    )
    full_copy = pltpu.make_async_copy(full_in, full, sems.at[2])
    full_copy.start()
    facts_now = facts[...]
    spread_taps(own[...], moved, 0, facts_now, dims[1])
    full_copy.wait()
    form_share(layer, moved, full, sums, product)
    share_copies = copy_pieces(product, shares, sems)
    spread_taps(other[...], moved, size, facts_now, dims[1])
    for n in range(2):
        moved[n * size + TAPS * ch : (n + 1) * size, :] = jnp.zeros(
            (size - TAPS * ch, moved.shape[1]), jnp.bfloat16
        )
    wait_all(copies)
    value = jnp.dot(weights[...], moved[...], preferred_element_type=jnp.float32)
    for k, out in enumerate(outs):
        out[...] = value[k * ch : (k + 1) * ch, :].astype(jnp.bfloat16)
    wait_all(share_copies)


def fold_kernel(*refs):
    count = (len(refs) - 2) // 2
    shares, outs, (blocks, sems) = refs[:count], refs[count:-2], refs[-2:]
    rows = outs[0].shape[0]
    copies = start_all(
        [pltpu.make_async_copy(share, blocks.at[n], sems.at[n]) for n, share in enumerate(shares)]
    )
    for n, copy in enumerate(copies):
        copy.wait()
        value = add_blocks([blocks.at[n, pl.ds(m * rows, rows)] for m in range(blocks.shape[1] // rows)])
        outs[n][...] = value.astype(jnp.bfloat16)


def choose_kernel(*refs):
    lasts, others, outs = refs[:4], refs[4:-4], refs[-4:]
    section, _, _ = place()
    value = add_blocks(lasts)
    value = value.astype(jnp.bfloat16)
    for k, out in enumerate(outs):

        @pl.when((section ^ k) == 0)
        def _():
            out[...] = value

        for layer, other in enumerate(others, 1):

            @pl.when((section ^ k) == layer)
            def _():
                out[: other.shape[0], :] = other[...]
                out[other.shape[0] :, :] = value[other.shape[0] :, :]


def turn_weights_kernel(layers, *refs):
    sources, own, others, (full, turned, stage, sems) = refs[:4], refs[4], refs[5:-4], refs[-4:]
    section, _, core = place()
    rows, channels = full.shape[1:]
    half = channels // 2
    ch = half // 4
    copies = [pick_layer(n, sources, 0, full.at[n], sems.at[n]) for n in range(layers)]
    stage[:, :, rows:] = jnp.zeros((*stage.shape[:2], stage.shape[2] - rows), jnp.bfloat16)
    for n in range(layers):
        copies[n].wait()
        turned[...] = full[n].T
        for j in range(2):
            for k in range(4):
                at = pl.multiple_of((core ^ j) * half + (section ^ k) * ch, ch)
                stage[j, n * half + k * ch : n * half + (k + 1) * ch, :rows] = turned[pl.ds(at, ch), :]
    copies = [pltpu.make_async_copy(stage.at[0], own, sems.at[0])]
    for n, other in enumerate(others):
        source = stage.at[1, pl.ds(n * half, half)]
        copies.append(pltpu.make_async_copy(source, other, sems.at[1 + n]))
    wait_all(start_all(copies))


def input_kernel(*refs):
    blocks, (hidden, inside, keep, *gives, full, sems) = refs[:4], refs[4:]
    section, _, core = place()
    ch = hidden.shape[0]
    copy = pltpu.make_async_copy(hidden, full.at[pl.ds(0, ch)], sems.at[0])
    copy.start()
    full[ch:, :] = (add_blocks(blocks) * inside[...]).astype(jnp.bfloat16)
    copy.wait()
    rows = 2 * ch
    width = keep.shape[1]
    outs = [keep.at[pl.ds(n * rows, rows)] for n in range(2)] + gives
    for m, out in enumerate(outs):
        at = pl.multiple_of((section ^ (2 * (core ^ (m // 2)) + m % 2)) * width, width)
        out[...] = full[:, pl.ds(at, width)]


def pair_kernel(keep, *refs):
    rows = keep.shape[0] // 2
    for n, (got, out) in enumerate(zip(refs[:2], refs[2:])):
        out[:rows, :] = keep[n * rows : (n + 1) * rows, :]
        out[rows:, :] = got[...]


def store_maps(blocks, pick, outs, full):
    _, plane, core = place()
    ch = blocks[0].shape[0] // 4
    for m, out in enumerate(outs):
        for j in range(2):
            for n in range(2):
                for h in range(2):
                    slot = slice_at(plane ^ (2 * (core ^ j) + n), core ^ j, 0, h)
                    at = pl.multiple_of(slot * ch, ch)
                    start = (2 * h + m) * ch
                    full[m, pl.ds(at, ch), :] = blocks[2 * j + n][start : start + ch, :]
        mine = lax.dot_general(pick[...], full[m], NT, preferred_element_type=jnp.float32)
        out[...] = mine.astype(out.dtype)


def outputs_kernel(*refs):
    blocks, pick, map_blocks, map_pick, refs = refs[:8], refs[8], refs[9:13], refs[13], refs[14:]
    (weight_out, shift_out, slope_out), map_outs, (full, maps_full) = refs[:3], refs[3:5], refs[5:]
    store_maps(map_blocks, map_pick, map_outs, maps_full)
    section, plane, core = place()
    taps, rows, channels = weight_out.shape
    for tap in range(taps):
        for (k, j), block in zip(peer_order(), blocks):
            at = pl.multiple_of(slice_at(section, core, k, j) * rows, rows)
            full[tap, pl.ds(at, rows), :] = block[tap * rows : (tap + 1) * rows, :]
        weight_out[tap] = lax.dot_general(pick[...], full[tap], NT, preferred_element_type=jnp.float32)
    shift_row = jnp.zeros((1, rows), jnp.float32)
    slope_row = jnp.zeros((1, rows), jnp.float32)
    slot = plane * 2 + core
    for (k, j), block in zip(peer_order(), blocks):
        tail = block[taps * rows :, :rows].astype(jnp.float32)
        at = lax.broadcasted_iota(jnp.int32, tail.shape, 0)
        mine = slice_at(section, core, k, j) == slot
        shift_row = shift_row + jnp.sum(jnp.where(mine & (at == 2 * section), tail, 0.0), axis=0, keepdims=True)
        slope_row = slope_row + jnp.sum(jnp.where(mine & (at == 2 * section + 1), tail, 0.0), axis=0, keepdims=True)
    shift_out[...] = shift_row
    slope_out[...] = slope_row


def call(
    kernel, outs, scratch, args, name, held=(), free=(), held_outs=(), loose=(), last=False, flops=0, copies=None
):
    shapes = [
        (jax.ShapeDtypeStruct if last else pltpu.HBM if n in held_outs else pltpu.VMEM)(shape, dtype)
        for n, (shape, dtype) in enumerate(outs)
    ]
    moved = sum(a.size * a.dtype.itemsize for a in args)
    moved += sum(math.prod(shape) * jnp.dtype(dtype).itemsize for shape, dtype in outs)
    spaces = [pl.ANY if n in free else pltpu.HBM if n in held else pltpu.VMEM for n in range(len(args))]
    out_spaces = [pltpu.HBM if n in held_outs else pltpu.VMEM for n in range(len(outs))]
    args = [
        a if n in loose or n in free else pltpu.with_memory_space_constraint(a, space)
        for n, (a, space) in enumerate(zip(args, spaces))
    ]
    scratch_shapes = [
        pltpu.SMEM(shape, dtype) if dtype == jnp.int32 else pltpu.VMEM(shape, dtype) for shape, dtype in scratch
    ]
    if copies is not None:
        scratch_shapes.append(pltpu.SemaphoreType.DMA((copies,)))
    return pl.pallas_call(
        kernel,
        out_shape=shapes,
        in_specs=[pl.BlockSpec(memory_space=space) for space in spaces],
        out_specs=[pl.BlockSpec(memory_space=space) for space in out_spaces],
        scratch_shapes=scratch_shapes,
        compiler_params=pltpu.CompilerParams(vmem_limit_bytes=VMEM_LIMIT),
        cost_estimate=pl.CostEstimate(flops=flops, bytes_accessed=moved, transcendentals=0),
        name=name,
    )(*args)


def plane_shards(images, image_group, group_size, conv_weight, bn_gain, bn_bias, cotangent):
    _, _, core = place()
    micro_total, _, rows, cols, channels = images.shape
    layers = lax.axis_size("section")
    last = layers - 1
    cells = rows * cols
    frames = 2 * micro_total
    length = frames * cells
    ch = channels // 8
    dims = (rows, cols)
    bf16, f32 = jnp.bfloat16, jnp.float32
    facts = grid_facts(frames, rows, cols)
    conv_flops = 2 * TAPS * ch * channels * length
    slice_rows = TAPS * ch + META_ROWS
    tap_rows = -(-TAPS * ch // LANES) * LANES

    full_map = ((channels, length), bf16)
    full_frames = ((length, channels), bf16)
    tap_scratch = ((TAPS * ch, length), f32)
    weight_slice = ((slice_rows, channels), bf16)
    map_out = ((ch, length), bf16)
    sums_out = ((ch, LANES), f32)
    kept_out = ((ch, length + LANES), f32)
    piece_rows = [slice_rows] + [TAPS * ch] * last

    taps_first = conv_weight[0].transpose(1, 2, 0, 3).reshape(TAPS, channels, channels)
    packed = call(
        pack_kernel,
        [weight_slice] * 4,
        [
            ((TAPS, channels, 4 * ch), bf16),
            ((2, 4 * ch, channels), bf16),
            ((2, 1, channels), f32),
        ],
        [bn_gain, bn_bias, taps_first],
        "weight_pack",
        held=range(3),
        copies=TAPS + 2,
    )
    slices = spread(packed, to_section)

    payload = ((cells + META_ROWS, channels), bf16)
    sent = call(
        partial(frames_kernel, dims),
        [payload] * 4,
        [
            ((micro_total, cells, channels), bf16),
            (image_group.shape[::-1], jnp.int32),
            (group_size.shape[::-1], jnp.int32),
        ],
        [image_group.T, group_size.T, after(images.reshape(micro_total, cells, channels), packed)],
        "frames",
        held=range(3),
        copies=3,
    )
    frames_in = with_core(spread(sent, to_plane))

    half = (core * ch + np.arange(ch))[:, None] == np.arange(2 * ch)[None, :]
    hidden, normed, full, inside = call(
        partial(forward_kernel, dims, 0, True, True, CONVS == 1),
        [map_out, kept_out, full_frames, ((1, length), f32)],
        [
            full_frames,
            tap_scratch,
            kept_out,
            weight_slice,
            ((frames * META_ROWS, channels), bf16),
        ],
        [*frames_in, *slices, facts],
        "forward",
        held_outs=(1, 2),
        loose=(8, 9, 10, 11, 12),
        flops=conv_flops,
        copies=4,
    )
    kept, fulls = [normed], [full]
    same_core = [[2 * z + c for z in range(layers)] for c in range(2)]
    for layer in range(1, layers):
        weights = call(
            partial(pick_kernel, layer),
            [weight_slice],
            [],
            after(slices, hidden),
            "pick",
            flops=PICK_FLOPS,
            held=range(4),
            copies=1,
        )
        beside = [*weights]
        if layer == 1:
            turned, *crossing = call(
                partial(turn_weights_kernel, layers),
                [((layers * 4 * ch, tap_rows), bf16)] + [((4 * ch, tap_rows), bf16)] * layers,
                [
                    ((layers, TAPS * ch, channels), bf16),
                    ((channels, TAPS * ch), bf16),
                    ((2, layers * 4 * ch, tap_rows), bf16),
                ],
                after(slices, hidden),
                "turn_weights",
                held=range(4),
                held_outs=range(1 + layers),
                copies=1 + layers,
            )
            beside.append((turned, crossing))
        if layer == COT_LAYER - 1:
            (cot_slots,) = call(
                cot_slice_kernel,
                [((micro_total * cells, LANES), bf16)],
                [((micro_total, cells, channels), bf16)],
                [after(cotangent.reshape(micro_total, cells, channels), hidden)],
                "cot_slices",
                held=(0,),
                copies=1,
            )
            beside.append(cot_slots)
        if layer == COT_LAYER:
            cot_slots = after(cot_slots, hidden)
            cots = lax.all_to_all(cot_slots, "dp", 0, 0, tiled=True, axis_index_groups=same_core)
        if layer == last:
            crossing[last] = to_core(after(crossing[last], hidden))
            cots = after(cots, hidden)
            (cot,) = call(
                cot_kernel,
                [map_out],
                [((length, LANES), bf16)],
                [cots, to_core(cots), half.astype(bf16)],
                "cotangent",
                loose=(0, 1, 2),
            )
            beside.append(cot)
        blocks = [hidden] + [to_section(hidden, k) for k in (1, 2, 3)]
        blocks[3] = after(blocks[3], *beside)
        blocks = with_core(blocks)
        if layer < last:
            hidden, normed, full = call(
                partial(forward_kernel, dims, layer, False, False, layer == CONVS - 1),
                [map_out, kept_out, full_map],
                [full_map, tap_scratch, kept_out],
                [*blocks, *weights, inside, facts],
                "forward",
                held_outs=(1, 2),
                loose=(9, 10),
                flops=conv_flops,
                copies=3,
            )
            kept.append(normed)
        else:
            activation, full, grad_pre, sums = call(
                partial(turn_kernel, dims, last, last == CONVS - 1),
                [map_out, full_map, map_out, sums_out],
                [full_map, tap_scratch, map_out],
                [*blocks, *weights, cot, inside, facts],
                "turn",
                held_outs=(0, 1),
                loose=(10, 11),
                flops=conv_flops,
                copies=3,
            )
        fulls.append(full)

    shares = [None] * layers
    for layer in range(last, -1, -1):
        share_out = ((4 * piece_rows[layer], 2 * ch), bf16)
        pieces = [share_out] if layer else [((slice_rows, 2 * ch), bf16)] * 4
        outs = call(
            partial(conv_back_kernel, dims, layer),
            [map_out] * 4 + pieces,
            [
                share_out,
                full_map if layer else full_frames,
                ((2 * tap_rows, length), bf16),
                ((4 * ch, 2 * tap_rows), bf16),
            ],
            [grad_pre, to_core(grad_pre), turned, crossing[layer], fulls[layer], facts]
            + ([] if layer else [sums]),
            "conv_back",
            held=(2, 4),
            free=(3,),
            held_outs=range(4, 8),
            loose=(5,) if layer else (5, 6),
            flops=BACK_FLOPS[layer],
            copies=7,
        )
        parts, share = outs[:4], outs[4:]
        if layer == 0:
            shares[0] = [share[0]] + [None] + [to_plane(share[k], k) for k in (2, 3)]
            break
        if layer < last:
            share = after(share, shares[layer + 1])
        shares[layer] = lax.all_to_all(share[0], "dp", 0, 0, tiled=True, axis_index_groups=same_core)
        if layer:
            crossing[layer - 1] = to_core(after(crossing[layer - 1], parts))
            held = call(
                partial(fetch_kernel, layer - 1),
                [kept_out, ((META_ROWS, channels), bf16)],
                [],
                [after(kept[layer - 1], parts), *slices],
                "fetch",
                held=range(5),
                copies=2,
            )
            blocks = spread(parts, to_section, held)
            grad_pre, sums = call(
                partial(norm_back_kernel, dims, layer - 1, layer - 1 == CONVS - 1),
                [map_out, sums_out],
                [],
                [*blocks, *held, inside, facts, sums],
                "norm_back",
                loose=(6, 7, 8),
            )
    blocks = [parts[0]] + [to_section(parts[k], k) for k in (1, 2, 3)]
    shares[0][1] = to_plane(after(share[1], blocks[1]), 1)
    folded = call(
        fold_kernel,
        [((rows, 2 * ch), bf16) for rows in piece_rows[1:]],
        [((last, 4 * TAPS * ch, 2 * ch), bf16)],
        shares[1:],
        "fold",
        held=range(last),
        copies=last,
    )
    blocks = after(blocks, folded)
    keep, *gives = call(
        input_kernel,
        [((4 * ch, 2 * cells), bf16)] + [((2 * ch, 2 * cells), bf16)] * 2,
        [((2 * ch, length), bf16)],
        [*blocks, activation, inside],
        "input",
        flops=INPUT_FLOPS,
        held=(4,),
        loose=(5,),
        copies=1,
    )
    maps = call(pair_kernel, [((4 * ch, 2 * cells), bf16)] * 2, [], [keep, *map(to_core, gives)], "pair")
    maps = [send(x, lambda s, z, c, n=n: (z, s ^ (2 * c + n), c)) for n, x in enumerate(maps)]
    chosen = call(
        choose_kernel,
        [((slice_rows, 2 * ch), bf16)] * 4,
        [],
        [*shares[0], *folded],
        "choose",
        loose=range(4),
    )
    landed = [chosen[0]] + [to_section(chosen[k], k) for k in (1, 2, 3)]
    landed, maps = lax.optimization_barrier((landed, maps))
    pick = (core * cells + np.arange(cells))[:, None] == np.arange(2 * cells)[None, :]
    map_pick = pick.astype(bf16)
    pick = (core * ch + np.arange(ch))[:, None] == np.arange(2 * ch)[None, :]
    weight_grad, bias_grad, gain_grad, activations, input_grad = call(
        outputs_kernel,
        [((TAPS, ch, channels), f32), ((1, ch), f32), ((1, ch), f32)] + [((cells, channels), bf16)] * 2,
        [((TAPS, channels, 2 * ch), bf16), ((2, channels, 2 * cells), bf16)],
        [
            *with_core(landed),
            pick.astype(bf16),
            *with_core(maps),
            map_pick,
        ],
        "outputs",
        loose=(8, 13),
        last=True,
    )
    weight_grad = weight_grad.reshape(3, 3, ch, channels).transpose(2, 0, 1, 3)[None]
    return (
        activations.reshape(1, 1, rows, cols, channels),
        input_grad.reshape(1, 1, rows, cols, channels),
        weight_grad,
        gain_grad,
        bias_grad,
    )


def fits_plane_plan(images, conv_weight, sections, dps):
    micro_total, images_total, rows, cols, channels = images.shape
    return (
        sections == 4
        and dps == 2 * sections
        and micro_total == sections
        and conv_weight.shape[0] == sections
        and images_total == dps
        and rows % 2 == 0
        and cols % 2 == 0
        and (rows * cols) % 64 == 0
        and channels == 512
    )


def solution(mesh):
    in_specs = (
        P(None, "dp", None, None, None),
        P(None, "dp"),
        P(),
        P("section", None, None, None, None),
        P("section", None),
        P("section", None),
        P(None, "dp", None, None, None),
    )
    out_specs = (
        P("section", "dp", None, None, None),
        P("section", "dp", None, None, None),
        P("section", "dp", None, None, None),
        P("section", "dp"),
        P("section", "dp"),
    )
    sections, dps = mesh.shape["section"], mesh.shape["dp"]

    def program(images, image_group, group_size, conv_weight, bn_gain, bn_bias, cotangent):
        plan = plane_shards if fits_plane_plan(images, conv_weight, sections, dps) else pipeline_shards
        sharded = jax.shard_map(plan, mesh=mesh, in_specs=in_specs, out_specs=out_specs, check_vma=False)
        return sharded(images, image_group, group_size, conv_weight, bn_gain, bn_bias, cotangent)

    return program
```

```python
import math
from functools import partial

import jax
import jax.numpy as jnp
import numpy as np
from jax import lax
from jax.experimental import pallas as pl
from jax.experimental.pallas import tpu as pltpu
from jax.sharding import PartitionSpec as P

CONVS = 2
BACK_FLOPS = (3 * 10**9, 52 * 10**8, 52 * 10**8, 0)
PICK_FLOPS = 2 * 10**9
COT_LAYER = 2
INPUT_FLOPS = 0 * 10**9


eps = 1e-05


def from_behind(x, axis, by):
    peers = lax.axis_size(axis)
    pairs = [(i, i + by) for i in range(peers) if 0 <= i + by < peers]
    return lax.ppermute(x, axis, pairs)


def canvas_mask(image_group, group_size, canvas_rows, canvas_cols):
    groups_n = group_size.shape[0]
    onehot = image_group[..., None] == jnp.arange(groups_n, dtype=jnp.int32)
    height = jnp.sum(jnp.where(onehot, group_size[:, 0], 0), axis=-1)
    breadth = jnp.sum(jnp.where(onehot, group_size[:, 1], 0), axis=-1)
    inside_rows = jnp.arange(canvas_rows, dtype=jnp.int32)[:, None] < height[..., None, None]
    inside_cols = jnp.arange(canvas_cols, dtype=jnp.int32)[None, :] < breadth[..., None, None]
    return (inside_rows & inside_cols).astype(jnp.float32)[..., None]


def window_pool(hidden):
    frames, height, breadth, channels = hidden.shape
    blocks = hidden.reshape(frames, height // 2, 2, breadth // 2, 2, channels)
    window_max = jnp.max(blocks, axis=(2, 4), keepdims=True)
    raised = jnp.exp(blocks - window_max)
    weights = raised / jnp.sum(raised, axis=(2, 4), keepdims=True)
    pooled = jnp.sum(weights * blocks, axis=(2, 4), keepdims=True)
    return (weights * pooled).reshape(frames, height, breadth, channels)


def activate(pre_act, inside, pooling):
    hidden = jax.nn.silu(pre_act) * inside
    return jnp.where(pooling, window_pool(hidden) * inside, hidden)


def conv_forward(layer_in, weight):
    return lax.conv_general_dilated(
        layer_in,
        weight,
        (1, 1),
        "SAME",
        dimension_numbers=("NHWC", "IHWO", "NHWC"),
        preferred_element_type=jnp.float32,
    )


def conv_data_back(grad_pre, weight):
    flipped = weight[:, ::-1, ::-1, :]
    return lax.conv_general_dilated(
        grad_pre,
        flipped,
        (1, 1),
        "SAME",
        dimension_numbers=("NHWC", "OHWI", "NHWC"),
        preferred_element_type=jnp.float32,
    )


def weight_back(layer_in, grad_pre):
    height = layer_in.shape[1]
    breadth = layer_in.shape[2]
    padded = jnp.pad(layer_in, ((0, 0), (1, 1), (1, 1), (0, 0)))
    pieces = []
    for tap_row in range(3):
        for tap_col in range(3):
            window = padded[:, tap_row : tap_row + height, tap_col : tap_col + breadth, :]
            pieces.append(
                jnp.einsum("nhwi,nhwo->io", window, grad_pre, preferred_element_type=jnp.float32)
            )
    return jnp.stack(pieces, axis=1).reshape(layer_in.shape[3], 3, 3, grad_pre.shape[3])


def layer_forward(layer_in, weight, gain_row, bias_row, inside, pooling):
    pre_norm = conv_forward(layer_in, weight)
    sums = lax.psum(
        (
            jnp.sum(pre_norm * inside, axis=(0, 1, 2)),
            jnp.sum(pre_norm * pre_norm * inside, axis=(0, 1, 2)),
            jnp.sum(inside),
        ),
        "dp",
    )
    pixel_total = sums[2]
    mean_val = sums[0] / pixel_total
    scale_inv = lax.rsqrt(sums[1] / pixel_total - mean_val * mean_val + eps)
    pre_act = (pre_norm - mean_val) * scale_inv * gain_row + bias_row
    hidden = activate(pre_act, inside, pooling)
    return (pre_norm, mean_val, scale_inv, pixel_total, hidden)


def layer_backward(
    grad_out,
    layer_in,
    pre_norm,
    mean_val,
    scale_inv,
    pixel_total,
    weight,
    gain_row,
    bias_row,
    inside,
    pooling,
):
    normed = (pre_norm - mean_val) * scale_inv
    pre_act = normed * gain_row + bias_row
    hidden_out, pullback = jax.vjp(partial(activate, inside=inside, pooling=pooling), pre_act)
    grad_act = pullback(grad_out)[0]
    sums = lax.psum(
        (jnp.sum(grad_act, axis=(0, 1, 2)), jnp.sum(grad_act * normed, axis=(0, 1, 2))), "dp"
    )
    shift_term = sums[0] / pixel_total
    slope_term = sums[1] / pixel_total
    grad_pre = (
        inside * scale_inv * gain_row * (grad_act - shift_term - normed * slope_term)
    ).astype(jnp.bfloat16)
    weight_term = weight_back(layer_in, grad_pre)
    grad_in = conv_data_back(grad_pre, weight).astype(jnp.bfloat16)
    return (grad_in, weight_term, sums[1], sums[0])


def pipeline_shards(images, image_group, group_size, conv_weight, bn_gain, bn_bias, cotangent):
    section_index = lax.axis_index("section")
    sections = lax.axis_size("section")
    micro_total = images.shape[0]
    channels = conv_weight.shape[1]
    inside_all = canvas_mask(image_group, group_size, images.shape[2], images.shape[3])
    ticks = micro_total + sections - 1
    weight = conv_weight[0]
    gain_row = bn_gain[0]
    bias_row = bn_bias[0]
    pool_here = section_index == CONVS - 1
    received = jnp.zeros(images.shape[1:], jnp.bfloat16)
    kept_in, kept_pre, kept_mean, kept_scale, kept_total, finished = ([], [], [], [], [], [])
    for tick in range(ticks):
        micro_pos = jnp.clip(tick - section_index, 0, micro_total - 1)
        inside = inside_all[micro_pos]
        fresh = (images[micro_pos].astype(jnp.float32) * inside).astype(jnp.bfloat16)
        layer_in = jnp.where(section_index == 0, fresh, received)
        pre_norm, mean_val, scale_inv, pixel_total, hidden = layer_forward(
            layer_in, weight, gain_row, bias_row, inside, pool_here
        )
        sent = hidden.astype(jnp.bfloat16)
        if tick < ticks - 1:
            received = from_behind(sent, "section", 1)
        kept_in.append(layer_in)
        kept_pre.append(pre_norm)
        kept_mean.append(mean_val)
        kept_scale.append(scale_inv)
        kept_total.append(pixel_total)
        finished.append(sent)
    stack_in = jnp.stack(kept_in)
    stack_pre = jnp.stack(kept_pre)
    stack_mean = jnp.stack(kept_mean)
    stack_scale = jnp.stack(kept_scale)
    stack_total = jnp.stack(kept_total)
    returned = jnp.zeros(images.shape[1:], jnp.bfloat16)
    weight_sum = jnp.zeros(conv_weight.shape[1:], jnp.float32)
    gain_sum = jnp.zeros((channels,), jnp.float32)
    bias_sum = jnp.zeros((channels,), jnp.float32)
    input_list = []
    for tick in range(ticks):
        micro_raw = tick - (sections - 1 - section_index)
        valid = ((micro_raw >= 0) & (micro_raw < micro_total)).astype(jnp.float32)
        micro_pos = jnp.clip(micro_raw, 0, micro_total - 1)
        forward_tick = jnp.clip(micro_pos + section_index, 0, ticks - 1)
        inside = inside_all[micro_pos]
        grad_out = jnp.where(
            section_index == sections - 1,
            cotangent[micro_pos].astype(jnp.float32),
            returned.astype(jnp.float32),
        )
        grad_in, weight_term, gain_term, bias_term = layer_backward(
            grad_out,
            stack_in[forward_tick],
            stack_pre[forward_tick],
            stack_mean[forward_tick],
            stack_scale[forward_tick],
            stack_total[forward_tick],
            weight,
            gain_row,
            bias_row,
            inside,
            pool_here,
        )
        weight_sum = weight_sum + valid * weight_term
        gain_sum = gain_sum + valid * gain_term
        bias_sum = bias_sum + valid * bias_term
        if tick < ticks - 1:
            returned = from_behind(grad_in, "section", -1)
        input_list.append((grad_in.astype(jnp.float32) * inside).astype(jnp.bfloat16))
    out_stack = jnp.stack(finished[sections - 1 :], axis=0)
    grad_stack = jnp.stack(input_list[sections - 1 :], axis=0)
    out_back, grad_back = (
        lax.all_to_all(out_stack, "section", split_axis=0, concat_axis=1, tiled=True),
        lax.all_to_all(grad_stack, "section", split_axis=0, concat_axis=1, tiled=True),
    )
    activations = out_back[:, sections - 1 : sections]
    input_grad = grad_back[:, 0:1]
    weight_grad = lax.psum_scatter(weight_sum[None], "dp", scatter_dimension=1, tiled=True)
    share = channels // lax.axis_size("dp")
    gain_grad = lax.dynamic_slice_in_dim(gain_sum, lax.axis_index("dp") * share, share)[None]
    bias_grad = lax.dynamic_slice_in_dim(bias_sum, lax.axis_index("dp") * share, share)[None]
    return (activations, input_grad, weight_grad, gain_grad, bias_grad)


AXES = ("section", "dp")
TAPS = 9
VMEM_LIMIT = 24 * 1024 * 1024
META_ROWS = 16
LANES = 128
ROW_AT, COL_AT, FRAME_AT = 6, 7, 8
NT = (((1,), (1,)), ((), ()))


def place():
    dp_index = lax.axis_index("dp")
    return lax.axis_index("section"), dp_index // 2, dp_index % 2


def peer_order():
    return [(k, j) for j in range(2) for k in range(4)]


def slice_at(section, core, k, j):
    return (core ^ j) * lax.axis_size("section") + (section ^ k)


def send(x, target):
    sections = lax.axis_size("section")
    dps = lax.axis_size("dp")
    pairs = []
    for s in range(sections):
        for d in range(dps):
            ts, tz, tc = target(s, d // 2, d % 2)
            pairs.append((s * dps + d, ts * dps + tz * 2 + tc))
    return lax.ppermute(x, AXES, pairs)


def to_section(x, k):
    return send(x, lambda s, z, c: (s ^ k, z, c))


def to_plane(x, k):
    return send(x, lambda s, z, c: (s, z ^ k, c))


def to_core(x):
    return send(x, lambda s, z, c: (s, z, c ^ 1))


def spread(blocks, move, *beside):
    moved = lax.optimization_barrier(([move(blocks[k], k) for k in (1, 2, 3)], beside))[0]
    return [blocks[0]] + moved


def with_core(blocks):
    return blocks + [to_core(x) for x in blocks]


def after(x, *first):
    return lax.optimization_barrier((x, first))[0]


def grid_facts(frames, rows, cols):
    at = np.arange(frames * rows * cols)
    col = at % cols
    row = (at // cols) % rows
    facts = [row > 0, row < rows - 1, col > 0, col < cols - 1, col % 2 == 0, row % 2 == 0, row, col]
    facts = facts + [at // (rows * cols) == frame for frame in range(frames)]
    return jnp.asarray(np.stack(facts).astype(np.float32))


def shift(x, by):
    length = x.shape[1]
    return pltpu.roll(x, (-by) % length, 1) if by % length else x


def row_ok(facts, d):
    return facts[0:1, :] if d < 0 else facts[1:2, :]


def col_ok(facts, d):
    return facts[2:3, :] if d < 0 else facts[3:4, :]


def sum_taps(taps_ref, facts, cols):
    ch = taps_ref.shape[0] // TAPS
    total = None
    for dx in (-1, 0, 1):
        column = None
        for dy in (-1, 0, 1):
            tap = (dy + 1) * 3 + dx + 1
            piece = taps_ref[tap * ch : (tap + 1) * ch, :]
            if dy:
                piece = shift(piece, dy * cols) * row_ok(facts, dy)
            column = piece if column is None else column + piece
        if dx:
            column = shift(column, dx) * col_ok(facts, dx)
        total = column if total is None else total + column
    return total


def spread_taps(grad, moved_ref, base, facts, cols):
    ch = grad.shape[0]
    facts = facts[:4, :].astype(grad.dtype)
    for dx in (-1, 0, 1):
        column = shift(grad, -dx) * col_ok(facts, -dx) if dx else grad
        for dy in (-1, 0, 1):
            piece = shift(column, -dy * cols) * row_ok(facts, -dy) if dy else column
            at = base + ((dy + 1) * 3 + dx + 1) * ch
            moved_ref[at : at + ch, :] = piece


def corner_sum(x, cols):
    x = x + shift(x, 1)
    return x + shift(x, cols)


def from_corner(x, facts, cols):
    x = jnp.where(facts[4:5, :] > 0.5, x, shift(x, -1))
    return jnp.where(facts[5:6, :] > 0.5, x, shift(x, -cols))


def lane_sum(x):
    return jnp.sum(x, axis=1, keepdims=True)


def normalise(pre, inside):
    count = lane_sum(inside)
    mean = lane_sum(pre * inside) / count
    square = lane_sum(pre * pre * inside) / count
    scale = lax.rsqrt(square - mean * mean + eps)
    return (pre - mean) * scale, scale


def hidden_of(normed, gain, bias, inside, facts, cols, pooling):
    pre_act = normed * gain + bias
    hidden = pre_act * jax.nn.sigmoid(pre_act) * inside
    if pooling:
        raised = jnp.exp(hidden)
        total = corner_sum(raised, cols)
        pooled = corner_sum(raised * hidden, cols) / total
        hidden = raised * from_corner(pooled / total, facts, cols) * inside
    return hidden


def norm_back(grad, normed, scale, gain, bias, inside, facts, cols, pooling):
    pre_act = normed * gain + bias
    gate = jax.nn.sigmoid(pre_act)
    if pooling:
        hidden = pre_act * gate * inside
        raised = jnp.exp(hidden)
        out = grad * inside
        total = 1.0 / corner_sum(raised, cols)
        pooled = corner_sum(raised * hidden, cols) * total
        d_pooled = corner_sum(raised * out, cols) * total
        by_out = from_corner(pooled * total, facts, cols)
        by_hidden = from_corner(d_pooled * total, facts, cols)
        rest = from_corner(d_pooled * total * (1.0 - 2.0 * pooled), facts, cols)
        grad = raised * (out * by_out + hidden * by_hidden + rest)
    grad_act = grad * inside * gate * (1.0 + pre_act * (1.0 - gate))
    count = lane_sum(inside)
    shift_sum = lane_sum(grad_act)
    slope_sum = lane_sum(grad_act * normed)
    grad_pre = inside * (scale * gain) * (grad_act - shift_sum / count - normed * (slope_sum / count))
    return grad_pre.astype(jnp.bfloat16), shift_sum, slope_sum


def assemble(blocks, full_ref):
    section, _, core = place()
    ch = blocks[0].shape[0]
    for (k, j), block in zip(peer_order(), blocks):
        at = pl.multiple_of(slice_at(section, core, k, j) * ch, ch)
        full_ref[pl.ds(at, ch), :] = block[...]


def assemble_frames(blocks, full_ref, rows, lanes):
    _, plane, core = place()
    size = rows.stop - rows.start
    for (k, j), block in zip(peer_order(), blocks):
        frame = (plane ^ k) * 2 + (core ^ j)
        full_ref[pl.ds(pl.multiple_of(frame * size, size), size), :] = block[rows, lanes]


def start_all(copies):
    for copy in copies:
        copy.start()
    return copies


def wait_all(copies):
    for copy in copies:
        copy.wait()


def tap_products(weight, full_ref, taps_ref, by_cells):
    length = taps_ref.shape[1]
    step = 512 if length % 512 == 0 else length
    for at in range(0, length, step):
        if by_cells:
            taps_ref[:, at : at + step] = lax.dot_general(
                weight, full_ref[at : at + step, :], NT, preferred_element_type=jnp.float32
            )
        else:
            taps_ref[:, at : at + step] = jnp.dot(
                weight, full_ref[:, at : at + step], preferred_element_type=jnp.float32
            )


def pick_layer(layer, sources, start, target, sem):
    section, _, _ = place()
    rows = pl.ds(start, target.shape[0])
    for k, source in enumerate(sources):

        @pl.when((section ^ layer) == k)
        def _():
            pltpu.make_async_copy(source.at[rows], target, sem).start()

    return pltpu.make_async_copy(sources[0].at[rows], target, sem)


def take_layer(layer, sources, target):
    section, _, _ = place()
    for k, source in enumerate(sources):

        @pl.when((section ^ layer) == k)
        def _():
            target[...] = source[...]


def affine(meta, ch):
    parts = meta[:, :LANES].astype(jnp.float32).T[:ch]
    return (
        parts[:, 0:1] + parts[:, 1:2] + parts[:, 2:3],
        parts[:, 3:4] + parts[:, 4:5] + parts[:, 5:6],
    )


def plane_inside(metas, facts):
    frames = metas.shape[0] // META_ROWS
    extents = []
    for line in (0, 1):
        total = None
        for f in range(frames):
            at = f * META_ROWS + line
            extent = metas[at : at + 1, 0:1].astype(jnp.float32) * facts[FRAME_AT + f : FRAME_AT + f + 1, :]
            total = extent if total is None else total + extent
        extents.append(total)
    on = (facts[ROW_AT : ROW_AT + 1, :] < extents[0]) & (facts[COL_AT : COL_AT + 1, :] < extents[1])
    return jnp.where(on, 1.0, 0.0)


def frames_kernel(dims, group_table, size_table, images, *refs):
    payloads, (image_in, groups, sizes, sems) = refs[:4], refs[4:]
    copies = start_all(
        [
            pltpu.make_async_copy(group_table, groups, sems.at[0]),
            pltpu.make_async_copy(size_table, sizes, sems.at[1]),
            pltpu.make_async_copy(images, image_in, sems.at[2]),
        ]
    )
    _, plane, _ = place()
    rows, cols = dims
    cells = rows * cols
    at = lax.broadcasted_iota(jnp.int32, (cells, LANES), 0).astype(jnp.float32)
    row = jnp.floor((at + 0.5) * (1.0 / cols))
    col = at - row * cols
    channels = images.shape[2]
    line = lax.broadcasted_iota(jnp.int32, (META_ROWS, channels), 0)
    wait_all(copies)
    for k in range(4):
        micro = plane ^ k
        group = groups[0, micro]
        height = sizes[0, 0]
        breadth = sizes[1, 0]
        for g in range(1, sizes.shape[1]):
            height = jnp.where(group == g, sizes[0, g], height)
            breadth = jnp.where(group == g, sizes[1, g], breadth)
        height = height.astype(jnp.float32)
        breadth = breadth.astype(jnp.float32)
        on = jnp.where((row < height) & (col < breadth), 1.0, 0.0)
        image = image_in[micro]
        for c in range(0, channels, LANES):
            piece = image[:, c : c + LANES].astype(jnp.float32) * on
            payloads[k][:cells, c : c + LANES] = piece.astype(jnp.bfloat16)
        payloads[k][cells:, :] = jnp.where(line == 0, height, breadth).astype(jnp.bfloat16)


def cot_slice_kernel(cots, out, cot_in, sems):
    copy = pltpu.make_async_copy(cots, cot_in, sems.at[0])
    copy.start()
    section, _, _ = place()
    micros, cells, channels = cots.shape
    half = channels // 2
    tile = section // 2 * LANES
    odd = section % 2 == 1
    lane = lax.broadcasted_iota(jnp.int32, (cells, LANES), 1)
    copy.wait()
    for micro in range(micros):
        low = cot_in[micro, :, pl.ds(pl.multiple_of(tile, LANES), LANES)].astype(jnp.float32)
        high = cot_in[micro, :, pl.ds(pl.multiple_of(half + tile, LANES), LANES)].astype(jnp.float32)
        low = jnp.where(odd, pltpu.roll(low, LANES // 2, 1), low)
        high = jnp.where(odd, high, pltpu.roll(high, LANES // 2, 1))
        both = jnp.where(lane < LANES // 2, low, high).astype(jnp.bfloat16)
        out[micro * cells : (micro + 1) * cells, :] = both


def cot_kernel(own, other, pick, out, full):
    _, _, core = place()
    cells = full.shape[0] // 8
    for n in range(4):
        for j, block in enumerate((own, other)):
            at = pl.multiple_of((2 * n + (core ^ j)) * cells, cells)
            full[pl.ds(at, cells), :] = block[n * cells : (n + 1) * cells, :]
    out[...] = lax.dot_general(pick[...], full[...], NT, preferred_element_type=jnp.float32).astype(
        jnp.bfloat16
    )


def pack_kernel(gain, bias, weight, *refs):
    outs, (columns, turned, tables, sems) = refs[:4], refs[4:]
    section, _, core = place()
    width = columns.shape[2]
    ch = width // 4
    start = pl.multiple_of(core * width, width)
    copies = start_all(
        [
            pltpu.make_async_copy(weight.at[tap, :, pl.ds(start, width)], columns.at[tap], sems.at[tap])
            for tap in range(TAPS)
        ]
    )
    table_copies = start_all(
        [
            pltpu.make_async_copy(gain, tables.at[0], sems.at[TAPS]),
            pltpu.make_async_copy(bias, tables.at[1], sems.at[TAPS + 1]),
        ]
    )
    for tap in range(TAPS):
        copies[tap].wait()
        turned[tap % 2] = columns[tap].T
        for k, out in enumerate(outs):
            rows = pl.ds(pl.multiple_of((section ^ k) * ch, ch), ch)
            out[tap * ch : (tap + 1) * ch, :] = turned[tap % 2, rows, :]
    wait_all(table_copies)
    for k, out in enumerate(outs):
        lines = []
        tile = pl.multiple_of(start + (section ^ k) // 2 * LANES, LANES)
        odd = (section ^ k) % 2 == 1
        for m in range(2):
            line = tables[m, :, pl.ds(tile, LANES)]
            line = jnp.where(odd, pltpu.roll(line, ch, 1), line)
            for _ in range(3):
                part = line.astype(jnp.bfloat16).astype(jnp.float32)
                lines.append(part)
                line = line - part
        lines.append(jnp.zeros((META_ROWS - len(lines), LANES), jnp.float32))
        out[TAPS * ch :, :] = jnp.zeros((META_ROWS, out.shape[1]), jnp.bfloat16)
        out[TAPS * ch :, :LANES] = jnp.concatenate(lines, axis=0).astype(jnp.bfloat16)


def pick_kernel(layer, *refs):
    sources, (out, sems) = refs[:4], refs[4:]
    pick_layer(layer, sources, 0, out, sems.at[0]).wait()


def forward_kernel(dims, layer, first, picks, pooling, *refs):
    blocks, weights, rest = refs[:8], refs[8 : 12 if picks else 9], refs[12 if picks else 9 :]
    rows, cols = dims
    cells = rows * cols
    if first:
        facts, hidden, kept, full_out, inside_out, full, taps, stage, weight, metas, sems = rest
    elif picks:
        inside, facts, hidden, kept, full_out, full, taps, stage, weight, sems = rest
    else:
        inside, facts, hidden, kept, full_out, full, taps, stage, sems = rest
        (weight,) = weights
    if first:
        take_layer(layer, weights, weight)
    elif picks:
        copy = pick_layer(layer, weights, 0, weight, sems.at[2])
    facts_now = facts[...]
    if first:
        channels = full.shape[1]
        assemble_frames(blocks, full, slice(0, cells), slice(0, channels))
    else:
        assemble(blocks, full)
    full_copy = pltpu.make_async_copy(full, full_out, sems.at[0])
    full_copy.start()
    if first:
        assemble_frames(blocks, metas, slice(cells, cells + META_ROWS), slice(0, channels))
        inside_now = plane_inside(metas, facts_now)
        inside_out[...] = inside_now
    else:
        inside_now = inside[...]
    if picks and not first:
        copy.wait()
    ch = hidden.shape[0]
    tap_products(weight[: TAPS * ch, :], full, taps, first)
    pre = sum_taps(taps, facts_now, cols)
    normed, scale = normalise(pre, inside_now)
    length = normed.shape[1]
    stage[:, :length] = normed
    stage[:, length:] = jnp.broadcast_to(scale, (ch, LANES))
    kept_copy = pltpu.make_async_copy(stage, kept, sems.at[1])
    kept_copy.start()
    gain, bias = affine(weight[TAPS * ch :, :], ch)
    hidden[...] = hidden_of(normed, gain, bias, inside_now, facts_now, cols, pooling).astype(jnp.bfloat16)
    full_copy.wait()
    kept_copy.wait()


def turn_kernel(dims, layer, pooling, *refs):
    blocks, (weight, cot_in, inside, facts) = refs[:8], refs[8:12]
    hidden_out, full_out, grad_pre, sums, full, taps, hidden, sems = refs[12:]
    cols = dims[1]
    assemble(blocks, full)
    full_copy = pltpu.make_async_copy(full, full_out, sems.at[1])
    full_copy.start()
    ch = grad_pre.shape[0]
    tap_products(weight[: TAPS * ch, :], full, taps, False)
    facts_now, inside_now = facts[...], inside[...]
    pre = sum_taps(taps, facts_now, cols)
    normed, scale = normalise(pre, inside_now)
    gain, bias = affine(weight[TAPS * ch :, :], ch)
    hidden[...] = hidden_of(normed, gain, bias, inside_now, facts_now, cols, pooling).astype(jnp.bfloat16)
    hidden_copy = pltpu.make_async_copy(hidden, hidden_out, sems.at[2])
    hidden_copy.start()
    grad_pre[...], shift_sum, slope_sum = norm_back(
        cot_in[...].astype(jnp.float32), normed, scale, gain, bias, inside_now, facts_now, cols, pooling
    )
    sums[...] = with_sums(layer, shift_sum, slope_sum, 0.0)
    full_copy.wait()
    hidden_copy.wait()


def with_sums(layer, shift_sum, slope_sum, others):
    at = lax.broadcasted_iota(jnp.int32, (shift_sum.shape[0], LANES), 1)
    return jnp.where(at == 2 * layer, shift_sum, jnp.where(at == 2 * layer + 1, slope_sum, others))


def add_blocks(blocks):
    total = blocks[0][...].astype(jnp.float32)
    for block in blocks[1:]:
        total = total + block[...].astype(jnp.float32)
    return total


def fetch_kernel(layer, kept, *refs):
    sources, (kept_out, meta_out, sems) = refs[:4], refs[4:]
    copy = pltpu.make_async_copy(kept, kept_out, sems.at[0])
    copy.start()
    start = sources[0].shape[0] - META_ROWS
    pick_layer(layer, sources, start, meta_out, sems.at[1]).wait()
    copy.wait()


def norm_back_kernel(dims, layer, pooling, *refs):
    blocks, (kept, meta, inside, facts, sums_in, grad_pre, sums) = refs[:4], refs[4:]
    ch, length = grad_pre.shape
    grad = add_blocks(blocks).astype(jnp.bfloat16).astype(jnp.float32)
    gain, bias = affine(meta[...], ch)
    grad_pre[...], shift_sum, slope_sum = norm_back(
        grad,
        kept[:, :length],
        kept[:, length : length + 1],
        gain,
        bias,
        inside[...],
        facts[...],
        dims[1],
        pooling,
    )
    sums[...] = with_sums(layer, shift_sum, slope_sum, sums_in[...])


def weight_product(moved, full, first):
    if first:
        return jnp.dot(moved, full, preferred_element_type=jnp.float32)
    return lax.dot_general(moved, full, NT, preferred_element_type=jnp.float32)


def sums_rows(sums, width):
    ch = sums.shape[0]
    turned = jnp.concatenate([sums[...].T, jnp.zeros((LANES, width - ch), jnp.float32)], axis=1)
    return turned[:META_ROWS].astype(jnp.bfloat16)


def form_share(layer, moved, full, sums, product):
    piece = product.shape[0] // 4
    rows = piece - META_ROWS * len(sums)
    width = product.shape[1]
    value = weight_product(moved[:rows, :], full[...], layer == 0)
    for n in range(4):
        product[n * piece : n * piece + rows, :] = value[:, n * width : (n + 1) * width].astype(jnp.bfloat16)
        for ref in sums:
            product[n * piece + rows : (n + 1) * piece, :] = sums_rows(ref, width)


def copy_pieces(product, shares, sems):
    if len(shares) == 1:
        return start_all([pltpu.make_async_copy(product, shares[0], sems.at[3])])
    _, plane, _ = place()
    piece = shares[0].shape[0]
    copies = []
    for k, share in enumerate(shares):
        at = pl.multiple_of((plane ^ k) * piece, META_ROWS)
        copies.append(pltpu.make_async_copy(product.at[pl.ds(at, piece)], share, sems.at[3 + k]))
    return start_all(copies)


def conv_back_kernel(dims, layer, own, other, own_weights, other_weights, full_in, facts, *refs):
    refs, (product, full, moved, weights, sems) = refs[:-5], refs[-5:]
    sums, outs, shares = (refs[:1], refs[1:5], refs[5:]) if layer == 0 else ((), refs[:4], refs[4:])
    ch = own.shape[0]
    size = moved.shape[0] // 2
    rows = pl.ds(layer * 4 * ch, 4 * ch)
    copies = start_all(
        [
            pltpu.make_async_copy(own_weights.at[rows], weights.at[:, pl.ds(0, size)], sems.at[0]),
            pltpu.make_async_copy(other_weights, weights.at[:, pl.ds(size, size)], sems.at[1]),
        ]
    )
    full_copy = pltpu.make_async_copy(full_in, full, sems.at[2])
    full_copy.start()
    facts_now = facts[...]
    spread_taps(own[...], moved, 0, facts_now, dims[1])
    full_copy.wait()
    form_share(layer, moved, full, sums, product)
    share_copies = copy_pieces(product, shares, sems)
    spread_taps(other[...], moved, size, facts_now, dims[1])
    for n in range(2):
        moved[n * size + TAPS * ch : (n + 1) * size, :] = jnp.zeros(
            (size - TAPS * ch, moved.shape[1]), jnp.bfloat16
        )
    wait_all(copies)
    value = jnp.dot(weights[...], moved[...], preferred_element_type=jnp.float32)
    for k, out in enumerate(outs):
        out[...] = value[k * ch : (k + 1) * ch, :].astype(jnp.bfloat16)
    wait_all(share_copies)


def fold_kernel(*refs):
    count = (len(refs) - 2) // 2
    shares, outs, (blocks, sems) = refs[:count], refs[count:-2], refs[-2:]
    rows = outs[0].shape[0]
    copies = start_all(
        [pltpu.make_async_copy(share, blocks.at[n], sems.at[n]) for n, share in enumerate(shares)]
    )
    for n, copy in enumerate(copies):
        copy.wait()
        value = add_blocks([blocks.at[n, pl.ds(m * rows, rows)] for m in range(blocks.shape[1] // rows)])
        outs[n][...] = value.astype(jnp.bfloat16)


def choose_kernel(*refs):
    lasts, others, outs = refs[:4], refs[4:-4], refs[-4:]
    section, _, _ = place()
    value = add_blocks(lasts)
    value = value.astype(jnp.bfloat16)
    for k, out in enumerate(outs):

        @pl.when((section ^ k) == 0)
        def _():
            out[...] = value

        for layer, other in enumerate(others, 1):

            @pl.when((section ^ k) == layer)
            def _():
                out[: other.shape[0], :] = other[...]
                out[other.shape[0] :, :] = value[other.shape[0] :, :]


def turn_weights_kernel(layers, *refs):
    sources, own, others, (full, turned, stage, sems) = refs[:4], refs[4], refs[5:-4], refs[-4:]
    section, _, core = place()
    rows, channels = full.shape[1:]
    half = channels // 2
    ch = half // 4
    copies = [pick_layer(n, sources, 0, full.at[n], sems.at[n]) for n in range(layers)]
    stage[:, :, rows:] = jnp.zeros((*stage.shape[:2], stage.shape[2] - rows), jnp.bfloat16)
    for n in range(layers):
        copies[n].wait()
        turned[...] = full[n].T
        for j in range(2):
            for k in range(4):
                at = pl.multiple_of((core ^ j) * half + (section ^ k) * ch, ch)
                stage[j, n * half + k * ch : n * half + (k + 1) * ch, :rows] = turned[pl.ds(at, ch), :]
    copies = [pltpu.make_async_copy(stage.at[0], own, sems.at[0])]
    for n, other in enumerate(others):
        source = stage.at[1, pl.ds(n * half, half)]
        copies.append(pltpu.make_async_copy(source, other, sems.at[1 + n]))
    wait_all(start_all(copies))


def input_kernel(*refs):
    blocks, (hidden, inside, keep, give, full, sems) = refs[:4], refs[4:]
    section, _, core = place()
    ch = hidden.shape[0]
    copy = pltpu.make_async_copy(hidden, full.at[pl.ds(0, ch)], sems.at[0])
    copy.start()
    full[ch:, :] = (add_blocks(blocks) * inside[...]).astype(jnp.bfloat16)
    copy.wait()
    rows = 2 * ch
    width = keep.shape[1]
    for j, out in enumerate((keep, give)):
        for n in range(2):
            at = pl.multiple_of((section ^ (2 * (core ^ j) + n)) * width, width)
            out[n * rows : (n + 1) * rows, :] = full[:, pl.ds(at, width)]


def pair_kernel(keep, got, *outs):
    rows = keep.shape[0] // 2
    for n, out in enumerate(outs):
        out[:rows, :] = keep[n * rows : (n + 1) * rows, :]
        out[rows:, :] = got[n * rows : (n + 1) * rows, :]


def store_maps(blocks, pick, outs, full):
    _, plane, core = place()
    ch = blocks[0].shape[0] // 4
    for m, out in enumerate(outs):
        for j in range(2):
            for n in range(2):
                for h in range(2):
                    slot = slice_at(plane ^ (2 * (core ^ j) + n), core ^ j, 0, h)
                    at = pl.multiple_of(slot * ch, ch)
                    start = (2 * h + m) * ch
                    full[m, pl.ds(at, ch), :] = blocks[2 * j + n][start : start + ch, :]
        mine = lax.dot_general(pick[...], full[m], NT, preferred_element_type=jnp.float32)
        out[...] = mine.astype(out.dtype)


def outputs_kernel(*refs):
    blocks, pick, map_blocks, map_pick, refs = refs[:8], refs[8], refs[9:13], refs[13], refs[14:]
    (weight_out, shift_out, slope_out), map_outs, (full, maps_full) = refs[:3], refs[3:5], refs[5:]
    store_maps(map_blocks, map_pick, map_outs, maps_full)
    section, plane, core = place()
    taps, rows, channels = weight_out.shape
    for tap in range(taps):
        for (k, j), block in zip(peer_order(), blocks):
            at = pl.multiple_of(slice_at(section, core, k, j) * rows, rows)
            full[tap, pl.ds(at, rows), :] = block[tap * rows : (tap + 1) * rows, :]
        weight_out[tap] = lax.dot_general(pick[...], full[tap], NT, preferred_element_type=jnp.float32)
    shift_row = jnp.zeros((1, rows), jnp.float32)
    slope_row = jnp.zeros((1, rows), jnp.float32)
    slot = plane * 2 + core
    for (k, j), block in zip(peer_order(), blocks):
        tail = block[taps * rows :, :rows].astype(jnp.float32)
        at = lax.broadcasted_iota(jnp.int32, tail.shape, 0)
        mine = slice_at(section, core, k, j) == slot
        shift_row = shift_row + jnp.sum(jnp.where(mine & (at == 2 * section), tail, 0.0), axis=0, keepdims=True)
        slope_row = slope_row + jnp.sum(jnp.where(mine & (at == 2 * section + 1), tail, 0.0), axis=0, keepdims=True)
    shift_out[...] = shift_row
    slope_out[...] = slope_row


def call(
    kernel, outs, scratch, args, name, held=(), free=(), held_outs=(), loose=(), last=False, flops=0, copies=None
):
    shapes = [
        (jax.ShapeDtypeStruct if last else pltpu.HBM if n in held_outs else pltpu.VMEM)(shape, dtype)
        for n, (shape, dtype) in enumerate(outs)
    ]
    moved = sum(a.size * a.dtype.itemsize for a in args)
    moved += sum(math.prod(shape) * jnp.dtype(dtype).itemsize for shape, dtype in outs)
    spaces = [pl.ANY if n in free else pltpu.HBM if n in held else pltpu.VMEM for n in range(len(args))]
    out_spaces = [pltpu.HBM if n in held_outs else pltpu.VMEM for n in range(len(outs))]
    args = [
        a if n in loose or n in free else pltpu.with_memory_space_constraint(a, space)
        for n, (a, space) in enumerate(zip(args, spaces))
    ]
    scratch_shapes = [
        pltpu.SMEM(shape, dtype) if dtype == jnp.int32 else pltpu.VMEM(shape, dtype) for shape, dtype in scratch
    ]
    if copies is not None:
        scratch_shapes.append(pltpu.SemaphoreType.DMA((copies,)))
    return pl.pallas_call(
        kernel,
        out_shape=shapes,
        in_specs=[pl.BlockSpec(memory_space=space) for space in spaces],
        out_specs=[pl.BlockSpec(memory_space=space) for space in out_spaces],
        scratch_shapes=scratch_shapes,
        compiler_params=pltpu.CompilerParams(vmem_limit_bytes=VMEM_LIMIT),
        cost_estimate=pl.CostEstimate(flops=flops, bytes_accessed=moved, transcendentals=0),
        name=name,
    )(*args)


def plane_shards(images, image_group, group_size, conv_weight, bn_gain, bn_bias, cotangent):
    _, _, core = place()
    micro_total, _, rows, cols, channels = images.shape
    layers = lax.axis_size("section")
    last = layers - 1
    cells = rows * cols
    frames = 2 * micro_total
    length = frames * cells
    ch = channels // 8
    dims = (rows, cols)
    bf16, f32 = jnp.bfloat16, jnp.float32
    facts = grid_facts(frames, rows, cols)
    conv_flops = 2 * TAPS * ch * channels * length
    slice_rows = TAPS * ch + META_ROWS
    tap_rows = -(-TAPS * ch // LANES) * LANES

    full_map = ((channels, length), bf16)
    full_frames = ((length, channels), bf16)
    tap_scratch = ((TAPS * ch, length), f32)
    weight_slice = ((slice_rows, channels), bf16)
    map_out = ((ch, length), bf16)
    sums_out = ((ch, LANES), f32)
    kept_out = ((ch, length + LANES), f32)
    piece_rows = [slice_rows] + [TAPS * ch] * last

    taps_first = conv_weight[0].transpose(1, 2, 0, 3).reshape(TAPS, channels, channels)
    packed = call(
        pack_kernel,
        [weight_slice] * 4,
        [
            ((TAPS, channels, 4 * ch), bf16),
            ((2, 4 * ch, channels), bf16),
            ((2, 1, channels), f32),
        ],
        [bn_gain, bn_bias, taps_first],
        "weight_pack",
        held=range(3),
        copies=TAPS + 2,
    )
    slices = spread(packed, to_section)

    payload = ((cells + META_ROWS, channels), bf16)
    sent = call(
        partial(frames_kernel, dims),
        [payload] * 4,
        [
            ((micro_total, cells, channels), bf16),
            (image_group.shape[::-1], jnp.int32),
            (group_size.shape[::-1], jnp.int32),
        ],
        [image_group.T, group_size.T, after(images.reshape(micro_total, cells, channels), packed)],
        "frames",
        held=range(3),
        copies=3,
    )
    frames_in = with_core(spread(sent, to_plane))

    half = (core * ch + np.arange(ch))[:, None] == np.arange(2 * ch)[None, :]
    hidden, normed, full, inside = call(
        partial(forward_kernel, dims, 0, True, True, CONVS == 1),
        [map_out, kept_out, full_frames, ((1, length), f32)],
        [
            full_frames,
            tap_scratch,
            kept_out,
            weight_slice,
            ((frames * META_ROWS, channels), bf16),
        ],
        [*frames_in, *slices, facts],
        "forward",
        held_outs=(1, 2),
        loose=(8, 9, 10, 11, 12),
        flops=conv_flops,
        copies=4,
    )
    kept, fulls = [normed], [full]
    same_core = [[2 * z + c for z in range(layers)] for c in range(2)]
    for layer in range(1, layers):
        weights = call(
            partial(pick_kernel, layer),
            [weight_slice],
            [],
            after(slices, hidden),
            "pick",
            flops=PICK_FLOPS,
            held=range(4),
            copies=1,
        )
        beside = [*weights]
        if layer == 1:
            turned, *crossing = call(
                partial(turn_weights_kernel, layers),
                [((layers * 4 * ch, tap_rows), bf16)] + [((4 * ch, tap_rows), bf16)] * layers,
                [
                    ((layers, TAPS * ch, channels), bf16),
                    ((channels, TAPS * ch), bf16),
                    ((2, layers * 4 * ch, tap_rows), bf16),
                ],
                after(slices, hidden),
                "turn_weights",
                held=range(4),
                held_outs=range(1 + layers),
                copies=1 + layers,
            )
            beside.append((turned, crossing))
        if layer == COT_LAYER - 1:
            (cot_slots,) = call(
                cot_slice_kernel,
                [((micro_total * cells, LANES), bf16)],
                [((micro_total, cells, channels), bf16)],
                [after(cotangent.reshape(micro_total, cells, channels), hidden)],
                "cot_slices",
                held=(0,),
                copies=1,
            )
            beside.append(cot_slots)
        if layer == COT_LAYER:
            cot_slots = after(cot_slots, hidden)
            cots = lax.all_to_all(cot_slots, "dp", 0, 0, tiled=True, axis_index_groups=same_core)
        if layer == last:
            crossing[last] = to_core(after(crossing[last], hidden))
            cots = after(cots, hidden)
            (cot,) = call(
                cot_kernel,
                [map_out],
                [((length, LANES), bf16)],
                [cots, to_core(cots), half.astype(bf16)],
                "cotangent",
                loose=(0, 1, 2),
            )
            beside.append(cot)
        blocks = [hidden] + [to_section(hidden, k) for k in (1, 2, 3)]
        blocks[3] = after(blocks[3], *beside)
        blocks = with_core(blocks)
        if layer < last:
            hidden, normed, full = call(
                partial(forward_kernel, dims, layer, False, False, layer == CONVS - 1),
                [map_out, kept_out, full_map],
                [full_map, tap_scratch, kept_out],
                [*blocks, *weights, inside, facts],
                "forward",
                held_outs=(1, 2),
                loose=(9, 10),
                flops=conv_flops,
                copies=3,
            )
            kept.append(normed)
        else:
            activation, full, grad_pre, sums = call(
                partial(turn_kernel, dims, last, last == CONVS - 1),
                [map_out, full_map, map_out, sums_out],
                [full_map, tap_scratch, map_out],
                [*blocks, *weights, cot, inside, facts],
                "turn",
                held_outs=(0, 1),
                loose=(10, 11),
                flops=conv_flops,
                copies=3,
            )
        fulls.append(full)

    shares = [None] * layers
    for layer in range(last, -1, -1):
        share_out = ((4 * piece_rows[layer], 2 * ch), bf16)
        other = to_core(grad_pre)
        if layer:
            held = call(
                partial(fetch_kernel, layer - 1),
                [kept_out, ((META_ROWS, channels), bf16)],
                [],
                [after(kept[layer - 1], grad_pre), *slices],
                "fetch",
                held=range(5),
                copies=2,
            )
            other, held = lax.optimization_barrier((other, held))
        pieces = [share_out] if layer else [((slice_rows, 2 * ch), bf16)] * 4
        outs = call(
            partial(conv_back_kernel, dims, layer),
            [map_out] * 4 + pieces,
            [
                share_out,
                full_map if layer else full_frames,
                ((2 * tap_rows, length), bf16),
                ((4 * ch, 2 * tap_rows), bf16),
            ],
            [grad_pre, other, turned, crossing[layer], fulls[layer], facts]
            + ([] if layer else [sums]),
            "conv_back",
            held=(2, 4),
            free=(3,),
            held_outs=range(4, 8),
            loose=(5,) if layer else (5, 6),
            flops=BACK_FLOPS[layer],
            copies=7,
        )
        parts, share = outs[:4], outs[4:]
        if layer == 0:
            shares[0] = [share[0]] + [None] + [to_plane(share[k], k) for k in (2, 3)]
            break
        if layer < last:
            share = after(share, shares[layer + 1])
        shares[layer] = lax.all_to_all(share[0], "dp", 0, 0, tiled=True, axis_index_groups=same_core)
        if layer:
            crossing[layer - 1] = to_core(after(crossing[layer - 1], parts))
            blocks = spread(parts, to_section)
            grad_pre, sums = call(
                partial(norm_back_kernel, dims, layer - 1, layer - 1 == CONVS - 1),
                [map_out, sums_out],
                [],
                [*blocks, *held, inside, facts, sums],
                "norm_back",
                loose=(6, 7, 8),
            )
    blocks = [parts[0]] + [to_section(parts[k], k) for k in (1, 2, 3)]
    shares[0][1] = to_plane(after(share[1], blocks[1]), 1)
    blocks = after(blocks, shares[1])
    keep, give = call(
        input_kernel,
        [((4 * ch, 2 * cells), bf16)] * 2,
        [((2 * ch, length), bf16)],
        [*blocks, activation, inside],
        "input",
        flops=INPUT_FLOPS,
        held=(4,),
        loose=(5,),
        copies=1,
    )
    maps = call(pair_kernel, [((4 * ch, 2 * cells), bf16)] * 2, [], [keep, to_core(give)], "pair")
    maps = [send(x, lambda s, z, c, n=n: (z, s ^ (2 * c + n), c)) for n, x in enumerate(maps)]
    folded = call(
        fold_kernel,
        [((rows, 2 * ch), bf16) for rows in piece_rows[1:]],
        [((last, 4 * TAPS * ch, 2 * ch), bf16)],
        shares[1:],
        "fold",
        held=range(last),
        copies=last,
    )
    chosen = call(
        choose_kernel,
        [((slice_rows, 2 * ch), bf16)] * 4,
        [],
        [*shares[0], *folded],
        "choose",
        loose=range(4),
    )
    pick = (core * cells + np.arange(cells))[:, None] == np.arange(2 * cells)[None, :]
    map_pick = pick.astype(bf16)
    pick = (core * ch + np.arange(ch))[:, None] == np.arange(2 * ch)[None, :]
    weight_grad, bias_grad, gain_grad, activations, input_grad = call(
        outputs_kernel,
        [((TAPS, ch, channels), f32), ((1, ch), f32), ((1, ch), f32)] + [((cells, channels), bf16)] * 2,
        [((TAPS, channels, 2 * ch), bf16), ((2, channels, 2 * cells), bf16)],
        [
            *with_core([chosen[0]] + [to_section(chosen[k], k) for k in (1, 2, 3)]),
            pick.astype(bf16),
            *with_core(after(maps, chosen)),
            map_pick,
        ],
        "outputs",
        loose=(8, 13),
        last=True,
    )
    weight_grad = weight_grad.reshape(3, 3, ch, channels).transpose(2, 0, 1, 3)[None]
    return (
        activations.reshape(1, 1, rows, cols, channels),
        input_grad.reshape(1, 1, rows, cols, channels),
        weight_grad,
        gain_grad,
        bias_grad,
    )


def fits_plane_plan(images, conv_weight, sections, dps):
    micro_total, images_total, rows, cols, channels = images.shape
    return (
        sections == 4
        and dps == 2 * sections
        and micro_total == sections
        and conv_weight.shape[0] == sections
        and images_total == dps
        and rows % 2 == 0
        and cols % 2 == 0
        and (rows * cols) % 64 == 0
        and channels == 512
    )


def solution(mesh):
    in_specs = (
        P(None, "dp", None, None, None),
        P(None, "dp"),
        P(),
        P("section", None, None, None, None),
        P("section", None),
        P("section", None),
        P(None, "dp", None, None, None),
    )
    out_specs = (
        P("section", "dp", None, None, None),
        P("section", "dp", None, None, None),
        P("section", "dp", None, None, None),
        P("section", "dp"),
        P("section", "dp"),
    )
    sections, dps = mesh.shape["section"], mesh.shape["dp"]

    def program(images, image_group, group_size, conv_weight, bn_gain, bn_bias, cotangent):
        plan = plane_shards if fits_plane_plan(images, conv_weight, sections, dps) else pipeline_shards
        sharded = jax.shard_map(plan, mesh=mesh, in_specs=in_specs, out_specs=out_specs, check_vma=False)
        return sharded(images, image_group, group_size, conv_weight, bn_gain, bn_bias, cotangent)

    return program
```

```python
import math
from functools import partial

import jax
import jax.numpy as jnp
import numpy as np
from jax import lax
from jax.experimental import pallas as pl
from jax.experimental.pallas import tpu as pltpu
from jax.sharding import PartitionSpec as P

CONVS = 2
BACK_FLOPS = (3 * 10**9, 56 * 10**8, 56 * 10**8, 0)
PICK_FLOPS = 2 * 10**9
COT_LAYER = 2
INPUT_FLOPS = 0 * 10**9


eps = 1e-05


def from_behind(x, axis, by):
    peers = lax.axis_size(axis)
    pairs = [(i, i + by) for i in range(peers) if 0 <= i + by < peers]
    return lax.ppermute(x, axis, pairs)


def canvas_mask(image_group, group_size, canvas_rows, canvas_cols):
    groups_n = group_size.shape[0]
    onehot = image_group[..., None] == jnp.arange(groups_n, dtype=jnp.int32)
    height = jnp.sum(jnp.where(onehot, group_size[:, 0], 0), axis=-1)
    breadth = jnp.sum(jnp.where(onehot, group_size[:, 1], 0), axis=-1)
    inside_rows = jnp.arange(canvas_rows, dtype=jnp.int32)[:, None] < height[..., None, None]
    inside_cols = jnp.arange(canvas_cols, dtype=jnp.int32)[None, :] < breadth[..., None, None]
    return (inside_rows & inside_cols).astype(jnp.float32)[..., None]


def window_pool(hidden):
    frames, height, breadth, channels = hidden.shape
    blocks = hidden.reshape(frames, height // 2, 2, breadth // 2, 2, channels)
    window_max = jnp.max(blocks, axis=(2, 4), keepdims=True)
    raised = jnp.exp(blocks - window_max)
    weights = raised / jnp.sum(raised, axis=(2, 4), keepdims=True)
    pooled = jnp.sum(weights * blocks, axis=(2, 4), keepdims=True)
    return (weights * pooled).reshape(frames, height, breadth, channels)


def activate(pre_act, inside, pooling):
    hidden = jax.nn.silu(pre_act) * inside
    return jnp.where(pooling, window_pool(hidden) * inside, hidden)


def conv_forward(layer_in, weight):
    return lax.conv_general_dilated(
        layer_in,
        weight,
        (1, 1),
        "SAME",
        dimension_numbers=("NHWC", "IHWO", "NHWC"),
        preferred_element_type=jnp.float32,
    )


def conv_data_back(grad_pre, weight):
    flipped = weight[:, ::-1, ::-1, :]
    return lax.conv_general_dilated(
        grad_pre,
        flipped,
        (1, 1),
        "SAME",
        dimension_numbers=("NHWC", "OHWI", "NHWC"),
        preferred_element_type=jnp.float32,
    )


def weight_back(layer_in, grad_pre):
    height = layer_in.shape[1]
    breadth = layer_in.shape[2]
    padded = jnp.pad(layer_in, ((0, 0), (1, 1), (1, 1), (0, 0)))
    pieces = []
    for tap_row in range(3):
        for tap_col in range(3):
            window = padded[:, tap_row : tap_row + height, tap_col : tap_col + breadth, :]
            pieces.append(
                jnp.einsum("nhwi,nhwo->io", window, grad_pre, preferred_element_type=jnp.float32)
            )
    return jnp.stack(pieces, axis=1).reshape(layer_in.shape[3], 3, 3, grad_pre.shape[3])


def layer_forward(layer_in, weight, gain_row, bias_row, inside, pooling):
    pre_norm = conv_forward(layer_in, weight)
    sums = lax.psum(
        (
            jnp.sum(pre_norm * inside, axis=(0, 1, 2)),
            jnp.sum(pre_norm * pre_norm * inside, axis=(0, 1, 2)),
            jnp.sum(inside),
        ),
        "dp",
    )
    pixel_total = sums[2]
    mean_val = sums[0] / pixel_total
    scale_inv = lax.rsqrt(sums[1] / pixel_total - mean_val * mean_val + eps)
    pre_act = (pre_norm - mean_val) * scale_inv * gain_row + bias_row
    hidden = activate(pre_act, inside, pooling)
    return (pre_norm, mean_val, scale_inv, pixel_total, hidden)


def layer_backward(
    grad_out,
    layer_in,
    pre_norm,
    mean_val,
    scale_inv,
    pixel_total,
    weight,
    gain_row,
    bias_row,
    inside,
    pooling,
):
    normed = (pre_norm - mean_val) * scale_inv
    pre_act = normed * gain_row + bias_row
    hidden_out, pullback = jax.vjp(partial(activate, inside=inside, pooling=pooling), pre_act)
    grad_act = pullback(grad_out)[0]
    sums = lax.psum(
        (jnp.sum(grad_act, axis=(0, 1, 2)), jnp.sum(grad_act * normed, axis=(0, 1, 2))), "dp"
    )
    shift_term = sums[0] / pixel_total
    slope_term = sums[1] / pixel_total
    grad_pre = (
        inside * scale_inv * gain_row * (grad_act - shift_term - normed * slope_term)
    ).astype(jnp.bfloat16)
    weight_term = weight_back(layer_in, grad_pre)
    grad_in = conv_data_back(grad_pre, weight).astype(jnp.bfloat16)
    return (grad_in, weight_term, sums[1], sums[0])


def pipeline_shards(images, image_group, group_size, conv_weight, bn_gain, bn_bias, cotangent):
    section_index = lax.axis_index("section")
    sections = lax.axis_size("section")
    micro_total = images.shape[0]
    channels = conv_weight.shape[1]
    inside_all = canvas_mask(image_group, group_size, images.shape[2], images.shape[3])
    ticks = micro_total + sections - 1
    weight = conv_weight[0]
    gain_row = bn_gain[0]
    bias_row = bn_bias[0]
    pool_here = section_index == CONVS - 1
    received = jnp.zeros(images.shape[1:], jnp.bfloat16)
    kept_in, kept_pre, kept_mean, kept_scale, kept_total, finished = ([], [], [], [], [], [])
    for tick in range(ticks):
        micro_pos = jnp.clip(tick - section_index, 0, micro_total - 1)
        inside = inside_all[micro_pos]
        fresh = (images[micro_pos].astype(jnp.float32) * inside).astype(jnp.bfloat16)
        layer_in = jnp.where(section_index == 0, fresh, received)
        pre_norm, mean_val, scale_inv, pixel_total, hidden = layer_forward(
            layer_in, weight, gain_row, bias_row, inside, pool_here
        )
        sent = hidden.astype(jnp.bfloat16)
        if tick < ticks - 1:
            received = from_behind(sent, "section", 1)
        kept_in.append(layer_in)
        kept_pre.append(pre_norm)
        kept_mean.append(mean_val)
        kept_scale.append(scale_inv)
        kept_total.append(pixel_total)
        finished.append(sent)
    stack_in = jnp.stack(kept_in)
    stack_pre = jnp.stack(kept_pre)
    stack_mean = jnp.stack(kept_mean)
    stack_scale = jnp.stack(kept_scale)
    stack_total = jnp.stack(kept_total)
    returned = jnp.zeros(images.shape[1:], jnp.bfloat16)
    weight_sum = jnp.zeros(conv_weight.shape[1:], jnp.float32)
    gain_sum = jnp.zeros((channels,), jnp.float32)
    bias_sum = jnp.zeros((channels,), jnp.float32)
    input_list = []
    for tick in range(ticks):
        micro_raw = tick - (sections - 1 - section_index)
        valid = ((micro_raw >= 0) & (micro_raw < micro_total)).astype(jnp.float32)
        micro_pos = jnp.clip(micro_raw, 0, micro_total - 1)
        forward_tick = jnp.clip(micro_pos + section_index, 0, ticks - 1)
        inside = inside_all[micro_pos]
        grad_out = jnp.where(
            section_index == sections - 1,
            cotangent[micro_pos].astype(jnp.float32),
            returned.astype(jnp.float32),
        )
        grad_in, weight_term, gain_term, bias_term = layer_backward(
            grad_out,
            stack_in[forward_tick],
            stack_pre[forward_tick],
            stack_mean[forward_tick],
            stack_scale[forward_tick],
            stack_total[forward_tick],
            weight,
            gain_row,
            bias_row,
            inside,
            pool_here,
        )
        weight_sum = weight_sum + valid * weight_term
        gain_sum = gain_sum + valid * gain_term
        bias_sum = bias_sum + valid * bias_term
        if tick < ticks - 1:
            returned = from_behind(grad_in, "section", -1)
        input_list.append((grad_in.astype(jnp.float32) * inside).astype(jnp.bfloat16))
    out_stack = jnp.stack(finished[sections - 1 :], axis=0)
    grad_stack = jnp.stack(input_list[sections - 1 :], axis=0)
    out_back, grad_back = (
        lax.all_to_all(out_stack, "section", split_axis=0, concat_axis=1, tiled=True),
        lax.all_to_all(grad_stack, "section", split_axis=0, concat_axis=1, tiled=True),
    )
    activations = out_back[:, sections - 1 : sections]
    input_grad = grad_back[:, 0:1]
    weight_grad = lax.psum_scatter(weight_sum[None], "dp", scatter_dimension=1, tiled=True)
    share = channels // lax.axis_size("dp")
    gain_grad = lax.dynamic_slice_in_dim(gain_sum, lax.axis_index("dp") * share, share)[None]
    bias_grad = lax.dynamic_slice_in_dim(bias_sum, lax.axis_index("dp") * share, share)[None]
    return (activations, input_grad, weight_grad, gain_grad, bias_grad)


AXES = ("section", "dp")
TAPS = 9
VMEM_LIMIT = 24 * 1024 * 1024
META_ROWS = 16
LANES = 128
ROW_AT, COL_AT, FRAME_AT = 6, 7, 8
NT = (((1,), (1,)), ((), ()))


def place():
    dp_index = lax.axis_index("dp")
    return lax.axis_index("section"), dp_index // 2, dp_index % 2


def peer_order():
    return [(k, j) for j in range(2) for k in range(4)]


def slice_at(section, core, k, j):
    return (core ^ j) * lax.axis_size("section") + (section ^ k)


def send(x, target):
    sections = lax.axis_size("section")
    dps = lax.axis_size("dp")
    pairs = []
    for s in range(sections):
        for d in range(dps):
            ts, tz, tc = target(s, d // 2, d % 2)
            pairs.append((s * dps + d, ts * dps + tz * 2 + tc))
    return lax.ppermute(x, AXES, pairs)


def to_section(x, k):
    return send(x, lambda s, z, c: (s ^ k, z, c))


def to_plane(x, k):
    return send(x, lambda s, z, c: (s, z ^ k, c))


def to_core(x):
    return send(x, lambda s, z, c: (s, z, c ^ 1))


def spread(blocks, move, *beside):
    moved = lax.optimization_barrier(([move(blocks[k], k) for k in (1, 2, 3)], beside))[0]
    return [blocks[0]] + moved


def with_core(blocks):
    return blocks + [to_core(x) for x in blocks]


def after(x, *first):
    return lax.optimization_barrier((x, first))[0]


def grid_facts(frames, rows, cols):
    at = np.arange(frames * rows * cols)
    col = at % cols
    row = (at // cols) % rows
    facts = [row > 0, row < rows - 1, col > 0, col < cols - 1, col % 2 == 0, row % 2 == 0, row, col]
    facts = facts + [at // (rows * cols) == frame for frame in range(frames)]
    return jnp.asarray(np.stack(facts).astype(np.float32))


def shift(x, by):
    length = x.shape[1]
    return pltpu.roll(x, (-by) % length, 1) if by % length else x


def row_ok(facts, d):
    return facts[0:1, :] if d < 0 else facts[1:2, :]


def col_ok(facts, d):
    return facts[2:3, :] if d < 0 else facts[3:4, :]


def sum_taps(taps_ref, facts, cols):
    ch = taps_ref.shape[0] // TAPS
    total = None
    for dx in (-1, 0, 1):
        column = None
        for dy in (-1, 0, 1):
            tap = (dy + 1) * 3 + dx + 1
            piece = taps_ref[tap * ch : (tap + 1) * ch, :]
            if dy:
                piece = shift(piece, dy * cols) * row_ok(facts, dy)
            column = piece if column is None else column + piece
        if dx:
            column = shift(column, dx) * col_ok(facts, dx)
        total = column if total is None else total + column
    return total


def spread_taps(grad, moved_ref, base, facts, cols):
    ch = grad.shape[0]
    facts = facts[:4, :].astype(grad.dtype)
    for dx in (-1, 0, 1):
        column = shift(grad, -dx) * col_ok(facts, -dx) if dx else grad
        for dy in (-1, 0, 1):
            piece = shift(column, -dy * cols) * row_ok(facts, -dy) if dy else column
            at = base + ((dy + 1) * 3 + dx + 1) * ch
            moved_ref[at : at + ch, :] = piece


def corner_sum(x, cols):
    x = x + shift(x, 1)
    return x + shift(x, cols)


def from_corner(x, facts, cols):
    x = jnp.where(facts[4:5, :] > 0.5, x, shift(x, -1))
    return jnp.where(facts[5:6, :] > 0.5, x, shift(x, -cols))


def lane_sum(x):
    return jnp.sum(x, axis=1, keepdims=True)


def normalise(pre, inside):
    count = lane_sum(inside)
    mean = lane_sum(pre * inside) / count
    square = lane_sum(pre * pre * inside) / count
    scale = lax.rsqrt(square - mean * mean + eps)
    return (pre - mean) * scale, scale


def hidden_of(normed, gain, bias, inside, facts, cols, pooling):
    pre_act = normed * gain + bias
    hidden = pre_act * jax.nn.sigmoid(pre_act) * inside
    if pooling:
        raised = jnp.exp(hidden)
        total = corner_sum(raised, cols)
        pooled = corner_sum(raised * hidden, cols) / total
        hidden = raised * from_corner(pooled / total, facts, cols) * inside
    return hidden


def norm_back(grad, normed, scale, gain, bias, inside, facts, cols, pooling):
    pre_act = normed * gain + bias
    gate = jax.nn.sigmoid(pre_act)
    if pooling:
        hidden = pre_act * gate * inside
        raised = jnp.exp(hidden)
        out = grad * inside
        total = 1.0 / corner_sum(raised, cols)
        pooled = corner_sum(raised * hidden, cols) * total
        d_pooled = corner_sum(raised * out, cols) * total
        by_out = from_corner(pooled * total, facts, cols)
        by_hidden = from_corner(d_pooled * total, facts, cols)
        rest = from_corner(d_pooled * total * (1.0 - 2.0 * pooled), facts, cols)
        grad = raised * (out * by_out + hidden * by_hidden + rest)
    grad_act = grad * inside * gate * (1.0 + pre_act * (1.0 - gate))
    count = lane_sum(inside)
    shift_sum = lane_sum(grad_act)
    slope_sum = lane_sum(grad_act * normed)
    grad_pre = inside * (scale * gain) * (grad_act - shift_sum / count - normed * (slope_sum / count))
    return grad_pre.astype(jnp.bfloat16), shift_sum, slope_sum


def assemble(blocks, full_ref):
    section, _, core = place()
    ch = blocks[0].shape[0]
    for (k, j), block in zip(peer_order(), blocks):
        at = pl.multiple_of(slice_at(section, core, k, j) * ch, ch)
        full_ref[pl.ds(at, ch), :] = block[...]


def assemble_frames(blocks, full_ref, rows, lanes):
    _, plane, core = place()
    size = rows.stop - rows.start
    for (k, j), block in zip(peer_order(), blocks):
        frame = (plane ^ k) * 2 + (core ^ j)
        full_ref[pl.ds(pl.multiple_of(frame * size, size), size), :] = block[rows, lanes]


def start_all(copies):
    for copy in copies:
        copy.start()
    return copies


def wait_all(copies):
    for copy in copies:
        copy.wait()


def tap_products(weight, full_ref, taps_ref, by_cells):
    length = taps_ref.shape[1]
    step = 512 if length % 512 == 0 else length
    for at in range(0, length, step):
        if by_cells:
            taps_ref[:, at : at + step] = lax.dot_general(
                weight, full_ref[at : at + step, :], NT, preferred_element_type=jnp.float32
            )
        else:
            taps_ref[:, at : at + step] = jnp.dot(
                weight, full_ref[:, at : at + step], preferred_element_type=jnp.float32
            )


def pick_layer(layer, sources, start, target, sem):
    section, _, _ = place()
    rows = pl.ds(start, target.shape[0])
    for k, source in enumerate(sources):

        @pl.when((section ^ layer) == k)
        def _():
            pltpu.make_async_copy(source.at[rows], target, sem).start()

    return pltpu.make_async_copy(sources[0].at[rows], target, sem)


def take_layer(layer, sources, target):
    section, _, _ = place()
    for k, source in enumerate(sources):

        @pl.when((section ^ layer) == k)
        def _():
            target[...] = source[...]


def affine(meta, ch):
    parts = meta[:, :LANES].astype(jnp.float32).T[:ch]
    return (
        parts[:, 0:1] + parts[:, 1:2] + parts[:, 2:3],
        parts[:, 3:4] + parts[:, 4:5] + parts[:, 5:6],
    )


def plane_inside(metas, facts):
    frames = metas.shape[0] // META_ROWS
    extents = []
    for line in (0, 1):
        total = None
        for f in range(frames):
            at = f * META_ROWS + line
            extent = metas[at : at + 1, 0:1].astype(jnp.float32) * facts[FRAME_AT + f : FRAME_AT + f + 1, :]
            total = extent if total is None else total + extent
        extents.append(total)
    on = (facts[ROW_AT : ROW_AT + 1, :] < extents[0]) & (facts[COL_AT : COL_AT + 1, :] < extents[1])
    return jnp.where(on, 1.0, 0.0)


def frames_kernel(dims, group_table, size_table, images, *refs):
    payloads, (image_in, groups, sizes, sems) = refs[:4], refs[4:]
    copies = start_all(
        [
            pltpu.make_async_copy(group_table, groups, sems.at[0]),
            pltpu.make_async_copy(size_table, sizes, sems.at[1]),
            pltpu.make_async_copy(images, image_in, sems.at[2]),
        ]
    )
    _, plane, _ = place()
    rows, cols = dims
    cells = rows * cols
    at = lax.broadcasted_iota(jnp.int32, (cells, LANES), 0).astype(jnp.float32)
    row = jnp.floor((at + 0.5) * (1.0 / cols))
    col = at - row * cols
    channels = images.shape[2]
    line = lax.broadcasted_iota(jnp.int32, (META_ROWS, channels), 0)
    wait_all(copies)
    for k in range(4):
        micro = plane ^ k
        group = groups[0, micro]
        height = sizes[0, 0]
        breadth = sizes[1, 0]
        for g in range(1, sizes.shape[1]):
            height = jnp.where(group == g, sizes[0, g], height)
            breadth = jnp.where(group == g, sizes[1, g], breadth)
        height = height.astype(jnp.float32)
        breadth = breadth.astype(jnp.float32)
        on = jnp.where((row < height) & (col < breadth), 1.0, 0.0)
        image = image_in[micro]
        for c in range(0, channels, LANES):
            piece = image[:, c : c + LANES].astype(jnp.float32) * on
            payloads[k][:cells, c : c + LANES] = piece.astype(jnp.bfloat16)
        payloads[k][cells:, :] = jnp.where(line == 0, height, breadth).astype(jnp.bfloat16)


def cot_slice_kernel(cots, out, cot_in, sems):
    copy = pltpu.make_async_copy(cots, cot_in, sems.at[0])
    copy.start()
    section, _, _ = place()
    micros, cells, channels = cots.shape
    half = channels // 2
    tile = section // 2 * LANES
    odd = section % 2 == 1
    lane = lax.broadcasted_iota(jnp.int32, (cells, LANES), 1)
    copy.wait()
    for micro in range(micros):
        low = cot_in[micro, :, pl.ds(pl.multiple_of(tile, LANES), LANES)].astype(jnp.float32)
        high = cot_in[micro, :, pl.ds(pl.multiple_of(half + tile, LANES), LANES)].astype(jnp.float32)
        low = jnp.where(odd, pltpu.roll(low, LANES // 2, 1), low)
        high = jnp.where(odd, high, pltpu.roll(high, LANES // 2, 1))
        both = jnp.where(lane < LANES // 2, low, high).astype(jnp.bfloat16)
        out[micro * cells : (micro + 1) * cells, :] = both


def cot_kernel(own, other, pick, out, full):
    _, _, core = place()
    cells = full.shape[0] // 8
    for n in range(4):
        for j, block in enumerate((own, other)):
            at = pl.multiple_of((2 * n + (core ^ j)) * cells, cells)
            full[pl.ds(at, cells), :] = block[n * cells : (n + 1) * cells, :]
    out[...] = lax.dot_general(pick[...], full[...], NT, preferred_element_type=jnp.float32).astype(
        jnp.bfloat16
    )


def pack_kernel(gain, bias, weight, *refs):
    outs, (columns, turned, tables, sems) = refs[:4], refs[4:]
    section, _, core = place()
    width = columns.shape[2]
    ch = width // 4
    start = pl.multiple_of(core * width, width)
    copies = start_all(
        [
            pltpu.make_async_copy(weight.at[tap, :, pl.ds(start, width)], columns.at[tap], sems.at[tap])
            for tap in range(TAPS)
        ]
    )
    table_copies = start_all(
        [
            pltpu.make_async_copy(gain, tables.at[0], sems.at[TAPS]),
            pltpu.make_async_copy(bias, tables.at[1], sems.at[TAPS + 1]),
        ]
    )
    for tap in range(TAPS):
        copies[tap].wait()
        turned[tap % 2] = columns[tap].T
        for k, out in enumerate(outs):
            rows = pl.ds(pl.multiple_of((section ^ k) * ch, ch), ch)
            out[tap * ch : (tap + 1) * ch, :] = turned[tap % 2, rows, :]
    wait_all(table_copies)
    for k, out in enumerate(outs):
        lines = []
        tile = pl.multiple_of(start + (section ^ k) // 2 * LANES, LANES)
        odd = (section ^ k) % 2 == 1
        for m in range(2):
            line = tables[m, :, pl.ds(tile, LANES)]
            line = jnp.where(odd, pltpu.roll(line, ch, 1), line)
            for _ in range(3):
                part = line.astype(jnp.bfloat16).astype(jnp.float32)
                lines.append(part)
                line = line - part
        lines.append(jnp.zeros((META_ROWS - len(lines), LANES), jnp.float32))
        out[TAPS * ch :, :] = jnp.zeros((META_ROWS, out.shape[1]), jnp.bfloat16)
        out[TAPS * ch :, :LANES] = jnp.concatenate(lines, axis=0).astype(jnp.bfloat16)


def pick_kernel(layer, *refs):
    sources, (out, sems) = refs[:4], refs[4:]
    pick_layer(layer, sources, 0, out, sems.at[0]).wait()


def forward_kernel(dims, layer, first, picks, pooling, *refs):
    blocks, weights, rest = refs[:8], refs[8 : 12 if picks else 9], refs[12 if picks else 9 :]
    rows, cols = dims
    cells = rows * cols
    if first:
        facts, hidden, kept, full_out, inside_out, full, taps, stage, weight, metas, sems = rest
    elif picks:
        inside, facts, hidden, kept, full_out, full, taps, stage, weight, sems = rest
    else:
        inside, facts, hidden, kept, full_out, full, taps, stage, sems = rest
        (weight,) = weights
    if first:
        take_layer(layer, weights, weight)
    elif picks:
        copy = pick_layer(layer, weights, 0, weight, sems.at[2])
    facts_now = facts[...]
    if first:
        channels = full.shape[1]
        assemble_frames(blocks, full, slice(0, cells), slice(0, channels))
    else:
        assemble(blocks, full)
    full_copy = pltpu.make_async_copy(full, full_out, sems.at[0])
    full_copy.start()
    if first:
        assemble_frames(blocks, metas, slice(cells, cells + META_ROWS), slice(0, channels))
        inside_now = plane_inside(metas, facts_now)
        inside_out[...] = inside_now
    else:
        inside_now = inside[...]
    if picks and not first:
        copy.wait()
    ch = hidden.shape[0]
    tap_products(weight[: TAPS * ch, :], full, taps, first)
    pre = sum_taps(taps, facts_now, cols)
    normed, scale = normalise(pre, inside_now)
    length = normed.shape[1]
    stage[:, :length] = normed
    stage[:, length:] = jnp.broadcast_to(scale, (ch, LANES))
    kept_copy = pltpu.make_async_copy(stage, kept, sems.at[1])
    kept_copy.start()
    gain, bias = affine(weight[TAPS * ch :, :], ch)
    hidden[...] = hidden_of(normed, gain, bias, inside_now, facts_now, cols, pooling).astype(jnp.bfloat16)
    full_copy.wait()
    kept_copy.wait()


def turn_kernel(dims, layer, pooling, *refs):
    blocks, (weight, cot_in, inside, facts) = refs[:8], refs[8:12]
    hidden_out, full_out, grad_pre, sums, full, taps, hidden, sems = refs[12:]
    cols = dims[1]
    assemble(blocks, full)
    full_copy = pltpu.make_async_copy(full, full_out, sems.at[1])
    full_copy.start()
    ch = grad_pre.shape[0]
    tap_products(weight[: TAPS * ch, :], full, taps, False)
    facts_now, inside_now = facts[...], inside[...]
    pre = sum_taps(taps, facts_now, cols)
    normed, scale = normalise(pre, inside_now)
    gain, bias = affine(weight[TAPS * ch :, :], ch)
    hidden[...] = hidden_of(normed, gain, bias, inside_now, facts_now, cols, pooling).astype(jnp.bfloat16)
    hidden_copy = pltpu.make_async_copy(hidden, hidden_out, sems.at[2])
    hidden_copy.start()
    grad_pre[...], shift_sum, slope_sum = norm_back(
        cot_in[...].astype(jnp.float32), normed, scale, gain, bias, inside_now, facts_now, cols, pooling
    )
    sums[...] = with_sums(layer, shift_sum, slope_sum, 0.0)
    full_copy.wait()
    hidden_copy.wait()


def with_sums(layer, shift_sum, slope_sum, others):
    at = lax.broadcasted_iota(jnp.int32, (shift_sum.shape[0], LANES), 1)
    return jnp.where(at == 2 * layer, shift_sum, jnp.where(at == 2 * layer + 1, slope_sum, others))


def add_blocks(blocks):
    total = blocks[0][...].astype(jnp.float32)
    for block in blocks[1:]:
        total = total + block[...].astype(jnp.float32)
    return total


def fetch_kernel(layer, kept, *refs):
    sources, (kept_out, meta_out, sems) = refs[:4], refs[4:]
    copy = pltpu.make_async_copy(kept, kept_out, sems.at[0])
    copy.start()
    start = sources[0].shape[0] - META_ROWS
    pick_layer(layer, sources, start, meta_out, sems.at[1]).wait()
    copy.wait()


def norm_back_kernel(dims, layer, pooling, *refs):
    blocks, (kept, meta, inside, facts, sums_in, grad_pre, sums) = refs[:4], refs[4:]
    ch, length = grad_pre.shape
    grad = add_blocks(blocks).astype(jnp.bfloat16).astype(jnp.float32)
    gain, bias = affine(meta[...], ch)
    grad_pre[...], shift_sum, slope_sum = norm_back(
        grad,
        kept[:, :length],
        kept[:, length : length + 1],
        gain,
        bias,
        inside[...],
        facts[...],
        dims[1],
        pooling,
    )
    sums[...] = with_sums(layer, shift_sum, slope_sum, sums_in[...])


def weight_product(moved, full, first):
    if first:
        return jnp.dot(moved, full, preferred_element_type=jnp.float32)
    return lax.dot_general(moved, full, NT, preferred_element_type=jnp.float32)


def sums_rows(sums, width):
    ch = sums.shape[0]
    turned = jnp.concatenate([sums[...].T, jnp.zeros((LANES, width - ch), jnp.float32)], axis=1)
    return turned[:META_ROWS].astype(jnp.bfloat16)


def form_share(layer, moved, full, sums, product):
    piece = product.shape[0] // 4
    rows = piece - META_ROWS * len(sums)
    width = product.shape[1]
    value = weight_product(moved[:rows, :], full[...], layer == 0)
    for n in range(4):
        product[n * piece : n * piece + rows, :] = value[:, n * width : (n + 1) * width].astype(jnp.bfloat16)
        for ref in sums:
            product[n * piece + rows : (n + 1) * piece, :] = sums_rows(ref, width)


def copy_pieces(product, shares, sems):
    if len(shares) == 1:
        return start_all([pltpu.make_async_copy(product, shares[0], sems.at[3])])
    _, plane, _ = place()
    piece = shares[0].shape[0]
    copies = []
    for k, share in enumerate(shares):
        at = pl.multiple_of((plane ^ k) * piece, META_ROWS)
        copies.append(pltpu.make_async_copy(product.at[pl.ds(at, piece)], share, sems.at[3 + k]))
    return start_all(copies)


def conv_back_kernel(dims, layer, own, other, own_weights, other_weights, full_in, facts, *refs):
    refs, (product, full, moved, weights, sems) = refs[:-5], refs[-5:]
    sums, outs, shares = (refs[:1], refs[1:5], refs[5:]) if layer == 0 else ((), refs[:4], refs[4:])
    ch = own.shape[0]
    size = moved.shape[0] // 2
    rows = pl.ds(layer * 4 * ch, 4 * ch)
    copies = start_all(
        [
            pltpu.make_async_copy(own_weights.at[rows], weights.at[:, pl.ds(0, size)], sems.at[0]),
            pltpu.make_async_copy(other_weights, weights.at[:, pl.ds(size, size)], sems.at[1]),
        ]
    )
    full_copy = pltpu.make_async_copy(full_in, full, sems.at[2])
    full_copy.start()
    facts_now = facts[...]
    spread_taps(own[...], moved, 0, facts_now, dims[1])
    full_copy.wait()
    form_share(layer, moved, full, sums, product)
    share_copies = copy_pieces(product, shares, sems)
    spread_taps(other[...], moved, size, facts_now, dims[1])
    for n in range(2):
        moved[n * size + TAPS * ch : (n + 1) * size, :] = jnp.zeros(
            (size - TAPS * ch, moved.shape[1]), jnp.bfloat16
        )
    wait_all(copies)
    value = jnp.dot(weights[...], moved[...], preferred_element_type=jnp.float32)
    for k, out in enumerate(outs):
        out[...] = value[k * ch : (k + 1) * ch, :].astype(jnp.bfloat16)
    wait_all(share_copies)


def fold_kernel(*refs):
    count = (len(refs) - 2) // 2
    shares, outs, (blocks, sems) = refs[:count], refs[count:-2], refs[-2:]
    rows = outs[0].shape[0]
    copies = start_all(
        [pltpu.make_async_copy(share, blocks.at[n], sems.at[n]) for n, share in enumerate(shares)]
    )
    for n, copy in enumerate(copies):
        copy.wait()
        value = add_blocks([blocks.at[n, pl.ds(m * rows, rows)] for m in range(blocks.shape[1] // rows)])
        outs[n][...] = value.astype(jnp.bfloat16)


def choose_kernel(*refs):
    lasts, others, outs = refs[:4], refs[4:-4], refs[-4:]
    section, _, _ = place()
    value = add_blocks(lasts)
    value = value.astype(jnp.bfloat16)
    for k, out in enumerate(outs):

        @pl.when((section ^ k) == 0)
        def _():
            out[...] = value

        for layer, other in enumerate(others, 1):

            @pl.when((section ^ k) == layer)
            def _():
                out[: other.shape[0], :] = other[...]
                out[other.shape[0] :, :] = value[other.shape[0] :, :]


def turn_weights_kernel(layers, *refs):
    sources, own, others, (full, turned, stage, sems) = refs[:4], refs[4], refs[5:-4], refs[-4:]
    section, _, core = place()
    rows, channels = full.shape[1:]
    half = channels // 2
    ch = half // 4
    copies = [pick_layer(n, sources, 0, full.at[n], sems.at[n]) for n in range(layers)]
    stage[:, :, rows:] = jnp.zeros((*stage.shape[:2], stage.shape[2] - rows), jnp.bfloat16)
    for n in range(layers):
        copies[n].wait()
        turned[...] = full[n].T
        for j in range(2):
            for k in range(4):
                at = pl.multiple_of((core ^ j) * half + (section ^ k) * ch, ch)
                stage[j, n * half + k * ch : n * half + (k + 1) * ch, :rows] = turned[pl.ds(at, ch), :]
    copies = [pltpu.make_async_copy(stage.at[0], own, sems.at[0])]
    for n, other in enumerate(others):
        source = stage.at[1, pl.ds(n * half, half)]
        copies.append(pltpu.make_async_copy(source, other, sems.at[1 + n]))
    wait_all(start_all(copies))


def input_kernel(*refs):
    blocks, (hidden, inside, keep, give, full, sems) = refs[:4], refs[4:]
    section, _, core = place()
    ch = hidden.shape[0]
    copy = pltpu.make_async_copy(hidden, full.at[pl.ds(0, ch)], sems.at[0])
    copy.start()
    full[ch:, :] = (add_blocks(blocks) * inside[...]).astype(jnp.bfloat16)
    copy.wait()
    rows = 2 * ch
    width = keep.shape[1]
    for j, out in enumerate((keep, give)):
        for n in range(2):
            at = pl.multiple_of((section ^ (2 * (core ^ j) + n)) * width, width)
            out[n * rows : (n + 1) * rows, :] = full[:, pl.ds(at, width)]


def pair_kernel(keep, got, *outs):
    rows = keep.shape[0] // 2
    for n, out in enumerate(outs):
        out[:rows, :] = keep[n * rows : (n + 1) * rows, :]
        out[rows:, :] = got[n * rows : (n + 1) * rows, :]


def store_maps(blocks, pick, outs, full):
    _, plane, core = place()
    ch = blocks[0].shape[0] // 4
    for m, out in enumerate(outs):
        for j in range(2):
            for n in range(2):
                for h in range(2):
                    slot = slice_at(plane ^ (2 * (core ^ j) + n), core ^ j, 0, h)
                    at = pl.multiple_of(slot * ch, ch)
                    start = (2 * h + m) * ch
                    full[m, pl.ds(at, ch), :] = blocks[2 * j + n][start : start + ch, :]
        mine = lax.dot_general(pick[...], full[m], NT, preferred_element_type=jnp.float32)
        out[...] = mine.astype(out.dtype)


def outputs_kernel(*refs):
    blocks, pick, map_blocks, map_pick, refs = refs[:8], refs[8], refs[9:13], refs[13], refs[14:]
    (weight_out, shift_out, slope_out), map_outs, (full, maps_full) = refs[:3], refs[3:5], refs[5:]
    store_maps(map_blocks, map_pick, map_outs, maps_full)
    section, plane, core = place()
    taps, rows, channels = weight_out.shape
    for tap in range(taps):
        for (k, j), block in zip(peer_order(), blocks):
            at = pl.multiple_of(slice_at(section, core, k, j) * rows, rows)
            full[tap, pl.ds(at, rows), :] = block[tap * rows : (tap + 1) * rows, :]
        weight_out[tap] = lax.dot_general(pick[...], full[tap], NT, preferred_element_type=jnp.float32)
    shift_row = jnp.zeros((1, rows), jnp.float32)
    slope_row = jnp.zeros((1, rows), jnp.float32)
    slot = plane * 2 + core
    for (k, j), block in zip(peer_order(), blocks):
        tail = block[taps * rows :, :rows].astype(jnp.float32)
        at = lax.broadcasted_iota(jnp.int32, tail.shape, 0)
        mine = slice_at(section, core, k, j) == slot
        shift_row = shift_row + jnp.sum(jnp.where(mine & (at == 2 * section), tail, 0.0), axis=0, keepdims=True)
        slope_row = slope_row + jnp.sum(jnp.where(mine & (at == 2 * section + 1), tail, 0.0), axis=0, keepdims=True)
    shift_out[...] = shift_row
    slope_out[...] = slope_row


def call(
    kernel, outs, scratch, args, name, held=(), free=(), held_outs=(), loose=(), last=False, flops=0, copies=None
):
    shapes = [
        (jax.ShapeDtypeStruct if last else pltpu.HBM if n in held_outs else pltpu.VMEM)(shape, dtype)
        for n, (shape, dtype) in enumerate(outs)
    ]
    moved = sum(a.size * a.dtype.itemsize for a in args)
    moved += sum(math.prod(shape) * jnp.dtype(dtype).itemsize for shape, dtype in outs)
    spaces = [pl.ANY if n in free else pltpu.HBM if n in held else pltpu.VMEM for n in range(len(args))]
    out_spaces = [pltpu.HBM if n in held_outs else pltpu.VMEM for n in range(len(outs))]
    args = [
        a if n in loose or n in free else pltpu.with_memory_space_constraint(a, space)
        for n, (a, space) in enumerate(zip(args, spaces))
    ]
    scratch_shapes = [
        pltpu.SMEM(shape, dtype) if dtype == jnp.int32 else pltpu.VMEM(shape, dtype) for shape, dtype in scratch
    ]
    if copies is not None:
        scratch_shapes.append(pltpu.SemaphoreType.DMA((copies,)))
    return pl.pallas_call(
        kernel,
        out_shape=shapes,
        in_specs=[pl.BlockSpec(memory_space=space) for space in spaces],
        out_specs=[pl.BlockSpec(memory_space=space) for space in out_spaces],
        scratch_shapes=scratch_shapes,
        compiler_params=pltpu.CompilerParams(vmem_limit_bytes=VMEM_LIMIT),
        cost_estimate=pl.CostEstimate(flops=flops, bytes_accessed=moved, transcendentals=0),
        name=name,
    )(*args)


def plane_shards(images, image_group, group_size, conv_weight, bn_gain, bn_bias, cotangent):
    _, _, core = place()
    micro_total, _, rows, cols, channels = images.shape
    layers = lax.axis_size("section")
    last = layers - 1
    cells = rows * cols
    frames = 2 * micro_total
    length = frames * cells
    ch = channels // 8
    dims = (rows, cols)
    bf16, f32 = jnp.bfloat16, jnp.float32
    facts = grid_facts(frames, rows, cols)
    conv_flops = 2 * TAPS * ch * channels * length
    slice_rows = TAPS * ch + META_ROWS
    tap_rows = -(-TAPS * ch // LANES) * LANES

    full_map = ((channels, length), bf16)
    full_frames = ((length, channels), bf16)
    tap_scratch = ((TAPS * ch, length), f32)
    weight_slice = ((slice_rows, channels), bf16)
    map_out = ((ch, length), bf16)
    sums_out = ((ch, LANES), f32)
    kept_out = ((ch, length + LANES), f32)
    piece_rows = [slice_rows] + [TAPS * ch] * last

    taps_first = conv_weight[0].transpose(1, 2, 0, 3).reshape(TAPS, channels, channels)
    packed = call(
        pack_kernel,
        [weight_slice] * 4,
        [
            ((TAPS, channels, 4 * ch), bf16),
            ((2, 4 * ch, channels), bf16),
            ((2, 1, channels), f32),
        ],
        [bn_gain, bn_bias, taps_first],
        "weight_pack",
        held=range(3),
        copies=TAPS + 2,
    )
    slices = spread(packed, to_section)

    payload = ((cells + META_ROWS, channels), bf16)
    sent = call(
        partial(frames_kernel, dims),
        [payload] * 4,
        [
            ((micro_total, cells, channels), bf16),
            (image_group.shape[::-1], jnp.int32),
            (group_size.shape[::-1], jnp.int32),
        ],
        [image_group.T, group_size.T, after(images.reshape(micro_total, cells, channels), packed)],
        "frames",
        held=range(3),
        copies=3,
    )
    frames_in = with_core(spread(sent, to_plane))

    half = (core * ch + np.arange(ch))[:, None] == np.arange(2 * ch)[None, :]
    hidden, normed, full, inside = call(
        partial(forward_kernel, dims, 0, True, True, CONVS == 1),
        [map_out, kept_out, full_frames, ((1, length), f32)],
        [
            full_frames,
            tap_scratch,
            kept_out,
            weight_slice,
            ((frames * META_ROWS, channels), bf16),
        ],
        [*frames_in, *slices, facts],
        "forward",
        held_outs=(1, 2),
        loose=(8, 9, 10, 11, 12),
        flops=conv_flops,
        copies=4,
    )
    kept, fulls = [normed], [full]
    same_core = [[2 * z + c for z in range(layers)] for c in range(2)]
    for layer in range(1, layers):
        weights = call(
            partial(pick_kernel, layer),
            [weight_slice],
            [],
            after(slices, hidden),
            "pick",
            flops=PICK_FLOPS,
            held=range(4),
            copies=1,
        )
        beside = [*weights]
        if layer == 1:
            turned, *crossing = call(
                partial(turn_weights_kernel, layers),
                [((layers * 4 * ch, tap_rows), bf16)] + [((4 * ch, tap_rows), bf16)] * layers,
                [
                    ((layers, TAPS * ch, channels), bf16),
                    ((channels, TAPS * ch), bf16),
                    ((2, layers * 4 * ch, tap_rows), bf16),
                ],
                after(slices, hidden),
                "turn_weights",
                held=range(4),
                held_outs=range(1 + layers),
                copies=1 + layers,
            )
            beside.append((turned, crossing))
        if layer == COT_LAYER - 1:
            (cot_slots,) = call(
                cot_slice_kernel,
                [((micro_total * cells, LANES), bf16)],
                [((micro_total, cells, channels), bf16)],
                [after(cotangent.reshape(micro_total, cells, channels), hidden)],
                "cot_slices",
                held=(0,),
                copies=1,
            )
            beside.append(cot_slots)
        if layer == COT_LAYER:
            cot_slots = after(cot_slots, hidden)
            cots = lax.all_to_all(cot_slots, "dp", 0, 0, tiled=True, axis_index_groups=same_core)
        if layer == last:
            crossing[last] = to_core(after(crossing[last], hidden))
            cots = after(cots, hidden)
            (cot,) = call(
                cot_kernel,
                [map_out],
                [((length, LANES), bf16)],
                [cots, to_core(cots), half.astype(bf16)],
                "cotangent",
                loose=(0, 1, 2),
            )
            beside.append(cot)
        blocks = [hidden] + [to_section(hidden, k) for k in (1, 2, 3)]
        blocks[3] = after(blocks[3], *beside)
        blocks = with_core(blocks)
        if layer < last:
            hidden, normed, full = call(
                partial(forward_kernel, dims, layer, False, False, layer == CONVS - 1),
                [map_out, kept_out, full_map],
                [full_map, tap_scratch, kept_out],
                [*blocks, *weights, inside, facts],
                "forward",
                held_outs=(1, 2),
                loose=(9, 10),
                flops=conv_flops,
                copies=3,
            )
            kept.append(normed)
        else:
            activation, full, grad_pre, sums = call(
                partial(turn_kernel, dims, last, last == CONVS - 1),
                [map_out, full_map, map_out, sums_out],
                [full_map, tap_scratch, map_out],
                [*blocks, *weights, cot, inside, facts],
                "turn",
                held_outs=(0, 1),
                loose=(10, 11),
                flops=conv_flops,
                copies=3,
            )
        fulls.append(full)

    shares = [None] * layers
    for layer in range(last, -1, -1):
        share_out = ((4 * piece_rows[layer], 2 * ch), bf16)
        other = to_core(grad_pre)
        if layer:
            held = call(
                partial(fetch_kernel, layer - 1),
                [kept_out, ((META_ROWS, channels), bf16)],
                [],
                [after(kept[layer - 1], grad_pre), *slices],
                "fetch",
                held=range(5),
                copies=2,
            )
            other, held = lax.optimization_barrier((other, held))
        pieces = [share_out] if layer else [((slice_rows, 2 * ch), bf16)] * 4
        outs = call(
            partial(conv_back_kernel, dims, layer),
            [map_out] * 4 + pieces,
            [
                share_out,
                full_map if layer else full_frames,
                ((2 * tap_rows, length), bf16),
                ((4 * ch, 2 * tap_rows), bf16),
            ],
            [grad_pre, other, turned, crossing[layer], fulls[layer], facts]
            + ([] if layer else [sums]),
            "conv_back",
            held=(2, 4),
            free=(3,),
            held_outs=range(4, 8),
            loose=(5,) if layer else (5, 6),
            flops=BACK_FLOPS[layer],
            copies=7,
        )
        parts, share = outs[:4], outs[4:]
        if layer == 0:
            shares[0] = [share[0]] + [None] + [to_plane(share[k], k) for k in (2, 3)]
            break
        if layer < last:
            share = after(share, shares[layer + 1])
        shares[layer] = lax.all_to_all(share[0], "dp", 0, 0, tiled=True, axis_index_groups=same_core)
        if layer:
            crossing[layer - 1] = to_core(after(crossing[layer - 1], parts))
            blocks = spread(parts, to_section)
            grad_pre, sums = call(
                partial(norm_back_kernel, dims, layer - 1, layer - 1 == CONVS - 1),
                [map_out, sums_out],
                [],
                [*blocks, *held, inside, facts, sums],
                "norm_back",
                loose=(6, 7, 8),
            )
    blocks = [parts[0]] + [to_section(parts[k], k) for k in (1, 2, 3)]
    shares[0][1] = to_plane(after(share[1], blocks[1]), 1)
    blocks = after(blocks, shares[1])
    keep, give = call(
        input_kernel,
        [((4 * ch, 2 * cells), bf16)] * 2,
        [((2 * ch, length), bf16)],
        [*blocks, activation, inside],
        "input",
        flops=INPUT_FLOPS,
        held=(4,),
        loose=(5,),
        copies=1,
    )
    maps = call(pair_kernel, [((4 * ch, 2 * cells), bf16)] * 2, [], [keep, to_core(give)], "pair")
    maps = [send(x, lambda s, z, c, n=n: (z, s ^ (2 * c + n), c)) for n, x in enumerate(maps)]
    folded = call(
        fold_kernel,
        [((rows, 2 * ch), bf16) for rows in piece_rows[1:]],
        [((last, 4 * TAPS * ch, 2 * ch), bf16)],
        shares[1:],
        "fold",
        held=range(last),
        copies=last,
    )
    chosen = call(
        choose_kernel,
        [((slice_rows, 2 * ch), bf16)] * 4,
        [],
        [*shares[0], *folded],
        "choose",
        loose=range(4),
    )
    pick = (core * cells + np.arange(cells))[:, None] == np.arange(2 * cells)[None, :]
    map_pick = pick.astype(bf16)
    pick = (core * ch + np.arange(ch))[:, None] == np.arange(2 * ch)[None, :]
    weight_grad, bias_grad, gain_grad, activations, input_grad = call(
        outputs_kernel,
        [((TAPS, ch, channels), f32), ((1, ch), f32), ((1, ch), f32)] + [((cells, channels), bf16)] * 2,
        [((TAPS, channels, 2 * ch), bf16), ((2, channels, 2 * cells), bf16)],
        [
            *with_core([chosen[0]] + [to_section(chosen[k], k) for k in (1, 2, 3)]),
            pick.astype(bf16),
            *with_core(after(maps, chosen)),
            map_pick,
        ],
        "outputs",
        loose=(8, 13),
        last=True,
    )
    weight_grad = weight_grad.reshape(3, 3, ch, channels).transpose(2, 0, 1, 3)[None]
    return (
        activations.reshape(1, 1, rows, cols, channels),
        input_grad.reshape(1, 1, rows, cols, channels),
        weight_grad,
        gain_grad,
        bias_grad,
    )


def fits_plane_plan(images, conv_weight, sections, dps):
    micro_total, images_total, rows, cols, channels = images.shape
    return (
        sections == 4
        and dps == 2 * sections
        and micro_total == sections
        and conv_weight.shape[0] == sections
        and images_total == dps
        and rows % 2 == 0
        and cols % 2 == 0
        and (rows * cols) % 64 == 0
        and channels == 512
    )


def solution(mesh):
    in_specs = (
        P(None, "dp", None, None, None),
        P(None, "dp"),
        P(),
        P("section", None, None, None, None),
        P("section", None),
        P("section", None),
        P(None, "dp", None, None, None),
    )
    out_specs = (
        P("section", "dp", None, None, None),
        P("section", "dp", None, None, None),
        P("section", "dp", None, None, None),
        P("section", "dp"),
        P("section", "dp"),
    )
    sections, dps = mesh.shape["section"], mesh.shape["dp"]

    def program(images, image_group, group_size, conv_weight, bn_gain, bn_bias, cotangent):
        plan = plane_shards if fits_plane_plan(images, conv_weight, sections, dps) else pipeline_shards
        sharded = jax.shard_map(plan, mesh=mesh, in_specs=in_specs, out_specs=out_specs, check_vma=False)
        return sharded(images, image_group, group_size, conv_weight, bn_gain, bn_bias, cotangent)

    return program
```
